32 devices in a mesh: gx: 4 (over z), gy: 8 (over y, x, core).
Axes of the slice: x: 2, y: 2, z: 4, core: 2. Of those that a mesh axis runs over, the one named last changes fastest.
Arguments:
- atm_blocks: bfloat16 [4, 8, 256, 6, 256], P('gx', 'gy'), may hold values from -6 to 6
- remap_weights: bfloat16 [4, 256, 4096], replicated, may hold values from -0.375 to 0.375
- ovl_source: int32 [4, 8, 512, 1], P('gx', 'gy'), may hold values from 0 to 31; in each aligned block of 512 rows (0 to 511, 512 to 1023, ..., all dimensions but the last counted through in order) at most 32 rows name the same one
- ovl_block: int32 [4, 8, 512], P('gx', 'gy'), may hold values from 0 to 255
- ovl_patch: int32 [4, 8, 512], P('gx', 'gy'), may hold values from 0 to 127
- ovl_weight: int32 [4, 8, 512], P('gx', 'gy'), may hold values from 0 to 3
- depth_field: float32 [4096, 4096], P('gx', 'gy'), may hold values from 0.5 to 2
- wet_mask: int32 [4096, 4096], P('gx', 'gy'), may hold values 0 or 1
- mom_x: float32 [4096, 4096], P('gx', 'gy'), may hold values from -2 to 2
- mom_y: float32 [4096, 4096], P('gx', 'gy'), may hold values from -2 to 2
- blend: float32 [], replicated, may hold values from 0.2 to 0.8
Outputs:
- surge_depth: float32 [4096, 4096], P('gx', 'gy')
- surge_mom_x: float32 [4096, 4096], P('gx', 'gy')
- surge_mom_y: float32 [4096, 4096], P('gx', 'gy')
The draws below stay inside these ranges and needn't reach their ends.
Inputs may be any that keep to these rules, and one draw needn't show every extreme that they name: `ovl_source`: among the 512 entries of one device, no source device is named more than 32 times, a bound that some block reaches.
All inputs are finite; a program needn't handle non-finite values. No bound on the sum of `wet_mask` on one device may be relied on, other than what follows from the above.
Results may differ from the reference program's by a relative error of at most 0.004.
Values may be sent and summed in bfloat16 or wider, within the bound.
No kernel may reach another device: no remote copies, remote signals or barrier semaphores. Data moves between devices by JAX's collectives and lax.ppermute only.
A program may use at most 192 MiB of HBM per device.

```python
import math
import jax
import jax.numpy as jnp
import numpy as np
from jax import lax

PATCH = 64
ABLK = 256
NW = 4
BPX = 16
BPY = 8
NB = 256
ENT = 512
CAP = 32
NX = 4096
NY = 4096
N_GX = 4
N_GY = 8
DEVICES = 32


def place_ends(array, rng, least, high):
    index_at = [jax.random.randint(jax.random.fold_in(rng, axis), (), 0, length) for axis, length in enumerate(array.shape)]
    widest = array.shape.index(max(array.shape))
    neighbour = index_at[:widest] + [(index_at[widest] + 1) % array.shape[widest]] + index_at[widest + 1:]
    return array.at[tuple(index_at)].set(least).at[tuple(neighbour)].set(high)


def shard_levels(rng, shape, shards, least, top_value):
    loudness = 1.0
    for axis_at, blocks in shards:
        draws = jax.random.uniform(jax.random.fold_in(jax.random.fold_in(rng, 6), axis_at), (blocks,), jnp.float32, least / len(shards), top_value / len(shards))
        loudness = loudness * jnp.repeat(jnp.exp(draws), shape[axis_at] // blocks).reshape((-1,) + (1,) * (len(shape) - 1 - axis_at))
    return loudness


def shared_out(key, own, number, rows, number_of, top, most, lean):
    order = jax.random.permutation(key, number_of)
    heavy_load, usual = load_shares(number_of, rows * top, most, lean, True), load_shares(number_of, rows * top, most, lean, False)
    places = jnp.arange(number_of)

    def named(lengths, offset_by):
        used = int((lengths > 0).sum())
        fixed = max(1, used // 4)
        moved = fixed + (places - fixed + offset_by * (used - fixed)) % max(1, number_of - fixed)
        return jnp.zeros((number_of,), jnp.int32).at[order[jnp.where(places < fixed, places, moved)]].set(jnp.asarray(lengths, jnp.int32))

    lengths = jnp.where(number % 4 == 0, named(heavy_load, number // 4), named(usual, number - number // 4 - 1))
    mixed = jax.random.permutation(jax.random.fold_in(own, 3), number_of)
    giver, sink = mixed[0:number_of // 2 * 2:2], mixed[1:number_of // 2 * 2:2]
    room = jnp.minimum(lengths[giver] - 1, most - lengths[sink]) // 2
    room = jnp.where((giver == order[0]) | (sink == order[0]) | (lengths[sink] == 0), 0, jnp.maximum(room, 0))
    moved = jax.random.randint(jax.random.fold_in(own, 4), (number_of // 2,), 0, 1 << 20) % (room + 1)
    lengths = lengths.at[giver].add(-moved).at[sink].add(moved)
    labels = jnp.searchsorted(jnp.cumsum(lengths), jnp.arange(rows * top), side="right").astype(jnp.int32)
    grid = labels.reshape(top, rows).T
    grid = grid[jax.random.permutation(jax.random.fold_in(own, 1), rows)]
    offset_by = jax.random.randint(jax.random.fold_in(own, 2), (rows, 1), 0, top)
    return jnp.take_along_axis(grid, (jnp.arange(top)[None, :] + offset_by) % top, axis=1)


def load_shares(count, total, bound, skew, full):
    loads = [(1 << 20) // math.isqrt(rank ** skew) + 1 for rank in range(1, count + 1)]
    largest = bound if full else min(bound, max(-(-total // count), total * loads[0] // sum(loads)))
    least = 1 if total - largest >= count - 1 else 0
    holding, rest = [largest] + [least] * (count - 1), total - largest - least * (count - 1)
    while rest > 0:
        free = [i for i in range(1, count) if holding[i] < largest] or [i for i in range(1, count) if holding[i] < bound]
        whole, left = sum([loads[i] for i in free]), rest
        for i in free:
            addition = min(bound - holding[i], max(1, left * loads[i] // whole), rest)
            holding[i] = holding[i] + addition
            rest = rest - addition
    return np.array(holding)


def centred(stream_key, shape, deviation, bound, cuts=(), kind=jnp.bfloat16):
    level = shard_levels(stream_key, shape, cuts, -0.22, 0.18) if cuts else 1.0
    values = jax.random.normal(stream_key, shape, jnp.float32) * deviation * level
    return jnp.minimum(jnp.maximum(values, -bound), bound).astype(kind)


def setup_inputs(seed: int = 0) -> dict:
    streams_of = jax.random.split(jax.random.key(seed), 12)
    atm_blocks = centred(streams_of[0], (N_GX, N_GY, NB, 6, ABLK), 1.0, 6.0, ((0, 4), (1, 8)))
    remap_weights = centred(streams_of[1], (NW, ABLK, PATCH * PATCH), ABLK ** -0.5, 0.375)
    ovl_source_keys = jax.random.split(jax.random.fold_in(streams_of[2], 1), N_GX * N_GY * ENT // ENT)
    ovl_source_turns = jax.random.permutation(jax.random.fold_in(streams_of[2], 3), N_GX * N_GY * ENT // ENT)
    ovl_source = jax.vmap(lambda own, number: shared_out(jax.random.fold_in(streams_of[2], 2), own, number, ENT, DEVICES, 1, CAP, 2))(ovl_source_keys, ovl_source_turns).reshape((N_GX, N_GY, ENT, 1))
    ovl_block = place_ends(jax.random.randint(streams_of[3], (N_GX, N_GY, ENT), 0, NB), jax.random.fold_in(streams_of[3], 1), 0, NB - 1).astype(jnp.int32)
    ovl_patch = place_ends(jax.random.randint(streams_of[4], (N_GX, N_GY, ENT), 0, BPX * BPY), jax.random.fold_in(streams_of[4], 1), 0, (BPX * BPY) - 1).astype(jnp.int32)
    ovl_weight = place_ends(jax.random.randint(streams_of[5], (N_GX, N_GY, ENT), 0, NW), jax.random.fold_in(streams_of[5], 1), 0, NW - 1).astype(jnp.int32)
    depth_field = jnp.clip(0.5 + 1.5 * jax.random.uniform(streams_of[6], (NX, NY), jnp.float32) ** shard_levels(streams_of[6], (NX, NY), ((0, 4), (1, 8)), -0.2, 0.2), 0.5, 2.0)
    wet_mask = place_ends((jax.random.randint(streams_of[7], (NX, NY), 0, 5) < 4).astype(jnp.int32), jax.random.fold_in(streams_of[7], 1), 0, 1)
    mom_x = centred(streams_of[8], (NX, NY), 0.3, 2.0, ((0, 4), (1, 8)), jnp.float32)
    mom_y = centred(streams_of[9], (NX, NY), 0.3, 2.0, ((0, 4), (1, 8)), jnp.float32)
    blend = jnp.clip(jax.random.uniform(streams_of[10], (), jnp.float32, 0.2, 0.8), 0.2, 0.8)
    return {"atm_blocks": atm_blocks, "remap_weights": remap_weights, "ovl_source": ovl_source, "ovl_block": ovl_block, "ovl_patch": ovl_patch, "ovl_weight": ovl_weight, "depth_field": depth_field, "wet_mask": wet_mask, "mom_x": mom_x, "mom_y": mom_y, "blend": blend}


GRAV = 1.0
DT_DX = 0.2
TIME_STEP = 0.2
STRESS = 0.5
PRESS = 0.5

def morton_split(ids, row_bits, col_bits):
    rows = jnp.zeros_like(ids)
    cols = jnp.zeros_like(ids)
    used_r = 0
    used_c = 0
    position = 0
    while used_r < row_bits or used_c < col_bits:
        value = jnp.bitwise_and(jnp.right_shift(ids, position), 1)
        if used_r < row_bits and (used_c >= col_bits or position % 2 == 0):
            rows = rows + value * (1 << used_r)
            used_r += 1
        else:
            cols = cols + value * (1 << used_c)
            used_c += 1
        position += 1
    return (rows, cols)

def fluctuations(hl, nl, tl, hr, nr, tr):
    wet_l = hl > 0.0
    wet_r = hr > 0.0
    h_left = jnp.where(wet_l, hl, jnp.where(wet_r, hr, 1.0))
    n_left = jnp.where(wet_l, nl, jnp.where(wet_r, -nr, 0.0))
    t_left = jnp.where(wet_l, tl, jnp.where(wet_r, tr, 0.0))
    h_right = jnp.where(wet_r, hr, jnp.where(wet_l, hl, 1.0))
    n_right = jnp.where(wet_r, nr, jnp.where(wet_l, -nl, 0.0))
    t_right = jnp.where(wet_r, tr, jnp.where(wet_l, tl, 0.0))
    root_l = jnp.sqrt(h_left)
    root_r = jnp.sqrt(h_right)
    total = root_l + root_r
    u_bar = (root_l * (n_left / h_left) + root_r * (n_right / h_right)) / total
    v_bar = (root_l * (t_left / h_left) + root_r * (t_right / h_right)) / total
    c_bar = jnp.sqrt(GRAV * 0.5 * (h_left + h_right))
    delta_h = h_right - h_left
    delta_n = n_right - n_left
    delta_t = t_right - t_left
    alpha_one = ((u_bar + c_bar) * delta_h - delta_n) / (2.0 * c_bar)
    alpha_three = (delta_n - (u_bar - c_bar) * delta_h) / (2.0 * c_bar)
    alpha_two = delta_t - v_bar * delta_h
    speed_one = u_bar - c_bar
    speed_three = u_bar + c_bar

    def waves(s_one, s_two, s_three):
        part_h = s_one * alpha_one + s_three * alpha_three
        part_n = s_one * alpha_one * speed_one + s_three * alpha_three * speed_three
        part_t = part_h * v_bar + s_two * alpha_two
        return (part_h, part_n, part_t)
    left_going = waves(jnp.minimum(speed_one, 0.0), jnp.minimum(u_bar, 0.0), jnp.minimum(speed_three, 0.0))
    right_going = waves(jnp.maximum(speed_one, 0.0), jnp.maximum(u_bar, 0.0), jnp.maximum(speed_three, 0.0))
    return (left_going, right_going)

def advance(padded, wind):
    depth = padded[0]
    momx = padded[1]
    momy = padded[2]
    press = padded[3]
    left_x, right_x = fluctuations(depth[:-1, 1:-1], momx[:-1, 1:-1], momy[:-1, 1:-1], depth[1:, 1:-1], momx[1:, 1:-1], momy[1:, 1:-1])
    left_y, right_y = fluctuations(depth[1:-1, :-1], momy[1:-1, :-1], momx[1:-1, :-1], depth[1:-1, 1:], momy[1:-1, 1:], momx[1:-1, 1:])
    change_h = right_x[0][:-1] + left_x[0][1:] + right_y[0][:, :-1] + left_y[0][:, 1:]
    change_x = right_x[1][:-1] + left_x[1][1:] + right_y[2][:, :-1] + left_y[2][:, 1:]
    change_y = right_x[2][:-1] + left_x[2][1:] + right_y[1][:, :-1] + left_y[1][:, 1:]
    old_h = depth[1:-1, 1:-1]
    wet = old_h > 0.0
    grad_x = 0.5 * (press[2:, 1:-1] - press[:-2, 1:-1])
    grad_y = 0.5 * (press[1:-1, 2:] - press[1:-1, :-2])
    wind_x = wind[0]
    wind_y = wind[1]
    speed = jnp.sqrt(wind_x * wind_x + wind_y * wind_y)
    new_h = old_h - DT_DX * change_h
    new_x = momx[1:-1, 1:-1] - DT_DX * change_x + TIME_STEP * (STRESS * speed * wind_x - PRESS * old_h * grad_x)
    new_y = momy[1:-1, 1:-1] - DT_DX * change_y + TIME_STEP * (STRESS * speed * wind_y - PRESS * old_h * grad_y)
    return (jnp.where(wet, new_h, 0.0), jnp.where(wet, new_x, 0.0), jnp.where(wet, new_y, 0.0))

def arrange(fields):
    placed = fields.reshape(3, BPX, BPY, PATCH, PATCH).transpose(0, 1, 3, 2, 4)
    return placed.reshape(3, BPX * PATCH, BPY * PATCH)

def reference(atm_blocks, remap_weights, ovl_source, ovl_block, ovl_patch, ovl_weight, depth_field, wet_mask, mom_x, mom_y, blend):
    devices = N_GX * N_GY
    npatch = BPX * BPY
    raw_tiles = atm_blocks.reshape(devices * NB, 2, 3 * ABLK).astype(jnp.float32)
    tiles = ((1.0 - blend) * raw_tiles[:, 0] + blend * raw_tiles[:, 1]).astype(jnp.bfloat16)
    sources = ovl_source.reshape(devices, -1)
    blocks = ovl_block.reshape(devices, -1)
    patches = ovl_patch.reshape(devices, -1)
    weight_ids = ovl_weight.reshape(devices, -1)
    row_bits = BPX.bit_length() - 1
    col_bits = BPY.bit_length() - 1
    weights_wide = remap_weights.astype(jnp.float32)
    categories = jnp.arange(NW * npatch, dtype=jnp.int32)

    def one_device(inputs):
        source, block, patch, weight_id = inputs
        gathered = tiles[source * NB + block]
        rows, cols = morton_split(patch, row_bits, col_bits)
        label = weight_id * npatch + rows * BPY + cols
        select = (label[None, :] == categories[:, None]).astype(jnp.bfloat16)
        summed = jnp.dot(select, gathered, preferred_element_type=jnp.float32).astype(jnp.bfloat16)
        summed = summed.reshape(NW, npatch, 3, ABLK).astype(jnp.float32)
        fields = jnp.einsum('wpca,wax->cpx', summed, weights_wide, precision=lax.Precision.HIGHEST)
        return arrange(fields)
    fields = lax.map(one_device, (sources, blocks, patches, weight_ids))
    fields = fields.reshape(N_GX, N_GY, 3, BPX * PATCH, BPY * PATCH).transpose(2, 0, 3, 1, 4).reshape(3, NX, NY)
    wet = wet_mask == 1
    depth = jnp.where(wet, depth_field, 0.0)
    momx = jnp.where(wet, mom_x, 0.0)
    momy = jnp.where(wet, mom_y, 0.0)
    padded = jnp.pad(jnp.stack([depth, momx, momy, fields[2]]), ((0, 0), (1, 1), (1, 1)))
    band = BPX * PATCH

    def one_band(index):
        start = (index * band).astype(jnp.int32)
        zero = jnp.zeros((), jnp.int32)
        piece = lax.dynamic_slice(padded, (zero, start, zero), (4, band + 2, NY + 2))
        wind = lax.dynamic_slice(fields, (zero, start, zero), (2, band, NY))
        return jnp.stack(advance(piece, wind))
    result = lax.map(one_band, jnp.arange(N_GX, dtype=jnp.int32))
    result = result.transpose(1, 0, 2, 3).reshape(3, NX, NY)
    return (result[0], result[1], result[2])
```

```python
import functools

import jax
import jax.numpy as jnp
from jax import lax
from jax.experimental import pallas as pl
from jax.experimental.pallas import tpu as pltpu
from jax.sharding import PartitionSpec as P

PATCH = 64
ABLK = 256
NW = 4
BPX = 16
BPY = 8
NPATCH = BPX * BPY

GRAV = 1.0
DT_DX = 0.2
TIME_STEP = 0.2
STRESS = 0.5
PRESS = 0.5

F32 = jnp.float32
BF16 = jnp.bfloat16
VMEM = pl.BlockSpec(memory_space=pltpu.VMEM)
SMEM = pl.BlockSpec(memory_space=pltpu.SMEM)
LANES = 128
TILE = 8
HALVES = BPX // TILE
QUADS = BPY // 2
SLAB = HALVES * QUADS * TILE


def params(limit=56 << 20, **kw):
    return pltpu.CompilerParams(vmem_limit_bytes=limit, **kw)


def iota(shape, dim):
    return lax.broadcasted_iota(jnp.int32, shape, dim)


def rank_kernel(capacity, src_ref, blk_ref, pat_ref, wgt_ref, want_ref, lab_ref):
    devices = want_ref.shape[0]
    src = src_ref[...]
    ent = src.shape[1]
    hits = (iota((devices, ent), 0) == src).astype(F32)
    order = (iota((ent, ent), 0) <= iota((ent, ent), 1)).astype(BF16)
    ranks = jnp.dot(hits.astype(BF16), order, preferred_element_type=F32)
    mine = jnp.sum(hits * ranks, axis=0, keepdims=True).astype(jnp.int32) - 1
    place = iota((capacity, ent), 0) == mine
    pat = pat_ref[...]
    row_bits = BPX.bit_length() - 1
    col_bits = BPY.bit_length() - 1
    rows = jnp.zeros_like(pat)
    cols = jnp.zeros_like(pat)
    used_r = used_c = position = 0
    while used_r < row_bits or used_c < col_bits:
        value = jnp.bitwise_and(jnp.right_shift(pat, position), 1)
        if used_r < row_bits and (used_c >= col_bits or position % 2 == 0):
            rows = rows + value * (1 << used_r)
            used_r += 1
        else:
            cols = cols + value * (1 << used_c)
            used_c += 1
        position += 1

    def spread(row):
        picked = jnp.where(place, row.astype(F32), 0.0).astype(BF16)
        return lax.dot_general(
            hits.astype(BF16), picked, (((1,), (1,)), ((), ())),
            preferred_element_type=F32,
        ).astype(jnp.int32)

    want_ref[...] = spread(blk_ref[...])
    slot = spread(cols * BPX + rows)
    group = spread(wgt_ref[...] + 1)
    lab_ref[...] = jnp.where(group > 0, (group - 1) * NPATCH + slot, -1)


def make_requests(src, blk, pat, wgt, devices, capacity):
    shape = jax.ShapeDtypeStruct((devices, capacity), jnp.int32)
    return pl.pallas_call(
        functools.partial(rank_kernel, capacity),
        out_shape=(shape, shape),
        in_specs=[VMEM] * 4,
        out_specs=(VMEM, VMEM),
        compiler_params=params(),
        name="requests",
    )(src, blk, pat, wgt)


def serve_kernel(blend_ref, asked_ref, atm_ref, press_ref, wind_ref):
    blend = blend_ref[0]
    keep = 1.0 - blend
    asked = asked_ref[...]
    pick = (asked == iota((asked.shape[0], atm_ref.shape[1]), 1)).astype(BF16)

    def mixed(k):
        first = atm_ref[k].astype(F32)
        second = atm_ref[3 + k].astype(F32)
        return (keep * first + blend * second).astype(BF16)

    press_ref[...] = jnp.dot(pick, mixed(2), preferred_element_type=F32).astype(BF16)
    for k in range(2):
        wind_ref[:, k * ABLK:(k + 1) * ABLK] = jnp.dot(
            pick, mixed(k), preferred_element_type=F32
        ).astype(BF16)


def serve(blend, asked, atm):
    slots = asked.shape[0]
    return pl.pallas_call(
        serve_kernel,
        out_shape=(
            jax.ShapeDtypeStruct((slots, ABLK), BF16),
            jax.ShapeDtypeStruct((slots, 2 * ABLK), BF16),
        ),
        in_specs=[SMEM, VMEM, VMEM],
        out_specs=(VMEM, VMEM),
        compiler_params=params(),
        name="serve",
    )(blend, asked, atm)


def edges_kernel(
    dl, ml, xl, yl, dr, mr, xr, yr, dt, mt, xt, yt, db, mb, xb, yb,
    top_ref, bottom_ref, left_ref, right_ref,
):
    def rows(d, m, x, y, at, out):
        wet = m[...] == 1
        for f, ref in enumerate((d, x, y)):
            out[f:f + 1, :] = jnp.where(wet, ref[...], 0.0)[at:at + 1]

    rows(dt, mt, xt, yt, 0, top_ref)
    rows(db, mb, xb, yb, TILE - 1, bottom_ref)
    lane = iota((LANES, LANES), 1)

    def step(b, carry):
        at = pl.ds(pl.multiple_of(b * LANES, LANES), LANES)
        wl = ml[at, :] == 1
        wr = mr[at, :] == 1
        packed = jnp.where(wl, dl[at, :], 0.0)
        packed = jnp.where(lane == 1, pltpu.roll(jnp.where(wl, xl[at, :], 0.0), 1, 1), packed)
        packed = jnp.where(lane == 2, pltpu.roll(jnp.where(wl, yl[at, :], 0.0), 2, 1), packed)
        packed = jnp.where(lane == 8, pltpu.roll(jnp.where(wr, dr[at, :], 0.0), 9, 1), packed)
        packed = jnp.where(lane == 9, pltpu.roll(jnp.where(wr, xr[at, :], 0.0), 10, 1), packed)
        packed = jnp.where(lane == 10, pltpu.roll(jnp.where(wr, yr[at, :], 0.0), 11, 1), packed)
        turned = packed.T
        left_ref[:, at] = turned[0:TILE]
        right_ref[:, at] = turned[TILE:2 * TILE]
        return carry

    lax.fori_loop(0, dl.shape[0] // LANES, step, 0)


def edge_cells(depth, mask, momx, momy):
    rows, cols = depth.shape
    fields = (depth, mask, momx, momy)
    left = pl.BlockSpec((rows, LANES), lambda i: (0, 0))
    right = pl.BlockSpec((rows, LANES), lambda i: (0, cols // LANES - 1))
    top = pl.BlockSpec((TILE, cols), lambda i: (0, 0))
    bottom = pl.BlockSpec((TILE, cols), lambda i: (rows // TILE - 1, 0))
    line = jax.ShapeDtypeStruct((TILE, cols), F32)
    column = jax.ShapeDtypeStruct((TILE, rows), F32)
    return pl.pallas_call(
        edges_kernel,
        grid=(1,),
        out_shape=(line, line, column, column),
        in_specs=[left] * 4 + [right] * 4 + [top] * 4 + [bottom] * 4,
        out_specs=(
            pl.BlockSpec((TILE, cols), lambda i: (0, 0)),
            pl.BlockSpec((TILE, cols), lambda i: (0, 0)),
            pl.BlockSpec((TILE, rows), lambda i: (0, 0)),
            pl.BlockSpec((TILE, rows), lambda i: (0, 0)),
        ),
        compiler_params=params(),
        name="edges",
    )(*(fields * 4))


def send(value, axis, step):
    count = lax.axis_size(axis)
    if step > 0:
        pairs = [(i, i + 1) for i in range(count - 1)]
    else:
        pairs = [(i + 1, i) for i in range(count - 1)]
    return lax.ppermute(value, axis, pairs)


def roe(hl, nl, tl, sl, ql, pl_, hr, nr, tr, sr, qr, pr, left=True, right=True):
    both = jnp.minimum(hl, hr) > 0.0
    half = jnp.where(both, 0.5, 1.0)
    level = (hl + hr) * half
    rc = lax.rsqrt(level)
    c = level * rc
    inv = 1.0 / (sl + sr)
    u = jnp.where(both, (ql + qr) * inv, 0.0)
    v = (pl_ + pr) * inv
    dh = jnp.where(both, hr - hl, 0.0)
    dn = (nr - nl) * (half + half)
    dt = jnp.where(both, tr - tl, 0.0)
    e = (dn - u * dh) * (0.5 * rc)
    mid = 0.5 * dh
    a1 = mid - e
    a3 = mid + e
    a2 = dt - v * dh
    s1 = u - c
    s3 = u + c
    w1 = s1 * a1
    w3 = s3 * a3
    w2 = u * a2
    zero = jnp.zeros_like(w1)
    n1 = s1 < 0.0
    n3 = s3 < 0.0
    n2 = u < 0.0
    out = []
    for going in ((True, left), (False, right)):
        if not going[1]:
            continue
        if going[0]:
            m1 = jnp.where(n1, w1, zero)
            m3 = jnp.where(n3, w3, zero)
            m2 = jnp.where(n2, w2, zero)
        else:
            m1 = jnp.where(n1, zero, w1)
            m3 = jnp.where(n3, zero, w3)
            m2 = jnp.where(n2, zero, w2)
        ph = m1 + m3
        out.append((ph, m1 * s1 + m3 * s3, ph * v + m2))
    return out


def stencil_kernel(
    d_ref, m_ref, x_ref, y_ref, up_ref, dn_ref, lh_ref, rh_ref, lo_ref, ro_ref,
    newh_ref, hu_ref, hv_ref, h_ref,
    sh, su, sv, ss, sq, sp, edge, ecol,
):
    rows, cols = d_ref.shape
    tiles = rows // TILE
    store = (sh, su, sv, ss, sq, sp)

    def derived(h, u, v):
        r = jnp.where(h > 0.0, lax.rsqrt(h), 0.0)
        return (h, u, v, h * r, u * r, v * r)

    for at, ref in ((0, up_ref), (rows + TILE, dn_ref)):
        vals = derived(ref[0:1, :], ref[1:2, :], ref[2:3, :])
        for dst, val in zip(store, vals):
            dst[at:at + TILE, :] = jnp.broadcast_to(val, (TILE, cols))

    def fill(t, carry):
        at = pl.ds(pl.multiple_of(t * TILE, TILE), TILE)
        wet = m_ref[at, :] == 1
        h = jnp.where(wet, d_ref[at, :], 0.0)
        u = jnp.where(wet, x_ref[at, :], 0.0)
        v = jnp.where(wet, y_ref[at, :], 0.0)
        to = pl.ds(pl.multiple_of(t * TILE + TILE, TILE), TILE)
        for dst, val in zip(store, derived(h, u, v)):
            dst[to, :] = val
        return carry

    lax.fori_loop(0, tiles, fill, 0, unroll=4)

    def line(ref):
        h, u, v, s, q, p = derived(ref[0:1, :], ref[1:2, :], ref[2:3, :])
        return (h, v, u, s, p, q)

    first = roe(*line(lh_ref), *line(lo_ref), left=False)[0]
    last = roe(*line(ro_ref), *line(rh_ref), right=False)[0]
    edge[...] = jnp.zeros_like(edge)
    for f, val in enumerate(first + last):
        edge[f:f + 1, :] = val

    def turn(b, carry):
        at = pl.ds(pl.multiple_of(b * LANES, LANES), LANES)
        ecol[at, :] = edge[:, at].T
        return carry

    lax.fori_loop(0, rows // LANES, turn, 0)

    row = iota((TILE, cols), 0)
    lane = iota((TILE, cols), 1)

    def down(value, before):
        rolled = pltpu.roll(value, 1, 0)
        return jnp.where(row == 0, before, rolled), rolled

    def load(start):
        return [ref[pl.ds(start, TILE), :] for ref in store]

    def below(now, after):
        return jnp.where(row == TILE - 1, pltpu.roll(after, TILE - 1, 0), pltpu.roll(now, TILE - 1, 0))

    def body(t, before):
        base = pl.multiple_of(t * TILE + TILE, TILE)
        now = load(base)
        after = load(pl.multiple_of(base + TILE, TILE))
        nxt = [below(a, b) for a, b in zip(now, after)]
        lx, rx = roe(*now, *nxt)
        moved, carry = [], []
        for a, b in zip(rx, before):
            m, c = down(a, b)
            moved.append(m)
            carry.append(c)
        h, u, v, s, q, p = now
        side = (h, v, u, s, p, q)
        other = [pltpu.roll(a, cols - 1, 1) for a in side]
        ly, ry = roe(*side, *other)
        at = pl.ds(pl.multiple_of(t * TILE, TILE), TILE)
        fl = ecol[at, :]
        ly = [jnp.where(lane == cols - 1, fl[:, 3 + f:4 + f], a) for f, a in enumerate(ly)]
        ry = [jnp.where(lane == 0, fl[:, f:f + 1], pltpu.roll(a, 1, 1)) for f, a in enumerate(ry)]
        ch = lx[0] + moved[0] + ly[0] + ry[0]
        cx = lx[1] + moved[1] + ly[2] + ry[2]
        cy = lx[2] + moved[2] + ly[1] + ry[1]
        wet = h > 0.0
        newh_ref[at, :] = jnp.where(wet, h - DT_DX * ch, 0.0)
        hu = u - DT_DX * cx
        hv = v - DT_DX * cy
        r = t // (PATCH // TILE)
        i0 = (t % (PATCH // TILE)) * TILE
        start = i0 * SLAB + (r // TILE) * (QUADS * TILE) + r % TILE
        for g in range(QUADS):
            to = pl.ds(start + g * TILE, TILE, stride=SLAB)
            cut = slice(g * LANES, (g + 1) * LANES)
            hu_ref[to, :] = hu[:, cut]
            hv_ref[to, :] = hv[:, cut]
            h_ref[to, :] = h[:, cut]
        return tuple(carry)

    lead = load(0)
    after = load(TILE)
    nxt = [below(a, b) for a, b in zip(lead, after)]
    rx = roe(*lead, *nxt, left=False)[0]
    start = tuple(pltpu.roll(a, 1, 0) for a in rx)
    lax.fori_loop(0, tiles, body, start)


def stencil(depth, mask, momx, momy, up, dn, lh, rh, lo, ro):
    rows, cols = depth.shape
    grouped = jax.ShapeDtypeStruct((rows * cols // LANES, LANES), F32)
    pad = pltpu.VMEM((rows + 2 * TILE, cols), F32)
    return pl.pallas_call(
        stencil_kernel,
        out_shape=(jax.ShapeDtypeStruct((rows, cols), F32), grouped, grouped, grouped),
        in_specs=[VMEM] * 10,
        out_specs=(VMEM,) * 4,
        scratch_shapes=[pad] * 6 + [pltpu.VMEM((LANES, rows), F32), pltpu.VMEM((rows, LANES), F32)],
        compiler_params=params(),
        cost_estimate=pl.CostEstimate(flops=200 * rows * cols, bytes_accessed=32 * rows * cols, transcendentals=0),
        name="stencil",
    )(depth, mask, momx, momy, up, dn, lh, rh, lo, ro)


def summed_of(lab, landed):
    select = (iota((NW * NPATCH, lab.shape[1]), 0) == lab).astype(BF16)
    return jnp.dot(select, landed, preferred_element_type=F32).astype(BF16)


def stack_left(left, summed, channels):
    for k in range(channels):
        for w in range(NW):
            left[k * NPATCH:(k + 1) * NPATCH, w * ABLK:(w + 1) * ABLK] = summed[
                w * NPATCH:(w + 1) * NPATCH, k * ABLK:(k + 1) * ABLK
            ]


def pair_rows(acc, k, t, half, g, low):
    cut = slice(t * LANES, (t + 1) * LANES)
    base = k * NPATCH + half * TILE
    even = acc[base + (2 * g) * BPX:base + (2 * g) * BPX + TILE, cut]
    odd = acc[base + (2 * g + 1) * BPX:base + (2 * g + 1) * BPX + TILE, cut]
    return (
        jnp.where(low, even, pltpu.roll(odd, LANES // 2, 1)),
        jnp.where(low, pltpu.roll(even, LANES // 2, 1), odd),
    )


def press_kernel(lab_ref, landed_ref, w_ref, out_ref, left, acc):
    @pl.when(pl.program_id(0) == 0)
    def _():
        stack_left(left, summed_of(lab_ref[...], landed_ref[...]), 1)

    acc[...] = jnp.dot(left[...], w_ref[...], preferred_element_type=F32)
    low = iota((TILE, LANES), 1) < LANES // 2
    for t in range(TILE // 2):
        for half in range(HALVES):
            for g in range(QUADS):
                pair = pair_rows(acc, 0, t, half, g, low)
                for odd in range(2):
                    at = (2 * t + odd) * SLAB + (half * QUADS + g) * TILE
                    out_ref[at:at + TILE, :] = pair[odd]


def pressure_field(lab, landed, weights):
    steps = PATCH // TILE
    chunk = TILE * PATCH
    cells = PATCH * SLAB
    return pl.pallas_call(
        press_kernel,
        grid=(steps,),
        out_shape=jax.ShapeDtypeStruct((cells, LANES), F32),
        in_specs=[
            pl.BlockSpec(lab.shape, lambda i: (0, 0)),
            pl.BlockSpec(landed.shape, lambda i: (0, 0)),
            pl.BlockSpec((NW * ABLK, chunk), lambda i: (0, i)),
        ],
        out_specs=pl.BlockSpec((cells // steps, LANES), lambda i: (i, 0)),
        scratch_shapes=[
            pltpu.VMEM((NPATCH, NW * ABLK), BF16),
            pltpu.VMEM((NPATCH, chunk), F32),
        ],
        compiler_params=params(),
        cost_estimate=pl.CostEstimate(
            flops=2 * NPATCH * NW * ABLK * PATCH * PATCH, bytes_accessed=12 << 20, transcendentals=0
        ),
        name="pressure",
    )(lab, landed, weights)


def press_edges_kernel(p_ref, top_ref, bottom_ref, left_ref, right_ref):
    last = (PATCH - 1) * SLAB
    for g in range(QUADS):
        cut = slice(g * LANES, (g + 1) * LANES)
        top_ref[:, cut] = p_ref[g * TILE:(g + 1) * TILE, :]
        at = last + (QUADS + g) * TILE
        bottom_ref[:, cut] = pltpu.roll(p_ref[at:at + TILE, :], 1, 0)
    lane = iota((LANES, LANES), 1)
    per = LANES // (HALVES * TILE)
    for b in range(PATCH // per):
        firsts, lasts = [], []
        for i in range(b * per, (b + 1) * per):
            for half in range(HALVES):
                at = i * SLAB + half * QUADS * TILE
                firsts.append(p_ref[at:at + TILE, :])
                at = at + (QUADS - 1) * TILE
                lasts.append(p_ref[at:at + TILE, :])
        packed = jnp.where(
            lane == TILE,
            pltpu.roll(jnp.concatenate(lasts, axis=0), TILE + 1, 1),
            jnp.concatenate(firsts, axis=0),
        )
        turned = packed.T
        left_ref[:, b * LANES:(b + 1) * LANES] = turned[0:TILE]
        right_ref[:, b * LANES:(b + 1) * LANES] = turned[TILE:2 * TILE]


def press_edges(p):
    rows = PATCH * BPX
    cols = PATCH * BPY
    line = jax.ShapeDtypeStruct((TILE, cols), F32)
    column = jax.ShapeDtypeStruct((TILE, rows), F32)
    return pl.pallas_call(
        press_edges_kernel,
        out_shape=(line, line, column, column),
        in_specs=[VMEM],
        out_specs=(VMEM,) * 4,
        compiler_params=params(),
        name="press_edges",
    )(p)


def gradient_kernel(
    p_ref, hu_ref, hv_ref, h_ref, up_ref, dn_ref, lh_ref, rh_ref,
    ox_ref, oy_ref, fac_ref, turned, ends,
):
    stacked = jnp.concatenate([lh_ref[...], rh_ref[...]], axis=0)
    for b in range(stacked.shape[1] // LANES):
        cut = slice(b * LANES, (b + 1) * LANES)
        square = jnp.concatenate(
            [stacked[:, cut], jnp.zeros((LANES - 2 * TILE, LANES), F32)], axis=0
        )
        turned[cut, :] = square.T
    row = iota((BPX, LANES), 0)
    last = (PATCH - 1) * SLAB
    for g in range(QUADS):
        cut = slice(g * LANES, (g + 1) * LANES)
        for at, end, halo, shift, edge in (
            (last, 0, up_ref, 1, 0),
            (0, 1, dn_ref, BPX - 1, BPX - 1),
        ):
            parts = [
                p_ref[at + (half * QUADS + g) * TILE:at + (half * QUADS + g + 1) * TILE, :]
                for half in range(HALVES)
            ]
            whole = pltpu.roll(jnp.concatenate(parts, axis=0), shift, 0)
            whole = jnp.where(row == edge, jnp.broadcast_to(halo[0:1, cut], (BPX, LANES)), whole)
            for half in range(HALVES):
                to = end * SLAB + (half * QUADS + g) * TILE
                ends[to:to + TILE, :] = whole[half * TILE:(half + 1) * TILE]

    lane = iota((TILE, LANES), 1)

    def cells(i, before, after):
        at = i * SLAB
        for half in range(HALVES):
            rows = pl.ds(pl.multiple_of((i * HALVES + half) * TILE, TILE), TILE)
            sides = turned[rows, :]
            tiles = [
                p_ref[pl.ds(pl.multiple_of(at + (half * QUADS + g) * TILE, TILE), TILE), :]
                for g in range(QUADS)
            ]
            ups = [pltpu.roll(a, 1, 1) for a in tiles]
            downs = [pltpu.roll(a, LANES - 1, 1) for a in tiles]
            for g in range(QUADS):
                off = (half * QUADS + g) * TILE
                here = pl.ds(pl.multiple_of(at + off, TILE), TILE)
                prev = jnp.where(lane == 0, ups[g - 1] if g else sides[:, 0:1], ups[g])
                if g < QUADS - 1:
                    nxt = jnp.where(lane == LANES - 1, downs[g + 1], downs[g])
                else:
                    nxt = jnp.where(lane == LANES - 1, sides[:, TILE:TILE + 1], downs[g])
                h = h_ref[here, :]
                wet = h > 0.0
                scale = (TIME_STEP * PRESS * 0.5) * h
                gx = after(off) - before(off)
                ox_ref[here, :] = jnp.where(wet, hu_ref[here, :] - scale * gx, 0.0)
                oy_ref[here, :] = jnp.where(wet, hv_ref[here, :] - scale * (nxt - prev), 0.0)
                fac_ref[here, :] = jnp.where(wet, TIME_STEP * STRESS, 0.0)

    def at_end(end):
        return lambda off: ends[end * SLAB + off:end * SLAB + off + TILE, :]

    def at_slab(i):
        return lambda off: p_ref[pl.ds(pl.multiple_of(i * SLAB + off, TILE), TILE), :]

    cells(0, at_end(0), at_slab(1))
    lax.fori_loop(
        1, PATCH - 1, lambda i, c: (cells(i, at_slab(i - 1), at_slab(i + 1)), c)[1], 0
    )
    cells(PATCH - 1, at_slab(PATCH - 2), at_end(1))


def gradient(p, hu, hv, h, up, dn, lh, rh):
    grouped = jax.ShapeDtypeStruct(p.shape, F32)
    return pl.pallas_call(
        gradient_kernel,
        out_shape=(grouped,) * 3,
        in_specs=[VMEM] * 8,
        out_specs=(VMEM,) * 3,
        scratch_shapes=[
            pltpu.VMEM((PATCH * BPX, LANES), F32),
            pltpu.VMEM((2 * SLAB, LANES), F32),
        ],
        compiler_params=params(),
        cost_estimate=pl.CostEstimate(
            flops=20 * p.size, bytes_accessed=28 * p.size, transcendentals=0
        ),
        name="gradient",
    )(p, hu, hv, h, up, dn, lh, rh)


def wind_kernel(lab_ref, landed_ref, w_ref, hu_ref, hv_ref, fac_ref, ox_ref, oy_ref, left, acc, sx, sy):
    @pl.when(pl.program_id(0) == 0)
    def _():
        stack_left(left, summed_of(lab_ref[...], landed_ref[...]), 2)

    acc[...] = jnp.dot(left[...], w_ref[...], preferred_element_type=F32)
    low = iota((TILE, LANES), 1) < LANES // 2
    for t in range(TILE // 2):
        for half in range(HALVES):
            for g in range(QUADS):
                xs = pair_rows(acc, 0, t, half, g, low)
                ys = pair_rows(acc, 1, t, half, g, low)
                for odd in range(2):
                    i = 2 * t + odd
                    at = i * SLAB + (half * QUADS + g) * TILE
                    wx = xs[odd]
                    wy = ys[odd]
                    speed = jnp.sqrt(wx * wx + wy * wy) * fac_ref[at:at + TILE, :]
                    to = pl.ds(half * TILE * TILE + i, TILE, stride=TILE)
                    sx[g, to, :] = hu_ref[at:at + TILE, :] + speed * wx
                    sy[g, to, :] = hv_ref[at:at + TILE, :] + speed * wy
    for src, dst in ((sx, ox_ref), (sy, oy_ref)):
        for g in range(QUADS):
            for r in range(BPX):
                dst[r, :, g * LANES:(g + 1) * LANES] = src[g, r * TILE:(r + 1) * TILE, :]


def wind_field(lab, landed, weights, hu, hv, fac):
    steps = PATCH // TILE
    chunk = TILE * PATCH
    cols = BPY * PATCH
    slab = pl.BlockSpec((TILE * SLAB, LANES), lambda i: (i, 0))
    out = pl.BlockSpec((BPX, TILE, cols), lambda i: (0, i, 0))
    shape = jax.ShapeDtypeStruct((BPX, PATCH, cols), F32)
    return pl.pallas_call(
        wind_kernel,
        grid=(steps,),
        out_shape=(shape, shape),
        in_specs=[
            pl.BlockSpec(lab.shape, lambda i: (0, 0)),
            pl.BlockSpec(landed.shape, lambda i: (0, 0)),
            pl.BlockSpec((NW * ABLK, chunk), lambda i: (0, i)),
            slab, slab, slab,
        ],
        out_specs=(out, out),
        scratch_shapes=[
            pltpu.VMEM((2 * NPATCH, NW * ABLK), BF16),
            pltpu.VMEM((2 * NPATCH, chunk), F32),
            pltpu.VMEM((QUADS, BPX * TILE, LANES), F32),
            pltpu.VMEM((QUADS, BPX * TILE, LANES), F32),
        ],
        compiler_params=params(),
        cost_estimate=pl.CostEstimate(
            flops=4 * NPATCH * NW * ABLK * PATCH * PATCH, bytes_accessed=20 << 20, transcendentals=0
        ),
        name="wind",
    )(lab, landed, weights, hu, hv, fac)


def body(
    atm_blocks,
    remap_weights,
    ovl_source,
    ovl_block,
    ovl_patch,
    ovl_weight,
    depth_field,
    wet_mask,
    mom_x,
    mom_y,
    blend,
):
    devices = lax.axis_size("gx") * lax.axis_size("gy")
    entries = ovl_source.size
    capacity = 2 * entries // devices
    both = ("gx", "gy")
    want, lab = make_requests(
        ovl_source.reshape(1, entries), ovl_block.reshape(1, entries),
        ovl_patch.reshape(1, entries), ovl_weight.reshape(1, entries), devices, capacity,
    )
    asked = lax.all_to_all(want, both, split_axis=0, concat_axis=0, tiled=True)
    atm = atm_blocks.reshape(atm_blocks.shape[2:]).transpose(1, 0, 2)
    press, wind = serve(blend.reshape(1), asked.reshape(devices * capacity, 1), atm)

    def exchange(rows):
        parts = rows.reshape(devices, capacity, rows.shape[1])
        got = lax.all_to_all(parts, both, split_axis=0, concat_axis=0, tiled=True)
        return got.reshape(rows.shape)

    press = exchange(press)
    wind = exchange(wind)
    lab = lab.reshape(1, devices * capacity)

    top, bottom, left, right = edge_cells(depth_field, wet_mask, mom_x, mom_y)
    newh, hu, hv, h = stencil(
        depth_field, wet_mask, mom_x, mom_y,
        send(bottom, "gx", 1), send(top, "gx", -1),
        send(right, "gy", 1), send(left, "gy", -1), left, right,
    )
    weights = remap_weights.reshape(NW * ABLK, PATCH * PATCH)
    p = pressure_field(lab, press, weights)
    top, bottom, left, right = press_edges(p)
    hu, hv, fac = gradient(
        p, hu, hv, h,
        send(bottom, "gx", 1), send(top, "gx", -1),
        send(right, "gy", 1), send(left, "gy", -1),
    )
    new_x, new_y = wind_field(lab, wind, weights, hu, hv, fac)
    return (newh, new_x.reshape(newh.shape), new_y.reshape(newh.shape))


def solution(mesh):
    placed = (
        P("gx", "gy", None, None, None),
        P(),
        P("gx", "gy", None, None),
        P("gx", "gy", None),
        P("gx", "gy", None),
        P("gx", "gy", None),
        P("gx", "gy"),
        P("gx", "gy"),
        P("gx", "gy"),
        P("gx", "gy"),
        P(),
    )
    return jax.shard_map(
        body,
        mesh=mesh,
        in_specs=placed,
        out_specs=(P("gx", "gy"), P("gx", "gy"), P("gx", "gy")),
        check_vma=False,
    )
```

```python
import functools

import jax
import jax.numpy as jnp
from jax import lax
from jax.experimental import pallas as pl
from jax.experimental.pallas import tpu as pltpu
from jax.sharding import PartitionSpec as P

PATCH = 64
ABLK = 256
NW = 4
BPX = 16
BPY = 8
NPATCH = BPX * BPY

GRAV = 1.0
DT_DX = 0.2
TIME_STEP = 0.2
STRESS = 0.5
PRESS = 0.5

F32 = jnp.float32
BF16 = jnp.bfloat16
VMEM = pl.BlockSpec(memory_space=pltpu.VMEM)
SMEM = pl.BlockSpec(memory_space=pltpu.SMEM)
LANES = 128
TILE = 8
HALVES = BPX // TILE
QUADS = BPY // 2
SLAB = HALVES * QUADS * TILE


def params(limit=56 << 20, **kw):
    return pltpu.CompilerParams(vmem_limit_bytes=limit, **kw)


def iota(shape, dim):
    return lax.broadcasted_iota(jnp.int32, shape, dim)


def mix_kernel(blend_ref, atm_ref, press_ref, wind_ref):
    blend = blend_ref[0]
    keep = 1.0 - blend

    def mixed(k):
        first = atm_ref[k].astype(F32)
        second = atm_ref[3 + k].astype(F32)
        return (keep * first + blend * second).astype(BF16)

    press_ref[...] = mixed(2)
    for k in range(2):
        wind_ref[:, k * ABLK:(k + 1) * ABLK] = mixed(k)


def mix(blend, atm):
    blocks = atm.shape[1]
    return pl.pallas_call(
        mix_kernel,
        out_shape=(
            jax.ShapeDtypeStruct((blocks, ABLK), BF16),
            jax.ShapeDtypeStruct((blocks, 2 * ABLK), BF16),
        ),
        in_specs=[SMEM, VMEM],
        out_specs=(VMEM, VMEM),
        compiler_params=params(),
        name="mix",
    )(blend, atm)


def morton_slot(pat):
    row_bits = BPX.bit_length() - 1
    col_bits = BPY.bit_length() - 1
    rows = jnp.zeros_like(pat)
    cols = jnp.zeros_like(pat)
    used_r = used_c = position = 0
    while used_r < row_bits or used_c < col_bits:
        value = jnp.bitwise_and(jnp.right_shift(pat, position), 1)
        if used_r < row_bits and (used_c >= col_bits or position % 2 == 0):
            rows = rows + value * (1 << used_r)
            used_r += 1
        else:
            cols = cols + value * (1 << used_c)
            used_c += 1
        position += 1
    return cols * BPX + rows


STEP = 2048


def count_kernel(lab_ref, block_ref, out_ref):
    ent = lab_ref.shape[1]
    labels = (iota((NW * NPATCH, ent), 0) == lab_ref[...]).astype(BF16)
    base = pl.program_id(0) * STEP
    blocks = (iota((ent, STEP), 1) + base == block_ref[...]).astype(BF16)
    out_ref[...] = jnp.dot(labels, blocks, preferred_element_type=F32).astype(BF16)


def count_matrix(lab, block, total):
    ent = lab.shape[1]
    return pl.pallas_call(
        count_kernel,
        grid=(total // STEP,),
        out_shape=jax.ShapeDtypeStruct((NW * NPATCH, total), BF16),
        in_specs=[pl.BlockSpec((1, ent), lambda i: (0, 0)), pl.BlockSpec((ent, 1), lambda i: (0, 0))],
        out_specs=pl.BlockSpec((NW * NPATCH, STEP), lambda i: (0, i)),
        compiler_params=params(),
        name="counts",
    )(lab, block)


def sum_kernel(s_ref, tiles_ref, out_ref, acc):
    at = pl.program_id(0)

    @pl.when(at == 0)
    def _():
        acc[...] = jnp.zeros_like(acc)

    acc[...] += jnp.dot(s_ref[...], tiles_ref[...], preferred_element_type=F32)

    @pl.when(at == pl.num_programs(0) - 1)
    def _():
        out_ref[...] = acc[...].astype(BF16)


def summed_blocks(counts, tiles):
    total, width = tiles.shape
    labels = counts.shape[0]
    return pl.pallas_call(
        sum_kernel,
        grid=(total // STEP,),
        out_shape=jax.ShapeDtypeStruct((labels, width), BF16),
        in_specs=[
            pl.BlockSpec((labels, STEP), lambda i: (0, i)),
            pl.BlockSpec((STEP, width), lambda i: (i, 0)),
        ],
        out_specs=pl.BlockSpec((labels, width), lambda i: (0, 0)),
        scratch_shapes=[pltpu.VMEM((labels, width), F32)],
        compiler_params=params(),
        name="summed",
    )(counts, tiles)


def edges_kernel(
    dl, ml, xl, yl, dr, mr, xr, yr, dt, mt, xt, yt, db, mb, xb, yb,
    top_ref, bottom_ref, left_ref, right_ref,
):
    def rows(d, m, x, y, at, out):
        wet = m[...] == 1
        for f, ref in enumerate((d, x, y)):
            out[f:f + 1, :] = jnp.where(wet, ref[...], 0.0)[at:at + 1]

    rows(dt, mt, xt, yt, 0, top_ref)
    rows(db, mb, xb, yb, TILE - 1, bottom_ref)
    lane = iota((LANES, LANES), 1)

    def step(b, carry):
        at = pl.ds(pl.multiple_of(b * LANES, LANES), LANES)
        wl = ml[at, :] == 1
        wr = mr[at, :] == 1
        packed = jnp.where(wl, dl[at, :], 0.0)
        packed = jnp.where(lane == 1, pltpu.roll(jnp.where(wl, xl[at, :], 0.0), 1, 1), packed)
        packed = jnp.where(lane == 2, pltpu.roll(jnp.where(wl, yl[at, :], 0.0), 2, 1), packed)
        packed = jnp.where(lane == 8, pltpu.roll(jnp.where(wr, dr[at, :], 0.0), 9, 1), packed)
        packed = jnp.where(lane == 9, pltpu.roll(jnp.where(wr, xr[at, :], 0.0), 10, 1), packed)
        packed = jnp.where(lane == 10, pltpu.roll(jnp.where(wr, yr[at, :], 0.0), 11, 1), packed)
        turned = packed.T
        left_ref[:, at] = turned[0:TILE]
        right_ref[:, at] = turned[TILE:2 * TILE]
        return carry

    lax.fori_loop(0, dl.shape[0] // LANES, step, 0)


def edge_cells(depth, mask, momx, momy):
    rows, cols = depth.shape
    fields = (depth, mask, momx, momy)
    left = pl.BlockSpec((rows, LANES), lambda i: (0, 0))
    right = pl.BlockSpec((rows, LANES), lambda i: (0, cols // LANES - 1))
    top = pl.BlockSpec((TILE, cols), lambda i: (0, 0))
    bottom = pl.BlockSpec((TILE, cols), lambda i: (rows // TILE - 1, 0))
    line = jax.ShapeDtypeStruct((TILE, cols), F32)
    column = jax.ShapeDtypeStruct((TILE, rows), F32)
    return pl.pallas_call(
        edges_kernel,
        grid=(1,),
        out_shape=(line, line, column, column),
        in_specs=[left] * 4 + [right] * 4 + [top] * 4 + [bottom] * 4,
        out_specs=(
            pl.BlockSpec((TILE, cols), lambda i: (0, 0)),
            pl.BlockSpec((TILE, cols), lambda i: (0, 0)),
            pl.BlockSpec((TILE, rows), lambda i: (0, 0)),
            pl.BlockSpec((TILE, rows), lambda i: (0, 0)),
        ),
        compiler_params=params(),
        name="edges",
    )(*(fields * 4))


def send(value, axis, step):
    count = lax.axis_size(axis)
    if step > 0:
        pairs = [(i, i + 1) for i in range(count - 1)]
    else:
        pairs = [(i + 1, i) for i in range(count - 1)]
    return lax.ppermute(value, axis, pairs)


def roe(hl, nl, tl, sl, ql, pl_, hr, nr, tr, sr, qr, pr, left=True, right=True):
    both = jnp.minimum(hl, hr) > 0.0
    half = jnp.where(both, 0.5, 1.0)
    level = (hl + hr) * half
    rc = lax.rsqrt(level)
    c = level * rc
    inv = 1.0 / (sl + sr)
    u = jnp.where(both, (ql + qr) * inv, 0.0)
    v = (pl_ + pr) * inv
    dh = jnp.where(both, hr - hl, 0.0)
    dn = (nr - nl) * (half + half)
    dt = jnp.where(both, tr - tl, 0.0)
    e = (dn - u * dh) * (0.5 * rc)
    mid = 0.5 * dh
    a1 = mid - e
    a3 = mid + e
    a2 = dt - v * dh
    s1 = u - c
    s3 = u + c
    w1 = s1 * a1
    w3 = s3 * a3
    w2 = u * a2
    zero = jnp.zeros_like(w1)
    n1 = s1 < 0.0
    n3 = s3 < 0.0
    n2 = u < 0.0
    out = []
    for going in ((True, left), (False, right)):
        if not going[1]:
            continue
        if going[0]:
            m1 = jnp.where(n1, w1, zero)
            m3 = jnp.where(n3, w3, zero)
            m2 = jnp.where(n2, w2, zero)
        else:
            m1 = jnp.where(n1, zero, w1)
            m3 = jnp.where(n3, zero, w3)
            m2 = jnp.where(n2, zero, w2)
        ph = m1 + m3
        out.append((ph, m1 * s1 + m3 * s3, ph * v + m2))
    return out


def stencil_kernel(
    d_ref, m_ref, x_ref, y_ref, up_ref, dn_ref, lh_ref, rh_ref, lo_ref, ro_ref,
    newh_ref, hu_ref, hv_ref, h_ref,
    sh, su, sv, ss, sq, sp, edge, ecol,
):
    rows, cols = d_ref.shape
    tiles = rows // TILE
    store = (sh, su, sv, ss, sq, sp)

    def derived(h, u, v):
        r = jnp.where(h > 0.0, lax.rsqrt(h), 0.0)
        return (h, u, v, h * r, u * r, v * r)

    for at, ref in ((0, up_ref), (rows + TILE, dn_ref)):
        vals = derived(ref[0:1, :], ref[1:2, :], ref[2:3, :])
        for dst, val in zip(store, vals):
            dst[at:at + TILE, :] = jnp.broadcast_to(val, (TILE, cols))

    def fill(t, carry):
        at = pl.ds(pl.multiple_of(t * TILE, TILE), TILE)
        wet = m_ref[at, :] == 1
        h = jnp.where(wet, d_ref[at, :], 0.0)
        u = jnp.where(wet, x_ref[at, :], 0.0)
        v = jnp.where(wet, y_ref[at, :], 0.0)
        to = pl.ds(pl.multiple_of(t * TILE + TILE, TILE), TILE)
        for dst, val in zip(store, derived(h, u, v)):
            dst[to, :] = val
        return carry

    lax.fori_loop(0, tiles, fill, 0, unroll=4)

    def line(ref):
        h, u, v, s, q, p = derived(ref[0:1, :], ref[1:2, :], ref[2:3, :])
        return (h, v, u, s, p, q)

    first = roe(*line(lh_ref), *line(lo_ref), left=False)[0]
    last = roe(*line(ro_ref), *line(rh_ref), right=False)[0]
    edge[...] = jnp.zeros_like(edge)
    for f, val in enumerate(first + last):
        edge[f:f + 1, :] = val

    def turn(b, carry):
        at = pl.ds(pl.multiple_of(b * LANES, LANES), LANES)
        ecol[at, :] = edge[:, at].T
        return carry

    lax.fori_loop(0, rows // LANES, turn, 0)

    row = iota((TILE, cols), 0)
    lane = iota((TILE, cols), 1)

    def down(value, before):
        rolled = pltpu.roll(value, 1, 0)
        return jnp.where(row == 0, before, rolled), rolled

    def load(start):
        return [ref[pl.ds(start, TILE), :] for ref in store]

    def below(now, after):
        return jnp.where(row == TILE - 1, pltpu.roll(after, TILE - 1, 0), pltpu.roll(now, TILE - 1, 0))

    def body(t, before):
        base = pl.multiple_of(t * TILE + TILE, TILE)
        now = load(base)
        after = load(pl.multiple_of(base + TILE, TILE))
        nxt = [below(a, b) for a, b in zip(now, after)]
        lx, rx = roe(*now, *nxt)
        moved, carry = [], []
        for a, b in zip(rx, before):
            m, c = down(a, b)
            moved.append(m)
            carry.append(c)
        h, u, v, s, q, p = now
        side = (h, v, u, s, p, q)
        other = [pltpu.roll(a, cols - 1, 1) for a in side]
        ly, ry = roe(*side, *other)
        at = pl.ds(pl.multiple_of(t * TILE, TILE), TILE)
        fl = ecol[at, :]
        ly = [jnp.where(lane == cols - 1, fl[:, 3 + f:4 + f], a) for f, a in enumerate(ly)]
        ry = [jnp.where(lane == 0, fl[:, f:f + 1], pltpu.roll(a, 1, 1)) for f, a in enumerate(ry)]
        ch = lx[0] + moved[0] + ly[0] + ry[0]
        cx = lx[1] + moved[1] + ly[2] + ry[2]
        cy = lx[2] + moved[2] + ly[1] + ry[1]
        wet = h > 0.0
        newh_ref[at, :] = jnp.where(wet, h - DT_DX * ch, 0.0)
        hu = u - DT_DX * cx
        hv = v - DT_DX * cy
        r = t // (PATCH // TILE)
        i0 = (t % (PATCH // TILE)) * TILE
        start = i0 * SLAB + (r // TILE) * (QUADS * TILE) + r % TILE
        for g in range(QUADS):
            to = pl.ds(start + g * TILE, TILE, stride=SLAB)
            cut = slice(g * LANES, (g + 1) * LANES)
            hu_ref[to, :] = hu[:, cut]
            hv_ref[to, :] = hv[:, cut]
            h_ref[to, :] = h[:, cut]
        return tuple(carry)

    lead = load(0)
    after = load(TILE)
    nxt = [below(a, b) for a, b in zip(lead, after)]
    rx = roe(*lead, *nxt, left=False)[0]
    start = tuple(pltpu.roll(a, 1, 0) for a in rx)
    lax.fori_loop(0, tiles, body, start)


def stencil(depth, mask, momx, momy, up, dn, lh, rh, lo, ro):
    rows, cols = depth.shape
    grouped = jax.ShapeDtypeStruct((rows * cols // LANES, LANES), F32)
    pad = pltpu.VMEM((rows + 2 * TILE, cols), F32)
    return pl.pallas_call(
        stencil_kernel,
        out_shape=(jax.ShapeDtypeStruct((rows, cols), F32), grouped, grouped, grouped),
        in_specs=[VMEM] * 10,
        out_specs=(VMEM,) * 4,
        scratch_shapes=[pad] * 6 + [pltpu.VMEM((LANES, rows), F32), pltpu.VMEM((rows, LANES), F32)],
        compiler_params=params(),
        cost_estimate=pl.CostEstimate(flops=200 * rows * cols, bytes_accessed=32 * rows * cols, transcendentals=0),
        name="stencil",
    )(depth, mask, momx, momy, up, dn, lh, rh, lo, ro)


def stack_left(left, summed, channels):
    for k in range(channels):
        for w in range(NW):
            left[k * NPATCH:(k + 1) * NPATCH, w * ABLK:(w + 1) * ABLK] = summed[
                w * NPATCH:(w + 1) * NPATCH, k * ABLK:(k + 1) * ABLK
            ]


def pair_rows(acc, k, t, half, g, low):
    cut = slice(t * LANES, (t + 1) * LANES)
    base = k * NPATCH + half * TILE
    even = acc[base + (2 * g) * BPX:base + (2 * g) * BPX + TILE, cut]
    odd = acc[base + (2 * g + 1) * BPX:base + (2 * g + 1) * BPX + TILE, cut]
    return (
        jnp.where(low, even, pltpu.roll(odd, LANES // 2, 1)),
        jnp.where(low, pltpu.roll(even, LANES // 2, 1), odd),
    )


def press_kernel(summed_ref, w_ref, out_ref, left, acc):
    @pl.when(pl.program_id(0) == 0)
    def _():
        stack_left(left, summed_ref, 1)

    acc[...] = jnp.dot(left[...], w_ref[...], preferred_element_type=F32)
    low = iota((TILE, LANES), 1) < LANES // 2
    for t in range(TILE // 2):
        for half in range(HALVES):
            for g in range(QUADS):
                pair = pair_rows(acc, 0, t, half, g, low)
                for odd in range(2):
                    at = (2 * t + odd) * SLAB + (half * QUADS + g) * TILE
                    out_ref[at:at + TILE, :] = pair[odd]


def pressure_field(summed, weights):
    steps = PATCH // TILE
    chunk = TILE * PATCH
    cells = PATCH * SLAB
    return pl.pallas_call(
        press_kernel,
        grid=(steps,),
        out_shape=jax.ShapeDtypeStruct((cells, LANES), F32),
        in_specs=[
            pl.BlockSpec(summed.shape, lambda i: (0, 0)),
            pl.BlockSpec((NW * ABLK, chunk), lambda i: (0, i)),
        ],
        out_specs=pl.BlockSpec((cells // steps, LANES), lambda i: (i, 0)),
        scratch_shapes=[
            pltpu.VMEM((NPATCH, NW * ABLK), BF16),
            pltpu.VMEM((NPATCH, chunk), F32),
        ],
        compiler_params=params(),
        cost_estimate=pl.CostEstimate(
            flops=2 * NPATCH * NW * ABLK * PATCH * PATCH, bytes_accessed=12 << 20, transcendentals=0
        ),
        name="pressure",
    )(summed, weights)


def press_edges_kernel(p_ref, top_ref, bottom_ref, left_ref, right_ref):
    last = (PATCH - 1) * SLAB
    for g in range(QUADS):
        cut = slice(g * LANES, (g + 1) * LANES)
        top_ref[:, cut] = p_ref[g * TILE:(g + 1) * TILE, :]
        at = last + (QUADS + g) * TILE
        bottom_ref[:, cut] = pltpu.roll(p_ref[at:at + TILE, :], 1, 0)
    lane = iota((LANES, LANES), 1)
    per = LANES // (HALVES * TILE)
    for b in range(PATCH // per):
        firsts, lasts = [], []
        for i in range(b * per, (b + 1) * per):
            for half in range(HALVES):
                at = i * SLAB + half * QUADS * TILE
                firsts.append(p_ref[at:at + TILE, :])
                at = at + (QUADS - 1) * TILE
                lasts.append(p_ref[at:at + TILE, :])
        packed = jnp.where(
            lane == TILE,
            pltpu.roll(jnp.concatenate(lasts, axis=0), TILE + 1, 1),
            jnp.concatenate(firsts, axis=0),
        )
        turned = packed.T
        left_ref[:, b * LANES:(b + 1) * LANES] = turned[0:TILE]
        right_ref[:, b * LANES:(b + 1) * LANES] = turned[TILE:2 * TILE]


def press_edges(p):
    rows = PATCH * BPX
    cols = PATCH * BPY
    line = jax.ShapeDtypeStruct((TILE, cols), F32)
    column = jax.ShapeDtypeStruct((TILE, rows), F32)
    return pl.pallas_call(
        press_edges_kernel,
        out_shape=(line, line, column, column),
        in_specs=[VMEM],
        out_specs=(VMEM,) * 4,
        compiler_params=params(),
        name="press_edges",
    )(p)


def gradient_kernel(
    p_ref, hu_ref, hv_ref, h_ref, up_ref, dn_ref, lh_ref, rh_ref,
    ox_ref, oy_ref, fac_ref, turned, ends,
):
    stacked = jnp.concatenate([lh_ref[...], rh_ref[...]], axis=0)
    for b in range(stacked.shape[1] // LANES):
        cut = slice(b * LANES, (b + 1) * LANES)
        square = jnp.concatenate(
            [stacked[:, cut], jnp.zeros((LANES - 2 * TILE, LANES), F32)], axis=0
        )
        turned[cut, :] = square.T
    row = iota((BPX, LANES), 0)
    last = (PATCH - 1) * SLAB
    for g in range(QUADS):
        cut = slice(g * LANES, (g + 1) * LANES)
        for at, end, halo, shift, edge in (
            (last, 0, up_ref, 1, 0),
            (0, 1, dn_ref, BPX - 1, BPX - 1),
        ):
            parts = [
                p_ref[at + (half * QUADS + g) * TILE:at + (half * QUADS + g + 1) * TILE, :]
                for half in range(HALVES)
            ]
            whole = pltpu.roll(jnp.concatenate(parts, axis=0), shift, 0)
            whole = jnp.where(row == edge, jnp.broadcast_to(halo[0:1, cut], (BPX, LANES)), whole)
            for half in range(HALVES):
                to = end * SLAB + (half * QUADS + g) * TILE
                ends[to:to + TILE, :] = whole[half * TILE:(half + 1) * TILE]

    lane = iota((TILE, LANES), 1)

    def cells(i, before, after):
        at = i * SLAB
        for half in range(HALVES):
            rows = pl.ds(pl.multiple_of((i * HALVES + half) * TILE, TILE), TILE)
            sides = turned[rows, :]
            tiles = [
                p_ref[pl.ds(pl.multiple_of(at + (half * QUADS + g) * TILE, TILE), TILE), :]
                for g in range(QUADS)
            ]
            ups = [pltpu.roll(a, 1, 1) for a in tiles]
            downs = [pltpu.roll(a, LANES - 1, 1) for a in tiles]
            for g in range(QUADS):
                off = (half * QUADS + g) * TILE
                here = pl.ds(pl.multiple_of(at + off, TILE), TILE)
                prev = jnp.where(lane == 0, ups[g - 1] if g else sides[:, 0:1], ups[g])
                if g < QUADS - 1:
                    nxt = jnp.where(lane == LANES - 1, downs[g + 1], downs[g])
                else:
                    nxt = jnp.where(lane == LANES - 1, sides[:, TILE:TILE + 1], downs[g])
                h = h_ref[here, :]
                wet = h > 0.0
                scale = (TIME_STEP * PRESS * 0.5) * h
                gx = after(off) - before(off)
                ox_ref[here, :] = jnp.where(wet, hu_ref[here, :] - scale * gx, 0.0)
                oy_ref[here, :] = jnp.where(wet, hv_ref[here, :] - scale * (nxt - prev), 0.0)
                fac_ref[here, :] = jnp.where(wet, TIME_STEP * STRESS, 0.0)

    def at_end(end):
        return lambda off: ends[end * SLAB + off:end * SLAB + off + TILE, :]

    def at_slab(i):
        return lambda off: p_ref[pl.ds(pl.multiple_of(i * SLAB + off, TILE), TILE), :]

    cells(0, at_end(0), at_slab(1))
    lax.fori_loop(
        1, PATCH - 1, lambda i, c: (cells(i, at_slab(i - 1), at_slab(i + 1)), c)[1], 0
    )
    cells(PATCH - 1, at_slab(PATCH - 2), at_end(1))


def gradient(p, hu, hv, h, up, dn, lh, rh):
    grouped = jax.ShapeDtypeStruct(p.shape, F32)
    return pl.pallas_call(
        gradient_kernel,
        out_shape=(grouped,) * 3,
        in_specs=[VMEM] * 8,
        out_specs=(VMEM,) * 3,
        scratch_shapes=[
            pltpu.VMEM((PATCH * BPX, LANES), F32),
            pltpu.VMEM((2 * SLAB, LANES), F32),
        ],
        compiler_params=params(),
        cost_estimate=pl.CostEstimate(
            flops=20 * p.size, bytes_accessed=28 * p.size, transcendentals=0
        ),
        name="gradient",
    )(p, hu, hv, h, up, dn, lh, rh)


def wind_kernel(summed_ref, w_ref, hu_ref, hv_ref, fac_ref, ox_ref, oy_ref, left, acc, sx, sy):
    @pl.when(pl.program_id(0) == 0)
    def _():
        stack_left(left, summed_ref, 2)

    acc[...] = jnp.dot(left[...], w_ref[...], preferred_element_type=F32)
    low = iota((TILE, LANES), 1) < LANES // 2
    for t in range(TILE // 2):
        for half in range(HALVES):
            for g in range(QUADS):
                xs = pair_rows(acc, 0, t, half, g, low)
                ys = pair_rows(acc, 1, t, half, g, low)
                for odd in range(2):
                    i = 2 * t + odd
                    at = i * SLAB + (half * QUADS + g) * TILE
                    wx = xs[odd]
                    wy = ys[odd]
                    speed = jnp.sqrt(wx * wx + wy * wy) * fac_ref[at:at + TILE, :]
                    to = pl.ds(half * TILE * TILE + i, TILE, stride=TILE)
                    sx[g, to, :] = hu_ref[at:at + TILE, :] + speed * wx
                    sy[g, to, :] = hv_ref[at:at + TILE, :] + speed * wy
    for src, dst in ((sx, ox_ref), (sy, oy_ref)):
        for g in range(QUADS):
            for r in range(BPX):
                dst[r, :, g * LANES:(g + 1) * LANES] = src[g, r * TILE:(r + 1) * TILE, :]


def wind_field(summed, weights, hu, hv, fac):
    steps = PATCH // TILE
    chunk = TILE * PATCH
    cols = BPY * PATCH
    slab = pl.BlockSpec((TILE * SLAB, LANES), lambda i: (i, 0))
    out = pl.BlockSpec((BPX, TILE, cols), lambda i: (0, i, 0))
    shape = jax.ShapeDtypeStruct((BPX, PATCH, cols), F32)
    return pl.pallas_call(
        wind_kernel,
        grid=(steps,),
        out_shape=(shape, shape),
        in_specs=[
            pl.BlockSpec(summed.shape, lambda i: (0, 0)),
            pl.BlockSpec((NW * ABLK, chunk), lambda i: (0, i)),
            slab, slab, slab,
        ],
        out_specs=(out, out),
        scratch_shapes=[
            pltpu.VMEM((2 * NPATCH, NW * ABLK), BF16),
            pltpu.VMEM((2 * NPATCH, chunk), F32),
            pltpu.VMEM((QUADS, BPX * TILE, LANES), F32),
            pltpu.VMEM((QUADS, BPX * TILE, LANES), F32),
        ],
        compiler_params=params(),
        cost_estimate=pl.CostEstimate(
            flops=4 * NPATCH * NW * ABLK * PATCH * PATCH, bytes_accessed=20 << 20, transcendentals=0
        ),
        name="wind",
    )(summed, weights, hu, hv, fac)


def body(
    atm_blocks,
    remap_weights,
    ovl_source,
    ovl_block,
    ovl_patch,
    ovl_weight,
    depth_field,
    wet_mask,
    mom_x,
    mom_y,
    blend,
):
    devices = lax.axis_size("gx") * lax.axis_size("gy")
    entries = ovl_source.size
    both = ("gx", "gy")
    atm = atm_blocks.reshape(atm_blocks.shape[2:]).transpose(1, 0, 2)
    blocks = atm.shape[1]
    press, wind = mix(blend.reshape(1), atm)
    press = lax.all_gather(press, both, axis=0, tiled=True)
    wind = lax.all_gather(wind, both, axis=0, tiled=True)
    lab = ovl_weight.reshape(1, entries) * NPATCH + morton_slot(ovl_patch.reshape(1, entries))
    block = ovl_source.reshape(entries, 1) * blocks + ovl_block.reshape(entries, 1)
    counts = count_matrix(lab, block, devices * blocks)

    top, bottom, left, right = edge_cells(depth_field, wet_mask, mom_x, mom_y)
    newh, hu, hv, h = stencil(
        depth_field, wet_mask, mom_x, mom_y,
        send(bottom, "gx", 1), send(top, "gx", -1),
        send(right, "gy", 1), send(left, "gy", -1), left, right,
    )
    weights = remap_weights.reshape(NW * ABLK, PATCH * PATCH)
    p = pressure_field(summed_blocks(counts, press), weights)
    top, bottom, left, right = press_edges(p)
    hu, hv, fac = gradient(
        p, hu, hv, h,
        send(bottom, "gx", 1), send(top, "gx", -1),
        send(right, "gy", 1), send(left, "gy", -1),
    )
    new_x, new_y = wind_field(summed_blocks(counts, wind), weights, hu, hv, fac)
    return (newh, new_x.reshape(newh.shape), new_y.reshape(newh.shape))


def solution(mesh):
    placed = (
        P("gx", "gy", None, None, None),
        P(),
        P("gx", "gy", None, None),
        P("gx", "gy", None),
        P("gx", "gy", None),
        P("gx", "gy", None),
        P("gx", "gy"),
        P("gx", "gy"),
        P("gx", "gy"),
        P("gx", "gy"),
        P(),
    )
    return jax.shard_map(
        body,
        mesh=mesh,
        in_specs=placed,
        out_specs=(P("gx", "gy"), P("gx", "gy"), P("gx", "gy")),
        check_vma=False,
    )
```

```python
import functools

import jax
import jax.numpy as jnp
from jax import lax
from jax.experimental import pallas as pl
from jax.experimental.pallas import tpu as pltpu
from jax.sharding import PartitionSpec as P

PATCH = 64
ABLK = 256
NW = 4
BPX = 16
BPY = 8
NPATCH = BPX * BPY

GRAV = 1.0
DT_DX = 0.2
TIME_STEP = 0.2
STRESS = 0.5
PRESS = 0.5

F32 = jnp.float32
BF16 = jnp.bfloat16
VMEM = pl.BlockSpec(memory_space=pltpu.VMEM)
SMEM = pl.BlockSpec(memory_space=pltpu.SMEM)
LANES = 128
TILE = 8
GROUPS = BPY * PATCH // LANES
HALVES = BPX // TILE
BAND = 128


def params(limit=56 << 20, **kw):
    return pltpu.CompilerParams(vmem_limit_bytes=limit, **kw)


def iota(shape, dim):
    return lax.broadcasted_iota(jnp.int32, shape, dim)


def rank_kernel(capacity, src_ref, blk_ref, pat_ref, wgt_ref, want_ref, lab_ref):
    devices = want_ref.shape[0]
    src = src_ref[...]
    ent = src.shape[1]
    hits = (iota((devices, ent), 0) == src).astype(F32)
    order = (iota((ent, ent), 0) <= iota((ent, ent), 1)).astype(BF16)
    ranks = jnp.dot(hits.astype(BF16), order, preferred_element_type=F32)
    mine = jnp.sum(hits * ranks, axis=0, keepdims=True).astype(jnp.int32) - 1
    place = iota((capacity, ent), 0) == mine
    pat = pat_ref[...]
    row_bits = BPX.bit_length() - 1
    col_bits = BPY.bit_length() - 1
    rows = jnp.zeros_like(pat)
    cols = jnp.zeros_like(pat)
    used_r = used_c = position = 0
    while used_r < row_bits or used_c < col_bits:
        value = jnp.bitwise_and(jnp.right_shift(pat, position), 1)
        if used_r < row_bits and (used_c >= col_bits or position % 2 == 0):
            rows = rows + value * (1 << used_r)
            used_r += 1
        else:
            cols = cols + value * (1 << used_c)
            used_c += 1
        position += 1

    def spread(row):
        picked = jnp.where(place, row.astype(F32), 0.0).astype(BF16)
        return lax.dot_general(
            hits.astype(BF16), picked, (((1,), (1,)), ((), ())),
            preferred_element_type=F32,
        ).astype(jnp.int32)

    want_ref[...] = spread(blk_ref[...])
    slot = spread(cols * BPX + rows)
    group = spread(wgt_ref[...] + 1)
    lab_ref[...] = jnp.where(group > 0, (group - 1) * NPATCH + slot, -1)


def make_requests(src, blk, pat, wgt, devices, capacity):
    shape = jax.ShapeDtypeStruct((devices, capacity), jnp.int32)
    return pl.pallas_call(
        functools.partial(rank_kernel, capacity),
        out_shape=(shape, shape),
        in_specs=[VMEM] * 4,
        out_specs=(VMEM, VMEM),
        compiler_params=params(16 << 20),
        name="requests",
    )(src, blk, pat, wgt)


def mix_kernel(blend_ref, atm_ref, press_ref, wind_ref):
    blend = blend_ref[0]
    keep = 1.0 - blend

    def mixed(k):
        first = atm_ref[k].astype(F32)
        second = atm_ref[3 + k].astype(F32)
        return (keep * first + blend * second).astype(BF16)

    press_ref[...] = mixed(2)
    for k in range(2):
        wind_ref[:, k * ABLK:(k + 1) * ABLK] = mixed(k)


def mix(blend, atm):
    blocks = atm.shape[1]
    return pl.pallas_call(
        mix_kernel,
        out_shape=(
            jax.ShapeDtypeStruct((blocks, ABLK), BF16),
            jax.ShapeDtypeStruct((blocks, 2 * ABLK), BF16),
        ),
        in_specs=[SMEM, VMEM],
        out_specs=(VMEM, VMEM),
        compiler_params=params(16 << 20),
        name="mix",
    )(blend, atm)


def serve_kernel(asked_ref, tiles_ref, out_ref):
    asked = asked_ref[...]
    pick = (asked == iota((asked.shape[0], tiles_ref.shape[0]), 1)).astype(BF16)
    out_ref[...] = jnp.dot(pick, tiles_ref[...], preferred_element_type=F32).astype(BF16)


def serve(asked, tiles):
    return pl.pallas_call(
        serve_kernel,
        out_shape=jax.ShapeDtypeStruct((asked.shape[0], tiles.shape[1]), BF16),
        in_specs=[VMEM, VMEM],
        out_specs=VMEM,
        compiler_params=params(32 << 20),
        name="serve",
    )(asked, tiles)


def edges_kernel(
    dl, ml, xl, yl, dr, mr, xr, yr, dt, mt, xt, yt, db, mb, xb, yb,
    top_ref, bottom_ref, left_ref, right_ref,
):
    def rows(d, m, x, y, at, out):
        wet = m[...] == 1
        for f, ref in enumerate((d, x, y)):
            out[f:f + 1, :] = jnp.where(wet, ref[...], 0.0)[at:at + 1]

    rows(dt, mt, xt, yt, 0, top_ref)
    rows(db, mb, xb, yb, TILE - 1, bottom_ref)
    lane = iota((LANES, LANES), 1)

    def step(b, carry):
        at = pl.ds(pl.multiple_of(b * LANES, LANES), LANES)
        wl = ml[at, :] == 1
        wr = mr[at, :] == 1
        packed = jnp.where(wl, dl[at, :], 0.0)
        packed = jnp.where(lane == 1, pltpu.roll(jnp.where(wl, xl[at, :], 0.0), 1, 1), packed)
        packed = jnp.where(lane == 2, pltpu.roll(jnp.where(wl, yl[at, :], 0.0), 2, 1), packed)
        packed = jnp.where(lane == 8, pltpu.roll(jnp.where(wr, dr[at, :], 0.0), 9, 1), packed)
        packed = jnp.where(lane == 9, pltpu.roll(jnp.where(wr, xr[at, :], 0.0), 10, 1), packed)
        packed = jnp.where(lane == 10, pltpu.roll(jnp.where(wr, yr[at, :], 0.0), 11, 1), packed)
        turned = packed.T
        left_ref[:, at] = turned[0:TILE]
        right_ref[:, at] = turned[TILE:2 * TILE]
        return carry

    lax.fori_loop(0, dl.shape[0] // LANES, step, 0)


def edge_cells(depth, mask, momx, momy):
    rows, cols = depth.shape
    fields = (depth, mask, momx, momy)
    left = pl.BlockSpec((rows, LANES), lambda i: (0, 0))
    right = pl.BlockSpec((rows, LANES), lambda i: (0, cols // LANES - 1))
    top = pl.BlockSpec((TILE, cols), lambda i: (0, 0))
    bottom = pl.BlockSpec((TILE, cols), lambda i: (rows // TILE - 1, 0))
    line = jax.ShapeDtypeStruct((TILE, cols), F32)
    column = jax.ShapeDtypeStruct((TILE, rows), F32)
    return pl.pallas_call(
        edges_kernel,
        grid=(1,),
        out_shape=(line, line, column, column),
        in_specs=[left] * 4 + [right] * 4 + [top] * 4 + [bottom] * 4,
        out_specs=(
            pl.BlockSpec((TILE, cols), lambda i: (0, 0)),
            pl.BlockSpec((TILE, cols), lambda i: (0, 0)),
            pl.BlockSpec((TILE, rows), lambda i: (0, 0)),
            pl.BlockSpec((TILE, rows), lambda i: (0, 0)),
        ),
        compiler_params=params(24 << 20),
        name="edges",
    )(*(fields * 4))


def send(value, axis, step):
    count = lax.axis_size(axis)
    if step > 0:
        pairs = [(i, i + 1) for i in range(count - 1)]
    else:
        pairs = [(i + 1, i) for i in range(count - 1)]
    return lax.ppermute(value, axis, pairs)


def derived(h, u, v):
    r = jnp.where(h > 0.0, lax.rsqrt(h), 0.0)
    s = h * r
    q = u * r
    p = v * r
    half = 0.5 * h * h
    return (h, u, v, s, q, p, q * q + half, p * p + half, q * p)


def along_x(c):
    return (c[0], c[1], c[2], c[3], c[4], c[5], c[6], c[8])


def along_y(c):
    return (c[0], c[2], c[1], c[3], c[5], c[4], c[7], c[8])


def flux(a, b):
    hl, nl, tl, sl, ql, pl_, fl, gl = a
    hr, nr, tr, sr, qr, pr, fr, gr = b
    both = jnp.minimum(hl, hr) > 0.0
    half = jnp.where(both, 0.5, 1.0)
    twice = half + half
    level = (hl + hr) * half
    rc = lax.rsqrt(level)
    c = level * rc
    total = sl + sr
    inv = pl.reciprocal(total, approx=True)
    inv = inv * (2.0 - total * inv)
    u = jnp.where(both, (ql + qr) * inv, 0.0)
    v = (pl_ + pr) * inv
    dh = jnp.where(both, hr - hl, 0.0)
    dn = (nr - nl) * twice
    dt = jnp.where(both, tr - tl, 0.0)
    mid = 0.5 * dh
    e = (0.5 * dn - u * mid) * rc
    s1 = u - c
    s3 = u + c
    b1 = jnp.abs(s1) * (mid - e)
    b3 = jnp.abs(s3) * (mid + e)
    b2 = jnp.abs(u) * (dt - v * dh)
    d = b1 + b3
    return (
        jnp.where(both, nl + nr, 0.0) - d,
        (fl + fr) * twice - (b1 * s1 + b3 * s3),
        jnp.where(both, gl + gr, 0.0) - (d * v + b2),
    )


CELL = 9


def stencil_kernel(
    d_ref, m_ref, x_ref, y_ref, up_ref, dn_ref, lh_ref, rh_ref, lo_ref,
    newh_ref, hu_ref, hv_ref, h_ref, *scratch,
):
    cell = scratch[:CELL]
    gx = scratch[CELL:CELL + 3]
    edge, ecol = scratch[CELL + 3:]
    step = pl.program_id(0)
    bands = pl.num_programs(0) - 1
    lane = iota((TILE, LANES), 1)

    @pl.when(step < bands)
    def _():
        def fill(t, carry):
            at = pl.ds(pl.multiple_of(t * TILE, TILE), TILE)
            to = pl.ds(pl.multiple_of(step * BAND + t * TILE + TILE, TILE), TILE)
            for g in range(GROUPS):
                cut = slice(g * LANES, (g + 1) * LANES)
                wet = m_ref[at, cut] == 1
                h = jnp.where(wet, d_ref[at, cut], 0.0)
                u = jnp.where(wet, x_ref[at, cut], 0.0)
                v = jnp.where(wet, y_ref[at, cut], 0.0)
                for dst, val in zip(cell, derived(h, u, v)):
                    dst[g, to, :] = val
            return carry

        lax.fori_loop(0, BAND // TILE, fill, 0, unroll=4)

    @pl.when(step == 0)
    def _():
        rows = bands * BAND
        for at, ref in ((0, up_ref), (rows + TILE, dn_ref)):
            for g in range(GROUPS):
                cut = slice(g * LANES, (g + 1) * LANES)
                line = [jnp.broadcast_to(ref[f:f + 1, cut], (TILE, LANES)) for f in range(3)]
                for dst, val in zip(cell, derived(*line)):
                    dst[g, pl.ds(at, TILE), :] = val
        outer = along_y(derived(lh_ref[0:1, :], lh_ref[1:2, :], lh_ref[2:3, :]))
        inner = along_y(derived(lo_ref[0:1, :], lo_ref[1:2, :], lo_ref[2:3, :]))
        edge[...] = jnp.zeros_like(edge)
        edge[0:3, :] = rh_ref[0:3, :]
        for f, val in enumerate(flux(outer, inner)):
            edge[3 + f:4 + f, :] = val

        def turn(b, carry):
            at = pl.ds(pl.multiple_of(b * LANES, LANES), LANES)
            ecol[at, :] = edge[:, at].T
            return carry

        lax.fori_loop(0, ecol.shape[0] // LANES, turn, 0)
        for g in range(GROUPS):
            now = along_x([ref[g, 0:TILE, :] for ref in cell])
            nxt = along_x([ref[g, 1:TILE + 1, :] for ref in cell])
            for dst, val in zip(gx, flux(now, nxt)):
                dst[g, 0:TILE, :] = val

    @pl.when(step > 0)
    def _():
        def body(t, carry):
            here = pl.multiple_of(t * TILE, TILE)
            mark = pl.multiple_of((step - 1) * BAND + t * TILE, TILE)
            base = pl.multiple_of(mark + TILE, TILE)
            sides = ecol[pl.ds(mark, TILE), :]
            now = [[ref[g, pl.ds(base, TILE), :] for ref in cell] for g in range(GROUPS)]
            back = [[pltpu.roll(val, LANES - 1, 1) for val in now[g][:3]] for g in range(GROUPS)]
            gy = []
            for g in range(GROUPS):
                if g < GROUPS - 1:
                    other = back[g + 1]
                else:
                    other = [sides[:, f:f + 1] for f in range(3)]
                right = [jnp.where(lane == LANES - 1, o, b) for o, b in zip(other, back[g])]
                gy.append(flux(along_y(now[g]), along_y(derived(*right))))
            moved = [[pltpu.roll(val, 1, 1) for val in gy[g]] for g in range(GROUPS)]
            for g in range(GROUPS):
                nxt = [ref[g, pl.ds(base + 1, TILE), :] for ref in cell]
                fx = flux(along_x(now[g]), along_x(nxt))
                for dst, val in zip(gx, fx):
                    dst[g, pl.ds(base, TILE), :] = val
                px = [src[g, pl.ds(base - 1, TILE), :] for src in gx]
                other = moved[g - 1] if g else [sides[:, 3 + f:4 + f] for f in range(3)]
                py = [jnp.where(lane == 0, o, b) for o, b in zip(other, moved[g])]
                fy = gy[g]
                h, u, v = now[g][:3]
                ch = (fx[0] - px[0]) + (fy[0] - py[0])
                cx = (fx[1] - px[1]) + (fy[2] - py[2])
                cy = (fx[2] - px[2]) + (fy[1] - py[1])
                at = pl.ds(here, TILE)
                newh_ref[at, g * LANES:(g + 1) * LANES] = jnp.where(
                    h > 0.0, h - (0.5 * DT_DX) * ch, 0.0
                )
                hu_ref[g, at, :] = u - (0.5 * DT_DX) * cx
                hv_ref[g, at, :] = v - (0.5 * DT_DX) * cy
                h_ref[g, at, :] = h
            return carry

        lax.fori_loop(0, BAND // TILE, body, 0, unroll=2)


def stencil(depth, mask, momx, momy, up, dn, lh, rh, lo):
    rows, cols = depth.shape
    bands = rows // BAND
    plane = jax.ShapeDtypeStruct((GROUPS, rows, LANES), F32)
    pad = pltpu.VMEM((GROUPS, rows + 2 * TILE, LANES), F32)
    band = pl.BlockSpec((BAND, cols), lambda i: (jnp.minimum(i, bands - 1), 0))
    line = pl.BlockSpec((TILE, cols), lambda i: (0, 0))
    column = pl.BlockSpec((TILE, rows), lambda i: (0, 0))
    part = pl.BlockSpec((GROUPS, BAND, LANES), lambda i: (0, jnp.maximum(i - 1, 0), 0))
    return pl.pallas_call(
        stencil_kernel,
        grid=(bands + 1,),
        out_shape=(jax.ShapeDtypeStruct((rows, cols), F32), plane, plane, plane),
        in_specs=[band] * 4 + [line] * 2 + [column] * 3,
        out_specs=(
            pl.BlockSpec((BAND, cols), lambda i: (jnp.maximum(i - 1, 0), 0)), part, part, part,
        ),
        scratch_shapes=[pad] * (CELL + 3)
        + [pltpu.VMEM((LANES, rows), F32), pltpu.VMEM((rows, LANES), F32)],
        compiler_params=params(48 << 20),
        cost_estimate=pl.CostEstimate(
            flops=200 * rows * cols, bytes_accessed=64 * rows * cols, transcendentals=0
        ),
        name="stencil",
    )(depth, mask, momx, momy, up, dn, lh, rh, lo)


def summed_of(lab, landed):
    select = (iota((NW * NPATCH, lab.shape[1]), 0) == lab).astype(BF16)
    return jnp.dot(select, landed, preferred_element_type=F32).astype(BF16)


def stack_left(left, summed, channels):
    for k in range(channels):
        for w in range(NW):
            left[k * NPATCH:(k + 1) * NPATCH, w * ABLK:(w + 1) * ABLK] = summed[
                w * NPATCH:(w + 1) * NPATCH, k * ABLK:(k + 1) * ABLK
            ]


PART = TILE * PATCH


def spread_rows(acc, field, k):
    low = iota((TILE, LANES), 1) < LANES // 2
    for t in range(TILE // 2):
        cut = slice(t * LANES, (t + 1) * LANES)
        for half in range(HALVES):
            for g in range(GROUPS):
                base = k * NPATCH + 2 * g * BPX + half * TILE
                even = acc[base:base + TILE, cut]
                odd = acc[base + BPX:base + BPX + TILE, cut]
                for i, val in (
                    (2 * t, jnp.where(low, even, pltpu.roll(odd, LANES // 2, 1))),
                    (2 * t + 1, jnp.where(low, pltpu.roll(even, LANES // 2, 1), odd)),
                ):
                    field[g, pl.ds(half * TILE * TILE + i, TILE, stride=TILE), :] = val


def press_kernel(
    lab_ref, landed_ref, w_ref, out_ref, top_ref, bottom_ref, left_ref, right_ref,
    left, acc, acc2, field, field2,
):
    step = pl.program_id(0)

    @pl.when(step == 0)
    def _():
        stack_left(left, summed_of(lab_ref[...], landed_ref[...]), 1)

    acc[...] = jnp.dot(left[...], w_ref[:, :PART], preferred_element_type=F32)
    acc2[...] = jnp.dot(left[...], w_ref[:, PART:], preferred_element_type=F32)
    for part, (src, mid) in enumerate(((acc, field), (acc2, field2))):
        spread_rows(src, mid, 0)
        for g in range(GROUPS):
            for r in range(BPX):
                to = pl.ds(pl.multiple_of(r * PATCH + (2 * step + part) * TILE, TILE), TILE)
                out_ref[g, to, :] = mid[g, r * TILE:(r + 1) * TILE, :]

    @pl.when(step == pl.num_programs(0) - 1)
    def _():
        rows = out_ref.shape[1]
        for g in range(GROUPS):
            cut = slice(g * LANES, (g + 1) * LANES)
            top_ref[:, cut] = out_ref[g, 0:TILE, :]
            bottom_ref[:, cut] = pltpu.roll(out_ref[g, rows - TILE:rows, :], 1, 0)
        lane = iota((LANES, LANES), 1)
        for b in range(rows // LANES):
            at = slice(b * LANES, (b + 1) * LANES)
            packed = jnp.where(
                lane == TILE,
                pltpu.roll(out_ref[GROUPS - 1, at, :], TILE + 1, 1),
                out_ref[0, at, :],
            )
            turned = packed.T
            left_ref[:, at] = turned[0:TILE]
            right_ref[:, at] = turned[TILE:2 * TILE]


def pressure_field(lab, landed, weights):
    steps = PATCH // (2 * TILE)
    rows = BPX * PATCH
    line = (TILE, BPY * PATCH)
    column = (TILE, rows)
    whole = (GROUPS, rows, LANES)

    def const(shape):
        return pl.BlockSpec(shape, lambda i: (0,) * len(shape))

    return pl.pallas_call(
        press_kernel,
        grid=(steps,),
        out_shape=tuple(jax.ShapeDtypeStruct(x, F32) for x in (whole, line, line, column, column)),
        in_specs=[
            const(lab.shape),
            const(landed.shape),
            pl.BlockSpec((NW * ABLK, 2 * PART), lambda i: (0, i)),
        ],
        out_specs=tuple(const(x) for x in (whole, line, line, column, column)),
        scratch_shapes=[
            pltpu.VMEM((NPATCH, NW * ABLK), BF16),
            pltpu.VMEM((NPATCH, PART), F32),
            pltpu.VMEM((NPATCH, PART), F32),
            pltpu.VMEM((GROUPS, BPX * TILE, LANES), F32),
            pltpu.VMEM((GROUPS, BPX * TILE, LANES), F32),
        ],
        compiler_params=params(32 << 20),
        cost_estimate=pl.CostEstimate(
            flops=2 * NPATCH * NW * ABLK * PATCH * PATCH, bytes_accessed=12 << 20, transcendentals=0
        ),
        name="pressure",
    )(lab, landed, weights)


def gradient_kernel(
    p_ref, hu_ref, hv_ref, h_ref, up_ref, dn_ref, lh_ref, rh_ref,
    ox_ref, oy_ref, fac_ref, padded, sides,
):
    step = pl.program_id(0)
    rows = p_ref.shape[1]

    @pl.when(step == 0)
    def _():
        stacked = jnp.concatenate([lh_ref[...], rh_ref[...]], axis=0)
        blank = jnp.zeros((LANES - 2 * TILE, LANES), F32)
        for b in range(rows // LANES):
            cut = slice(b * LANES, (b + 1) * LANES)
            sides[cut, :] = jnp.concatenate([stacked[:, cut], blank], axis=0).T
        for g in range(GROUPS):
            cut = slice(g * LANES, (g + 1) * LANES)
            padded[g, TILE:TILE + rows, :] = p_ref[g]
            padded[g, 0:TILE, :] = jnp.broadcast_to(up_ref[0:1, cut], (TILE, LANES))
            padded[g, rows + TILE:, :] = jnp.broadcast_to(dn_ref[0:1, cut], (TILE, LANES))

    lane = iota((TILE, LANES), 1)

    def body(t, carry):
        at = pl.ds(pl.multiple_of(t * TILE, TILE), TILE)
        mark = pl.multiple_of(step * BAND + t * TILE, TILE)
        base = pl.multiple_of(mark + TILE, TILE)
        ends = sides[pl.ds(mark, TILE), :]
        tiles = [padded[g, pl.ds(base, TILE), :] for g in range(GROUPS)]
        ups = [pltpu.roll(a, 1, 1) for a in tiles]
        downs = [pltpu.roll(a, LANES - 1, 1) for a in tiles]
        for g in range(GROUPS):
            before = ups[g - 1] if g else ends[:, 0:1]
            after = downs[g + 1] if g < GROUPS - 1 else ends[:, TILE:TILE + 1]
            prev = jnp.where(lane == 0, before, ups[g])
            nxt = jnp.where(lane == LANES - 1, after, downs[g])
            h = h_ref[g, at, :]
            wet = h > 0.0
            scale = (TIME_STEP * PRESS * 0.5) * h
            gx = padded[g, pl.ds(base + 1, TILE), :] - padded[g, pl.ds(base - 1, TILE), :]
            ox_ref[g, at, :] = jnp.where(wet, hu_ref[g, at, :] - scale * gx, 0.0)
            oy_ref[g, at, :] = jnp.where(wet, hv_ref[g, at, :] - scale * (nxt - prev), 0.0)
            fac_ref[g, at, :] = jnp.where(wet, TIME_STEP * STRESS, 0.0)
        return carry

    lax.fori_loop(0, BAND // TILE, body, 0, unroll=4)


def gradient(p, hu, hv, h, up, dn, lh, rh):
    rows = p.shape[1]
    plane = jax.ShapeDtypeStruct(p.shape, F32)
    part = pl.BlockSpec((GROUPS, BAND, LANES), lambda i: (0, i, 0))
    line = pl.BlockSpec(up.shape, lambda i: (0, 0))
    column = pl.BlockSpec(lh.shape, lambda i: (0, 0))
    return pl.pallas_call(
        gradient_kernel,
        grid=(rows // BAND,),
        out_shape=(plane,) * 3,
        in_specs=[pl.BlockSpec(p.shape, lambda i: (0, 0, 0))] + [part] * 3 + [line] * 2 + [column] * 2,
        out_specs=(part,) * 3,
        scratch_shapes=[
            pltpu.VMEM((GROUPS, rows + 2 * TILE, LANES), F32),
            pltpu.VMEM((rows, LANES), F32),
        ],
        compiler_params=params(24 << 20),
        cost_estimate=pl.CostEstimate(
            flops=20 * p.size, bytes_accessed=28 * p.size, transcendentals=0
        ),
        name="gradient",
    )(p, hu, hv, h, up, dn, lh, rh)


def wind_kernel(
    lab_ref, landed_ref, w_ref, hu_ref, hv_ref, fac_ref, ox_ref, oy_ref,
    left, acc, acc2, fx, fy, fx2, fy2,
):
    @pl.when(pl.program_id(0) == 0)
    def _():
        stack_left(left, summed_of(lab_ref[...], landed_ref[...]), 2)

    acc[...] = jnp.dot(left[...], w_ref[:, :PART], preferred_element_type=F32)
    acc2[...] = jnp.dot(left[...], w_ref[:, PART:], preferred_element_type=F32)
    for part, (src, mx, my) in enumerate(((acc, fx, fy), (acc2, fx2, fy2))):
        spread_rows(src, mx, 0)
        spread_rows(src, my, 1)
        cells = slice(part * TILE, (part + 1) * TILE)
        for g in range(GROUPS):
            for r in range(BPX):
                at = slice(r * TILE, (r + 1) * TILE)
                wx = mx[g, at, :]
                wy = my[g, at, :]
                speed = jnp.sqrt(wx * wx + wy * wy) * fac_ref[g, r, cells, :]
                cut = slice(g * LANES, (g + 1) * LANES)
                ox_ref[r, cells, cut] = hu_ref[g, r, cells, :] + speed * wx
                oy_ref[r, cells, cut] = hv_ref[g, r, cells, :] + speed * wy


def wind_field(lab, landed, weights, hu, hv, fac):
    deep = 2 * TILE
    steps = PATCH // deep
    cols = BPY * PATCH
    split = (GROUPS, BPX, PATCH, LANES)
    slab = pl.BlockSpec((GROUPS, BPX, deep, LANES), lambda i: (0, 0, i, 0))
    out = pl.BlockSpec((BPX, deep, cols), lambda i: (0, i, 0))
    shape = jax.ShapeDtypeStruct((BPX, PATCH, cols), F32)
    field = pltpu.VMEM((GROUPS, BPX * TILE, LANES), F32)
    return pl.pallas_call(
        wind_kernel,
        grid=(steps,),
        out_shape=(shape, shape),
        in_specs=[
            pl.BlockSpec(lab.shape, lambda i: (0, 0)),
            pl.BlockSpec(landed.shape, lambda i: (0, 0)),
            pl.BlockSpec((NW * ABLK, 2 * PART), lambda i: (0, i)),
            slab, slab, slab,
        ],
        out_specs=(out, out),
        scratch_shapes=[
            pltpu.VMEM((2 * NPATCH, NW * ABLK), BF16),
            pltpu.VMEM((2 * NPATCH, PART), F32),
            pltpu.VMEM((2 * NPATCH, PART), F32),
            field, field, field, field,
        ],
        compiler_params=params(40 << 20),
        cost_estimate=pl.CostEstimate(
            flops=4 * NPATCH * NW * ABLK * PATCH * PATCH, bytes_accessed=20 << 20, transcendentals=0
        ),
        name="wind",
    )(lab, landed, weights, hu.reshape(split), hv.reshape(split), fac.reshape(split))


def body(
    atm_blocks,
    remap_weights,
    ovl_source,
    ovl_block,
    ovl_patch,
    ovl_weight,
    depth_field,
    wet_mask,
    mom_x,
    mom_y,
    blend,
):
    count_x = lax.axis_size("gx")
    count_y = lax.axis_size("gy")
    devices = count_x * count_y
    entries = ovl_source.size
    capacity = 2 * entries // devices
    slots = devices * capacity
    atm = atm_blocks.reshape(atm_blocks.shape[2:]).transpose(1, 0, 2)
    blocks = atm.shape[1]
    press, wind = mix(blend.reshape(1), atm)
    press = lax.all_gather(press, "gx", axis=0, tiled=True)
    wind = lax.all_gather(wind, "gx", axis=0, tiled=True)

    source = ovl_source.reshape(1, entries)
    source = (source % count_y) * count_x + source // count_y
    want, lab = make_requests(
        source, ovl_block.reshape(1, entries),
        ovl_patch.reshape(1, entries), ovl_weight.reshape(1, entries), devices, capacity,
    )
    asked = lax.all_to_all(
        want.reshape(count_y, count_x, capacity), "gy", split_axis=0, concat_axis=0, tiled=True
    )
    asked = asked + blocks * jnp.arange(count_x, dtype=jnp.int32)[None, :, None]
    asked = asked.reshape(slots, 1)
    lab = lab.reshape(1, slots)

    def exchange(tiles):
        rows = serve(asked, tiles)
        parts = rows.reshape(count_y, slots // count_y, rows.shape[1])
        got = lax.all_to_all(parts, "gy", split_axis=0, concat_axis=0, tiled=True)
        return got.reshape(rows.shape)

    press = exchange(press)
    wind = exchange(wind)

    top, bottom, left, right = edge_cells(depth_field, wet_mask, mom_x, mom_y)
    newh, hu, hv, h = stencil(
        depth_field, wet_mask, mom_x, mom_y,
        send(bottom, "gx", 1), send(top, "gx", -1),
        send(right, "gy", 1), send(left, "gy", -1), left,
    )
    weights = remap_weights.reshape(NW * ABLK, PATCH * PATCH)
    p, top, bottom, left, right = pressure_field(lab, press, weights)
    hu, hv, fac = gradient(
        p, hu, hv, h,
        send(bottom, "gx", 1), send(top, "gx", -1),
        send(right, "gy", 1), send(left, "gy", -1),
    )
    new_x, new_y = wind_field(lab, wind, weights, hu, hv, fac)
    return (newh, new_x.reshape(newh.shape), new_y.reshape(newh.shape))


def solution(mesh):
    placed = (
        P("gx", "gy", None, None, None),
        P(),
        P("gx", "gy", None, None),
        P("gx", "gy", None),
        P("gx", "gy", None),
        P("gx", "gy", None),
        P("gx", "gy"),
        P("gx", "gy"),
        P("gx", "gy"),
        P("gx", "gy"),
        P(),
    )
    return jax.shard_map(
        body,
        mesh=mesh,
        in_specs=placed,
        out_specs=(P("gx", "gy"), P("gx", "gy"), P("gx", "gy")),
        check_vma=False,
    )
```

```python
import functools

import jax
import jax.numpy as jnp
from jax import lax
from jax.experimental import pallas as pl
from jax.experimental.pallas import tpu as pltpu
from jax.sharding import PartitionSpec as P

PATCH = 64
ABLK = 256
NW = 4
BPX = 16
BPY = 8
NPATCH = BPX * BPY

GRAV = 1.0
DT_DX = 0.2
TIME_STEP = 0.2
STRESS = 0.5
PRESS = 0.5

F32 = jnp.float32
BF16 = jnp.bfloat16
VMEM = pl.BlockSpec(memory_space=pltpu.VMEM)
SMEM = pl.BlockSpec(memory_space=pltpu.SMEM)
LANES = 128
TILE = 8
GROUPS = BPY * PATCH // LANES
HALVES = BPX // TILE
BAND = 128


def params(limit=56 << 20, **kw):
    return pltpu.CompilerParams(vmem_limit_bytes=limit, **kw)


def iota(shape, dim):
    return lax.broadcasted_iota(jnp.int32, shape, dim)


def rank_kernel(capacity, src_ref, blk_ref, pat_ref, wgt_ref, want_ref, lab_ref):
    devices = want_ref.shape[0]
    src = src_ref[...]
    ent = src.shape[1]
    hits = (iota((devices, ent), 0) == src).astype(F32)
    order = (iota((ent, ent), 0) <= iota((ent, ent), 1)).astype(BF16)
    ranks = jnp.dot(hits.astype(BF16), order, preferred_element_type=F32)
    mine = jnp.sum(hits * ranks, axis=0, keepdims=True).astype(jnp.int32) - 1
    place = iota((capacity, ent), 0) == mine
    pat = pat_ref[...]
    row_bits = BPX.bit_length() - 1
    col_bits = BPY.bit_length() - 1
    rows = jnp.zeros_like(pat)
    cols = jnp.zeros_like(pat)
    used_r = used_c = position = 0
    while used_r < row_bits or used_c < col_bits:
        value = jnp.bitwise_and(jnp.right_shift(pat, position), 1)
        if used_r < row_bits and (used_c >= col_bits or position % 2 == 0):
            rows = rows + value * (1 << used_r)
            used_r += 1
        else:
            cols = cols + value * (1 << used_c)
            used_c += 1
        position += 1

    def spread(row):
        picked = jnp.where(place, row.astype(F32), 0.0).astype(BF16)
        return lax.dot_general(
            hits.astype(BF16), picked, (((1,), (1,)), ((), ())),
            preferred_element_type=F32,
        ).astype(jnp.int32)

    want_ref[...] = spread(blk_ref[...])
    slot = spread(cols * BPX + rows)
    group = spread(wgt_ref[...] + 1)
    lab_ref[...] = jnp.where(group > 0, (group - 1) * NPATCH + slot, -1)


def make_requests(src, blk, pat, wgt, devices, capacity):
    shape = jax.ShapeDtypeStruct((devices, capacity), jnp.int32)
    return pl.pallas_call(
        functools.partial(rank_kernel, capacity),
        out_shape=(shape, shape),
        in_specs=[VMEM] * 4,
        out_specs=(VMEM, VMEM),
        compiler_params=params(16 << 20),
        name="requests",
    )(src, blk, pat, wgt)


def mix_kernel(blend_ref, atm_ref, press_ref, wind_ref):
    blend = blend_ref[0]
    keep = 1.0 - blend

    def mixed(k):
        first = atm_ref[k].astype(F32)
        second = atm_ref[3 + k].astype(F32)
        return (keep * first + blend * second).astype(BF16)

    press_ref[...] = mixed(2)
    for k in range(2):
        wind_ref[:, k * ABLK:(k + 1) * ABLK] = mixed(k)


def mix(blend, atm):
    blocks = atm.shape[1]
    return pl.pallas_call(
        mix_kernel,
        out_shape=(
            jax.ShapeDtypeStruct((blocks, ABLK), BF16),
            jax.ShapeDtypeStruct((blocks, 2 * ABLK), BF16),
        ),
        in_specs=[SMEM, VMEM],
        out_specs=(VMEM, VMEM),
        compiler_params=params(16 << 20),
        name="mix",
    )(blend, atm)


def serve_kernel(after_ref, asked_ref, tiles_ref, out_ref, turned, pick):
    peers, _, capacity = asked_ref.shape
    width = turned.shape[0]
    turned[...] = jnp.zeros_like(turned)
    turned[0:peers, 0:capacity] = asked_ref[:, 0, :]
    columns = turned[...].T
    blocks = tiles_ref.shape[0]
    names = iota((capacity, blocks), 1)
    for d in range(peers):
        pick[d * capacity:(d + 1) * capacity, :] = (columns[0:capacity, d:d + 1] == names).astype(F32)
    out_ref[...] = jnp.dot(
        pick[...].astype(BF16), tiles_ref[...], preferred_element_type=F32
    ).astype(BF16)


def serve(after, asked, tiles):
    peers, _, capacity = asked.shape
    slots = peers * capacity
    width = -(-max(peers, capacity) // LANES) * LANES
    return pl.pallas_call(
        serve_kernel,
        out_shape=jax.ShapeDtypeStruct((slots, tiles.shape[1]), BF16),
        in_specs=[pl.BlockSpec(memory_space=pl.ANY), VMEM, VMEM],
        out_specs=VMEM,
        scratch_shapes=[
            pltpu.VMEM((width, width), jnp.int32),
            pltpu.VMEM((slots, tiles.shape[0]), F32),
        ],
        compiler_params=params(32 << 20),
        name="serve",
    )(after, asked, tiles)


def edges_kernel(
    dl, ml, xl, yl, dr, mr, xr, yr, dt, mt, xt, yt, db, mb, xb, yb,
    top_ref, bottom_ref, left_ref, right_ref,
):
    def rows(d, m, x, y, at, out):
        wet = m[...] == 1
        for f, ref in enumerate((d, x, y)):
            out[f:f + 1, :] = jnp.where(wet, ref[...], 0.0)[at:at + 1]

    rows(dt, mt, xt, yt, 0, top_ref)
    rows(db, mb, xb, yb, TILE - 1, bottom_ref)
    lane = iota((LANES, LANES), 1)

    def step(b, carry):
        at = pl.ds(pl.multiple_of(b * LANES, LANES), LANES)
        wl = ml[at, :] == 1
        wr = mr[at, :] == 1
        packed = jnp.where(wl, dl[at, :], 0.0)
        packed = jnp.where(lane == 1, pltpu.roll(jnp.where(wl, xl[at, :], 0.0), 1, 1), packed)
        packed = jnp.where(lane == 2, pltpu.roll(jnp.where(wl, yl[at, :], 0.0), 2, 1), packed)
        packed = jnp.where(lane == 8, pltpu.roll(jnp.where(wr, dr[at, :], 0.0), 9, 1), packed)
        packed = jnp.where(lane == 9, pltpu.roll(jnp.where(wr, xr[at, :], 0.0), 10, 1), packed)
        packed = jnp.where(lane == 10, pltpu.roll(jnp.where(wr, yr[at, :], 0.0), 11, 1), packed)
        turned = packed.T
        left_ref[:, at] = turned[0:TILE]
        right_ref[:, at] = turned[TILE:2 * TILE]
        return carry

    lax.fori_loop(0, dl.shape[0] // LANES, step, 0)


def edge_cells(depth, mask, momx, momy):
    rows, cols = depth.shape
    fields = (depth, mask, momx, momy)
    left = pl.BlockSpec((rows, LANES), lambda i: (0, 0))
    right = pl.BlockSpec((rows, LANES), lambda i: (0, cols // LANES - 1))
    top = pl.BlockSpec((TILE, cols), lambda i: (0, 0))
    bottom = pl.BlockSpec((TILE, cols), lambda i: (rows // TILE - 1, 0))
    line = jax.ShapeDtypeStruct((TILE, cols), F32)
    column = jax.ShapeDtypeStruct((TILE, rows), F32)
    return pl.pallas_call(
        edges_kernel,
        grid=(1,),
        out_shape=(line, line, column, column),
        in_specs=[left] * 4 + [right] * 4 + [top] * 4 + [bottom] * 4,
        out_specs=(
            pl.BlockSpec((TILE, cols), lambda i: (0, 0)),
            pl.BlockSpec((TILE, cols), lambda i: (0, 0)),
            pl.BlockSpec((TILE, rows), lambda i: (0, 0)),
            pl.BlockSpec((TILE, rows), lambda i: (0, 0)),
        ),
        compiler_params=params(),
        name="edges",
    )(*(fields * 4))


def send(value, axis, step):
    count = lax.axis_size(axis)
    if step > 0:
        pairs = [(i, i + 1) for i in range(count - 1)]
    else:
        pairs = [(i + 1, i) for i in range(count - 1)]
    return lax.ppermute(value, axis, pairs)


def derived(h, u, v):
    r = jnp.where(h > 0.0, lax.rsqrt(h), 0.0)
    s = h * r
    q = u * r
    p = v * r
    half = 0.5 * h * h
    return (h, u, v, s, q, p, q * q + half, p * p + half, q * p)


def along_x(c):
    return (c[0], c[1], c[2], c[3], c[4], c[5], c[6], c[8])


def along_y(c):
    return (c[0], c[2], c[1], c[3], c[5], c[4], c[7], c[8])


def flux(a, b):
    hl, nl, tl, sl, ql, pl_, fl, gl = a
    hr, nr, tr, sr, qr, pr, fr, gr = b
    both = jnp.minimum(hl, hr) > 0.0
    half = jnp.where(both, 0.5, 1.0)
    twice = half + half
    level = (hl + hr) * half
    rc = lax.rsqrt(level)
    c = level * rc
    total = sl + sr
    inv = pl.reciprocal(total, approx=True)
    inv = inv * (2.0 - total * inv)
    u = jnp.where(both, (ql + qr) * inv, 0.0)
    v = (pl_ + pr) * inv
    dh = jnp.where(both, hr - hl, 0.0)
    dn = (nr - nl) * twice
    dt = jnp.where(both, tr - tl, 0.0)
    mid = 0.5 * dh
    e = (0.5 * dn - u * mid) * rc
    s1 = u - c
    s3 = u + c
    b1 = jnp.abs(s1) * (mid - e)
    b3 = jnp.abs(s3) * (mid + e)
    b2 = jnp.abs(u) * (dt - v * dh)
    d = b1 + b3
    return (
        jnp.where(both, nl + nr, 0.0) - d,
        (fl + fr) * twice - (b1 * s1 + b3 * s3),
        jnp.where(both, gl + gr, 0.0) - (d * v + b2),
    )


CELL = 9


def stencil_kernel(
    d_ref, m_ref, x_ref, y_ref, up_ref, dn_ref, lh_ref, rh_ref, lo_ref,
    newh_ref, hu_ref, hv_ref, h_ref, *scratch,
):
    cell = scratch[:CELL]
    gx = scratch[CELL:CELL + 3]
    edge, ecol = scratch[CELL + 3:]
    step = pl.program_id(0)
    bands = pl.num_programs(0) - 1
    lane = iota((TILE, LANES), 1)

    @pl.when(step < bands)
    def _():
        def fill(t, carry):
            at = pl.ds(pl.multiple_of(t * TILE, TILE), TILE)
            to = pl.ds(pl.multiple_of(step * BAND + t * TILE + TILE, TILE), TILE)
            for g in range(GROUPS):
                cut = slice(g * LANES, (g + 1) * LANES)
                wet = m_ref[at, cut] == 1
                h = jnp.where(wet, d_ref[at, cut], 0.0)
                u = jnp.where(wet, x_ref[at, cut], 0.0)
                v = jnp.where(wet, y_ref[at, cut], 0.0)
                for dst, val in zip(cell, derived(h, u, v)):
                    dst[g, to, :] = val
            return carry

        lax.fori_loop(0, BAND // TILE, fill, 0, unroll=4)

    @pl.when(step == 0)
    def _():
        rows = bands * BAND
        for at, ref in ((0, up_ref), (rows + TILE, dn_ref)):
            for g in range(GROUPS):
                cut = slice(g * LANES, (g + 1) * LANES)
                line = [jnp.broadcast_to(ref[f:f + 1, cut], (TILE, LANES)) for f in range(3)]
                for dst, val in zip(cell, derived(*line)):
                    dst[g, pl.ds(at, TILE), :] = val
        outer = along_y(derived(lh_ref[0:1, :], lh_ref[1:2, :], lh_ref[2:3, :]))
        inner = along_y(derived(lo_ref[0:1, :], lo_ref[1:2, :], lo_ref[2:3, :]))
        edge[...] = jnp.zeros_like(edge)
        edge[0:3, :] = rh_ref[0:3, :]
        for f, val in enumerate(flux(outer, inner)):
            edge[3 + f:4 + f, :] = val

        def turn(b, carry):
            at = pl.ds(pl.multiple_of(b * LANES, LANES), LANES)
            ecol[at, :] = edge[:, at].T
            return carry

        lax.fori_loop(0, ecol.shape[0] // LANES, turn, 0)
        for g in range(GROUPS):
            now = along_x([ref[g, 0:TILE, :] for ref in cell])
            nxt = along_x([ref[g, 1:TILE + 1, :] for ref in cell])
            for dst, val in zip(gx, flux(now, nxt)):
                dst[g, 0:TILE, :] = val

    @pl.when(step > 0)
    def _():
        start = pl.multiple_of((step - 1) * BAND, BAND)

        def across(t, carry):
            base = pl.multiple_of(start + t * TILE + TILE, TILE)
            for g in range(GROUPS):
                now = along_x([ref[g, pl.ds(base, TILE), :] for ref in cell])
                nxt = along_x([ref[g, pl.ds(base + 1, TILE), :] for ref in cell])
                for dst, val in zip(gx, flux(now, nxt)):
                    dst[g, pl.ds(base, TILE), :] = val
            return carry

        lax.fori_loop(0, BAND // TILE, across, 0, unroll=2)

        def body(t, carry):
            mark = pl.multiple_of(start + t * TILE, TILE)
            base = pl.multiple_of(mark + TILE, TILE)
            at = pl.ds(pl.multiple_of(t * TILE, TILE), TILE)
            sides = ecol[pl.ds(mark, TILE), :]
            before = [pltpu.roll(sides, LANES - 4 - f, 1) for f in range(3)]
            for g in range(GROUPS):
                now = [ref[g, pl.ds(base, TILE), :] for ref in cell]
                if g < GROUPS - 1:
                    other = [ref[g + 1, pl.ds(base, TILE), :] for ref in cell[:3]]
                else:
                    other = [sides] + [pltpu.roll(sides, LANES - f, 1) for f in (1, 2)]
                right = [
                    pltpu.roll(jnp.where(lane == 0, o, c), LANES - 1, 1)
                    for o, c in zip(other, now[:3])
                ]
                fy = flux(along_y(now), along_y(derived(*right)))
                py = [
                    pltpu.roll(jnp.where(lane == LANES - 1, o, c), 1, 1)
                    for o, c in zip(before, fy)
                ]
                before = fy
                fx = [src[g, pl.ds(base, TILE), :] for src in gx]
                px = [src[g, pl.ds(base - 1, TILE), :] for src in gx]
                h, u, v = now[:3]
                ch = (fx[0] - px[0]) + (fy[0] - py[0])
                cx = (fx[1] - px[1]) + (fy[2] - py[2])
                cy = (fx[2] - px[2]) + (fy[1] - py[1])
                newh_ref[at, g * LANES:(g + 1) * LANES] = jnp.where(
                    h > 0.0, h - (0.5 * DT_DX) * ch, 0.0
                )
                hu_ref[g, at, :] = u - (0.5 * DT_DX) * cx
                hv_ref[g, at, :] = v - (0.5 * DT_DX) * cy
                h_ref[g, at, :] = h
            return carry

        lax.fori_loop(0, BAND // TILE, body, 0, unroll=2)


def stencil(depth, mask, momx, momy, up, dn, lh, rh, lo):
    rows, cols = depth.shape
    bands = rows // BAND
    plane = jax.ShapeDtypeStruct((GROUPS, rows, LANES), F32)
    pad = pltpu.VMEM((GROUPS, rows + 2 * TILE, LANES), F32)
    band = pl.BlockSpec((BAND, cols), lambda i: (jnp.minimum(i, bands - 1), 0))
    line = pl.BlockSpec((TILE, cols), lambda i: (0, 0))
    column = pl.BlockSpec((TILE, rows), lambda i: (0, 0))
    part = pl.BlockSpec((GROUPS, BAND, LANES), lambda i: (0, jnp.maximum(i - 1, 0), 0))
    return pl.pallas_call(
        stencil_kernel,
        grid=(bands + 1,),
        out_shape=(jax.ShapeDtypeStruct((rows, cols), F32), plane, plane, plane),
        in_specs=[band] * 4 + [line] * 2 + [column] * 3,
        out_specs=(
            pl.BlockSpec((BAND, cols), lambda i: (jnp.maximum(i - 1, 0), 0)), part, part, part,
        ),
        scratch_shapes=[pad] * (CELL + 3)
        + [pltpu.VMEM((LANES, rows), F32), pltpu.VMEM((rows, LANES), F32)],
        compiler_params=params(),
        cost_estimate=pl.CostEstimate(
            flops=200 * rows * cols, bytes_accessed=64 * rows * cols, transcendentals=0
        ),
        name="stencil",
    )(depth, mask, momx, momy, up, dn, lh, rh, lo)


def summed_of(lab, landed):
    select = (iota((NW * NPATCH, lab.shape[1]), 0) == lab).astype(BF16)
    return jnp.dot(select, landed, preferred_element_type=F32).astype(BF16)


def stack_left(left, summed, channels):
    for k in range(channels):
        for w in range(NW):
            left[k * NPATCH:(k + 1) * NPATCH, w * ABLK:(w + 1) * ABLK] = summed[
                w * NPATCH:(w + 1) * NPATCH, k * ABLK:(k + 1) * ABLK
            ]


PART = TILE * PATCH


def spread_rows(acc, field, k):
    low = iota((TILE, LANES), 1) < LANES // 2
    for t in range(TILE // 2):
        cut = slice(t * LANES, (t + 1) * LANES)
        for half in range(HALVES):
            for g in range(GROUPS):
                base = k * NPATCH + 2 * g * BPX + half * TILE
                even = acc[base:base + TILE, cut]
                odd = acc[base + BPX:base + BPX + TILE, cut]
                for i, val in (
                    (2 * t, jnp.where(low, even, pltpu.roll(odd, LANES // 2, 1))),
                    (2 * t + 1, jnp.where(low, pltpu.roll(even, LANES // 2, 1), odd)),
                ):
                    field[g, pl.ds(half * TILE * TILE + i, TILE, stride=TILE), :] = val


def press_kernel(
    lab_ref, landed_ref, w_ref, out_ref, top_ref, bottom_ref, left_ref, right_ref,
    left, acc, acc2, field, field2,
):
    step = pl.program_id(0)

    @pl.when(step == 0)
    def _():
        stack_left(left, summed_of(lab_ref[...], landed_ref[...]), 1)

    acc[...] = jnp.dot(left[...], w_ref[:, :PART], preferred_element_type=F32)
    acc2[...] = jnp.dot(left[...], w_ref[:, PART:], preferred_element_type=F32)
    for part, (src, mid) in enumerate(((acc, field), (acc2, field2))):
        spread_rows(src, mid, 0)
        for g in range(GROUPS):
            for r in range(BPX):
                to = pl.ds(pl.multiple_of(r * PATCH + (2 * step + part) * TILE, TILE), TILE)
                out_ref[g, to, :] = mid[g, r * TILE:(r + 1) * TILE, :]

    @pl.when(step == pl.num_programs(0) - 1)
    def _():
        rows = out_ref.shape[1]
        for g in range(GROUPS):
            cut = slice(g * LANES, (g + 1) * LANES)
            top_ref[:, cut] = out_ref[g, 0:TILE, :]
            bottom_ref[:, cut] = pltpu.roll(out_ref[g, rows - TILE:rows, :], 1, 0)
        lane = iota((LANES, LANES), 1)
        for b in range(rows // LANES):
            at = slice(b * LANES, (b + 1) * LANES)
            packed = jnp.where(
                lane == TILE,
                pltpu.roll(out_ref[GROUPS - 1, at, :], TILE + 1, 1),
                out_ref[0, at, :],
            )
            turned = packed.T
            left_ref[:, at] = turned[0:TILE]
            right_ref[:, at] = turned[TILE:2 * TILE]


def pressure_field(lab, landed, weights):
    steps = PATCH // (2 * TILE)
    rows = BPX * PATCH
    line = (TILE, BPY * PATCH)
    column = (TILE, rows)
    whole = (GROUPS, rows, LANES)

    def const(shape):
        return pl.BlockSpec(shape, lambda i: (0,) * len(shape))

    return pl.pallas_call(
        press_kernel,
        grid=(steps,),
        out_shape=tuple(jax.ShapeDtypeStruct(x, F32) for x in (whole, line, line, column, column)),
        in_specs=[
            const(lab.shape),
            const(landed.shape),
            pl.BlockSpec((NW * ABLK, 2 * PART), lambda i: (0, i)),
        ],
        out_specs=tuple(const(x) for x in (whole, line, line, column, column)),
        scratch_shapes=[
            pltpu.VMEM((NPATCH, NW * ABLK), BF16),
            pltpu.VMEM((NPATCH, PART), F32),
            pltpu.VMEM((NPATCH, PART), F32),
            pltpu.VMEM((GROUPS, BPX * TILE, LANES), F32),
            pltpu.VMEM((GROUPS, BPX * TILE, LANES), F32),
        ],
        compiler_params=params(32 << 20),
        cost_estimate=pl.CostEstimate(
            flops=2 * NPATCH * NW * ABLK * PATCH * PATCH, bytes_accessed=12 << 20, transcendentals=0
        ),
        name="pressure",
    )(lab, landed, weights)


def gradient_kernel(
    p_ref, hu_ref, hv_ref, h_ref, up_ref, dn_ref, lh_ref, rh_ref,
    ox_ref, oy_ref, fac_ref, padded, sides,
):
    step = pl.program_id(0)
    rows = p_ref.shape[1]

    @pl.when(step == 0)
    def _():
        stacked = jnp.concatenate([lh_ref[...], rh_ref[...]], axis=0)
        blank = jnp.zeros((LANES - 2 * TILE, LANES), F32)
        for b in range(rows // LANES):
            cut = slice(b * LANES, (b + 1) * LANES)
            sides[cut, :] = jnp.concatenate([stacked[:, cut], blank], axis=0).T
        for g in range(GROUPS):
            cut = slice(g * LANES, (g + 1) * LANES)
            padded[g, TILE:TILE + rows, :] = p_ref[g]
            padded[g, 0:TILE, :] = jnp.broadcast_to(up_ref[0:1, cut], (TILE, LANES))
            padded[g, rows + TILE:, :] = jnp.broadcast_to(dn_ref[0:1, cut], (TILE, LANES))

    lane = iota((TILE, LANES), 1)

    def body(t, carry):
        at = pl.ds(pl.multiple_of(t * TILE, TILE), TILE)
        mark = pl.multiple_of(step * BAND + t * TILE, TILE)
        base = pl.multiple_of(mark + TILE, TILE)
        ends = sides[pl.ds(mark, TILE), :]
        tiles = [padded[g, pl.ds(base, TILE), :] for g in range(GROUPS)]
        ups = [pltpu.roll(a, 1, 1) for a in tiles]
        downs = [pltpu.roll(a, LANES - 1, 1) for a in tiles]
        for g in range(GROUPS):
            before = ups[g - 1] if g else ends[:, 0:1]
            after = downs[g + 1] if g < GROUPS - 1 else ends[:, TILE:TILE + 1]
            prev = jnp.where(lane == 0, before, ups[g])
            nxt = jnp.where(lane == LANES - 1, after, downs[g])
            h = h_ref[g, at, :]
            wet = h > 0.0
            scale = (TIME_STEP * PRESS * 0.5) * h
            gx = padded[g, pl.ds(base + 1, TILE), :] - padded[g, pl.ds(base - 1, TILE), :]
            ox_ref[g, at, :] = jnp.where(wet, hu_ref[g, at, :] - scale * gx, 0.0)
            oy_ref[g, at, :] = jnp.where(wet, hv_ref[g, at, :] - scale * (nxt - prev), 0.0)
            fac_ref[g, at, :] = jnp.where(wet, TIME_STEP * STRESS, 0.0)
        return carry

    lax.fori_loop(0, BAND // TILE, body, 0, unroll=4)


def gradient(p, hu, hv, h, up, dn, lh, rh):
    rows = p.shape[1]
    plane = jax.ShapeDtypeStruct(p.shape, F32)
    part = pl.BlockSpec((GROUPS, BAND, LANES), lambda i: (0, i, 0))
    line = pl.BlockSpec(up.shape, lambda i: (0, 0))
    column = pl.BlockSpec(lh.shape, lambda i: (0, 0))
    return pl.pallas_call(
        gradient_kernel,
        grid=(rows // BAND,),
        out_shape=(plane,) * 3,
        in_specs=[pl.BlockSpec(p.shape, lambda i: (0, 0, 0))] + [part] * 3 + [line] * 2 + [column] * 2,
        out_specs=(part,) * 3,
        scratch_shapes=[
            pltpu.VMEM((GROUPS, rows + 2 * TILE, LANES), F32),
            pltpu.VMEM((rows, LANES), F32),
        ],
        compiler_params=params(24 << 20),
        cost_estimate=pl.CostEstimate(
            flops=20 * p.size, bytes_accessed=28 * p.size, transcendentals=0
        ),
        name="gradient",
    )(p, hu, hv, h, up, dn, lh, rh)


def wind_kernel(
    lab_ref, landed_ref, w_ref, hu_ref, hv_ref, fac_ref, ox_ref, oy_ref,
    left, acc, acc2, fx, fy, fx2, fy2,
):
    @pl.when(pl.program_id(0) == 0)
    def _():
        stack_left(left, summed_of(lab_ref[...], landed_ref[...]), 2)

    acc[...] = jnp.dot(left[...], w_ref[:, :PART], preferred_element_type=F32)
    acc2[...] = jnp.dot(left[...], w_ref[:, PART:], preferred_element_type=F32)
    for part, (src, mx, my) in enumerate(((acc, fx, fy), (acc2, fx2, fy2))):
        spread_rows(src, mx, 0)
        spread_rows(src, my, 1)
        cells = slice(part * TILE, (part + 1) * TILE)
        for g in range(GROUPS):
            for r in range(BPX):
                at = slice(r * TILE, (r + 1) * TILE)
                wx = mx[g, at, :]
                wy = my[g, at, :]
                speed = jnp.sqrt(wx * wx + wy * wy) * fac_ref[g, r, cells, :]
                cut = slice(g * LANES, (g + 1) * LANES)
                ox_ref[r, cells, cut] = hu_ref[g, r, cells, :] + speed * wx
                oy_ref[r, cells, cut] = hv_ref[g, r, cells, :] + speed * wy


def wind_field(lab, landed, weights, hu, hv, fac):
    deep = 2 * TILE
    steps = PATCH // deep
    cols = BPY * PATCH
    split = (GROUPS, BPX, PATCH, LANES)
    slab = pl.BlockSpec((GROUPS, BPX, deep, LANES), lambda i: (0, 0, i, 0))
    out = pl.BlockSpec((BPX, deep, cols), lambda i: (0, i, 0))
    shape = jax.ShapeDtypeStruct((BPX, PATCH, cols), F32)
    field = pltpu.VMEM((GROUPS, BPX * TILE, LANES), F32)
    return pl.pallas_call(
        wind_kernel,
        grid=(steps,),
        out_shape=(shape, shape),
        in_specs=[
            pl.BlockSpec(lab.shape, lambda i: (0, 0)),
            pl.BlockSpec(landed.shape, lambda i: (0, 0)),
            pl.BlockSpec((NW * ABLK, 2 * PART), lambda i: (0, i)),
            slab, slab, slab,
        ],
        out_specs=(out, out),
        scratch_shapes=[
            pltpu.VMEM((2 * NPATCH, NW * ABLK), BF16),
            pltpu.VMEM((2 * NPATCH, PART), F32),
            pltpu.VMEM((2 * NPATCH, PART), F32),
            field, field, field, field,
        ],
        compiler_params=params(40 << 20),
        cost_estimate=pl.CostEstimate(
            flops=4 * NPATCH * NW * ABLK * PATCH * PATCH, bytes_accessed=20 << 20, transcendentals=0
        ),
        name="wind",
    )(lab, landed, weights, hu.reshape(split), hv.reshape(split), fac.reshape(split))


def body(
    atm_blocks,
    remap_weights,
    ovl_source,
    ovl_block,
    ovl_patch,
    ovl_weight,
    depth_field,
    wet_mask,
    mom_x,
    mom_y,
    blend,
):
    count_x = lax.axis_size("gx")
    count_y = lax.axis_size("gy")
    devices = count_x * count_y
    entries = ovl_source.size
    capacity = 2 * entries // devices
    slots = devices * capacity
    atm = atm_blocks.reshape(atm_blocks.shape[2:]).transpose(1, 0, 2)
    both = ("gx", "gy")
    want, lab = make_requests(
        ovl_source.reshape(1, entries), ovl_block.reshape(1, entries),
        ovl_patch.reshape(1, entries), ovl_weight.reshape(1, entries), devices, capacity,
    )
    asked = lax.all_to_all(
        want.reshape(devices, 1, capacity), both, split_axis=0, concat_axis=0, tiled=True
    )
    lab = lab.reshape(1, slots)
    press, wind = mix(blend.reshape(1), atm)
    top, bottom, left, right = edge_cells(depth_field, wet_mask, mom_x, mom_y)

    def exchange(after, tiles):
        rows = serve(after, asked, tiles)
        parts = rows.reshape(devices, capacity, rows.shape[1])
        got = lax.all_to_all(parts, both, split_axis=0, concat_axis=0, tiled=True)
        return got.reshape(rows.shape)

    press = exchange(top, press)
    newh, hu, hv, h = stencil(
        depth_field, wet_mask, mom_x, mom_y,
        send(bottom, "gx", 1), send(top, "gx", -1),
        send(right, "gy", 1), send(left, "gy", -1), left,
    )
    wind = exchange(newh, wind)
    weights = remap_weights.reshape(NW * ABLK, PATCH * PATCH)
    p, top, bottom, left, right = pressure_field(lab, press, weights)
    hu, hv, fac = gradient(
        p, hu, hv, h,
        send(bottom, "gx", 1), send(top, "gx", -1),
        send(right, "gy", 1), send(left, "gy", -1),
    )
    new_x, new_y = wind_field(lab, wind, weights, hu, hv, fac)
    return (newh, new_x.reshape(newh.shape), new_y.reshape(newh.shape))


def solution(mesh):
    placed = (
        P("gx", "gy", None, None, None),
        P(),
        P("gx", "gy", None, None),
        P("gx", "gy", None),
        P("gx", "gy", None),
        P("gx", "gy", None),
        P("gx", "gy"),
        P("gx", "gy"),
        P("gx", "gy"),
        P("gx", "gy"),
        P(),
    )
    return jax.shard_map(
        body,
        mesh=mesh,
        in_specs=placed,
        out_specs=(P("gx", "gy"), P("gx", "gy"), P("gx", "gy")),
        check_vma=False,
    )
```

```python
import functools

import jax
import jax.numpy as jnp
from jax import lax
from jax.experimental import pallas as pl
from jax.experimental.pallas import tpu as pltpu
from jax.sharding import PartitionSpec as P

PATCH = 64
ABLK = 256
NW = 4
BPX = 16
BPY = 8
NPATCH = BPX * BPY

GRAV = 1.0
DT_DX = 0.2
TIME_STEP = 0.2
STRESS = 0.5
PRESS = 0.5

F32 = jnp.float32
BF16 = jnp.bfloat16
VMEM = pl.BlockSpec(memory_space=pltpu.VMEM)
SMEM = pl.BlockSpec(memory_space=pltpu.SMEM)
LANES = 128
TILE = 8
GROUPS = BPY * PATCH // LANES
HALVES = BPX // TILE
BAND = 128


def params(limit=56 << 20, **kw):
    return pltpu.CompilerParams(vmem_limit_bytes=limit, **kw)


def iota(shape, dim):
    return lax.broadcasted_iota(jnp.int32, shape, dim)


def rank_kernel(capacity, src_ref, blk_ref, pat_ref, wgt_ref, want_ref, lab_ref):
    devices = want_ref.shape[0]
    src = src_ref[...]
    ent = src.shape[1]
    hits = (iota((devices, ent), 0) == src).astype(F32)
    order = (iota((ent, ent), 0) <= iota((ent, ent), 1)).astype(BF16)
    ranks = jnp.dot(hits.astype(BF16), order, preferred_element_type=F32)
    mine = jnp.sum(hits * ranks, axis=0, keepdims=True).astype(jnp.int32) - 1
    place = iota((capacity, ent), 0) == mine
    pat = pat_ref[...]
    row_bits = BPX.bit_length() - 1
    col_bits = BPY.bit_length() - 1
    rows = jnp.zeros_like(pat)
    cols = jnp.zeros_like(pat)
    used_r = used_c = position = 0
    while used_r < row_bits or used_c < col_bits:
        value = jnp.bitwise_and(jnp.right_shift(pat, position), 1)
        if used_r < row_bits and (used_c >= col_bits or position % 2 == 0):
            rows = rows + value * (1 << used_r)
            used_r += 1
        else:
            cols = cols + value * (1 << used_c)
            used_c += 1
        position += 1

    def spread(row):
        picked = jnp.where(place, row.astype(F32), 0.0).astype(BF16)
        return lax.dot_general(
            hits.astype(BF16), picked, (((1,), (1,)), ((), ())),
            preferred_element_type=F32,
        ).astype(jnp.int32)

    want_ref[...] = spread(blk_ref[...])
    slot = spread(cols * BPX + rows)
    group = spread(wgt_ref[...] + 1)
    lab_ref[...] = jnp.where(group > 0, (group - 1) * NPATCH + slot, -1)


def make_requests(src, blk, pat, wgt, devices, capacity):
    shape = jax.ShapeDtypeStruct((devices, capacity), jnp.int32)
    return pl.pallas_call(
        functools.partial(rank_kernel, capacity),
        out_shape=(shape, shape),
        in_specs=[VMEM] * 4,
        out_specs=(VMEM, VMEM),
        compiler_params=params(),
        name="requests",
    )(src, blk, pat, wgt)


def mix_kernel(blend_ref, atm_ref, press_ref, wind_ref):
    blend = blend_ref[0]
    keep = 1.0 - blend

    def mixed(k):
        first = atm_ref[k].astype(F32)
        second = atm_ref[3 + k].astype(F32)
        return (keep * first + blend * second).astype(BF16)

    press_ref[...] = mixed(2)
    for k in range(2):
        wind_ref[:, k * ABLK:(k + 1) * ABLK] = mixed(k)


def mix(blend, atm):
    blocks = atm.shape[1]
    return pl.pallas_call(
        mix_kernel,
        out_shape=(
            jax.ShapeDtypeStruct((blocks, ABLK), BF16),
            jax.ShapeDtypeStruct((blocks, 2 * ABLK), BF16),
        ),
        in_specs=[SMEM, VMEM],
        out_specs=(VMEM, VMEM),
        compiler_params=params(),
        name="mix",
    )(blend, atm)


def serve_kernel(after_ref, asked_ref, tiles_ref, out_ref, turned, pick):
    peers, _, capacity = asked_ref.shape
    width = turned.shape[0]
    turned[...] = jnp.zeros_like(turned)
    turned[0:peers, 0:capacity] = asked_ref[:, 0, :]
    columns = turned[...].T
    blocks = tiles_ref.shape[0]
    names = iota((capacity, blocks), 1)
    for d in range(peers):
        pick[d * capacity:(d + 1) * capacity, :] = (columns[0:capacity, d:d + 1] == names).astype(F32)
    out_ref[...] = jnp.dot(
        pick[...].astype(BF16), tiles_ref[...], preferred_element_type=F32
    ).astype(BF16)


def serve(after, asked, tiles):
    peers, _, capacity = asked.shape
    slots = peers * capacity
    width = -(-max(peers, capacity) // LANES) * LANES
    return pl.pallas_call(
        serve_kernel,
        out_shape=jax.ShapeDtypeStruct((slots, tiles.shape[1]), BF16),
        in_specs=[pl.BlockSpec(memory_space=pl.ANY), VMEM, VMEM],
        out_specs=VMEM,
        scratch_shapes=[
            pltpu.VMEM((width, width), jnp.int32),
            pltpu.VMEM((slots, tiles.shape[0]), F32),
        ],
        compiler_params=params(32 << 20),
        name="serve",
    )(after, asked, tiles)


def edges_kernel(
    dl, ml, xl, yl, dr, mr, xr, yr, dt, mt, xt, yt, db, mb, xb, yb,
    top_ref, bottom_ref, left_ref, right_ref,
):
    def rows(d, m, x, y, at, out):
        wet = m[...] == 1
        for f, ref in enumerate((d, x, y)):
            out[f:f + 1, :] = jnp.where(wet, ref[...], 0.0)[at:at + 1]

    rows(dt, mt, xt, yt, 0, top_ref)
    rows(db, mb, xb, yb, TILE - 1, bottom_ref)
    lane = iota((LANES, LANES), 1)

    def step(b, carry):
        at = pl.ds(pl.multiple_of(b * LANES, LANES), LANES)
        wl = ml[at, :] == 1
        wr = mr[at, :] == 1
        packed = jnp.where(wl, dl[at, :], 0.0)
        packed = jnp.where(lane == 1, pltpu.roll(jnp.where(wl, xl[at, :], 0.0), 1, 1), packed)
        packed = jnp.where(lane == 2, pltpu.roll(jnp.where(wl, yl[at, :], 0.0), 2, 1), packed)
        packed = jnp.where(lane == 8, pltpu.roll(jnp.where(wr, dr[at, :], 0.0), 9, 1), packed)
        packed = jnp.where(lane == 9, pltpu.roll(jnp.where(wr, xr[at, :], 0.0), 10, 1), packed)
        packed = jnp.where(lane == 10, pltpu.roll(jnp.where(wr, yr[at, :], 0.0), 11, 1), packed)
        turned = packed.T
        left_ref[:, at] = turned[0:TILE]
        right_ref[:, at] = turned[TILE:2 * TILE]
        return carry

    lax.fori_loop(0, dl.shape[0] // LANES, step, 0)


def edge_cells(depth, mask, momx, momy):
    rows, cols = depth.shape
    fields = (depth, mask, momx, momy)
    left = pl.BlockSpec((rows, LANES), lambda i: (0, 0))
    right = pl.BlockSpec((rows, LANES), lambda i: (0, cols // LANES - 1))
    top = pl.BlockSpec((TILE, cols), lambda i: (0, 0))
    bottom = pl.BlockSpec((TILE, cols), lambda i: (rows // TILE - 1, 0))
    line = jax.ShapeDtypeStruct((TILE, cols), F32)
    column = jax.ShapeDtypeStruct((TILE, rows), F32)
    return pl.pallas_call(
        edges_kernel,
        grid=(1,),
        out_shape=(line, line, column, column),
        in_specs=[left] * 4 + [right] * 4 + [top] * 4 + [bottom] * 4,
        out_specs=(
            pl.BlockSpec((TILE, cols), lambda i: (0, 0)),
            pl.BlockSpec((TILE, cols), lambda i: (0, 0)),
            pl.BlockSpec((TILE, rows), lambda i: (0, 0)),
            pl.BlockSpec((TILE, rows), lambda i: (0, 0)),
        ),
        compiler_params=params(),
        name="edges",
    )(*(fields * 4))


def send(value, axis, step):
    count = lax.axis_size(axis)
    if step > 0:
        pairs = [(i, i + 1) for i in range(count - 1)]
    else:
        pairs = [(i + 1, i) for i in range(count - 1)]
    return lax.ppermute(value, axis, pairs)


def derived(h, u, v):
    r = jnp.where(h > 0.0, lax.rsqrt(h), 0.0)
    s = h * r
    q = u * r
    p = v * r
    half = 0.5 * h * h
    return (h, u, v, s, q, p, q * q + half, p * p + half, q * p)


def along_x(c):
    return (c[0], c[1], c[2], c[3], c[4], c[5], c[6], c[8])


def along_y(c):
    return (c[0], c[2], c[1], c[3], c[5], c[4], c[7], c[8])


def flux(a, b):
    hl, nl, tl, sl, ql, pl_, fl, gl = a
    hr, nr, tr, sr, qr, pr, fr, gr = b
    both = jnp.minimum(hl, hr) > 0.0
    half = jnp.where(both, 0.5, 1.0)
    twice = half + half
    level = (hl + hr) * half
    rc = lax.rsqrt(level)
    c = level * rc
    total = sl + sr
    inv = pl.reciprocal(total, approx=True)
    inv = inv * (2.0 - total * inv)
    u = jnp.where(both, (ql + qr) * inv, 0.0)
    v = (pl_ + pr) * inv
    dh = jnp.where(both, hr - hl, 0.0)
    dn = (nr - nl) * twice
    dt = jnp.where(both, tr - tl, 0.0)
    mid = 0.5 * dh
    e = (0.5 * dn - u * mid) * rc
    s1 = u - c
    s3 = u + c
    b1 = jnp.abs(s1) * (mid - e)
    b3 = jnp.abs(s3) * (mid + e)
    b2 = jnp.abs(u) * (dt - v * dh)
    d = b1 + b3
    return (
        jnp.where(both, nl + nr, 0.0) - d,
        (fl + fr) * twice - (b1 * s1 + b3 * s3),
        jnp.where(both, gl + gr, 0.0) - (d * v + b2),
    )


CELL = 9


def stencil_kernel(
    d_ref, m_ref, x_ref, y_ref, newh_ref, hu_ref, hv_ref, h_ref, *scratch,
):
    cell = scratch[:CELL]
    gx = scratch[CELL:]
    step = pl.program_id(0)
    bands = pl.num_programs(0) - 1
    lane = iota((TILE, LANES), 1)

    @pl.when(step < bands)
    def _():
        def fill(t, carry):
            at = pl.ds(pl.multiple_of(t * TILE, TILE), TILE)
            to = pl.ds(pl.multiple_of(step * BAND + t * TILE + TILE, TILE), TILE)
            for g in range(GROUPS):
                cut = slice(g * LANES, (g + 1) * LANES)
                wet = m_ref[at, cut] == 1
                h = jnp.where(wet, d_ref[at, cut], 0.0)
                u = jnp.where(wet, x_ref[at, cut], 0.0)
                v = jnp.where(wet, y_ref[at, cut], 0.0)
                for dst, val in zip(cell, derived(h, u, v)):
                    dst[g, to, :] = val
            return carry

        lax.fori_loop(0, BAND // TILE, fill, 0, unroll=4)

    rows = bands * BAND

    @pl.when(step == 0)
    def _():
        for dst in cell:
            dst[:, rows + TILE:, :] = jnp.zeros((GROUPS, TILE, LANES), F32)
        for dst in gx:
            dst[:, 0:TILE, :] = jnp.zeros((GROUPS, TILE, LANES), F32)

    @pl.when(step > 0)
    def _():
        start = pl.multiple_of((step - 1) * BAND, BAND)

        def across(t, carry):
            base = pl.multiple_of(start + t * TILE + TILE, TILE)
            for g in range(GROUPS):
                now = along_x([ref[g, pl.ds(base, TILE), :] for ref in cell])
                nxt = along_x([ref[g, pl.ds(base + 1, TILE), :] for ref in cell])
                for dst, val in zip(gx, flux(now, nxt)):
                    dst[g, pl.ds(base, TILE), :] = val
            return carry

        lax.fori_loop(0, BAND // TILE, across, 0, unroll=4)

        @pl.when(step == bands)
        def _():
            for dst in gx:
                dst[:, rows + TILE - 1:rows + TILE, :] = jnp.zeros((GROUPS, 1, LANES), F32)

        def body(t, carry):
            mark = pl.multiple_of(start + t * TILE, TILE)
            base = pl.multiple_of(mark + TILE, TILE)
            at = pl.ds(pl.multiple_of(t * TILE, TILE), TILE)
            before = [jnp.zeros((TILE, LANES), F32)] * 3
            for g in range(GROUPS):
                now = [ref[g, pl.ds(base, TILE), :] for ref in cell]
                if g < GROUPS - 1:
                    other = [ref[g + 1, pl.ds(base, TILE), :] for ref in cell[:3]]
                else:
                    other = now[:3]
                right = [
                    pltpu.roll(jnp.where(lane == 0, o, c), LANES - 1, 1)
                    for o, c in zip(other, now[:3])
                ]
                fy = flux(along_y(now), along_y(derived(*right)))
                if g == GROUPS - 1:
                    fy = [jnp.where(lane == LANES - 1, 0.0, val) for val in fy]
                py = [
                    pltpu.roll(jnp.where(lane == LANES - 1, o, c), 1, 1)
                    for o, c in zip(before, fy)
                ]
                before = fy
                fx = [src[g, pl.ds(base, TILE), :] for src in gx]
                px = [src[g, pl.ds(base - 1, TILE), :] for src in gx]
                h, u, v = now[:3]
                ch = (fx[0] - px[0]) + (fy[0] - py[0])
                cx = (fx[1] - px[1]) + (fy[2] - py[2])
                cy = (fx[2] - px[2]) + (fy[1] - py[1])
                newh_ref[g, at, :] = h - (0.5 * DT_DX) * ch
                hu_ref[g, at, :] = u - (0.5 * DT_DX) * cx
                hv_ref[g, at, :] = v - (0.5 * DT_DX) * cy
                h_ref[g, at, :] = h
            return carry

        lax.fori_loop(0, BAND // TILE, body, 0, unroll=4)


def stencil(depth, mask, momx, momy):
    rows, cols = depth.shape
    bands = rows // BAND
    plane = jax.ShapeDtypeStruct((GROUPS, rows, LANES), F32)
    pad = pltpu.VMEM((GROUPS, rows + 2 * TILE, LANES), F32)
    band = pl.BlockSpec((BAND, cols), lambda i: (jnp.minimum(i, bands - 1), 0))
    part = pl.BlockSpec((GROUPS, BAND, LANES), lambda i: (0, jnp.maximum(i - 1, 0), 0))
    return pl.pallas_call(
        stencil_kernel,
        grid=(bands + 1,),
        out_shape=(plane,) * 4,
        in_specs=[band] * 4,
        out_specs=(part,) * 4,
        scratch_shapes=[pad] * (CELL + 3),
        compiler_params=params(),
        cost_estimate=pl.CostEstimate(
            flops=200 * rows * cols, bytes_accessed=64 * rows * cols, transcendentals=0
        ),
        name="stencil",
    )(depth, mask, momx, momy)


def summed_of(lab, landed):
    select = (iota((NW * NPATCH, lab.shape[1]), 0) == lab).astype(BF16)
    return jnp.dot(select, landed, preferred_element_type=F32).astype(BF16)


def stack_left(left, summed, channels):
    for k in range(channels):
        for w in range(NW):
            left[k * NPATCH:(k + 1) * NPATCH, w * ABLK:(w + 1) * ABLK] = summed[
                w * NPATCH:(w + 1) * NPATCH, k * ABLK:(k + 1) * ABLK
            ]


PART = TILE * PATCH


def spread_rows(acc, field, k):
    low = iota((TILE, LANES), 1) < LANES // 2
    for t in range(TILE // 2):
        cut = slice(t * LANES, (t + 1) * LANES)
        for half in range(HALVES):
            for g in range(GROUPS):
                base = k * NPATCH + 2 * g * BPX + half * TILE
                even = acc[base:base + TILE, cut]
                odd = acc[base + BPX:base + BPX + TILE, cut]
                for i, val in (
                    (2 * t, jnp.where(low, even, pltpu.roll(odd, LANES // 2, 1))),
                    (2 * t + 1, jnp.where(low, pltpu.roll(even, LANES // 2, 1), odd)),
                ):
                    field[g, pl.ds(half * TILE * TILE + i, TILE, stride=TILE), :] = val


def press_kernel(
    lab_ref, landed_ref, w_ref, top0_ref, bottom0_ref, left0_ref, right0_ref,
    out_ref, top_ref, bottom_ref, left_ref, right_ref,
    left, acc, acc2, field, field2,
):
    step = pl.program_id(0)

    @pl.when(step == 0)
    def _():
        stack_left(left, summed_of(lab_ref[...], landed_ref[...]), 1)

    acc[...] = jnp.dot(left[...], w_ref[:, :PART], preferred_element_type=F32)
    acc2[...] = jnp.dot(left[...], w_ref[:, PART:], preferred_element_type=F32)
    for part, (src, mid) in enumerate(((acc, field), (acc2, field2))):
        spread_rows(src, mid, 0)
        for g in range(GROUPS):
            for r in range(BPX):
                to = pl.ds(pl.multiple_of(r * PATCH + (2 * step + part) * TILE, TILE), TILE)
                out_ref[g, to, :] = mid[g, r * TILE:(r + 1) * TILE, :]

    @pl.when(step == pl.num_programs(0) - 1)
    def _():
        rows = out_ref.shape[1]
        mine = iota((TILE, LANES), 0) == 3
        for g in range(GROUPS):
            cut = slice(g * LANES, (g + 1) * LANES)
            head = pltpu.roll(out_ref[g, 0:TILE, :], 3, 0)
            tail = pltpu.roll(out_ref[g, rows - TILE:rows, :], 4, 0)
            top_ref[:, cut] = jnp.where(mine, head, top0_ref[:, cut])
            bottom_ref[:, cut] = jnp.where(mine, tail, bottom0_ref[:, cut])
        lane = iota((LANES, LANES), 1)
        for b in range(rows // LANES):
            at = slice(b * LANES, (b + 1) * LANES)
            packed = jnp.where(
                lane == TILE + 3,
                pltpu.roll(out_ref[GROUPS - 1, at, :], TILE + 4, 1),
                pltpu.roll(out_ref[0, at, :], 3, 1),
            )
            turned = packed.T
            left_ref[:, at] = jnp.where(mine, turned[0:TILE], left0_ref[:, at])
            right_ref[:, at] = jnp.where(mine, turned[TILE:2 * TILE], right0_ref[:, at])


def pressure_field(lab, landed, weights, edges):
    steps = PATCH // (2 * TILE)
    rows = BPX * PATCH
    line = (TILE, BPY * PATCH)
    column = (TILE, rows)
    whole = (GROUPS, rows, LANES)

    def const(shape):
        return pl.BlockSpec(shape, lambda i: (0,) * len(shape))

    return pl.pallas_call(
        press_kernel,
        grid=(steps,),
        out_shape=tuple(jax.ShapeDtypeStruct(x, F32) for x in (whole, line, line, column, column)),
        in_specs=[
            const(lab.shape),
            const(landed.shape),
            pl.BlockSpec((NW * ABLK, 2 * PART), lambda i: (0, i)),
        ] + [const(x) for x in (line, line, column, column)],
        out_specs=tuple(const(x) for x in (whole, line, line, column, column)),
        scratch_shapes=[
            pltpu.VMEM((NPATCH, NW * ABLK), BF16),
            pltpu.VMEM((NPATCH, PART), F32),
            pltpu.VMEM((NPATCH, PART), F32),
            pltpu.VMEM((GROUPS, BPX * TILE, LANES), F32),
            pltpu.VMEM((GROUPS, BPX * TILE, LANES), F32),
        ],
        compiler_params=params(),
        cost_estimate=pl.CostEstimate(
            flops=2 * NPATCH * NW * ABLK * PATCH * PATCH, bytes_accessed=12 << 20, transcendentals=0
        ),
        name="pressure",
    )(lab, landed, weights, *edges)


def settle_kernel(
    p_ref, newh_ref, hu_ref, hv_ref, h_ref, up_ref, dn_ref, lh_ref, rh_ref,
    top_ref, bottom_ref, left_ref, right_ref,
    oh_ref, ox_ref, oy_ref, fac_ref, padded, edge, sides,
):
    step = pl.program_id(0)
    rows = p_ref.shape[1]

    def cells(ref):
        return derived(ref[0:1, :], ref[1:2, :], ref[2:3, :])

    def add_row(before, after, at, own_ref, sign):
        gh, gn, gt = flux(along_x(cells(before)), along_x(cells(after)))
        wet = own_ref[0:1, :] > 0.0
        fix = [jnp.where(wet, (sign * 0.5 * DT_DX) * val, 0.0) for val in (gh, gn, gt)]
        oh_ref[at:at + 1, :] += fix[0]
        for g in range(GROUPS):
            cut = slice(g * LANES, (g + 1) * LANES)
            ox_ref[g, at:at + 1, :] += fix[1][:, cut]
            oy_ref[g, at:at + 1, :] += fix[2][:, cut]

    @pl.when(step == 0)
    def _():
        edge[0:1, :] = lh_ref[3:4, :]
        edge[1:2, :] = rh_ref[3:4, :]
        for at, before, after, sign in ((2, lh_ref, left_ref, 1.0), (5, right_ref, rh_ref, -1.0)):
            gh, gn, gt = flux(along_y(cells(before)), along_y(cells(after)))
            for f, val in enumerate((gh, gt, gn)):
                edge[at + f:at + f + 1, :] = (sign * 0.5 * DT_DX) * val
        blank = jnp.zeros((LANES - TILE, LANES), F32)
        for b in range(rows // LANES):
            cut = slice(b * LANES, (b + 1) * LANES)
            sides[cut, :] = jnp.concatenate([edge[:, cut], blank], axis=0).T
        for g in range(GROUPS):
            cut = slice(g * LANES, (g + 1) * LANES)
            padded[g, TILE:TILE + rows, :] = p_ref[g]
            padded[g, 0:TILE, :] = jnp.broadcast_to(up_ref[3:4, cut], (TILE, LANES))
            padded[g, rows + TILE:, :] = jnp.broadcast_to(dn_ref[3:4, cut], (TILE, LANES))

    lane = iota((TILE, LANES), 1)

    def body(t, carry):
        at = pl.ds(pl.multiple_of(t * TILE, TILE), TILE)
        mark = pl.multiple_of(step * BAND + t * TILE, TILE)
        base = pl.multiple_of(mark + TILE, TILE)
        ends = sides[pl.ds(mark, TILE), :]
        tiles = [padded[g, pl.ds(base, TILE), :] for g in range(GROUPS)]
        ups = [pltpu.roll(a, 1, 1) for a in tiles]
        downs = [pltpu.roll(a, LANES - 1, 1) for a in tiles]
        for g in range(GROUPS):
            before = ups[g - 1] if g else ends[:, 0:1]
            after = downs[g + 1] if g < GROUPS - 1 else ends[:, 1:2]
            prev = jnp.where(lane == 0, before, ups[g])
            nxt = jnp.where(lane == LANES - 1, after, downs[g])
            h = h_ref[g, at, :]
            wet = h > 0.0
            scale = (TIME_STEP * PRESS * 0.5) * h
            gx = padded[g, pl.ds(base + 1, TILE), :] - padded[g, pl.ds(base - 1, TILE), :]
            new = [
                newh_ref[g, at, :],
                hu_ref[g, at, :] - scale * gx,
                hv_ref[g, at, :] - scale * (nxt - prev),
            ]
            if g == 0:
                new = [jnp.where(lane == 0, a + ends[:, 2 + f:3 + f], a) for f, a in enumerate(new)]
            if g == GROUPS - 1:
                new = [
                    jnp.where(lane == LANES - 1, a + ends[:, 5 + f:6 + f], a)
                    for f, a in enumerate(new)
                ]
            oh_ref[at, g * LANES:(g + 1) * LANES] = jnp.where(wet, new[0], 0.0)
            ox_ref[g, at, :] = jnp.where(wet, new[1], 0.0)
            oy_ref[g, at, :] = jnp.where(wet, new[2], 0.0)
            fac_ref[g, at, :] = jnp.where(wet, TIME_STEP * STRESS, 0.0)
        return carry

    lax.fori_loop(0, BAND // TILE, body, 0, unroll=4)

    @pl.when(step == 0)
    def _():
        add_row(up_ref, top_ref, 0, top_ref, 1.0)

    @pl.when(step == pl.num_programs(0) - 1)
    def _():
        add_row(bottom_ref, dn_ref, BAND - 1, bottom_ref, -1.0)


def settle(p, newh, hu, hv, h, halos, edges):
    rows = p.shape[1]
    cols = GROUPS * LANES
    plane = jax.ShapeDtypeStruct(p.shape, F32)
    part = pl.BlockSpec((GROUPS, BAND, LANES), lambda i: (0, i, 0))
    line = pl.BlockSpec((TILE, cols), lambda i: (0, 0))
    column = pl.BlockSpec((TILE, rows), lambda i: (0, 0))
    return pl.pallas_call(
        settle_kernel,
        grid=(rows // BAND,),
        out_shape=(jax.ShapeDtypeStruct((rows, cols), F32),) + (plane,) * 3,
        in_specs=[pl.BlockSpec(p.shape, lambda i: (0, 0, 0))] + [part] * 4
        + [line, line, column, column] * 2,
        out_specs=(pl.BlockSpec((BAND, cols), lambda i: (i, 0)),) + (part,) * 3,
        scratch_shapes=[
            pltpu.VMEM((GROUPS, rows + 2 * TILE, LANES), F32),
            pltpu.VMEM((TILE, rows), F32),
            pltpu.VMEM((rows, LANES), F32),
        ],
        compiler_params=params(),
        cost_estimate=pl.CostEstimate(
            flops=20 * p.size, bytes_accessed=36 * p.size, transcendentals=0
        ),
        name="settle",
    )(p, newh, hu, hv, h, *halos, *edges)


def wind_kernel(
    lab_ref, landed_ref, w_ref, hu_ref, hv_ref, fac_ref, ox_ref, oy_ref,
    left, acc, acc2, fx, fy, fx2, fy2,
):
    @pl.when(pl.program_id(0) == 0)
    def _():
        stack_left(left, summed_of(lab_ref[...], landed_ref[...]), 2)

    acc[...] = jnp.dot(left[...], w_ref[:, :PART], preferred_element_type=F32)
    acc2[...] = jnp.dot(left[...], w_ref[:, PART:], preferred_element_type=F32)
    for part, (src, mx, my) in enumerate(((acc, fx, fy), (acc2, fx2, fy2))):
        spread_rows(src, mx, 0)
        spread_rows(src, my, 1)
        cells = slice(part * TILE, (part + 1) * TILE)
        for g in range(GROUPS):
            for r in range(BPX):
                at = slice(r * TILE, (r + 1) * TILE)
                wx = mx[g, at, :]
                wy = my[g, at, :]
                speed = jnp.sqrt(wx * wx + wy * wy) * fac_ref[g, r, cells, :]
                cut = slice(g * LANES, (g + 1) * LANES)
                ox_ref[r, cells, cut] = hu_ref[g, r, cells, :] + speed * wx
                oy_ref[r, cells, cut] = hv_ref[g, r, cells, :] + speed * wy


def wind_field(lab, landed, weights, hu, hv, fac):
    deep = 2 * TILE
    steps = PATCH // deep
    cols = BPY * PATCH
    split = (GROUPS, BPX, PATCH, LANES)
    slab = pl.BlockSpec((GROUPS, BPX, deep, LANES), lambda i: (0, 0, i, 0))
    out = pl.BlockSpec((BPX, deep, cols), lambda i: (0, i, 0))
    shape = jax.ShapeDtypeStruct((BPX, PATCH, cols), F32)
    field = pltpu.VMEM((GROUPS, BPX * TILE, LANES), F32)
    return pl.pallas_call(
        wind_kernel,
        grid=(steps,),
        out_shape=(shape, shape),
        in_specs=[
            pl.BlockSpec(lab.shape, lambda i: (0, 0)),
            pl.BlockSpec(landed.shape, lambda i: (0, 0)),
            pl.BlockSpec((NW * ABLK, 2 * PART), lambda i: (0, i)),
            slab, slab, slab,
        ],
        out_specs=(out, out),
        scratch_shapes=[
            pltpu.VMEM((2 * NPATCH, NW * ABLK), BF16),
            pltpu.VMEM((2 * NPATCH, PART), F32),
            pltpu.VMEM((2 * NPATCH, PART), F32),
            field, field, field, field,
        ],
        compiler_params=params(),
        cost_estimate=pl.CostEstimate(
            flops=4 * NPATCH * NW * ABLK * PATCH * PATCH, bytes_accessed=20 << 20, transcendentals=0
        ),
        name="wind",
    )(lab, landed, weights, hu.reshape(split), hv.reshape(split), fac.reshape(split))


def body(
    atm_blocks,
    remap_weights,
    ovl_source,
    ovl_block,
    ovl_patch,
    ovl_weight,
    depth_field,
    wet_mask,
    mom_x,
    mom_y,
    blend,
):
    count_x = lax.axis_size("gx")
    count_y = lax.axis_size("gy")
    devices = count_x * count_y
    entries = ovl_source.size
    capacity = 2 * entries // devices
    slots = devices * capacity
    atm = atm_blocks.reshape(atm_blocks.shape[2:]).transpose(1, 0, 2)
    both = ("gx", "gy")
    want, lab = make_requests(
        ovl_source.reshape(1, entries), ovl_block.reshape(1, entries),
        ovl_patch.reshape(1, entries), ovl_weight.reshape(1, entries), devices, capacity,
    )
    asked = lax.all_to_all(
        want.reshape(devices, 1, capacity), both, split_axis=0, concat_axis=0, tiled=True
    )
    lab = lab.reshape(1, slots)
    press, wind = mix(blend.reshape(1), atm)
    top, bottom, left, right = edge_cells(depth_field, wet_mask, mom_x, mom_y)

    def exchange(after, tiles):
        rows = serve(after, asked, tiles)
        parts = rows.reshape(devices, capacity, rows.shape[1])
        got = lax.all_to_all(parts, both, split_axis=0, concat_axis=0, tiled=True)
        return got.reshape(rows.shape)

    press = exchange(top, press)
    newh, hu, hv, h = stencil(depth_field, wet_mask, mom_x, mom_y)
    wind = exchange(newh, wind)
    weights = remap_weights.reshape(NW * ABLK, PATCH * PATCH)
    p, top, bottom, left, right = pressure_field(lab, press, weights, (top, bottom, left, right))
    halos = (
        send(bottom, "gx", 1), send(top, "gx", -1), send(right, "gy", 1), send(left, "gy", -1),
    )
    newh, hu, hv, fac = settle(p, newh, hu, hv, h, halos, (top, bottom, left, right))
    new_x, new_y = wind_field(lab, wind, weights, hu, hv, fac)
    return (newh, new_x.reshape(newh.shape), new_y.reshape(newh.shape))


def solution(mesh):
    placed = (
        P("gx", "gy", None, None, None),
        P(),
        P("gx", "gy", None, None),
        P("gx", "gy", None),
        P("gx", "gy", None),
        P("gx", "gy", None),
        P("gx", "gy"),
        P("gx", "gy"),
        P("gx", "gy"),
        P("gx", "gy"),
        P(),
    )
    return jax.shard_map(
        body,
        mesh=mesh,
        in_specs=placed,
        out_specs=(P("gx", "gy"), P("gx", "gy"), P("gx", "gy")),
        check_vma=False,
    )
```

```python
import functools

import jax
import jax.numpy as jnp
from jax import lax
from jax.experimental import pallas as pl
from jax.experimental.pallas import tpu as pltpu
from jax.sharding import PartitionSpec as P

PATCH = 64
ABLK = 256
NW = 4
BPX = 16
BPY = 8
NPATCH = BPX * BPY

GRAV = 1.0
DT_DX = 0.2
TIME_STEP = 0.2
STRESS = 0.5
PRESS = 0.5

F32 = jnp.float32
BF16 = jnp.bfloat16
VMEM = pl.BlockSpec(memory_space=pltpu.VMEM)
SMEM = pl.BlockSpec(memory_space=pltpu.SMEM)
LANES = 128
TILE = 8
GROUPS = BPY * PATCH // LANES
HALVES = BPX // TILE
BAND = 128


def params(limit=56 << 20, **kw):
    return pltpu.CompilerParams(vmem_limit_bytes=limit, **kw)


def iota(shape, dim):
    return lax.broadcasted_iota(jnp.int32, shape, dim)


def rank_kernel(capacity, src_ref, blk_ref, pat_ref, wgt_ref, want_ref, lab_ref):
    devices = want_ref.shape[0]
    src = src_ref[...]
    ent = src.shape[1]
    hits = (iota((devices, ent), 0) == src).astype(F32)
    order = (iota((ent, ent), 0) <= iota((ent, ent), 1)).astype(BF16)
    ranks = jnp.dot(hits.astype(BF16), order, preferred_element_type=F32)
    mine = jnp.sum(hits * ranks, axis=0, keepdims=True).astype(jnp.int32) - 1
    place = iota((capacity, ent), 0) == mine
    pat = pat_ref[...]
    row_bits = BPX.bit_length() - 1
    col_bits = BPY.bit_length() - 1
    rows = jnp.zeros_like(pat)
    cols = jnp.zeros_like(pat)
    used_r = used_c = position = 0
    while used_r < row_bits or used_c < col_bits:
        value = jnp.bitwise_and(jnp.right_shift(pat, position), 1)
        if used_r < row_bits and (used_c >= col_bits or position % 2 == 0):
            rows = rows + value * (1 << used_r)
            used_r += 1
        else:
            cols = cols + value * (1 << used_c)
            used_c += 1
        position += 1

    def spread(row):
        picked = jnp.where(place, row.astype(F32), 0.0).astype(BF16)
        return lax.dot_general(
            hits.astype(BF16), picked, (((1,), (1,)), ((), ())),
            preferred_element_type=F32,
        ).astype(jnp.int32)

    want_ref[...] = spread(blk_ref[...])
    slot = spread(cols * BPX + rows)
    group = spread(wgt_ref[...] + 1)
    lab_ref[...] = jnp.where(group > 0, (group - 1) * NPATCH + slot, -1)


def make_requests(src, blk, pat, wgt, devices, capacity):
    shape = jax.ShapeDtypeStruct((devices, capacity), jnp.int32)
    return pl.pallas_call(
        functools.partial(rank_kernel, capacity),
        out_shape=(shape, shape),
        in_specs=[VMEM] * 4,
        out_specs=(VMEM, VMEM),
        compiler_params=params(),
        name="requests",
    )(src, blk, pat, wgt)


def mix_kernel(blend_ref, atm_ref, press_ref, wind_ref):
    blend = blend_ref[0]
    keep = 1.0 - blend

    def mixed(k):
        first = atm_ref[k].astype(F32)
        second = atm_ref[3 + k].astype(F32)
        return (keep * first + blend * second).astype(BF16)

    press_ref[...] = mixed(2)
    for k in range(2):
        wind_ref[:, k * ABLK:(k + 1) * ABLK] = mixed(k)


def mix(blend, atm):
    blocks = atm.shape[1]
    return pl.pallas_call(
        mix_kernel,
        out_shape=(
            jax.ShapeDtypeStruct((blocks, ABLK), BF16),
            jax.ShapeDtypeStruct((blocks, 2 * ABLK), BF16),
        ),
        in_specs=[SMEM, VMEM],
        out_specs=(VMEM, VMEM),
        compiler_params=params(),
        name="mix",
    )(blend, atm)


def serve_kernel(after_ref, asked_ref, tiles_ref, out_ref, turned, pick):
    peers, _, capacity = asked_ref.shape
    width = turned.shape[0]
    turned[...] = jnp.zeros_like(turned)
    turned[0:peers, 0:capacity] = asked_ref[:, 0, :]
    columns = turned[...].T
    blocks = tiles_ref.shape[0]
    names = iota((capacity, blocks), 1)
    for d in range(peers):
        pick[d * capacity:(d + 1) * capacity, :] = (columns[0:capacity, d:d + 1] == names).astype(F32)
    out_ref[...] = jnp.dot(
        pick[...].astype(BF16), tiles_ref[...], preferred_element_type=F32
    ).astype(BF16)


def serve(after, asked, tiles):
    peers, _, capacity = asked.shape
    slots = peers * capacity
    width = -(-max(peers, capacity) // LANES) * LANES
    return pl.pallas_call(
        serve_kernel,
        out_shape=jax.ShapeDtypeStruct((slots, tiles.shape[1]), BF16),
        in_specs=[pl.BlockSpec(memory_space=pl.ANY), VMEM, VMEM],
        out_specs=VMEM,
        scratch_shapes=[
            pltpu.VMEM((width, width), jnp.int32),
            pltpu.VMEM((slots, tiles.shape[0]), F32),
        ],
        compiler_params=params(32 << 20),
        name="serve",
    )(after, asked, tiles)


def edges_kernel(
    dl, ml, xl, yl, dr, mr, xr, yr, dt, mt, xt, yt, db, mb, xb, yb,
    top_ref, bottom_ref, left_ref, right_ref,
):
    def rows(d, m, x, y, at, out):
        wet = m[...] == 1
        for f, ref in enumerate((d, x, y)):
            out[f:f + 1, :] = jnp.where(wet, ref[...], 0.0)[at:at + 1]

    rows(dt, mt, xt, yt, 0, top_ref)
    rows(db, mb, xb, yb, TILE - 1, bottom_ref)
    lane = iota((LANES, LANES), 1)

    def step(b, carry):
        at = pl.ds(pl.multiple_of(b * LANES, LANES), LANES)
        wl = ml[at, :] == 1
        wr = mr[at, :] == 1
        packed = jnp.where(wl, dl[at, :], 0.0)
        packed = jnp.where(lane == 1, pltpu.roll(jnp.where(wl, xl[at, :], 0.0), 1, 1), packed)
        packed = jnp.where(lane == 2, pltpu.roll(jnp.where(wl, yl[at, :], 0.0), 2, 1), packed)
        packed = jnp.where(lane == 8, pltpu.roll(jnp.where(wr, dr[at, :], 0.0), 9, 1), packed)
        packed = jnp.where(lane == 9, pltpu.roll(jnp.where(wr, xr[at, :], 0.0), 10, 1), packed)
        packed = jnp.where(lane == 10, pltpu.roll(jnp.where(wr, yr[at, :], 0.0), 11, 1), packed)
        turned = packed.T
        left_ref[:, at] = turned[0:TILE]
        right_ref[:, at] = turned[TILE:2 * TILE]
        return carry

    lax.fori_loop(0, dl.shape[0] // LANES, step, 0)


def edge_cells(depth, mask, momx, momy):
    rows, cols = depth.shape
    fields = (depth, mask, momx, momy)
    left = pl.BlockSpec((rows, LANES), lambda i: (0, 0))
    right = pl.BlockSpec((rows, LANES), lambda i: (0, cols // LANES - 1))
    top = pl.BlockSpec((TILE, cols), lambda i: (0, 0))
    bottom = pl.BlockSpec((TILE, cols), lambda i: (rows // TILE - 1, 0))
    line = jax.ShapeDtypeStruct((TILE, cols), F32)
    column = jax.ShapeDtypeStruct((TILE, rows), F32)
    return pl.pallas_call(
        edges_kernel,
        grid=(1,),
        out_shape=(line, line, column, column),
        in_specs=[left] * 4 + [right] * 4 + [top] * 4 + [bottom] * 4,
        out_specs=(
            pl.BlockSpec((TILE, cols), lambda i: (0, 0)),
            pl.BlockSpec((TILE, cols), lambda i: (0, 0)),
            pl.BlockSpec((TILE, rows), lambda i: (0, 0)),
            pl.BlockSpec((TILE, rows), lambda i: (0, 0)),
        ),
        compiler_params=params(),
        name="edges",
    )(*(fields * 4))


def send(value, axis, step):
    count = lax.axis_size(axis)
    if step > 0:
        pairs = [(i, i + 1) for i in range(count - 1)]
    else:
        pairs = [(i + 1, i) for i in range(count - 1)]
    return lax.ppermute(value, axis, pairs)


def derived(h, u, v):
    r = jnp.where(h > 0.0, lax.rsqrt(h), 0.0)
    s = h * r
    q = u * r
    p = v * r
    half = 0.5 * h * h
    return (h, u, v, s, q, p, q * q + half, p * p + half, q * p)


def along_x(c):
    return (c[0], c[1], c[2], c[3], c[4], c[5], c[6], c[8])


def along_y(c):
    return (c[0], c[2], c[1], c[3], c[5], c[4], c[7], c[8])


def flux(a, b):
    hl, nl, tl, sl, ql, pl_, fl, gl = a
    hr, nr, tr, sr, qr, pr, fr, gr = b
    both = jnp.minimum(hl, hr) > 0.0
    half = jnp.where(both, 0.5, 1.0)
    twice = half + half
    level = (hl + hr) * half
    rc = lax.rsqrt(level)
    c = level * rc
    total = sl + sr
    inv = pl.reciprocal(total, approx=True)
    inv = inv * (2.0 - total * inv)
    u = jnp.where(both, (ql + qr) * inv, 0.0)
    v = (pl_ + pr) * inv
    dh = jnp.where(both, hr - hl, 0.0)
    dn = (nr - nl) * twice
    dt = jnp.where(both, tr - tl, 0.0)
    mid = 0.5 * dh
    e = (0.5 * dn - u * mid) * rc
    s1 = u - c
    s3 = u + c
    b1 = jnp.abs(s1) * (mid - e)
    b3 = jnp.abs(s3) * (mid + e)
    b2 = jnp.abs(u) * (dt - v * dh)
    d = b1 + b3
    return (
        jnp.where(both, nl + nr, 0.0) - d,
        (fl + fr) * twice - (b1 * s1 + b3 * s3),
        jnp.where(both, gl + gr, 0.0) - (d * v + b2),
    )


CELL = 9


def stencil_kernel(
    d_ref, m_ref, x_ref, y_ref, newh_ref, hu_ref, hv_ref, h_ref, token_ref, *scratch,
):
    cell = scratch[:CELL]
    gx = scratch[CELL:]
    step = pl.program_id(0)
    bands = pl.num_programs(0) - 1
    lane = iota((TILE, LANES), 1)

    @pl.when(step < bands)
    def _():
        def fill(t, carry):
            at = pl.ds(pl.multiple_of(t * TILE, TILE), TILE)
            to = pl.ds(pl.multiple_of(step * BAND + t * TILE + TILE, TILE), TILE)
            for g in range(GROUPS):
                cut = slice(g * LANES, (g + 1) * LANES)
                wet = m_ref[at, cut] == 1
                h = jnp.where(wet, d_ref[at, cut], 0.0)
                u = jnp.where(wet, x_ref[at, cut], 0.0)
                v = jnp.where(wet, y_ref[at, cut], 0.0)
                for dst, val in zip(cell, derived(h, u, v)):
                    dst[g, to, :] = val
            return carry

        lax.fori_loop(0, BAND // TILE, fill, 0, unroll=4)

    rows = bands * BAND

    @pl.when(step == 0)
    def _():
        token_ref[...] = jnp.zeros_like(token_ref)
        for dst in cell:
            dst[:, rows + TILE:, :] = jnp.zeros((GROUPS, TILE, LANES), F32)
        for dst in gx:
            dst[:, 0:TILE, :] = jnp.zeros((GROUPS, TILE, LANES), F32)

    @pl.when(step > 0)
    def _():
        start = pl.multiple_of((step - 1) * BAND, BAND)

        def across(t, carry):
            base = pl.multiple_of(start + t * TILE + TILE, TILE)
            for g in range(GROUPS):
                now = along_x([ref[g, pl.ds(base, TILE), :] for ref in cell])
                nxt = along_x([ref[g, pl.ds(base + 1, TILE), :] for ref in cell])
                for dst, val in zip(gx, flux(now, nxt)):
                    dst[g, pl.ds(base, TILE), :] = val
            return carry

        lax.fori_loop(0, BAND // TILE, across, 0, unroll=4)

        @pl.when(step == bands)
        def _():
            for dst in gx:
                dst[:, rows + TILE - 1:rows + TILE, :] = jnp.zeros((GROUPS, 1, LANES), F32)

        def body(t, carry):
            mark = pl.multiple_of(start + t * TILE, TILE)
            base = pl.multiple_of(mark + TILE, TILE)
            at = pl.ds(pl.multiple_of(t * TILE, TILE), TILE)
            before = [jnp.zeros((TILE, LANES), F32)] * 3
            for g in range(GROUPS):
                now = [ref[g, pl.ds(base, TILE), :] for ref in cell]
                if g < GROUPS - 1:
                    other = [ref[g + 1, pl.ds(base, TILE), :] for ref in cell[:3]]
                else:
                    other = now[:3]
                right = [
                    pltpu.roll(jnp.where(lane == 0, o, c), LANES - 1, 1)
                    for o, c in zip(other, now[:3])
                ]
                fy = flux(along_y(now), along_y(derived(*right)))
                if g == GROUPS - 1:
                    fy = [jnp.where(lane == LANES - 1, 0.0, val) for val in fy]
                py = [
                    pltpu.roll(jnp.where(lane == LANES - 1, o, c), 1, 1)
                    for o, c in zip(before, fy)
                ]
                before = fy
                fx = [src[g, pl.ds(base, TILE), :] for src in gx]
                px = [src[g, pl.ds(base - 1, TILE), :] for src in gx]
                h, u, v = now[:3]
                ch = (fx[0] - px[0]) + (fy[0] - py[0])
                cx = (fx[1] - px[1]) + (fy[2] - py[2])
                cy = (fx[2] - px[2]) + (fy[1] - py[1])
                newh_ref[at, g * LANES:(g + 1) * LANES] = jnp.where(
                    h > 0.0, h - (0.5 * DT_DX) * ch, 0.0
                )
                hu_ref[g, at, :] = u - (0.5 * DT_DX) * cx
                hv_ref[g, at, :] = v - (0.5 * DT_DX) * cy
                h_ref[g, at, :] = h
            return carry

        lax.fori_loop(0, BAND // TILE, body, 0, unroll=4)


def stencil(depth, mask, momx, momy):
    rows, cols = depth.shape
    bands = rows // BAND
    plane = jax.ShapeDtypeStruct((GROUPS, rows, LANES), F32)
    pad = pltpu.VMEM((GROUPS, rows + 2 * TILE, LANES), F32)
    band = pl.BlockSpec((BAND, cols), lambda i: (jnp.minimum(i, bands - 1), 0))
    part = pl.BlockSpec((GROUPS, BAND, LANES), lambda i: (0, jnp.maximum(i - 1, 0), 0))
    return pl.pallas_call(
        stencil_kernel,
        grid=(bands + 1,),
        out_shape=(
            jax.ShapeDtypeStruct((rows, cols), F32), plane, plane, plane,
            jax.ShapeDtypeStruct((TILE, LANES), F32),
        ),
        in_specs=[band] * 4,
        out_specs=(
            pl.BlockSpec((BAND, cols), lambda i: (jnp.maximum(i - 1, 0), 0)), part, part, part,
            pl.BlockSpec((TILE, LANES), lambda i: (0, 0)),
        ),
        scratch_shapes=[pad] * (CELL + 3),
        compiler_params=params(),
        cost_estimate=pl.CostEstimate(
            flops=200 * rows * cols, bytes_accessed=64 * rows * cols, transcendentals=0
        ),
        name="stencil",
    )(depth, mask, momx, momy)


def summed_of(lab, landed):
    select = (iota((NW * NPATCH, lab.shape[1]), 0) == lab).astype(BF16)
    return jnp.dot(select, landed, preferred_element_type=F32).astype(BF16)


def stack_left(left, summed, channels):
    for k in range(channels):
        for w in range(NW):
            left[k * NPATCH:(k + 1) * NPATCH, w * ABLK:(w + 1) * ABLK] = summed[
                w * NPATCH:(w + 1) * NPATCH, k * ABLK:(k + 1) * ABLK
            ]


PART = TILE * PATCH


def spread_rows(acc, field, k):
    low = iota((TILE, LANES), 1) < LANES // 2
    for t in range(TILE // 2):
        cut = slice(t * LANES, (t + 1) * LANES)
        for half in range(HALVES):
            for g in range(GROUPS):
                base = k * NPATCH + 2 * g * BPX + half * TILE
                even = acc[base:base + TILE, cut]
                odd = acc[base + BPX:base + BPX + TILE, cut]
                for i, val in (
                    (2 * t, jnp.where(low, even, pltpu.roll(odd, LANES // 2, 1))),
                    (2 * t + 1, jnp.where(low, pltpu.roll(even, LANES // 2, 1), odd)),
                ):
                    field[g, pl.ds(half * TILE * TILE + i, TILE, stride=TILE), :] = val


def press_kernel(
    lab_ref, landed_ref, w_ref, top0_ref, bottom0_ref, left0_ref, right0_ref,
    out_ref, top_ref, bottom_ref, left_ref, right_ref,
    left, acc, acc2, field, field2,
):
    step = pl.program_id(0)

    @pl.when(step == 0)
    def _():
        stack_left(left, summed_of(lab_ref[...], landed_ref[...]), 1)

    acc[...] = jnp.dot(left[...], w_ref[:, :PART], preferred_element_type=F32)
    acc2[...] = jnp.dot(left[...], w_ref[:, PART:], preferred_element_type=F32)
    for part, (src, mid) in enumerate(((acc, field), (acc2, field2))):
        spread_rows(src, mid, 0)
        for g in range(GROUPS):
            for r in range(BPX):
                to = pl.ds(pl.multiple_of(r * PATCH + (2 * step + part) * TILE, TILE), TILE)
                out_ref[g, to, :] = mid[g, r * TILE:(r + 1) * TILE, :]

    @pl.when(step == pl.num_programs(0) - 1)
    def _():
        rows = out_ref.shape[1]
        mine = iota((TILE, LANES), 0) == 3
        for g in range(GROUPS):
            cut = slice(g * LANES, (g + 1) * LANES)
            head = pltpu.roll(out_ref[g, 0:TILE, :], 3, 0)
            tail = pltpu.roll(out_ref[g, rows - TILE:rows, :], 4, 0)
            top_ref[:, cut] = jnp.where(mine, head, top0_ref[:, cut])
            bottom_ref[:, cut] = jnp.where(mine, tail, bottom0_ref[:, cut])
        lane = iota((LANES, LANES), 1)
        for b in range(rows // LANES):
            at = slice(b * LANES, (b + 1) * LANES)
            packed = jnp.where(
                lane == TILE + 3,
                pltpu.roll(out_ref[GROUPS - 1, at, :], TILE + 4, 1),
                pltpu.roll(out_ref[0, at, :], 3, 1),
            )
            turned = packed.T
            left_ref[:, at] = jnp.where(mine, turned[0:TILE], left0_ref[:, at])
            right_ref[:, at] = jnp.where(mine, turned[TILE:2 * TILE], right0_ref[:, at])


def pressure_field(lab, landed, weights, edges):
    steps = PATCH // (2 * TILE)
    rows = BPX * PATCH
    line = (TILE, BPY * PATCH)
    column = (TILE, rows)
    whole = (GROUPS, rows, LANES)

    def const(shape):
        return pl.BlockSpec(shape, lambda i: (0,) * len(shape))

    return pl.pallas_call(
        press_kernel,
        grid=(steps,),
        out_shape=tuple(jax.ShapeDtypeStruct(x, F32) for x in (whole, line, line, column, column)),
        in_specs=[
            const(lab.shape),
            const(landed.shape),
            pl.BlockSpec((NW * ABLK, 2 * PART), lambda i: (0, i)),
        ] + [const(x) for x in (line, line, column, column)],
        out_specs=tuple(const(x) for x in (whole, line, line, column, column)),
        scratch_shapes=[
            pltpu.VMEM((NPATCH, NW * ABLK), BF16),
            pltpu.VMEM((NPATCH, PART), F32),
            pltpu.VMEM((NPATCH, PART), F32),
            pltpu.VMEM((GROUPS, BPX * TILE, LANES), F32),
            pltpu.VMEM((GROUPS, BPX * TILE, LANES), F32),
        ],
        compiler_params=params(),
        cost_estimate=pl.CostEstimate(
            flops=2 * NPATCH * NW * ABLK * PATCH * PATCH, bytes_accessed=12 << 20, transcendentals=0
        ),
        name="pressure",
    )(lab, landed, weights, *edges)


def border_kernel(
    up_ref, dn_ref, lh_ref, rh_ref, top_ref, bottom_ref, left_ref, right_ref, old_ref,
    new_ref, sides_ref, ends_ref, edge, first, last, head, tail, load, save,
):
    rows, cols = old_ref.shape
    middle = pl.ds(LANES, cols - 2 * LANES)
    places = (
        (slice(None), pl.ds(0, LANES)),
        (slice(None), pl.ds(cols - LANES, LANES)),
        (pl.ds(0, TILE), middle),
        (pl.ds(rows - TILE, TILE), middle),
    )
    parts = (first, last, head, tail)
    loads = [
        pltpu.make_async_copy(old_ref.at[at], part, load.at[n])
        for n, (at, part) in enumerate(zip(places, parts))
    ]
    for copy in loads:
        copy.start()

    def cells(ref):
        return derived(ref[0:1, :], ref[1:2, :], ref[2:3, :])

    edge[0:1, :] = lh_ref[3:4, :]
    edge[1:2, :] = rh_ref[3:4, :]
    for at, before, after, own, sign in (
        (2, lh_ref, left_ref, left_ref, 1.0), (5, right_ref, rh_ref, right_ref, -1.0),
    ):
        gh, gn, gt = flux(along_y(cells(before)), along_y(cells(after)))
        wet = own[0:1, :] > 0.0
        for f, val in enumerate((gh, gt, gn)):
            edge[at + f:at + f + 1, :] = jnp.where(wet, (sign * 0.5 * DT_DX) * val, 0.0)
    blank = jnp.zeros((LANES - TILE, LANES), F32)
    for b in range(rows // LANES):
        cut = slice(b * LANES, (b + 1) * LANES)
        sides_ref[cut, :] = jnp.concatenate([edge[:, cut], blank], axis=0).T
    ends_ref[...] = jnp.zeros_like(ends_ref)
    for at, before, after, own, sign in (
        (0, up_ref, top_ref, top_ref, 1.0), (3, bottom_ref, dn_ref, bottom_ref, -1.0),
    ):
        fluxes = flux(along_x(cells(before)), along_x(cells(after)))
        wet = own[0:1, :] > 0.0
        for f, val in enumerate(fluxes):
            ends_ref[at + f:at + f + 1, :] = jnp.where(wet, (sign * 0.5 * DT_DX) * val, 0.0)

    for copy in loads:
        copy.wait()
    lane = iota((rows, LANES), 1)
    sides = sides_ref[...]
    first[...] += jnp.where(lane == 0, pltpu.roll(sides, LANES - 2, 1), 0.0)
    last[...] += jnp.where(lane == LANES - 1, pltpu.roll(sides, LANES - 6, 1), 0.0)
    for at, line in ((0, 0), (rows - 1, 3)):
        first[at:at + 1, :] += ends_ref[line:line + 1, 0:LANES]
        last[at:at + 1, :] += ends_ref[line:line + 1, cols - LANES:cols]
    head[0:1, :] += ends_ref[0:1, LANES:cols - LANES]
    tail[TILE - 1:TILE, :] += ends_ref[3:4, LANES:cols - LANES]
    saves = [
        pltpu.make_async_copy(part, new_ref.at[at], save.at[n])
        for n, (at, part) in enumerate(zip(places, parts))
    ]
    for copy in saves:
        copy.start()
    for copy in saves:
        copy.wait()


def border(halos, edges, newh):
    rows, cols = newh.shape
    whole = pl.BlockSpec(memory_space=pl.ANY)
    return pl.pallas_call(
        border_kernel,
        out_shape=(
            jax.ShapeDtypeStruct((rows, cols), F32),
            jax.ShapeDtypeStruct((rows, LANES), F32),
            jax.ShapeDtypeStruct((TILE, cols), F32),
        ),
        in_specs=[VMEM] * 8 + [whole],
        out_specs=(whole, VMEM, VMEM),
        input_output_aliases={8: 0},
        scratch_shapes=[
            pltpu.VMEM((TILE, rows), F32),
            pltpu.VMEM((rows, LANES), F32),
            pltpu.VMEM((rows, LANES), F32),
            pltpu.VMEM((TILE, cols - 2 * LANES), F32),
            pltpu.VMEM((TILE, cols - 2 * LANES), F32),
            pltpu.SemaphoreType.DMA((4,)),
            pltpu.SemaphoreType.DMA((4,)),
        ],
        compiler_params=params(),
        name="border",
    )(*halos, *edges, newh)


def finish_kernel(
    lab_ref, landed_ref, w_ref, p_ref, up_ref, dn_ref, sides_ref, ends_ref,
    hu_ref, hv_ref, h_ref, ox_ref, oy_ref,
    left, acc, acc2, fx, fy, fx2, fy2, padded,
):
    step = pl.program_id(0)
    rows = p_ref.shape[1]

    @pl.when(step == 0)
    def _():
        stack_left(left, summed_of(lab_ref[...], landed_ref[...]), 2)
        for g in range(GROUPS):
            cut = slice(g * LANES, (g + 1) * LANES)
            padded[g, TILE:TILE + rows, :] = p_ref[g]
            padded[g, 0:TILE, :] = jnp.broadcast_to(up_ref[3:4, cut], (TILE, LANES))
            padded[g, rows + TILE:, :] = jnp.broadcast_to(dn_ref[3:4, cut], (TILE, LANES))

    acc[...] = jnp.dot(left[...], w_ref[:, :PART], preferred_element_type=F32)
    acc2[...] = jnp.dot(left[...], w_ref[:, PART:], preferred_element_type=F32)
    lane = iota((TILE, LANES), 1)
    for part, (src, mx, my) in enumerate(((acc, fx, fy), (acc2, fx2, fy2))):
        spread_rows(src, mx, 0)
        spread_rows(src, my, 1)
        cells = slice(part * TILE, (part + 1) * TILE)
        for r in range(BPX):
            at = slice(r * TILE, (r + 1) * TILE)
            mark = pl.multiple_of(r * PATCH + (2 * step + part) * TILE, TILE)
            base = pl.multiple_of(mark + TILE, TILE)
            ends = sides_ref[pl.ds(mark, TILE), :]
            tiles = [padded[g, pl.ds(base, TILE), :] for g in range(GROUPS)]
            for g in range(GROUPS):
                before = tiles[g - 1] if g else pltpu.roll(ends, LANES - 1, 1)
                after = tiles[g + 1] if g < GROUPS - 1 else pltpu.roll(ends, LANES - 1, 1)
                prev = pltpu.roll(jnp.where(lane == LANES - 1, before, tiles[g]), 1, 1)
                nxt = pltpu.roll(jnp.where(lane == 0, after, tiles[g]), LANES - 1, 1)
                h = h_ref[g, r, cells, :]
                wet = h > 0.0
                scale = (TIME_STEP * PRESS * 0.5) * h
                gx = padded[g, pl.ds(base + 1, TILE), :] - padded[g, pl.ds(base - 1, TILE), :]
                wx = mx[g, at, :]
                wy = my[g, at, :]
                speed = (TIME_STEP * STRESS) * jnp.sqrt(wx * wx + wy * wy)
                new = [
                    hu_ref[g, r, cells, :] - scale * gx + speed * wx,
                    hv_ref[g, r, cells, :] - scale * (nxt - prev) + speed * wy,
                ]
                for own, edge, shift in ((0, 0, 3), (GROUPS - 1, LANES - 1, 6)):
                    if g == own:
                        new = [
                            jnp.where(
                                lane == edge,
                                a + pltpu.roll(ends, (edge - shift - f) % LANES, 1),
                                a,
                            )
                            for f, a in enumerate(new)
                        ]
                cut = slice(g * LANES, (g + 1) * LANES)
                ox_ref[r, cells, cut] = jnp.where(wet, new[0], 0.0)
                oy_ref[r, cells, cut] = jnp.where(wet, new[1], 0.0)

    @pl.when(step == 0)
    def _():
        ox_ref[0, 0:1, :] += ends_ref[1:2, :]
        oy_ref[0, 0:1, :] += ends_ref[2:3, :]

    @pl.when(step == pl.num_programs(0) - 1)
    def _():
        deep = ox_ref.shape[1]
        ox_ref[BPX - 1, deep - 1:deep, :] += ends_ref[4:5, :]
        oy_ref[BPX - 1, deep - 1:deep, :] += ends_ref[5:6, :]


def finish(lab, landed, weights, p, up, dn, sides, ends, hu, hv, h):
    deep = 2 * TILE
    steps = PATCH // deep
    cols = BPY * PATCH
    rows = p.shape[1]
    split = (GROUPS, BPX, PATCH, LANES)
    slab = pl.BlockSpec((GROUPS, BPX, deep, LANES), lambda i: (0, 0, i, 0))
    out = pl.BlockSpec((BPX, deep, cols), lambda i: (0, i, 0))
    shape = jax.ShapeDtypeStruct((BPX, PATCH, cols), F32)
    field = pltpu.VMEM((GROUPS, BPX * TILE, LANES), F32)

    def const(x):
        return pl.BlockSpec(x.shape, lambda i: (0,) * x.ndim)

    return pl.pallas_call(
        finish_kernel,
        grid=(steps,),
        out_shape=(shape, shape),
        in_specs=[
            const(lab), const(landed),
            pl.BlockSpec((NW * ABLK, 2 * PART), lambda i: (0, i)),
            const(p), const(up), const(dn), const(sides), const(ends),
            slab, slab, slab,
        ],
        out_specs=(out, out),
        scratch_shapes=[
            pltpu.VMEM((2 * NPATCH, NW * ABLK), BF16),
            pltpu.VMEM((2 * NPATCH, PART), F32),
            pltpu.VMEM((2 * NPATCH, PART), F32),
            field, field, field, field,
            pltpu.VMEM((GROUPS, rows + 2 * TILE, LANES), F32),
        ],
        compiler_params=params(),
        cost_estimate=pl.CostEstimate(
            flops=4 * NPATCH * NW * ABLK * PATCH * PATCH, bytes_accessed=20 << 20, transcendentals=0
        ),
        name="finish",
    )(
        lab, landed, weights, p, up, dn, sides, ends,
        hu.reshape(split), hv.reshape(split), h.reshape(split),
    )


def body(
    atm_blocks,
    remap_weights,
    ovl_source,
    ovl_block,
    ovl_patch,
    ovl_weight,
    depth_field,
    wet_mask,
    mom_x,
    mom_y,
    blend,
):
    count_x = lax.axis_size("gx")
    count_y = lax.axis_size("gy")
    devices = count_x * count_y
    entries = ovl_source.size
    capacity = 2 * entries // devices
    slots = devices * capacity
    atm = atm_blocks.reshape(atm_blocks.shape[2:]).transpose(1, 0, 2)
    both = ("gx", "gy")
    want, lab = make_requests(
        ovl_source.reshape(1, entries), ovl_block.reshape(1, entries),
        ovl_patch.reshape(1, entries), ovl_weight.reshape(1, entries), devices, capacity,
    )
    asked = lax.all_to_all(
        want.reshape(devices, 1, capacity), both, split_axis=0, concat_axis=0, tiled=True
    )
    lab = lab.reshape(1, slots)
    press, wind = mix(blend.reshape(1), atm)
    top, bottom, left, right = edge_cells(depth_field, wet_mask, mom_x, mom_y)

    def exchange(after, tiles):
        rows = serve(after, asked, tiles)
        parts = rows.reshape(devices, capacity, rows.shape[1])
        got = lax.all_to_all(parts, both, split_axis=0, concat_axis=0, tiled=True)
        return got.reshape(rows.shape)

    press = exchange(top, press)
    newh, hu, hv, h, token = stencil(depth_field, wet_mask, mom_x, mom_y)
    wind = exchange(token, wind)
    weights = remap_weights.reshape(NW * ABLK, PATCH * PATCH)
    p, *edges = pressure_field(lab, press, weights, (top, bottom, left, right))
    top, bottom, left, right = edges
    halos = (
        send(bottom, "gx", 1), send(top, "gx", -1), send(right, "gy", 1), send(left, "gy", -1),
    )
    newh, sides, ends = border(halos, edges, newh)
    new_x, new_y = finish(lab, wind, weights, p, halos[0], halos[1], sides, ends, hu, hv, h)
    return (newh, new_x.reshape(newh.shape), new_y.reshape(newh.shape))


def solution(mesh):
    placed = (
        P("gx", "gy", None, None, None),
        P(),
        P("gx", "gy", None, None),
        P("gx", "gy", None),
        P("gx", "gy", None),
        P("gx", "gy", None),
        P("gx", "gy"),
        P("gx", "gy"),
        P("gx", "gy"),
        P("gx", "gy"),
        P(),
    )
    return jax.shard_map(
        body,
        mesh=mesh,
        in_specs=placed,
        out_specs=(P("gx", "gy"), P("gx", "gy"), P("gx", "gy")),
        check_vma=False,
    )
```

```python
import functools

import jax
import jax.numpy as jnp
from jax import lax
from jax.experimental import pallas as pl
from jax.experimental.pallas import tpu as pltpu
from jax.sharding import PartitionSpec as P

PATCH = 64
ABLK = 256
NW = 4
BPX = 16
BPY = 8
NPATCH = BPX * BPY

GRAV = 1.0
DT_DX = 0.2
TIME_STEP = 0.2
STRESS = 0.5
PRESS = 0.5

F32 = jnp.float32
BF16 = jnp.bfloat16
VMEM = pl.BlockSpec(memory_space=pltpu.VMEM)
SMEM = pl.BlockSpec(memory_space=pltpu.SMEM)
LANES = 128
TILE = 8
GROUPS = BPY * PATCH // LANES
HALVES = BPX // TILE
BAND = 128


def params(limit=56 << 20, **kw):
    return pltpu.CompilerParams(vmem_limit_bytes=limit, **kw)


def iota(shape, dim):
    return lax.broadcasted_iota(jnp.int32, shape, dim)


def rank_kernel(capacity, src_ref, blk_ref, pat_ref, wgt_ref, want_ref, lab_ref):
    devices = want_ref.shape[0]
    src = src_ref[...]
    ent = src.shape[1]
    hits = (iota((devices, ent), 0) == src).astype(F32)
    order = (iota((ent, ent), 0) <= iota((ent, ent), 1)).astype(BF16)
    ranks = jnp.dot(hits.astype(BF16), order, preferred_element_type=F32)
    mine = jnp.sum(hits * ranks, axis=0, keepdims=True).astype(jnp.int32) - 1
    place = iota((capacity, ent), 0) == mine
    pat = pat_ref[...]
    row_bits = BPX.bit_length() - 1
    col_bits = BPY.bit_length() - 1
    rows = jnp.zeros_like(pat)
    cols = jnp.zeros_like(pat)
    used_r = used_c = position = 0
    while used_r < row_bits or used_c < col_bits:
        value = jnp.bitwise_and(jnp.right_shift(pat, position), 1)
        if used_r < row_bits and (used_c >= col_bits or position % 2 == 0):
            rows = rows + value * (1 << used_r)
            used_r += 1
        else:
            cols = cols + value * (1 << used_c)
            used_c += 1
        position += 1

    def spread(row):
        picked = jnp.where(place, row.astype(F32), 0.0).astype(BF16)
        return lax.dot_general(
            hits.astype(BF16), picked, (((1,), (1,)), ((), ())),
            preferred_element_type=F32,
        ).astype(jnp.int32)

    want_ref[...] = spread(blk_ref[...])
    slot = spread(cols * BPX + rows)
    group = spread(wgt_ref[...] + 1)
    lab_ref[...] = jnp.where(group > 0, (group - 1) * NPATCH + slot, -1)


def make_requests(src, blk, pat, wgt, devices, capacity):
    shape = jax.ShapeDtypeStruct((devices, capacity), jnp.int32)
    return pl.pallas_call(
        functools.partial(rank_kernel, capacity),
        out_shape=(shape, shape),
        in_specs=[VMEM] * 4,
        out_specs=(VMEM, VMEM),
        compiler_params=params(),
        name="requests",
    )(src, blk, pat, wgt)


def mix_kernel(blend_ref, atm_ref, press_ref, wind_ref):
    blend = blend_ref[0]
    keep = 1.0 - blend

    def mixed(k):
        first = atm_ref[k].astype(F32)
        second = atm_ref[3 + k].astype(F32)
        return (keep * first + blend * second).astype(BF16)

    press_ref[...] = mixed(2)
    for k in range(2):
        wind_ref[:, k * ABLK:(k + 1) * ABLK] = mixed(k)


def mix(blend, atm):
    blocks = atm.shape[1]
    return pl.pallas_call(
        mix_kernel,
        out_shape=(
            jax.ShapeDtypeStruct((blocks, ABLK), BF16),
            jax.ShapeDtypeStruct((blocks, 2 * ABLK), BF16),
        ),
        in_specs=[SMEM, VMEM],
        out_specs=(VMEM, VMEM),
        compiler_params=params(),
        name="mix",
    )(blend, atm)


def serve_kernel(after_ref, asked_ref, tiles_ref, out_ref, turned, pick):
    peers, _, capacity = asked_ref.shape
    width = turned.shape[0]
    turned[...] = jnp.zeros_like(turned)
    turned[0:peers, 0:capacity] = asked_ref[:, 0, :]
    columns = turned[...].T
    blocks = tiles_ref.shape[0]
    names = iota((capacity, blocks), 1)
    for d in range(peers):
        pick[d * capacity:(d + 1) * capacity, :] = (columns[0:capacity, d:d + 1] == names).astype(F32)
    out_ref[...] = jnp.dot(
        pick[...].astype(BF16), tiles_ref[...], preferred_element_type=F32
    ).astype(BF16)


def serve(after, asked, tiles):
    peers, _, capacity = asked.shape
    slots = peers * capacity
    width = -(-max(peers, capacity) // LANES) * LANES
    return pl.pallas_call(
        serve_kernel,
        out_shape=jax.ShapeDtypeStruct((slots, tiles.shape[1]), BF16),
        in_specs=[pl.BlockSpec(memory_space=pl.ANY), VMEM, VMEM],
        out_specs=VMEM,
        scratch_shapes=[
            pltpu.VMEM((width, width), jnp.int32),
            pltpu.VMEM((slots, tiles.shape[0]), F32),
        ],
        compiler_params=params(32 << 20),
        name="serve",
    )(after, asked, tiles)


def edges_kernel(
    dl, ml, xl, yl, dr, mr, xr, yr, dt, mt, xt, yt, db, mb, xb, yb,
    top_ref, bottom_ref, left_ref, right_ref,
):
    def rows(d, m, x, y, at, out):
        wet = m[...] == 1
        for f, ref in enumerate((d, x, y)):
            out[f:f + 1, :] = jnp.where(wet, ref[...], 0.0)[at:at + 1]

    rows(dt, mt, xt, yt, 0, top_ref)
    rows(db, mb, xb, yb, TILE - 1, bottom_ref)
    lane = iota((LANES, LANES), 1)

    def step(b, carry):
        at = pl.ds(pl.multiple_of(b * LANES, LANES), LANES)
        wl = ml[at, :] == 1
        wr = mr[at, :] == 1
        packed = jnp.where(wl, dl[at, :], 0.0)
        packed = jnp.where(lane == 1, pltpu.roll(jnp.where(wl, xl[at, :], 0.0), 1, 1), packed)
        packed = jnp.where(lane == 2, pltpu.roll(jnp.where(wl, yl[at, :], 0.0), 2, 1), packed)
        packed = jnp.where(lane == 8, pltpu.roll(jnp.where(wr, dr[at, :], 0.0), 9, 1), packed)
        packed = jnp.where(lane == 9, pltpu.roll(jnp.where(wr, xr[at, :], 0.0), 10, 1), packed)
        packed = jnp.where(lane == 10, pltpu.roll(jnp.where(wr, yr[at, :], 0.0), 11, 1), packed)
        turned = packed.T
        left_ref[:, at] = turned[0:TILE]
        right_ref[:, at] = turned[TILE:2 * TILE]
        return carry

    lax.fori_loop(0, dl.shape[0] // LANES, step, 0)


def edge_cells(depth, mask, momx, momy):
    rows, cols = depth.shape
    fields = (depth, mask, momx, momy)
    left = pl.BlockSpec((rows, LANES), lambda i: (0, 0))
    right = pl.BlockSpec((rows, LANES), lambda i: (0, cols // LANES - 1))
    top = pl.BlockSpec((TILE, cols), lambda i: (0, 0))
    bottom = pl.BlockSpec((TILE, cols), lambda i: (rows // TILE - 1, 0))
    line = jax.ShapeDtypeStruct((TILE, cols), F32)
    column = jax.ShapeDtypeStruct((TILE, rows), F32)
    return pl.pallas_call(
        edges_kernel,
        grid=(1,),
        out_shape=(line, line, column, column),
        in_specs=[left] * 4 + [right] * 4 + [top] * 4 + [bottom] * 4,
        out_specs=(
            pl.BlockSpec((TILE, cols), lambda i: (0, 0)),
            pl.BlockSpec((TILE, cols), lambda i: (0, 0)),
            pl.BlockSpec((TILE, rows), lambda i: (0, 0)),
            pl.BlockSpec((TILE, rows), lambda i: (0, 0)),
        ),
        compiler_params=params(56 << 20),
        cost_estimate=pl.CostEstimate(flops=0, bytes_accessed=8 << 20, transcendentals=0),
        name="edges",
    )(*(fields * 4))


def send(value, axis, step):
    count = lax.axis_size(axis)
    if step > 0:
        pairs = [(i, i + 1) for i in range(count - 1)]
    else:
        pairs = [(i + 1, i) for i in range(count - 1)]
    return lax.ppermute(value, axis, pairs)


def derived(h, u, v):
    r = jnp.where(h > 0.0, lax.rsqrt(h), 0.0)
    s = h * r
    q = u * r
    p = v * r
    half = 0.5 * h * h
    return (h, u, v, s, q, p, q * q + half, p * p + half, q * p)


def along_x(c):
    return (c[0], c[1], c[2], c[3], c[4], c[5], c[6], c[8])


def along_y(c):
    return (c[0], c[2], c[1], c[3], c[5], c[4], c[7], c[8])


def flux(a, b):
    hl, nl, tl, sl, ql, pl_, fl, gl = a
    hr, nr, tr, sr, qr, pr, fr, gr = b
    both = jnp.minimum(hl, hr) > 0.0
    half = jnp.where(both, 0.5, 1.0)
    twice = half + half
    level = (hl + hr) * half
    rc = lax.rsqrt(level)
    c = level * rc
    total = sl + sr
    inv = pl.reciprocal(total, approx=True)
    inv = inv * (2.0 - total * inv)
    u = jnp.where(both, (ql + qr) * inv, 0.0)
    v = (pl_ + pr) * inv
    dh = jnp.where(both, hr - hl, 0.0)
    dn = (nr - nl) * twice
    dt = jnp.where(both, tr - tl, 0.0)
    mid = 0.5 * dh
    e = (0.5 * dn - u * mid) * rc
    s1 = u - c
    s3 = u + c
    b1 = jnp.abs(s1) * (mid - e)
    b3 = jnp.abs(s3) * (mid + e)
    b2 = jnp.abs(u) * (dt - v * dh)
    d = b1 + b3
    return (
        jnp.where(both, nl + nr, 0.0) - d,
        (fl + fr) * twice - (b1 * s1 + b3 * s3),
        jnp.where(both, gl + gr, 0.0) - (d * v + b2),
    )


CELL = 9


def stencil_kernel(
    d_ref, m_ref, x_ref, y_ref, newh_ref, hu_ref, hv_ref, h_ref, token_ref, *scratch,
):
    cell = scratch[:CELL]
    gx = scratch[CELL:]
    step = pl.program_id(0)
    bands = pl.num_programs(0) - 1
    lane = iota((TILE, LANES), 1)

    @pl.when(step < bands)
    def _():
        def fill(t, carry):
            at = pl.ds(pl.multiple_of(t * TILE, TILE), TILE)
            to = pl.ds(pl.multiple_of(step * BAND + t * TILE + TILE, TILE), TILE)
            for g in range(GROUPS):
                cut = slice(g * LANES, (g + 1) * LANES)
                wet = m_ref[at, cut] == 1
                h = jnp.where(wet, d_ref[at, cut], 0.0)
                u = jnp.where(wet, x_ref[at, cut], 0.0)
                v = jnp.where(wet, y_ref[at, cut], 0.0)
                for dst, val in zip(cell, derived(h, u, v)):
                    dst[g, to, :] = val
            return carry

        lax.fori_loop(0, BAND // TILE, fill, 0, unroll=4)

    rows = bands * BAND

    @pl.when(step == 0)
    def _():
        token_ref[...] = jnp.zeros_like(token_ref)
        for dst in cell:
            dst[:, rows + TILE:, :] = jnp.zeros((GROUPS, TILE, LANES), F32)
        for dst in gx:
            dst[:, 0:TILE, :] = jnp.zeros((GROUPS, TILE, LANES), F32)

    @pl.when(step > 0)
    def _():
        start = pl.multiple_of((step - 1) * BAND, BAND)

        def across(t, carry):
            base = pl.multiple_of(start + t * TILE + TILE, TILE)
            for g in range(GROUPS):
                now = along_x([ref[g, pl.ds(base, TILE), :] for ref in cell])
                nxt = along_x([ref[g, pl.ds(base + 1, TILE), :] for ref in cell])
                for dst, val in zip(gx, flux(now, nxt)):
                    dst[g, pl.ds(base, TILE), :] = val
            return carry

        lax.fori_loop(0, BAND // TILE, across, 0, unroll=4)

        @pl.when(step == bands)
        def _():
            for dst in gx:
                dst[:, rows + TILE - 1:rows + TILE, :] = jnp.zeros((GROUPS, 1, LANES), F32)

        def body(t, carry):
            mark = pl.multiple_of(start + t * TILE, TILE)
            base = pl.multiple_of(mark + TILE, TILE)
            at = pl.ds(pl.multiple_of(t * TILE, TILE), TILE)
            before = [jnp.zeros((TILE, LANES), F32)] * 3
            for g in range(GROUPS):
                now = [ref[g, pl.ds(base, TILE), :] for ref in cell]
                if g < GROUPS - 1:
                    other = [ref[g + 1, pl.ds(base, TILE), :] for ref in cell[:3]]
                else:
                    other = now[:3]
                right = [
                    pltpu.roll(jnp.where(lane == 0, o, c), LANES - 1, 1)
                    for o, c in zip(other, now[:3])
                ]
                fy = flux(along_y(now), along_y(derived(*right)))
                if g == GROUPS - 1:
                    fy = [jnp.where(lane == LANES - 1, 0.0, val) for val in fy]
                py = [
                    pltpu.roll(jnp.where(lane == LANES - 1, o, c), 1, 1)
                    for o, c in zip(before, fy)
                ]
                before = fy
                fx = [src[g, pl.ds(base, TILE), :] for src in gx]
                px = [src[g, pl.ds(base - 1, TILE), :] for src in gx]
                h, u, v = now[:3]
                ch = (fx[0] - px[0]) + (fy[0] - py[0])
                cx = (fx[1] - px[1]) + (fy[2] - py[2])
                cy = (fx[2] - px[2]) + (fy[1] - py[1])
                newh_ref[at, g * LANES:(g + 1) * LANES] = jnp.where(
                    h > 0.0, h - (0.5 * DT_DX) * ch, 0.0
                )
                hu_ref[g, at, :] = u - (0.5 * DT_DX) * cx
                hv_ref[g, at, :] = v - (0.5 * DT_DX) * cy
                h_ref[g, at, :] = h
            return carry

        lax.fori_loop(0, BAND // TILE, body, 0, unroll=4)


def stencil(depth, mask, momx, momy):
    rows, cols = depth.shape
    bands = rows // BAND
    plane = jax.ShapeDtypeStruct((GROUPS, rows, LANES), F32)
    pad = pltpu.VMEM((GROUPS, rows + 2 * TILE, LANES), F32)
    band = pl.BlockSpec((BAND, cols), lambda i: (jnp.minimum(i, bands - 1), 0))
    part = pl.BlockSpec((GROUPS, BAND, LANES), lambda i: (0, jnp.maximum(i - 1, 0), 0))
    return pl.pallas_call(
        stencil_kernel,
        grid=(bands + 1,),
        out_shape=(
            jax.ShapeDtypeStruct((rows, cols), F32), plane, plane, plane,
            jax.ShapeDtypeStruct((TILE, LANES), F32),
        ),
        in_specs=[band] * 4,
        out_specs=(
            pl.BlockSpec((BAND, cols), lambda i: (jnp.maximum(i - 1, 0), 0)), part, part, part,
            pl.BlockSpec((TILE, LANES), lambda i: (0, 0)),
        ),
        scratch_shapes=[pad] * (CELL + 3),
        compiler_params=params(36 << 20),
        cost_estimate=pl.CostEstimate(
            flops=200 * rows * cols, bytes_accessed=64 * rows * cols, transcendentals=0
        ),
        name="stencil",
    )(depth, mask, momx, momy)


def summed_of(lab, landed):
    select = (iota((NW * NPATCH, lab.shape[1]), 0) == lab).astype(BF16)
    return jnp.dot(select, landed, preferred_element_type=F32).astype(BF16)


def stack_left(left, summed, channels):
    for k in range(channels):
        for w in range(NW):
            left[k * NPATCH:(k + 1) * NPATCH, w * ABLK:(w + 1) * ABLK] = summed[
                w * NPATCH:(w + 1) * NPATCH, k * ABLK:(k + 1) * ABLK
            ]


PART = TILE * PATCH


def spread_rows(acc, field, k):
    low = iota((TILE, LANES), 1) < LANES // 2
    for t in range(TILE // 2):
        cut = slice(t * LANES, (t + 1) * LANES)
        for half in range(HALVES):
            for g in range(GROUPS):
                base = k * NPATCH + 2 * g * BPX + half * TILE
                even = acc[base:base + TILE, cut]
                odd = acc[base + BPX:base + BPX + TILE, cut]
                for i, val in (
                    (2 * t, jnp.where(low, even, pltpu.roll(odd, LANES // 2, 1))),
                    (2 * t + 1, jnp.where(low, pltpu.roll(even, LANES // 2, 1), odd)),
                ):
                    field[g, pl.ds(half * TILE * TILE + i, TILE, stride=TILE), :] = val


def press_kernel(
    lab_ref, landed_ref, w_ref, top0_ref, bottom0_ref, left0_ref, right0_ref,
    out_ref, top_ref, bottom_ref, left_ref, right_ref,
    left, acc, acc2, field, field2,
):
    step = pl.program_id(0)

    @pl.when(step == 0)
    def _():
        stack_left(left, summed_of(lab_ref[...], landed_ref[...]), 1)

    acc[...] = jnp.dot(left[...], w_ref[:, :PART], preferred_element_type=F32)
    acc2[...] = jnp.dot(left[...], w_ref[:, PART:], preferred_element_type=F32)
    for part, (src, mid) in enumerate(((acc, field), (acc2, field2))):
        spread_rows(src, mid, 0)
        for g in range(GROUPS):
            for r in range(BPX):
                to = pl.ds(pl.multiple_of(r * PATCH + (2 * step + part) * TILE, TILE), TILE)
                out_ref[g, to, :] = mid[g, r * TILE:(r + 1) * TILE, :]

    @pl.when(step == pl.num_programs(0) - 1)
    def _():
        rows = out_ref.shape[1]
        mine = iota((TILE, LANES), 0) == 3
        for g in range(GROUPS):
            cut = slice(g * LANES, (g + 1) * LANES)
            head = pltpu.roll(out_ref[g, 0:TILE, :], 3, 0)
            tail = pltpu.roll(out_ref[g, rows - TILE:rows, :], 4, 0)
            top_ref[:, cut] = jnp.where(mine, head, top0_ref[:, cut])
            bottom_ref[:, cut] = jnp.where(mine, tail, bottom0_ref[:, cut])
        lane = iota((LANES, LANES), 1)
        for b in range(rows // LANES):
            at = slice(b * LANES, (b + 1) * LANES)
            packed = jnp.where(
                lane == TILE + 3,
                pltpu.roll(out_ref[GROUPS - 1, at, :], TILE + 4, 1),
                pltpu.roll(out_ref[0, at, :], 3, 1),
            )
            turned = packed.T
            left_ref[:, at] = jnp.where(mine, turned[0:TILE], left0_ref[:, at])
            right_ref[:, at] = jnp.where(mine, turned[TILE:2 * TILE], right0_ref[:, at])


def pressure_field(lab, landed, weights, edges):
    steps = PATCH // (2 * TILE)
    rows = BPX * PATCH
    line = (TILE, BPY * PATCH)
    column = (TILE, rows)
    whole = (GROUPS, rows, LANES)

    def const(shape):
        return pl.BlockSpec(shape, lambda i: (0,) * len(shape))

    return pl.pallas_call(
        press_kernel,
        grid=(steps,),
        out_shape=tuple(jax.ShapeDtypeStruct(x, F32) for x in (whole, line, line, column, column)),
        in_specs=[
            const(lab.shape),
            const(landed.shape),
            pl.BlockSpec((NW * ABLK, 2 * PART), lambda i: (0, i)),
        ] + [const(x) for x in (line, line, column, column)],
        out_specs=tuple(const(x) for x in (whole, line, line, column, column)),
        scratch_shapes=[
            pltpu.VMEM((NPATCH, NW * ABLK), BF16),
            pltpu.VMEM((NPATCH, PART), F32),
            pltpu.VMEM((NPATCH, PART), F32),
            pltpu.VMEM((GROUPS, BPX * TILE, LANES), F32),
            pltpu.VMEM((GROUPS, BPX * TILE, LANES), F32),
        ],
        compiler_params=params(24 << 20),
        cost_estimate=pl.CostEstimate(
            flops=2 * NPATCH * NW * ABLK * PATCH * PATCH, bytes_accessed=12 << 20, transcendentals=0
        ),
        name="pressure",
    )(lab, landed, weights, *edges)


def border_kernel(
    up_ref, dn_ref, lh_ref, rh_ref, top_ref, bottom_ref, left_ref, right_ref, old_ref,
    new_ref, sides_ref, ends_ref, edge, first, last, head, tail, load, save,
):
    rows, cols = old_ref.shape
    middle = pl.ds(LANES, cols - 2 * LANES)
    places = (
        (slice(None), pl.ds(0, LANES)),
        (slice(None), pl.ds(cols - LANES, LANES)),
        (pl.ds(0, TILE), middle),
        (pl.ds(rows - TILE, TILE), middle),
    )
    parts = (first, last, head, tail)
    loads = [
        pltpu.make_async_copy(old_ref.at[at], part, load.at[n])
        for n, (at, part) in enumerate(zip(places, parts))
    ]
    for copy in loads:
        copy.start()

    def cells(ref):
        return derived(ref[0:1, :], ref[1:2, :], ref[2:3, :])

    edge[0:1, :] = lh_ref[3:4, :]
    edge[1:2, :] = rh_ref[3:4, :]
    for at, before, after, own, sign in (
        (2, lh_ref, left_ref, left_ref, 1.0), (5, right_ref, rh_ref, right_ref, -1.0),
    ):
        gh, gn, gt = flux(along_y(cells(before)), along_y(cells(after)))
        wet = own[0:1, :] > 0.0
        for f, val in enumerate((gh, gt, gn)):
            edge[at + f:at + f + 1, :] = jnp.where(wet, (sign * 0.5 * DT_DX) * val, 0.0)
    blank = jnp.zeros((LANES - TILE, LANES), F32)
    for b in range(rows // LANES):
        cut = slice(b * LANES, (b + 1) * LANES)
        sides_ref[cut, :] = jnp.concatenate([edge[:, cut], blank], axis=0).T
    ends_ref[...] = jnp.zeros_like(ends_ref)
    for at, before, after, own, sign in (
        (0, up_ref, top_ref, top_ref, 1.0), (3, bottom_ref, dn_ref, bottom_ref, -1.0),
    ):
        fluxes = flux(along_x(cells(before)), along_x(cells(after)))
        wet = own[0:1, :] > 0.0
        for f, val in enumerate(fluxes):
            ends_ref[at + f:at + f + 1, :] = jnp.where(wet, (sign * 0.5 * DT_DX) * val, 0.0)

    for copy in loads:
        copy.wait()
    lane = iota((rows, LANES), 1)
    sides = sides_ref[...]
    first[...] += jnp.where(lane == 0, pltpu.roll(sides, LANES - 2, 1), 0.0)
    last[...] += jnp.where(lane == LANES - 1, pltpu.roll(sides, LANES - 6, 1), 0.0)
    for at, line in ((0, 0), (rows - 1, 3)):
        first[at:at + 1, :] += ends_ref[line:line + 1, 0:LANES]
        last[at:at + 1, :] += ends_ref[line:line + 1, cols - LANES:cols]
    head[0:1, :] += ends_ref[0:1, LANES:cols - LANES]
    tail[TILE - 1:TILE, :] += ends_ref[3:4, LANES:cols - LANES]
    saves = [
        pltpu.make_async_copy(part, new_ref.at[at], save.at[n])
        for n, (at, part) in enumerate(zip(places, parts))
    ]
    for copy in saves:
        copy.start()
    for copy in saves:
        copy.wait()


def border(halos, edges, newh):
    rows, cols = newh.shape
    whole = pl.BlockSpec(memory_space=pl.ANY)
    return pl.pallas_call(
        border_kernel,
        out_shape=(
            jax.ShapeDtypeStruct((rows, cols), F32),
            jax.ShapeDtypeStruct((rows, LANES), F32),
            jax.ShapeDtypeStruct((TILE, cols), F32),
        ),
        in_specs=[VMEM] * 8 + [whole],
        out_specs=(whole, VMEM, VMEM),
        input_output_aliases={8: 0},
        scratch_shapes=[
            pltpu.VMEM((TILE, rows), F32),
            pltpu.VMEM((rows, LANES), F32),
            pltpu.VMEM((rows, LANES), F32),
            pltpu.VMEM((TILE, cols - 2 * LANES), F32),
            pltpu.VMEM((TILE, cols - 2 * LANES), F32),
            pltpu.SemaphoreType.DMA((4,)),
            pltpu.SemaphoreType.DMA((4,)),
        ],
        compiler_params=params(16 << 20),
        cost_estimate=pl.CostEstimate(flops=0, bytes_accessed=6 << 20, transcendentals=0),
        name="border",
    )(*halos, *edges, newh)


def finish_kernel(
    lab_ref, landed_ref, w_ref, p_ref, up_ref, dn_ref, sides_ref, ends_ref,
    hu_ref, hv_ref, h_ref, ox_ref, oy_ref,
    left, acc, acc2, fx, fy, fx2, fy2, padded,
):
    step = pl.program_id(0)
    rows = p_ref.shape[1]

    @pl.when(step == 0)
    def _():
        stack_left(left, summed_of(lab_ref[...], landed_ref[...]), 2)
        for g in range(GROUPS):
            cut = slice(g * LANES, (g + 1) * LANES)
            padded[g, TILE:TILE + rows, :] = p_ref[g]
            padded[g, 0:TILE, :] = jnp.broadcast_to(up_ref[3:4, cut], (TILE, LANES))
            padded[g, rows + TILE:, :] = jnp.broadcast_to(dn_ref[3:4, cut], (TILE, LANES))

    acc[...] = jnp.dot(left[...], w_ref[:, :PART], preferred_element_type=F32)
    acc2[...] = jnp.dot(left[...], w_ref[:, PART:], preferred_element_type=F32)
    lane = iota((TILE, LANES), 1)
    for part, (src, mx, my) in enumerate(((acc, fx, fy), (acc2, fx2, fy2))):
        spread_rows(src, mx, 0)
        spread_rows(src, my, 1)
        cells = slice(part * TILE, (part + 1) * TILE)
        for r in range(BPX):
            at = slice(r * TILE, (r + 1) * TILE)
            mark = pl.multiple_of(r * PATCH + (2 * step + part) * TILE, TILE)
            base = pl.multiple_of(mark + TILE, TILE)
            ends = sides_ref[pl.ds(mark, TILE), :]
            tiles = [padded[g, pl.ds(base, TILE), :] for g in range(GROUPS)]
            for g in range(GROUPS):
                before = tiles[g - 1] if g else pltpu.roll(ends, LANES - 1, 1)
                after = tiles[g + 1] if g < GROUPS - 1 else pltpu.roll(ends, LANES - 1, 1)
                prev = pltpu.roll(jnp.where(lane == LANES - 1, before, tiles[g]), 1, 1)
                nxt = pltpu.roll(jnp.where(lane == 0, after, tiles[g]), LANES - 1, 1)
                h = h_ref[g, r, cells, :]
                wet = h > 0.0
                scale = (TIME_STEP * PRESS * 0.5) * h
                gx = padded[g, pl.ds(base + 1, TILE), :] - padded[g, pl.ds(base - 1, TILE), :]
                wx = mx[g, at, :]
                wy = my[g, at, :]
                speed = (TIME_STEP * STRESS) * jnp.sqrt(wx * wx + wy * wy)
                new = [
                    hu_ref[g, r, cells, :] - scale * gx + speed * wx,
                    hv_ref[g, r, cells, :] - scale * (nxt - prev) + speed * wy,
                ]
                for own, edge, shift in ((0, 0, 3), (GROUPS - 1, LANES - 1, 6)):
                    if g == own:
                        new = [
                            jnp.where(
                                lane == edge,
                                a + pltpu.roll(ends, (edge - shift - f) % LANES, 1),
                                a,
                            )
                            for f, a in enumerate(new)
                        ]
                cut = slice(g * LANES, (g + 1) * LANES)
                ox_ref[r, cells, cut] = jnp.where(wet, new[0], 0.0)
                oy_ref[r, cells, cut] = jnp.where(wet, new[1], 0.0)

    @pl.when(step == 0)
    def _():
        ox_ref[0, 0:1, :] += ends_ref[1:2, :]
        oy_ref[0, 0:1, :] += ends_ref[2:3, :]

    @pl.when(step == pl.num_programs(0) - 1)
    def _():
        deep = ox_ref.shape[1]
        ox_ref[BPX - 1, deep - 1:deep, :] += ends_ref[4:5, :]
        oy_ref[BPX - 1, deep - 1:deep, :] += ends_ref[5:6, :]


def finish(lab, landed, weights, p, up, dn, sides, ends, hu, hv, h):
    deep = 2 * TILE
    steps = PATCH // deep
    cols = BPY * PATCH
    rows = p.shape[1]
    split = (GROUPS, BPX, PATCH, LANES)
    slab = pl.BlockSpec((GROUPS, BPX, deep, LANES), lambda i: (0, 0, i, 0))
    out = pl.BlockSpec((BPX, deep, cols), lambda i: (0, i, 0))
    shape = jax.ShapeDtypeStruct((BPX, PATCH, cols), F32)
    field = pltpu.VMEM((GROUPS, BPX * TILE, LANES), F32)

    def const(x):
        return pl.BlockSpec(x.shape, lambda i: (0,) * x.ndim)

    return pl.pallas_call(
        finish_kernel,
        grid=(steps,),
        out_shape=(shape, shape),
        in_specs=[
            const(lab), const(landed),
            pl.BlockSpec((NW * ABLK, 2 * PART), lambda i: (0, i)),
            const(p), const(up), const(dn), const(sides), const(ends),
            slab, slab, slab,
        ],
        out_specs=(out, out),
        scratch_shapes=[
            pltpu.VMEM((2 * NPATCH, NW * ABLK), BF16),
            pltpu.VMEM((2 * NPATCH, PART), F32),
            pltpu.VMEM((2 * NPATCH, PART), F32),
            field, field, field, field,
            pltpu.VMEM((GROUPS, rows + 2 * TILE, LANES), F32),
        ],
        compiler_params=params(34 << 20),
        cost_estimate=pl.CostEstimate(
            flops=4 * NPATCH * NW * ABLK * PATCH * PATCH, bytes_accessed=20 << 20, transcendentals=0
        ),
        name="finish",
    )(
        lab, landed, weights, p, up, dn, sides, ends,
        hu.reshape(split), hv.reshape(split), h.reshape(split),
    )


def body(
    atm_blocks,
    remap_weights,
    ovl_source,
    ovl_block,
    ovl_patch,
    ovl_weight,
    depth_field,
    wet_mask,
    mom_x,
    mom_y,
    blend,
):
    count_x = lax.axis_size("gx")
    count_y = lax.axis_size("gy")
    devices = count_x * count_y
    entries = ovl_source.size
    capacity = 2 * entries // devices
    slots = devices * capacity
    atm = atm_blocks.reshape(atm_blocks.shape[2:]).transpose(1, 0, 2)
    both = ("gx", "gy")
    want, lab = make_requests(
        ovl_source.reshape(1, entries), ovl_block.reshape(1, entries),
        ovl_patch.reshape(1, entries), ovl_weight.reshape(1, entries), devices, capacity,
    )
    asked = lax.all_to_all(
        want.reshape(devices, 1, capacity), both, split_axis=0, concat_axis=0, tiled=True
    )
    lab = lab.reshape(1, slots)
    press, wind = mix(blend.reshape(1), atm)
    top, bottom, left, right = edge_cells(depth_field, wet_mask, mom_x, mom_y)

    def exchange(after, tiles):
        rows = serve(after, asked, tiles)
        parts = rows.reshape(devices, capacity, rows.shape[1])
        got = lax.all_to_all(parts, both, split_axis=0, concat_axis=0, tiled=True)
        return got.reshape(rows.shape)

    press = exchange(top, press)
    newh, hu, hv, h, token = stencil(depth_field, wet_mask, mom_x, mom_y)
    wind = exchange(token, wind)
    weights = remap_weights.reshape(NW * ABLK, PATCH * PATCH)
    p, *edges = pressure_field(lab, press, weights, (top, bottom, left, right))
    top, bottom, left, right = edges
    halos = (
        send(bottom, "gx", 1), send(top, "gx", -1), send(right, "gy", 1), send(left, "gy", -1),
    )
    newh, sides, ends = border(halos, edges, newh)
    new_x, new_y = finish(lab, wind, weights, p, halos[0], halos[1], sides, ends, hu, hv, h)
    return (newh, new_x.reshape(newh.shape), new_y.reshape(newh.shape))


def solution(mesh):
    placed = (
        P("gx", "gy", None, None, None),
        P(),
        P("gx", "gy", None, None),
        P("gx", "gy", None),
        P("gx", "gy", None),
        P("gx", "gy", None),
        P("gx", "gy"),
        P("gx", "gy"),
        P("gx", "gy"),
        P("gx", "gy"),
        P(),
    )
    return jax.shard_map(
        body,
        mesh=mesh,
        in_specs=placed,
        out_specs=(P("gx", "gy"), P("gx", "gy"), P("gx", "gy")),
        check_vma=False,
    )
```

```python
import functools

import jax
import jax.numpy as jnp
from jax import lax
from jax.experimental import pallas as pl
from jax.experimental.pallas import tpu as pltpu
from jax.sharding import PartitionSpec as P

PATCH = 64
ABLK = 256
NW = 4
BPX = 16
BPY = 8
NPATCH = BPX * BPY

GRAV = 1.0
DT_DX = 0.2
TIME_STEP = 0.2
STRESS = 0.5
PRESS = 0.5

F32 = jnp.float32
BF16 = jnp.bfloat16
VMEM = pl.BlockSpec(memory_space=pltpu.VMEM)
SMEM = pl.BlockSpec(memory_space=pltpu.SMEM)
LANES = 128
TILE = 8
GROUPS = BPY * PATCH // LANES
HALVES = BPX // TILE
BAND = 128


def params(limit=56 << 20, **kw):
    return pltpu.CompilerParams(vmem_limit_bytes=limit, **kw)


def iota(shape, dim):
    return lax.broadcasted_iota(jnp.int32, shape, dim)


def rank_kernel(capacity, src_ref, blk_ref, pat_ref, wgt_ref, want_ref, lab_ref):
    devices = want_ref.shape[0]
    src = src_ref[...]
    ent = src.shape[1]
    hits = (iota((devices, ent), 0) == src).astype(F32)
    order = (iota((ent, ent), 0) <= iota((ent, ent), 1)).astype(BF16)
    ranks = jnp.dot(hits.astype(BF16), order, preferred_element_type=F32)
    mine = jnp.sum(hits * ranks, axis=0, keepdims=True).astype(jnp.int32) - 1
    place = iota((capacity, ent), 0) == mine
    pat = pat_ref[...]
    row_bits = BPX.bit_length() - 1
    col_bits = BPY.bit_length() - 1
    rows = jnp.zeros_like(pat)
    cols = jnp.zeros_like(pat)
    used_r = used_c = position = 0
    while used_r < row_bits or used_c < col_bits:
        value = jnp.bitwise_and(jnp.right_shift(pat, position), 1)
        if used_r < row_bits and (used_c >= col_bits or position % 2 == 0):
            rows = rows + value * (1 << used_r)
            used_r += 1
        else:
            cols = cols + value * (1 << used_c)
            used_c += 1
        position += 1

    def spread(row):
        picked = jnp.where(place, row.astype(F32), 0.0).astype(BF16)
        return lax.dot_general(
            hits.astype(BF16), picked, (((1,), (1,)), ((), ())),
            preferred_element_type=F32,
        ).astype(jnp.int32)

    want_ref[...] = spread(blk_ref[...])
    slot = spread(cols * BPX + rows)
    group = spread(wgt_ref[...] + 1)
    lab_ref[...] = jnp.where(group > 0, (group - 1) * NPATCH + slot, -1)


def make_requests(src, blk, pat, wgt, devices, capacity):
    shape = jax.ShapeDtypeStruct((devices, capacity), jnp.int32)
    return pl.pallas_call(
        functools.partial(rank_kernel, capacity),
        out_shape=(shape, shape),
        in_specs=[VMEM] * 4,
        out_specs=(VMEM, VMEM),
        compiler_params=params(),
        name="requests",
    )(src, blk, pat, wgt)


def mix_kernel(blend_ref, atm_ref, press_ref, wind_ref):
    blend = blend_ref[0]
    keep = 1.0 - blend

    def mixed(k):
        first = atm_ref[k].astype(F32)
        second = atm_ref[3 + k].astype(F32)
        return (keep * first + blend * second).astype(BF16)

    press_ref[...] = mixed(2)
    for k in range(2):
        wind_ref[:, k * ABLK:(k + 1) * ABLK] = mixed(k)


def mix(blend, atm):
    blocks = atm.shape[1]
    return pl.pallas_call(
        mix_kernel,
        out_shape=(
            jax.ShapeDtypeStruct((blocks, ABLK), BF16),
            jax.ShapeDtypeStruct((blocks, 2 * ABLK), BF16),
        ),
        in_specs=[SMEM, VMEM],
        out_specs=(VMEM, VMEM),
        compiler_params=params(),
        name="mix",
    )(blend, atm)


def serve_kernel(after_ref, asked_ref, tiles_ref, out_ref, turned, pick):
    peers, _, capacity = asked_ref.shape
    width = turned.shape[0]
    turned[...] = jnp.zeros_like(turned)
    turned[0:peers, 0:capacity] = asked_ref[:, 0, :]
    columns = turned[...].T
    blocks = tiles_ref.shape[0]
    names = iota((capacity, blocks), 1)
    for d in range(peers):
        pick[d * capacity:(d + 1) * capacity, :] = (columns[0:capacity, d:d + 1] == names).astype(F32)
    out_ref[...] = jnp.dot(
        pick[...].astype(BF16), tiles_ref[...], preferred_element_type=F32
    ).astype(BF16)


def serve(after, asked, tiles):
    peers, _, capacity = asked.shape
    slots = peers * capacity
    width = -(-max(peers, capacity) // LANES) * LANES
    return pl.pallas_call(
        serve_kernel,
        out_shape=jax.ShapeDtypeStruct((slots, tiles.shape[1]), BF16),
        in_specs=[pl.BlockSpec(memory_space=pl.ANY), VMEM, VMEM],
        out_specs=VMEM,
        scratch_shapes=[
            pltpu.VMEM((width, width), jnp.int32),
            pltpu.VMEM((slots, tiles.shape[0]), F32),
        ],
        compiler_params=params(32 << 20),
        name="serve",
    )(after, asked, tiles)


def edges_kernel(
    dl, ml, xl, yl, dr, mr, xr, yr, dt, mt, xt, yt, db, mb, xb, yb,
    top_ref, bottom_ref, left_ref, right_ref,
):
    def rows(d, m, x, y, at, out):
        wet = m[...] == 1
        for f, ref in enumerate((d, x, y)):
            out[f:f + 1, :] = jnp.where(wet, ref[...], 0.0)[at:at + 1]

    rows(dt, mt, xt, yt, 0, top_ref)
    rows(db, mb, xb, yb, TILE - 1, bottom_ref)
    lane = iota((LANES, LANES), 1)

    def step(b, carry):
        at = pl.ds(pl.multiple_of(b * LANES, LANES), LANES)
        wl = ml[at, :] == 1
        wr = mr[at, :] == 1
        packed = jnp.where(wl, dl[at, :], 0.0)
        packed = jnp.where(lane == 1, pltpu.roll(jnp.where(wl, xl[at, :], 0.0), 1, 1), packed)
        packed = jnp.where(lane == 2, pltpu.roll(jnp.where(wl, yl[at, :], 0.0), 2, 1), packed)
        packed = jnp.where(lane == 8, pltpu.roll(jnp.where(wr, dr[at, :], 0.0), 9, 1), packed)
        packed = jnp.where(lane == 9, pltpu.roll(jnp.where(wr, xr[at, :], 0.0), 10, 1), packed)
        packed = jnp.where(lane == 10, pltpu.roll(jnp.where(wr, yr[at, :], 0.0), 11, 1), packed)
        turned = packed.T
        left_ref[:, at] = turned[0:TILE]
        right_ref[:, at] = turned[TILE:2 * TILE]
        return carry

    lax.fori_loop(0, dl.shape[0] // LANES, step, 0)


def edge_cells(depth, mask, momx, momy):
    rows, cols = depth.shape
    fields = (depth, mask, momx, momy)
    left = pl.BlockSpec((rows, LANES), lambda i: (0, 0))
    right = pl.BlockSpec((rows, LANES), lambda i: (0, cols // LANES - 1))
    top = pl.BlockSpec((TILE, cols), lambda i: (0, 0))
    bottom = pl.BlockSpec((TILE, cols), lambda i: (rows // TILE - 1, 0))
    line = jax.ShapeDtypeStruct((TILE, cols), F32)
    column = jax.ShapeDtypeStruct((TILE, rows), F32)
    return pl.pallas_call(
        edges_kernel,
        grid=(1,),
        out_shape=(line, line, column, column),
        in_specs=[left] * 4 + [right] * 4 + [top] * 4 + [bottom] * 4,
        out_specs=(
            pl.BlockSpec((TILE, cols), lambda i: (0, 0)),
            pl.BlockSpec((TILE, cols), lambda i: (0, 0)),
            pl.BlockSpec((TILE, rows), lambda i: (0, 0)),
            pl.BlockSpec((TILE, rows), lambda i: (0, 0)),
        ),
        compiler_params=params(),
        name="edges",
    )(*(fields * 4))


def send(value, axis, step):
    count = lax.axis_size(axis)
    if step > 0:
        pairs = [(i, i + 1) for i in range(count - 1)]
    else:
        pairs = [(i + 1, i) for i in range(count - 1)]
    return lax.ppermute(value, axis, pairs)


def derived(h, u, v):
    r = jnp.where(h > 0.0, lax.rsqrt(h), 0.0)
    s = h * r
    q = u * r
    p = v * r
    half = 0.5 * h * h
    return (h, u, v, s, q, p, q * q + half, p * p + half, q * p)


def along_x(c):
    return (c[0], c[1], c[2], c[3], c[4], c[5], c[6], c[8])


def along_y(c):
    return (c[0], c[2], c[1], c[3], c[5], c[4], c[7], c[8])


def flux(a, b):
    hl, nl, tl, sl, ql, pl_, fl, gl = a
    hr, nr, tr, sr, qr, pr, fr, gr = b
    both = jnp.minimum(hl, hr) > 0.0
    half = jnp.where(both, 0.5, 1.0)
    twice = half + half
    level = (hl + hr) * half
    rc = lax.rsqrt(level)
    c = level * rc
    total = sl + sr
    inv = pl.reciprocal(total, approx=True)
    inv = inv * (2.0 - total * inv)
    u = jnp.where(both, (ql + qr) * inv, 0.0)
    v = (pl_ + pr) * inv
    dh = jnp.where(both, hr - hl, 0.0)
    dn = (nr - nl) * twice
    dt = jnp.where(both, tr - tl, 0.0)
    mid = 0.5 * dh
    e = (0.5 * dn - u * mid) * rc
    s1 = u - c
    s3 = u + c
    b1 = jnp.abs(s1) * (mid - e)
    b3 = jnp.abs(s3) * (mid + e)
    b2 = jnp.abs(u) * (dt - v * dh)
    d = b1 + b3
    return (
        jnp.where(both, nl + nr, 0.0) - d,
        (fl + fr) * twice - (b1 * s1 + b3 * s3),
        jnp.where(both, gl + gr, 0.0) - (d * v + b2),
    )


CELL = 9


def stencil_kernel(
    d_ref, m_ref, x_ref, y_ref, newh_ref, hu_ref, hv_ref, h_ref, token_ref, *scratch,
):
    cell = scratch[:CELL]
    gx = scratch[CELL:]
    step = pl.program_id(0)
    bands = pl.num_programs(0) - 1
    lane = iota((TILE, LANES), 1)

    @pl.when(step < bands)
    def _():
        def fill(t, carry):
            at = pl.ds(pl.multiple_of(t * TILE, TILE), TILE)
            to = pl.ds(pl.multiple_of(step * BAND + t * TILE + TILE, TILE), TILE)
            for g in range(GROUPS):
                cut = slice(g * LANES, (g + 1) * LANES)
                wet = m_ref[at, cut] == 1
                h = jnp.where(wet, d_ref[at, cut], 0.0)
                u = jnp.where(wet, x_ref[at, cut], 0.0)
                v = jnp.where(wet, y_ref[at, cut], 0.0)
                for dst, val in zip(cell, derived(h, u, v)):
                    dst[g, to, :] = val
            return carry

        lax.fori_loop(0, BAND // TILE, fill, 0, unroll=8)

    rows = bands * BAND

    @pl.when(step == 0)
    def _():
        token_ref[...] = jnp.zeros_like(token_ref)
        for dst in cell:
            dst[:, rows + TILE:, :] = jnp.zeros((GROUPS, TILE, LANES), F32)
        for dst in gx:
            dst[:, 0:TILE, :] = jnp.zeros((GROUPS, TILE, LANES), F32)

    @pl.when(step > 0)
    def _():
        start = pl.multiple_of((step - 1) * BAND, BAND)

        def across(t, carry):
            base = pl.multiple_of(start + t * TILE + TILE, TILE)
            for g in range(GROUPS):
                now = along_x([ref[g, pl.ds(base, TILE), :] for ref in cell])
                nxt = along_x([ref[g, pl.ds(base + 1, TILE), :] for ref in cell])
                for dst, val in zip(gx, flux(now, nxt)):
                    dst[g, pl.ds(base, TILE), :] = val
            return carry

        lax.fori_loop(0, BAND // TILE, across, 0, unroll=8)

        @pl.when(step == bands)
        def _():
            for dst in gx:
                dst[:, rows + TILE - 1:rows + TILE, :] = jnp.zeros((GROUPS, 1, LANES), F32)

        def body(t, carry):
            mark = pl.multiple_of(start + t * TILE, TILE)
            base = pl.multiple_of(mark + TILE, TILE)
            at = pl.ds(pl.multiple_of(t * TILE, TILE), TILE)
            before = [jnp.zeros((TILE, LANES), F32)] * 3
            for g in range(GROUPS):
                now = [ref[g, pl.ds(base, TILE), :] for ref in cell]
                if g < GROUPS - 1:
                    other = [ref[g + 1, pl.ds(base, TILE), :] for ref in cell[:3]]
                else:
                    other = now[:3]
                right = [
                    pltpu.roll(jnp.where(lane == 0, o, c), LANES - 1, 1)
                    for o, c in zip(other, now[:3])
                ]
                fy = flux(along_y(now), along_y(derived(*right)))
                if g == GROUPS - 1:
                    fy = [jnp.where(lane == LANES - 1, 0.0, val) for val in fy]
                py = [
                    pltpu.roll(jnp.where(lane == LANES - 1, o, c), 1, 1)
                    for o, c in zip(before, fy)
                ]
                before = fy
                fx = [src[g, pl.ds(base, TILE), :] for src in gx]
                px = [src[g, pl.ds(base - 1, TILE), :] for src in gx]
                h, u, v = now[:3]
                ch = (fx[0] - px[0]) + (fy[0] - py[0])
                cx = (fx[1] - px[1]) + (fy[2] - py[2])
                cy = (fx[2] - px[2]) + (fy[1] - py[1])
                newh_ref[at, g * LANES:(g + 1) * LANES] = jnp.where(
                    h > 0.0, h - (0.5 * DT_DX) * ch, 0.0
                )
                hu_ref[g, at, :] = u - (0.5 * DT_DX) * cx
                hv_ref[g, at, :] = v - (0.5 * DT_DX) * cy
                h_ref[g, at, :] = h
            return carry

        lax.fori_loop(0, BAND // TILE, body, 0, unroll=8)


def stencil(depth, mask, momx, momy):
    rows, cols = depth.shape
    bands = rows // BAND
    plane = jax.ShapeDtypeStruct((GROUPS, rows, LANES), F32)
    pad = pltpu.VMEM((GROUPS, rows + 2 * TILE, LANES), F32)
    band = pl.BlockSpec((BAND, cols), lambda i: (jnp.minimum(i, bands - 1), 0))
    part = pl.BlockSpec((GROUPS, BAND, LANES), lambda i: (0, jnp.maximum(i - 1, 0), 0))
    return pl.pallas_call(
        stencil_kernel,
        grid=(bands + 1,),
        out_shape=(
            jax.ShapeDtypeStruct((rows, cols), F32), plane, plane, plane,
            jax.ShapeDtypeStruct((TILE, LANES), F32),
        ),
        in_specs=[band] * 4,
        out_specs=(
            pl.BlockSpec((BAND, cols), lambda i: (jnp.maximum(i - 1, 0), 0)), part, part, part,
            pl.BlockSpec((TILE, LANES), lambda i: (0, 0)),
        ),
        scratch_shapes=[pad] * (CELL + 3),
        compiler_params=params(),
        cost_estimate=pl.CostEstimate(
            flops=200 * rows * cols, bytes_accessed=64 * rows * cols, transcendentals=0
        ),
        name="stencil",
    )(depth, mask, momx, momy)


def summed_of(lab, landed):
    select = (iota((NW * NPATCH, lab.shape[1]), 0) == lab).astype(BF16)
    return jnp.dot(select, landed, preferred_element_type=F32).astype(BF16)


def stack_left(left, summed, channels):
    for k in range(channels):
        for w in range(NW):
            left[k * NPATCH:(k + 1) * NPATCH, w * ABLK:(w + 1) * ABLK] = summed[
                w * NPATCH:(w + 1) * NPATCH, k * ABLK:(k + 1) * ABLK
            ]


PART = TILE * PATCH


def spread_rows(acc, field, k):
    low = iota((TILE, LANES), 1) < LANES // 2
    for t in range(TILE // 2):
        cut = slice(t * LANES, (t + 1) * LANES)
        for half in range(HALVES):
            for g in range(GROUPS):
                base = k * NPATCH + 2 * g * BPX + half * TILE
                even = acc[base:base + TILE, cut]
                odd = acc[base + BPX:base + BPX + TILE, cut]
                for i, val in (
                    (2 * t, jnp.where(low, even, pltpu.roll(odd, LANES // 2, 1))),
                    (2 * t + 1, jnp.where(low, pltpu.roll(even, LANES // 2, 1), odd)),
                ):
                    field[g, pl.ds(half * TILE * TILE + i, TILE, stride=TILE), :] = val


def press_kernel(
    lab_ref, landed_ref, w_ref, top0_ref, bottom0_ref, left0_ref, right0_ref,
    out_ref, top_ref, bottom_ref, left_ref, right_ref,
    left, acc, acc2, field, field2,
):
    step = pl.program_id(0)

    @pl.when(step == 0)
    def _():
        stack_left(left, summed_of(lab_ref[...], landed_ref[...]), 1)

    acc[...] = jnp.dot(left[...], w_ref[:, :PART], preferred_element_type=F32)
    acc2[...] = jnp.dot(left[...], w_ref[:, PART:], preferred_element_type=F32)
    for part, (src, mid) in enumerate(((acc, field), (acc2, field2))):
        spread_rows(src, mid, 0)
        for g in range(GROUPS):
            for r in range(BPX):
                to = pl.ds(pl.multiple_of(TILE + r * PATCH + (2 * step + part) * TILE, TILE), TILE)
                out_ref[g, to, :] = mid[g, r * TILE:(r + 1) * TILE, :]

    @pl.when(step == pl.num_programs(0) - 1)
    def _():
        rows = out_ref.shape[1] - 2 * TILE
        mine = iota((TILE, LANES), 0) == 3
        blank = jnp.zeros((TILE, LANES), F32)
        for g in range(GROUPS):
            cut = slice(g * LANES, (g + 1) * LANES)
            head = pltpu.roll(out_ref[g, TILE:2 * TILE, :], 3, 0)
            tail = pltpu.roll(out_ref[g, rows:rows + TILE, :], 4, 0)
            out_ref[g, 0:TILE, :] = blank
            out_ref[g, rows + TILE:, :] = blank
            top_ref[:, cut] = jnp.where(mine, head, top0_ref[:, cut])
            bottom_ref[:, cut] = jnp.where(mine, tail, bottom0_ref[:, cut])
        lane = iota((LANES, LANES), 1)
        for b in range(rows // LANES):
            at = slice(b * LANES, (b + 1) * LANES)
            inner = slice(TILE + b * LANES, TILE + (b + 1) * LANES)
            packed = jnp.where(
                lane == TILE + 3,
                pltpu.roll(out_ref[GROUPS - 1, inner, :], TILE + 4, 1),
                pltpu.roll(out_ref[0, inner, :], 3, 1),
            )
            turned = packed.T
            left_ref[:, at] = jnp.where(mine, turned[0:TILE], left0_ref[:, at])
            right_ref[:, at] = jnp.where(mine, turned[TILE:2 * TILE], right0_ref[:, at])


def pressure_field(lab, landed, weights, edges):
    steps = PATCH // (2 * TILE)
    rows = BPX * PATCH
    line = (TILE, BPY * PATCH)
    column = (TILE, rows)
    whole = (GROUPS, rows + 2 * TILE, LANES)

    def const(shape):
        return pl.BlockSpec(shape, lambda i: (0,) * len(shape))

    return pl.pallas_call(
        press_kernel,
        grid=(steps,),
        out_shape=tuple(jax.ShapeDtypeStruct(x, F32) for x in (whole, line, line, column, column)),
        in_specs=[
            const(lab.shape),
            const(landed.shape),
            pl.BlockSpec((NW * ABLK, 2 * PART), lambda i: (0, i)),
        ] + [const(x) for x in (line, line, column, column)],
        out_specs=tuple(const(x) for x in (whole, line, line, column, column)),
        scratch_shapes=[
            pltpu.VMEM((NPATCH, NW * ABLK), BF16),
            pltpu.VMEM((NPATCH, PART), F32),
            pltpu.VMEM((NPATCH, PART), F32),
            pltpu.VMEM((GROUPS, BPX * TILE, LANES), F32),
            pltpu.VMEM((GROUPS, BPX * TILE, LANES), F32),
        ],
        compiler_params=params(),
        cost_estimate=pl.CostEstimate(
            flops=2 * NPATCH * NW * ABLK * PATCH * PATCH, bytes_accessed=12 << 20, transcendentals=0
        ),
        name="pressure",
    )(lab, landed, weights, *edges)


def border_kernel(
    up_ref, dn_ref, lh_ref, rh_ref, top_ref, bottom_ref, left_ref, right_ref, old_ref,
    new_ref, sides_ref, ends_ref, edge, first, last, head, tail, load, save,
):
    rows, cols = old_ref.shape
    middle = pl.ds(LANES, cols - 2 * LANES)
    places = (
        (slice(None), pl.ds(0, LANES)),
        (slice(None), pl.ds(cols - LANES, LANES)),
        (pl.ds(0, TILE), middle),
        (pl.ds(rows - TILE, TILE), middle),
    )
    parts = (first, last, head, tail)
    loads = [
        pltpu.make_async_copy(old_ref.at[at], part, load.at[n])
        for n, (at, part) in enumerate(zip(places, parts))
    ]
    for copy in loads:
        copy.start()

    def cells(ref):
        return derived(ref[0:1, :], ref[1:2, :], ref[2:3, :])

    pull = TIME_STEP * PRESS * 0.5
    edge[...] = jnp.zeros_like(edge)
    for at, before, after, own, far, sign in (
        (0, lh_ref, left_ref, left_ref, lh_ref, 1.0),
        (3, right_ref, rh_ref, right_ref, rh_ref, -1.0),
    ):
        gh, gn, gt = flux(along_y(cells(before)), along_y(cells(after)))
        wet = own[0:1, :] > 0.0
        press = (pull * own[0:1, :]) * far[3:4, :]
        for f, val in enumerate((gh * (0.5 * DT_DX), gt * (0.5 * DT_DX), gn * (0.5 * DT_DX) + press)):
            edge[at + f:at + f + 1, :] = jnp.where(wet, sign * val, 0.0)
    blank = jnp.zeros((LANES - TILE, LANES), F32)
    for b in range(rows // LANES):
        cut = slice(b * LANES, (b + 1) * LANES)
        sides_ref[cut, :] = jnp.concatenate([edge[:, cut], blank], axis=0).T
    ends_ref[...] = jnp.zeros_like(ends_ref)
    for at, before, after, own, far, sign in (
        (0, up_ref, top_ref, top_ref, up_ref, 1.0),
        (3, bottom_ref, dn_ref, bottom_ref, dn_ref, -1.0),
    ):
        gh, gn, gt = flux(along_x(cells(before)), along_x(cells(after)))
        wet = own[0:1, :] > 0.0
        press = (pull * own[0:1, :]) * far[3:4, :]
        for f, val in enumerate((gh * (0.5 * DT_DX), gn * (0.5 * DT_DX) + press, gt * (0.5 * DT_DX))):
            ends_ref[at + f:at + f + 1, :] = jnp.where(wet, sign * val, 0.0)

    for copy in loads:
        copy.wait()
    lane = iota((rows, LANES), 1)
    sides = sides_ref[...]
    first[...] += jnp.where(lane == 0, sides, 0.0)
    last[...] += jnp.where(lane == LANES - 1, pltpu.roll(sides, LANES - 4, 1), 0.0)
    for at, line in ((0, 0), (rows - 1, 3)):
        first[at:at + 1, :] += ends_ref[line:line + 1, 0:LANES]
        last[at:at + 1, :] += ends_ref[line:line + 1, cols - LANES:cols]
    head[0:1, :] += ends_ref[0:1, LANES:cols - LANES]
    tail[TILE - 1:TILE, :] += ends_ref[3:4, LANES:cols - LANES]
    saves = [
        pltpu.make_async_copy(part, new_ref.at[at], save.at[n])
        for n, (at, part) in enumerate(zip(places, parts))
    ]
    for copy in saves:
        copy.start()
    for copy in saves:
        copy.wait()


def border(halos, edges, newh):
    rows, cols = newh.shape
    whole = pl.BlockSpec(memory_space=pl.ANY)
    return pl.pallas_call(
        border_kernel,
        out_shape=(
            jax.ShapeDtypeStruct((rows, cols), F32),
            jax.ShapeDtypeStruct((rows, LANES), F32),
            jax.ShapeDtypeStruct((TILE, cols), F32),
        ),
        in_specs=[VMEM] * 8 + [whole],
        out_specs=(whole, VMEM, VMEM),
        input_output_aliases={8: 0},
        scratch_shapes=[
            pltpu.VMEM((TILE, rows), F32),
            pltpu.VMEM((rows, LANES), F32),
            pltpu.VMEM((rows, LANES), F32),
            pltpu.VMEM((TILE, cols - 2 * LANES), F32),
            pltpu.VMEM((TILE, cols - 2 * LANES), F32),
            pltpu.SemaphoreType.DMA((4,)),
            pltpu.SemaphoreType.DMA((4,)),
        ],
        compiler_params=params(),
        name="border",
    )(*halos, *edges, newh)


def finish_kernel(
    lab_ref, landed_ref, w_ref, p_ref, sides_ref, ends_ref,
    hu_ref, hv_ref, h_ref, ox_ref, oy_ref,
    left, acc, acc2, fx, fy, fx2, fy2,
):
    step = pl.program_id(0)

    @pl.when(step == 0)
    def _():
        stack_left(left, summed_of(lab_ref[...], landed_ref[...]), 2)

    acc[...] = jnp.dot(left[...], w_ref[:, :PART], preferred_element_type=F32)
    acc2[...] = jnp.dot(left[...], w_ref[:, PART:], preferred_element_type=F32)
    lane = iota((TILE, LANES), 1)
    for part, (src, mx, my) in enumerate(((acc, fx, fy), (acc2, fx2, fy2))):
        spread_rows(src, mx, 0)
        spread_rows(src, my, 1)
        cells = slice(part * TILE, (part + 1) * TILE)
        for r in range(BPX):
            at = slice(r * TILE, (r + 1) * TILE)
            mark = pl.multiple_of(r * PATCH + (2 * step + part) * TILE, TILE)
            base = pl.multiple_of(mark + TILE, TILE)
            ends = sides_ref[pl.ds(mark, TILE), :]
            tiles = [p_ref[g, pl.ds(base, TILE), :] for g in range(GROUPS)]
            for g in range(GROUPS):
                before = tiles[g - 1] if g else 0.0
                after = tiles[g + 1] if g < GROUPS - 1 else 0.0
                prev = pltpu.roll(jnp.where(lane == LANES - 1, before, tiles[g]), 1, 1)
                nxt = pltpu.roll(jnp.where(lane == 0, after, tiles[g]), LANES - 1, 1)
                h = h_ref[g, r, cells, :]
                wet = h > 0.0
                scale = (TIME_STEP * PRESS * 0.5) * h
                gx = p_ref[g, pl.ds(base + 1, TILE), :] - p_ref[g, pl.ds(base - 1, TILE), :]
                wx = mx[g, at, :]
                wy = my[g, at, :]
                power = wx * wx + wy * wy
                speed = jnp.where(power > 0.0, power * lax.rsqrt(power), 0.0) * (TIME_STEP * STRESS)
                new = [
                    hu_ref[g, r, cells, :] - scale * gx + speed * wx,
                    hv_ref[g, r, cells, :] - scale * (nxt - prev) + speed * wy,
                ]
                for own, edge, shift in ((0, 0, 1), (GROUPS - 1, LANES - 1, 4)):
                    if g == own:
                        new = [
                            jnp.where(
                                lane == edge,
                                a + pltpu.roll(ends, (edge - shift - f) % LANES, 1),
                                a,
                            )
                            for f, a in enumerate(new)
                        ]
                cut = slice(g * LANES, (g + 1) * LANES)
                ox_ref[r, cells, cut] = jnp.where(wet, new[0], 0.0)
                oy_ref[r, cells, cut] = jnp.where(wet, new[1], 0.0)

    @pl.when(step == 0)
    def _():
        ox_ref[0, 0:1, :] += ends_ref[1:2, :]
        oy_ref[0, 0:1, :] += ends_ref[2:3, :]

    @pl.when(step == pl.num_programs(0) - 1)
    def _():
        deep = ox_ref.shape[1]
        ox_ref[BPX - 1, deep - 1:deep, :] += ends_ref[4:5, :]
        oy_ref[BPX - 1, deep - 1:deep, :] += ends_ref[5:6, :]


def finish(lab, landed, weights, p, sides, ends, hu, hv, h):
    deep = 2 * TILE
    steps = PATCH // deep
    cols = BPY * PATCH
    split = (GROUPS, BPX, PATCH, LANES)
    slab = pl.BlockSpec((GROUPS, BPX, deep, LANES), lambda i: (0, 0, i, 0))
    out = pl.BlockSpec((BPX, deep, cols), lambda i: (0, i, 0))
    shape = jax.ShapeDtypeStruct((BPX, PATCH, cols), F32)
    field = pltpu.VMEM((GROUPS, BPX * TILE, LANES), F32)

    def const(x):
        return pl.BlockSpec(x.shape, lambda i: (0,) * x.ndim)

    return pl.pallas_call(
        finish_kernel,
        grid=(steps,),
        out_shape=(shape, shape),
        in_specs=[
            const(lab), const(landed),
            pl.BlockSpec((NW * ABLK, 2 * PART), lambda i: (0, i)),
            const(p), const(sides), const(ends),
            slab, slab, slab,
        ],
        out_specs=(out, out),
        scratch_shapes=[
            pltpu.VMEM((2 * NPATCH, NW * ABLK), BF16),
            pltpu.VMEM((2 * NPATCH, PART), F32),
            pltpu.VMEM((2 * NPATCH, PART), F32),
            field, field, field, field,
        ],
        compiler_params=params(),
        cost_estimate=pl.CostEstimate(
            flops=4 * NPATCH * NW * ABLK * PATCH * PATCH, bytes_accessed=20 << 20, transcendentals=0
        ),
        name="finish",
    )(
        lab, landed, weights, p, sides, ends,
        hu.reshape(split), hv.reshape(split), h.reshape(split),
    )


def body(
    atm_blocks,
    remap_weights,
    ovl_source,
    ovl_block,
    ovl_patch,
    ovl_weight,
    depth_field,
    wet_mask,
    mom_x,
    mom_y,
    blend,
):
    count_x = lax.axis_size("gx")
    count_y = lax.axis_size("gy")
    devices = count_x * count_y
    entries = ovl_source.size
    capacity = 2 * entries // devices
    slots = devices * capacity
    atm = atm_blocks.reshape(atm_blocks.shape[2:]).transpose(1, 0, 2)
    both = ("gx", "gy")
    want, lab = make_requests(
        ovl_source.reshape(1, entries), ovl_block.reshape(1, entries),
        ovl_patch.reshape(1, entries), ovl_weight.reshape(1, entries), devices, capacity,
    )
    asked = lax.all_to_all(
        want.reshape(devices, 1, capacity), both, split_axis=0, concat_axis=0, tiled=True
    )
    lab = lab.reshape(1, slots)
    press, wind = mix(blend.reshape(1), atm)
    top, bottom, left, right = edge_cells(depth_field, wet_mask, mom_x, mom_y)

    def exchange(after, tiles):
        rows = serve(after, asked, tiles)
        parts = rows.reshape(devices, capacity, rows.shape[1])
        got = lax.all_to_all(parts, both, split_axis=0, concat_axis=0, tiled=True)
        return got.reshape(rows.shape)

    press = exchange(top, press)
    newh, hu, hv, h, token = stencil(depth_field, wet_mask, mom_x, mom_y)
    wind = exchange(token, wind)
    weights = remap_weights.reshape(NW * ABLK, PATCH * PATCH)
    p, *edges = pressure_field(lab, press, weights, (top, bottom, left, right))
    top, bottom, left, right = edges
    halos = (
        send(bottom, "gx", 1), send(top, "gx", -1), send(right, "gy", 1), send(left, "gy", -1),
    )
    newh, sides, ends = border(halos, edges, newh)
    new_x, new_y = finish(lab, wind, weights, p, sides, ends, hu, hv, h)
    return (newh, new_x.reshape(newh.shape), new_y.reshape(newh.shape))


def solution(mesh):
    placed = (
        P("gx", "gy", None, None, None),
        P(),
        P("gx", "gy", None, None),
        P("gx", "gy", None),
        P("gx", "gy", None),
        P("gx", "gy", None),
        P("gx", "gy"),
        P("gx", "gy"),
        P("gx", "gy"),
        P("gx", "gy"),
        P(),
    )
    return jax.shard_map(
        body,
        mesh=mesh,
        in_specs=placed,
        out_specs=(P("gx", "gy"), P("gx", "gy"), P("gx", "gy")),
        check_vma=False,
    )
```

```python
import functools

import jax
import jax.numpy as jnp
from jax import lax
from jax.experimental import pallas as pl
from jax.experimental.pallas import tpu as pltpu
from jax.sharding import PartitionSpec as P

PATCH = 64
ABLK = 256
NW = 4
BPX = 16
BPY = 8
NPATCH = BPX * BPY

GRAV = 1.0
DT_DX = 0.2
TIME_STEP = 0.2
STRESS = 0.5
PRESS = 0.5

F32 = jnp.float32
BF16 = jnp.bfloat16
VMEM = pl.BlockSpec(memory_space=pltpu.VMEM)
SMEM = pl.BlockSpec(memory_space=pltpu.SMEM)
LANES = 128
TILE = 8
GROUPS = BPY * PATCH // LANES
HALVES = BPX // TILE
BAND = 128


def params(limit=56 << 20, **kw):
    return pltpu.CompilerParams(vmem_limit_bytes=limit, **kw)


def iota(shape, dim):
    return lax.broadcasted_iota(jnp.int32, shape, dim)


def rank_kernel(capacity, src_ref, blk_ref, pat_ref, wgt_ref, want_ref, lab_ref):
    devices = want_ref.shape[0]
    src = src_ref[...]
    ent = src.shape[1]
    hits = (iota((devices, ent), 0) == src).astype(F32)
    order = (iota((ent, ent), 0) <= iota((ent, ent), 1)).astype(BF16)
    ranks = jnp.dot(hits.astype(BF16), order, preferred_element_type=F32)
    mine = jnp.sum(hits * ranks, axis=0, keepdims=True).astype(jnp.int32) - 1
    place = iota((capacity, ent), 0) == mine
    pat = pat_ref[...]
    row_bits = BPX.bit_length() - 1
    col_bits = BPY.bit_length() - 1
    rows = jnp.zeros_like(pat)
    cols = jnp.zeros_like(pat)
    used_r = used_c = position = 0
    while used_r < row_bits or used_c < col_bits:
        value = jnp.bitwise_and(jnp.right_shift(pat, position), 1)
        if used_r < row_bits and (used_c >= col_bits or position % 2 == 0):
            rows = rows + value * (1 << used_r)
            used_r += 1
        else:
            cols = cols + value * (1 << used_c)
            used_c += 1
        position += 1

    def spread(row):
        picked = jnp.where(place, row.astype(F32), 0.0).astype(BF16)
        return lax.dot_general(
            hits.astype(BF16), picked, (((1,), (1,)), ((), ())),
            preferred_element_type=F32,
        ).astype(jnp.int32)

    want_ref[...] = spread(blk_ref[...])
    slot = spread(cols * BPX + rows)
    group = spread(wgt_ref[...] + 1)
    lab_ref[...] = jnp.where(group > 0, (group - 1) * NPATCH + slot, -1)


def make_requests(src, blk, pat, wgt, devices, capacity):
    shape = jax.ShapeDtypeStruct((devices, capacity), jnp.int32)
    return pl.pallas_call(
        functools.partial(rank_kernel, capacity),
        out_shape=(shape, shape),
        in_specs=[VMEM] * 4,
        out_specs=(VMEM, VMEM),
        compiler_params=params(),
        name="requests",
    )(src, blk, pat, wgt)


def mix_kernel(blend_ref, atm_ref, press_ref, wind_ref):
    blend = blend_ref[0]
    keep = 1.0 - blend

    def mixed(k):
        first = atm_ref[k].astype(F32)
        second = atm_ref[3 + k].astype(F32)
        return (keep * first + blend * second).astype(BF16)

    press_ref[...] = mixed(2)
    for k in range(2):
        wind_ref[:, k * ABLK:(k + 1) * ABLK] = mixed(k)


def mix(blend, atm):
    blocks = atm.shape[1]
    return pl.pallas_call(
        mix_kernel,
        out_shape=(
            jax.ShapeDtypeStruct((blocks, ABLK), BF16),
            jax.ShapeDtypeStruct((blocks, 2 * ABLK), BF16),
        ),
        in_specs=[SMEM, VMEM],
        out_specs=(VMEM, VMEM),
        compiler_params=params(),
        name="mix",
    )(blend, atm)


def serve_kernel(after_ref, asked_ref, tiles_ref, out_ref, turned, pick):
    peers, _, capacity = asked_ref.shape
    width = turned.shape[0]
    turned[...] = jnp.zeros_like(turned)
    turned[0:peers, 0:capacity] = asked_ref[:, 0, :]
    columns = turned[...].T
    blocks = tiles_ref.shape[0]
    names = iota((capacity, blocks), 1)
    for d in range(peers):
        pick[d * capacity:(d + 1) * capacity, :] = (columns[0:capacity, d:d + 1] == names).astype(F32)
    out_ref[...] = jnp.dot(
        pick[...].astype(BF16), tiles_ref[...], preferred_element_type=F32
    ).astype(BF16)


def serve(after, asked, tiles):
    peers, _, capacity = asked.shape
    slots = peers * capacity
    width = -(-max(peers, capacity) // LANES) * LANES
    return pl.pallas_call(
        serve_kernel,
        out_shape=jax.ShapeDtypeStruct((slots, tiles.shape[1]), BF16),
        in_specs=[pl.BlockSpec(memory_space=pl.ANY), VMEM, VMEM],
        out_specs=VMEM,
        scratch_shapes=[
            pltpu.VMEM((width, width), jnp.int32),
            pltpu.VMEM((slots, tiles.shape[0]), F32),
        ],
        compiler_params=params(32 << 20),
        name="serve",
    )(after, asked, tiles)


def edges_kernel(
    dl, ml, xl, yl, dr, mr, xr, yr, dt, mt, xt, yt, db, mb, xb, yb,
    top_ref, bottom_ref, left_ref, right_ref,
):
    def rows(d, m, x, y, at, out):
        wet = m[...] == 1
        for f, ref in enumerate((d, x, y)):
            out[f:f + 1, :] = jnp.where(wet, ref[...], 0.0)[at:at + 1]

    rows(dt, mt, xt, yt, 0, top_ref)
    rows(db, mb, xb, yb, TILE - 1, bottom_ref)
    lane = iota((LANES, LANES), 1)

    def step(b, carry):
        at = pl.ds(pl.multiple_of(b * LANES, LANES), LANES)
        wl = ml[at, :] == 1
        wr = mr[at, :] == 1
        packed = jnp.where(wl, dl[at, :], 0.0)
        packed = jnp.where(lane == 1, pltpu.roll(jnp.where(wl, xl[at, :], 0.0), 1, 1), packed)
        packed = jnp.where(lane == 2, pltpu.roll(jnp.where(wl, yl[at, :], 0.0), 2, 1), packed)
        packed = jnp.where(lane == 8, pltpu.roll(jnp.where(wr, dr[at, :], 0.0), 9, 1), packed)
        packed = jnp.where(lane == 9, pltpu.roll(jnp.where(wr, xr[at, :], 0.0), 10, 1), packed)
        packed = jnp.where(lane == 10, pltpu.roll(jnp.where(wr, yr[at, :], 0.0), 11, 1), packed)
        turned = packed.T
        left_ref[:, at] = turned[0:TILE]
        right_ref[:, at] = turned[TILE:2 * TILE]
        return carry

    lax.fori_loop(0, dl.shape[0] // LANES, step, 0)


def edge_cells(depth, mask, momx, momy):
    rows, cols = depth.shape
    fields = (depth, mask, momx, momy)
    left = pl.BlockSpec((rows, LANES), lambda i: (0, 0))
    right = pl.BlockSpec((rows, LANES), lambda i: (0, cols // LANES - 1))
    top = pl.BlockSpec((TILE, cols), lambda i: (0, 0))
    bottom = pl.BlockSpec((TILE, cols), lambda i: (rows // TILE - 1, 0))
    line = jax.ShapeDtypeStruct((TILE, cols), F32)
    column = jax.ShapeDtypeStruct((TILE, rows), F32)
    return pl.pallas_call(
        edges_kernel,
        grid=(1,),
        out_shape=(line, line, column, column),
        in_specs=[left] * 4 + [right] * 4 + [top] * 4 + [bottom] * 4,
        out_specs=(
            pl.BlockSpec((TILE, cols), lambda i: (0, 0)),
            pl.BlockSpec((TILE, cols), lambda i: (0, 0)),
            pl.BlockSpec((TILE, rows), lambda i: (0, 0)),
            pl.BlockSpec((TILE, rows), lambda i: (0, 0)),
        ),
        compiler_params=params(),
        name="edges",
    )(*(fields * 4))


def send(value, axis, step):
    count = lax.axis_size(axis)
    if step > 0:
        pairs = [(i, i + 1) for i in range(count - 1)]
    else:
        pairs = [(i + 1, i) for i in range(count - 1)]
    return lax.ppermute(value, axis, pairs)


def derived(h, u, v):
    r = jnp.where(h > 0.0, lax.rsqrt(h), 0.0)
    s = h * r
    q = u * r
    p = v * r
    half = 0.5 * h * h
    return (h, u, v, s, q, p, q * q + half, p * p + half, q * p)


def along_x(c):
    return (c[0], c[1], c[2], c[3], c[4], c[5], c[6], c[8])


def along_y(c):
    return (c[0], c[2], c[1], c[3], c[5], c[4], c[7], c[8])


def flux(a, b):
    hl, nl, tl, sl, ql, pl_, fl, gl = a
    hr, nr, tr, sr, qr, pr, fr, gr = b
    both = jnp.minimum(hl, hr) > 0.0
    half = jnp.where(both, 0.5, 1.0)
    twice = half + half
    level = (hl + hr) * half
    rc = lax.rsqrt(level)
    c = level * rc
    total = sl + sr
    inv = pl.reciprocal(total, approx=True)
    inv = inv * (2.0 - total * inv)
    u = jnp.where(both, (ql + qr) * inv, 0.0)
    v = (pl_ + pr) * inv
    dh = jnp.where(both, hr - hl, 0.0)
    dn = (nr - nl) * twice
    dt = jnp.where(both, tr - tl, 0.0)
    mid = 0.5 * dh
    e = (0.5 * dn - u * mid) * rc
    s1 = u - c
    s3 = u + c
    b1 = jnp.abs(s1) * (mid - e)
    b3 = jnp.abs(s3) * (mid + e)
    b2 = jnp.abs(u) * (dt - v * dh)
    d = b1 + b3
    return (
        jnp.where(both, nl + nr, 0.0) - d,
        (fl + fr) * twice - (b1 * s1 + b3 * s3),
        jnp.where(both, gl + gr, 0.0) - (d * v + b2),
    )


CELL = 9


def stencil_kernel(opening, closing, *refs):
    fields = refs[:4]
    refs = refs[5:]
    above = () if opening else refs[:4]
    if not opening:
        refs = refs[8:]
    newh_ref, hu_ref, hv_ref, h_ref, token_ref = refs[:5]
    cell = refs[5:5 + CELL]
    gx = refs[5 + CELL:]
    step = pl.program_id(0)
    bands = pl.num_programs(0) - 1
    lane = iota((TILE, LANES), 1)

    def masked(d, m, x, y, at, cut):
        wet = m[at, cut] == 1
        return derived(*[jnp.where(wet, ref[at, cut], 0.0) for ref in (d, x, y)])

    def fill_band():
        def fill(t, carry):
            at = pl.ds(pl.multiple_of(t * TILE, TILE), TILE)
            to = pl.ds(pl.multiple_of(step * BAND + t * TILE + TILE, TILE), TILE)
            for g in range(GROUPS):
                cut = slice(g * LANES, (g + 1) * LANES)
                for dst, val in zip(cell, masked(*fields, at, cut)):
                    dst[g, to, :] = val
            return carry

        lax.fori_loop(0, BAND // TILE, fill, 0, unroll=8)

    if closing:
        pl.when(step < bands)(fill_band)
    else:
        fill_band()

    @pl.when(step == 0)
    def _():
        token_ref[...] = jnp.zeros_like(token_ref)
        if closing:
            for dst in cell:
                dst[:, dst.shape[1] - BAND:dst.shape[1] - BAND + TILE, :] = jnp.zeros(
                    (GROUPS, TILE, LANES), F32
                )
        if opening:
            for dst in gx:
                dst[:, 0:TILE, :] = jnp.zeros((GROUPS, TILE, LANES), F32)
        else:
            for g in range(GROUPS):
                cut = slice(g * LANES, (g + 1) * LANES)
                for dst, val in zip(cell, masked(*above, slice(None), cut)):
                    dst[g, 0:TILE, :] = val
                now = along_x([ref[g, 0:TILE, :] for ref in cell])
                nxt = along_x([ref[g, 1:TILE + 1, :] for ref in cell])
                for dst, val in zip(gx, flux(now, nxt)):
                    dst[g, 0:TILE, :] = val

    @pl.when(step > 0)
    def _():
        start = pl.multiple_of((step - 1) * BAND, BAND)

        def across(t, carry):
            base = pl.multiple_of(start + t * TILE + TILE, TILE)
            for g in range(GROUPS):
                now = along_x([ref[g, pl.ds(base, TILE), :] for ref in cell])
                nxt = along_x([ref[g, pl.ds(base + 1, TILE), :] for ref in cell])
                for dst, val in zip(gx, flux(now, nxt)):
                    dst[g, pl.ds(base, TILE), :] = val
            return carry

        lax.fori_loop(0, BAND // TILE, across, 0, unroll=8)

        if closing:
            @pl.when(step == bands)
            def _():
                for dst in gx:
                    at = dst.shape[1] - BAND - 1
                    dst[:, at:at + 1, :] = jnp.zeros((GROUPS, 1, LANES), F32)

        def body(t, carry):
            mark = pl.multiple_of(start + t * TILE, TILE)
            base = pl.multiple_of(mark + TILE, TILE)
            at = pl.ds(pl.multiple_of(t * TILE, TILE), TILE)
            before = [jnp.zeros((TILE, LANES), F32)] * 3
            for g in range(GROUPS):
                now = [ref[g, pl.ds(base, TILE), :] for ref in cell]
                if g < GROUPS - 1:
                    other = [ref[g + 1, pl.ds(base, TILE), :] for ref in cell[:3]]
                else:
                    other = now[:3]
                right = [
                    pltpu.roll(jnp.where(lane == 0, o, c), LANES - 1, 1)
                    for o, c in zip(other, now[:3])
                ]
                fy = flux(along_y(now), along_y(derived(*right)))
                if g == GROUPS - 1:
                    fy = [jnp.where(lane == LANES - 1, 0.0, val) for val in fy]
                py = [
                    pltpu.roll(jnp.where(lane == LANES - 1, o, c), 1, 1)
                    for o, c in zip(before, fy)
                ]
                before = fy
                fx = [src[g, pl.ds(base, TILE), :] for src in gx]
                px = [src[g, pl.ds(base - 1, TILE), :] for src in gx]
                h, u, v = now[:3]
                ch = (fx[0] - px[0]) + (fy[0] - py[0])
                cx = (fx[1] - px[1]) + (fy[2] - py[2])
                cy = (fx[2] - px[2]) + (fy[1] - py[1])
                newh_ref[at, g * LANES:(g + 1) * LANES] = jnp.where(
                    h > 0.0, h - (0.5 * DT_DX) * ch, 0.0
                )
                hu_ref[g, at, :] = u - (0.5 * DT_DX) * cx
                hv_ref[g, at, :] = v - (0.5 * DT_DX) * cy
                h_ref[g, at, :] = h
            return carry

        lax.fori_loop(0, BAND // TILE, body, 0, unroll=8)


def stencil(fields, after, first, count, old=()):
    rows, cols = fields[0].shape
    bands = rows // BAND
    opening = first == 0
    closing = first + count == bands
    plane = jax.ShapeDtypeStruct((GROUPS, rows, LANES), F32)
    scratch = pltpu.VMEM((GROUPS, (count + 1) * BAND + TILE, LANES), F32)
    band = pl.BlockSpec((BAND, cols), lambda i: (jnp.minimum(first + i, bands - 1), 0))
    above = pl.BlockSpec((TILE, cols), lambda i: (first * BAND // TILE - 1, 0))
    whole = pl.BlockSpec(memory_space=pl.ANY)
    part = pl.BlockSpec((GROUPS, BAND, LANES), lambda i: (0, first + jnp.maximum(i - 1, 0), 0))
    return pl.pallas_call(
        functools.partial(stencil_kernel, opening, closing),
        grid=(count + 1,),
        out_shape=(
            jax.ShapeDtypeStruct((rows, cols), F32), plane, plane, plane,
            jax.ShapeDtypeStruct((TILE, LANES), F32),
        ),
        in_specs=[band] * 4 + [whole] + ([] if opening else [above] * 4 + [whole] * 4),
        out_specs=(
            pl.BlockSpec((BAND, cols), lambda i: (first + jnp.maximum(i - 1, 0), 0)),
            part, part, part,
            pl.BlockSpec((TILE, LANES), lambda i: (0, 0)),
        ),
        scratch_shapes=[scratch] * (CELL + 3),
        input_output_aliases={} if opening else {9 + n: n for n in range(4)},
        compiler_params=params(),
        cost_estimate=pl.CostEstimate(
            flops=200 * count * BAND * cols, bytes_accessed=64 * count * BAND * cols,
            transcendentals=0,
        ),
        name="stencil",
    )(*fields, after, *(() if opening else fields), *old)


def summed_of(lab, landed):
    select = (iota((NW * NPATCH, lab.shape[1]), 0) == lab).astype(BF16)
    return jnp.dot(select, landed, preferred_element_type=F32).astype(BF16)


def stack_left(left, summed, channels):
    for k in range(channels):
        for w in range(NW):
            left[k * NPATCH:(k + 1) * NPATCH, w * ABLK:(w + 1) * ABLK] = summed[
                w * NPATCH:(w + 1) * NPATCH, k * ABLK:(k + 1) * ABLK
            ]


PART = TILE * PATCH


def spread_rows(acc, field, k):
    low = iota((TILE, LANES), 1) < LANES // 2
    for t in range(TILE // 2):
        cut = slice(t * LANES, (t + 1) * LANES)
        for half in range(HALVES):
            for g in range(GROUPS):
                base = k * NPATCH + 2 * g * BPX + half * TILE
                even = acc[base:base + TILE, cut]
                odd = acc[base + BPX:base + BPX + TILE, cut]
                for i, val in (
                    (2 * t, jnp.where(low, even, pltpu.roll(odd, LANES // 2, 1))),
                    (2 * t + 1, jnp.where(low, pltpu.roll(even, LANES // 2, 1), odd)),
                ):
                    field[g, pl.ds(half * TILE * TILE + i, TILE, stride=TILE), :] = val


def press_kernel(
    lab_ref, landed_ref, w_ref, top0_ref, bottom0_ref, left0_ref, right0_ref,
    out_ref, top_ref, bottom_ref, left_ref, right_ref,
    left, acc, acc2, field, field2,
):
    step = pl.program_id(0)

    @pl.when(step == 0)
    def _():
        stack_left(left, summed_of(lab_ref[...], landed_ref[...]), 1)

    acc[...] = jnp.dot(left[...], w_ref[:, :PART], preferred_element_type=F32)
    acc2[...] = jnp.dot(left[...], w_ref[:, PART:], preferred_element_type=F32)
    for part, (src, mid) in enumerate(((acc, field), (acc2, field2))):
        spread_rows(src, mid, 0)
        for g in range(GROUPS):
            for r in range(BPX):
                to = pl.ds(pl.multiple_of(TILE + r * PATCH + (2 * step + part) * TILE, TILE), TILE)
                out_ref[g, to, :] = mid[g, r * TILE:(r + 1) * TILE, :]

    @pl.when(step == pl.num_programs(0) - 1)
    def _():
        rows = out_ref.shape[1] - 2 * TILE
        mine = iota((TILE, LANES), 0) == 3
        blank = jnp.zeros((TILE, LANES), F32)
        for g in range(GROUPS):
            cut = slice(g * LANES, (g + 1) * LANES)
            head = pltpu.roll(out_ref[g, TILE:2 * TILE, :], 3, 0)
            tail = pltpu.roll(out_ref[g, rows:rows + TILE, :], 4, 0)
            out_ref[g, 0:TILE, :] = blank
            out_ref[g, rows + TILE:, :] = blank
            top_ref[:, cut] = jnp.where(mine, head, top0_ref[:, cut])
            bottom_ref[:, cut] = jnp.where(mine, tail, bottom0_ref[:, cut])
        lane = iota((LANES, LANES), 1)
        for b in range(rows // LANES):
            at = slice(b * LANES, (b + 1) * LANES)
            inner = slice(TILE + b * LANES, TILE + (b + 1) * LANES)
            packed = jnp.where(
                lane == TILE + 3,
                pltpu.roll(out_ref[GROUPS - 1, inner, :], TILE + 4, 1),
                pltpu.roll(out_ref[0, inner, :], 3, 1),
            )
            turned = packed.T
            left_ref[:, at] = jnp.where(mine, turned[0:TILE], left0_ref[:, at])
            right_ref[:, at] = jnp.where(mine, turned[TILE:2 * TILE], right0_ref[:, at])


def pressure_field(lab, landed, weights, edges):
    steps = PATCH // (2 * TILE)
    rows = BPX * PATCH
    line = (TILE, BPY * PATCH)
    column = (TILE, rows)
    whole = (GROUPS, rows + 2 * TILE, LANES)

    def const(shape):
        return pl.BlockSpec(shape, lambda i: (0,) * len(shape))

    return pl.pallas_call(
        press_kernel,
        grid=(steps,),
        out_shape=tuple(jax.ShapeDtypeStruct(x, F32) for x in (whole, line, line, column, column)),
        in_specs=[
            const(lab.shape),
            const(landed.shape),
            pl.BlockSpec((NW * ABLK, 2 * PART), lambda i: (0, i)),
        ] + [const(x) for x in (line, line, column, column)],
        out_specs=tuple(const(x) for x in (whole, line, line, column, column)),
        scratch_shapes=[
            pltpu.VMEM((NPATCH, NW * ABLK), BF16),
            pltpu.VMEM((NPATCH, PART), F32),
            pltpu.VMEM((NPATCH, PART), F32),
            pltpu.VMEM((GROUPS, BPX * TILE, LANES), F32),
            pltpu.VMEM((GROUPS, BPX * TILE, LANES), F32),
        ],
        compiler_params=params(),
        cost_estimate=pl.CostEstimate(
            flops=2 * NPATCH * NW * ABLK * PATCH * PATCH, bytes_accessed=12 << 20, transcendentals=0
        ),
        name="pressure",
    )(lab, landed, weights, *edges)


def border_kernel(
    up_ref, dn_ref, lh_ref, rh_ref, top_ref, bottom_ref, left_ref, right_ref, old_ref,
    new_ref, sides_ref, ends_ref, edge, first, last, head, tail, load, save,
):
    rows, cols = old_ref.shape
    middle = pl.ds(LANES, cols - 2 * LANES)
    places = (
        (slice(None), pl.ds(0, LANES)),
        (slice(None), pl.ds(cols - LANES, LANES)),
        (pl.ds(0, TILE), middle),
        (pl.ds(rows - TILE, TILE), middle),
    )
    parts = (first, last, head, tail)
    loads = [
        pltpu.make_async_copy(old_ref.at[at], part, load.at[n])
        for n, (at, part) in enumerate(zip(places, parts))
    ]
    for copy in loads:
        copy.start()

    def cells(ref):
        return derived(ref[0:1, :], ref[1:2, :], ref[2:3, :])

    pull = TIME_STEP * PRESS * 0.5
    edge[...] = jnp.zeros_like(edge)
    for at, before, after, own, far, sign in (
        (0, lh_ref, left_ref, left_ref, lh_ref, 1.0),
        (3, right_ref, rh_ref, right_ref, rh_ref, -1.0),
    ):
        gh, gn, gt = flux(along_y(cells(before)), along_y(cells(after)))
        wet = own[0:1, :] > 0.0
        press = (pull * own[0:1, :]) * far[3:4, :]
        for f, val in enumerate((gh * (0.5 * DT_DX), gt * (0.5 * DT_DX), gn * (0.5 * DT_DX) + press)):
            edge[at + f:at + f + 1, :] = jnp.where(wet, sign * val, 0.0)
    blank = jnp.zeros((LANES - TILE, LANES), F32)
    for b in range(rows // LANES):
        cut = slice(b * LANES, (b + 1) * LANES)
        sides_ref[cut, :] = jnp.concatenate([edge[:, cut], blank], axis=0).T
    ends_ref[...] = jnp.zeros_like(ends_ref)
    for at, before, after, own, far, sign in (
        (0, up_ref, top_ref, top_ref, up_ref, 1.0),
        (3, bottom_ref, dn_ref, bottom_ref, dn_ref, -1.0),
    ):
        gh, gn, gt = flux(along_x(cells(before)), along_x(cells(after)))
        wet = own[0:1, :] > 0.0
        press = (pull * own[0:1, :]) * far[3:4, :]
        for f, val in enumerate((gh * (0.5 * DT_DX), gn * (0.5 * DT_DX) + press, gt * (0.5 * DT_DX))):
            ends_ref[at + f:at + f + 1, :] = jnp.where(wet, sign * val, 0.0)

    for copy in loads:
        copy.wait()
    lane = iota((rows, LANES), 1)
    sides = sides_ref[...]
    first[...] += jnp.where(lane == 0, sides, 0.0)
    last[...] += jnp.where(lane == LANES - 1, pltpu.roll(sides, LANES - 4, 1), 0.0)
    for at, line in ((0, 0), (rows - 1, 3)):
        first[at:at + 1, :] += ends_ref[line:line + 1, 0:LANES]
        last[at:at + 1, :] += ends_ref[line:line + 1, cols - LANES:cols]
    head[0:1, :] += ends_ref[0:1, LANES:cols - LANES]
    tail[TILE - 1:TILE, :] += ends_ref[3:4, LANES:cols - LANES]
    saves = [
        pltpu.make_async_copy(part, new_ref.at[at], save.at[n])
        for n, (at, part) in enumerate(zip(places, parts))
    ]
    for copy in saves:
        copy.start()
    for copy in saves:
        copy.wait()


def border(halos, edges, newh):
    rows, cols = newh.shape
    whole = pl.BlockSpec(memory_space=pl.ANY)
    return pl.pallas_call(
        border_kernel,
        out_shape=(
            jax.ShapeDtypeStruct((rows, cols), F32),
            jax.ShapeDtypeStruct((rows, LANES), F32),
            jax.ShapeDtypeStruct((TILE, cols), F32),
        ),
        in_specs=[VMEM] * 8 + [whole],
        out_specs=(whole, VMEM, VMEM),
        input_output_aliases={8: 0},
        scratch_shapes=[
            pltpu.VMEM((TILE, rows), F32),
            pltpu.VMEM((rows, LANES), F32),
            pltpu.VMEM((rows, LANES), F32),
            pltpu.VMEM((TILE, cols - 2 * LANES), F32),
            pltpu.VMEM((TILE, cols - 2 * LANES), F32),
            pltpu.SemaphoreType.DMA((4,)),
            pltpu.SemaphoreType.DMA((4,)),
        ],
        compiler_params=params(),
        name="border",
    )(*halos, *edges, newh)


def finish_kernel(
    lab_ref, landed_ref, w_ref, p_ref, sides_ref, ends_ref,
    hu_ref, hv_ref, h_ref, ox_ref, oy_ref,
    left, acc, acc2, fx, fy, fx2, fy2,
):
    step = pl.program_id(0)

    @pl.when(step == 0)
    def _():
        stack_left(left, summed_of(lab_ref[...], landed_ref[...]), 2)

    acc[...] = jnp.dot(left[...], w_ref[:, :PART], preferred_element_type=F32)
    acc2[...] = jnp.dot(left[...], w_ref[:, PART:], preferred_element_type=F32)
    lane = iota((TILE, LANES), 1)
    for part, (src, mx, my) in enumerate(((acc, fx, fy), (acc2, fx2, fy2))):
        spread_rows(src, mx, 0)
        spread_rows(src, my, 1)
        cells = slice(part * TILE, (part + 1) * TILE)
        for r in range(BPX):
            at = slice(r * TILE, (r + 1) * TILE)
            mark = pl.multiple_of(r * PATCH + (2 * step + part) * TILE, TILE)
            base = pl.multiple_of(mark + TILE, TILE)
            ends = sides_ref[pl.ds(mark, TILE), :]
            tiles = [p_ref[g, pl.ds(base, TILE), :] for g in range(GROUPS)]
            for g in range(GROUPS):
                before = tiles[g - 1] if g else 0.0
                after = tiles[g + 1] if g < GROUPS - 1 else 0.0
                prev = pltpu.roll(jnp.where(lane == LANES - 1, before, tiles[g]), 1, 1)
                nxt = pltpu.roll(jnp.where(lane == 0, after, tiles[g]), LANES - 1, 1)
                h = h_ref[g, r, cells, :]
                wet = h > 0.0
                scale = (TIME_STEP * PRESS * 0.5) * h
                gx = p_ref[g, pl.ds(base + 1, TILE), :] - p_ref[g, pl.ds(base - 1, TILE), :]
                wx = mx[g, at, :]
                wy = my[g, at, :]
                power = wx * wx + wy * wy
                speed = jnp.where(power > 0.0, power * lax.rsqrt(power), 0.0) * (TIME_STEP * STRESS)
                new = [
                    hu_ref[g, r, cells, :] - scale * gx + speed * wx,
                    hv_ref[g, r, cells, :] - scale * (nxt - prev) + speed * wy,
                ]
                for own, edge, shift in ((0, 0, 1), (GROUPS - 1, LANES - 1, 4)):
                    if g == own:
                        new = [
                            jnp.where(
                                lane == edge,
                                a + pltpu.roll(ends, (edge - shift - f) % LANES, 1),
                                a,
                            )
                            for f, a in enumerate(new)
                        ]
                cut = slice(g * LANES, (g + 1) * LANES)
                ox_ref[r, cells, cut] = jnp.where(wet, new[0], 0.0)
                oy_ref[r, cells, cut] = jnp.where(wet, new[1], 0.0)

    @pl.when(step == 0)
    def _():
        ox_ref[0, 0:1, :] += ends_ref[1:2, :]
        oy_ref[0, 0:1, :] += ends_ref[2:3, :]

    @pl.when(step == pl.num_programs(0) - 1)
    def _():
        deep = ox_ref.shape[1]
        ox_ref[BPX - 1, deep - 1:deep, :] += ends_ref[4:5, :]
        oy_ref[BPX - 1, deep - 1:deep, :] += ends_ref[5:6, :]


def finish(lab, landed, weights, p, sides, ends, hu, hv, h):
    deep = 2 * TILE
    steps = PATCH // deep
    cols = BPY * PATCH
    split = (GROUPS, BPX, PATCH, LANES)
    slab = pl.BlockSpec((GROUPS, BPX, deep, LANES), lambda i: (0, 0, i, 0))
    out = pl.BlockSpec((BPX, deep, cols), lambda i: (0, i, 0))
    shape = jax.ShapeDtypeStruct((BPX, PATCH, cols), F32)
    field = pltpu.VMEM((GROUPS, BPX * TILE, LANES), F32)

    def const(x):
        return pl.BlockSpec(x.shape, lambda i: (0,) * x.ndim)

    return pl.pallas_call(
        finish_kernel,
        grid=(steps,),
        out_shape=(shape, shape),
        in_specs=[
            const(lab), const(landed),
            pl.BlockSpec((NW * ABLK, 2 * PART), lambda i: (0, i)),
            const(p), const(sides), const(ends),
            slab, slab, slab,
        ],
        out_specs=(out, out),
        scratch_shapes=[
            pltpu.VMEM((2 * NPATCH, NW * ABLK), BF16),
            pltpu.VMEM((2 * NPATCH, PART), F32),
            pltpu.VMEM((2 * NPATCH, PART), F32),
            field, field, field, field,
        ],
        compiler_params=params(),
        cost_estimate=pl.CostEstimate(
            flops=4 * NPATCH * NW * ABLK * PATCH * PATCH, bytes_accessed=20 << 20, transcendentals=0
        ),
        name="finish",
    )(
        lab, landed, weights, p, sides, ends,
        hu.reshape(split), hv.reshape(split), h.reshape(split),
    )


def body(
    atm_blocks,
    remap_weights,
    ovl_source,
    ovl_block,
    ovl_patch,
    ovl_weight,
    depth_field,
    wet_mask,
    mom_x,
    mom_y,
    blend,
):
    count_x = lax.axis_size("gx")
    count_y = lax.axis_size("gy")
    devices = count_x * count_y
    entries = ovl_source.size
    capacity = 2 * entries // devices
    slots = devices * capacity
    atm = atm_blocks.reshape(atm_blocks.shape[2:]).transpose(1, 0, 2)
    both = ("gx", "gy")
    want, lab = make_requests(
        ovl_source.reshape(1, entries), ovl_block.reshape(1, entries),
        ovl_patch.reshape(1, entries), ovl_weight.reshape(1, entries), devices, capacity,
    )
    asked = lax.all_to_all(
        want.reshape(devices, 1, capacity), both, split_axis=0, concat_axis=0, tiled=True
    )
    lab = lab.reshape(1, slots)
    press, wind = mix(blend.reshape(1), atm)
    top, bottom, left, right = edge_cells(depth_field, wet_mask, mom_x, mom_y)

    def exchange(after, tiles):
        rows = serve(after, asked, tiles)
        parts = rows.reshape(devices, capacity, rows.shape[1])
        got = lax.all_to_all(parts, both, split_axis=0, concat_axis=0, tiled=True)
        return got.reshape(rows.shape)

    press = exchange(top, press)
    fields = (depth_field, wet_mask, mom_x, mom_y)
    bands = depth_field.shape[0] // BAND
    ahead = bands * 5 // 8
    *planes, token = stencil(fields, lab, 0, ahead)
    wind = exchange(token, wind)
    weights = remap_weights.reshape(NW * ABLK, PATCH * PATCH)
    p, *edges = pressure_field(lab, press, weights, (top, bottom, left, right))
    top, bottom, left, right = edges
    halos = (
        send(bottom, "gx", 1), send(top, "gx", -1), send(right, "gy", 1), send(left, "gy", -1),
    )
    newh, hu, hv, h, _ = stencil(fields, top, ahead, bands - ahead, planes)
    newh, sides, ends = border(halos, edges, newh)
    new_x, new_y = finish(lab, wind, weights, p, sides, ends, hu, hv, h)
    return (newh, new_x.reshape(newh.shape), new_y.reshape(newh.shape))


def solution(mesh):
    placed = (
        P("gx", "gy", None, None, None),
        P(),
        P("gx", "gy", None, None),
        P("gx", "gy", None),
        P("gx", "gy", None),
        P("gx", "gy", None),
        P("gx", "gy"),
        P("gx", "gy"),
        P("gx", "gy"),
        P("gx", "gy"),
        P(),
    )
    return jax.shard_map(
        body,
        mesh=mesh,
        in_specs=placed,
        out_specs=(P("gx", "gy"), P("gx", "gy"), P("gx", "gy")),
        check_vma=False,
    )
```

```python
import functools

import jax
import jax.numpy as jnp
from jax import lax
from jax.experimental import pallas as pl
from jax.experimental.pallas import tpu as pltpu
from jax.sharding import PartitionSpec as P

PATCH = 64
ABLK = 256
NW = 4
BPX = 16
BPY = 8
NPATCH = BPX * BPY

GRAV = 1.0
DT_DX = 0.2
TIME_STEP = 0.2
STRESS = 0.5
PRESS = 0.5

F32 = jnp.float32
BF16 = jnp.bfloat16
VMEM = pl.BlockSpec(memory_space=pltpu.VMEM)
SMEM = pl.BlockSpec(memory_space=pltpu.SMEM)
LANES = 128
TILE = 8
GROUPS = BPY * PATCH // LANES
HALVES = BPX // TILE
BAND = 128


def params(limit=56 << 20, **kw):
    return pltpu.CompilerParams(vmem_limit_bytes=limit, **kw)


def iota(shape, dim):
    return lax.broadcasted_iota(jnp.int32, shape, dim)


def rank_kernel(capacity, src_ref, blk_ref, pat_ref, wgt_ref, want_ref, lab_ref):
    devices = want_ref.shape[0]
    src = src_ref[...]
    ent = src.shape[1]
    hits = (iota((devices, ent), 0) == src).astype(F32)
    order = (iota((ent, ent), 0) <= iota((ent, ent), 1)).astype(BF16)
    ranks = jnp.dot(hits.astype(BF16), order, preferred_element_type=F32)
    mine = jnp.sum(hits * ranks, axis=0, keepdims=True).astype(jnp.int32) - 1
    place = iota((capacity, ent), 0) == mine
    pat = pat_ref[...]
    row_bits = BPX.bit_length() - 1
    col_bits = BPY.bit_length() - 1
    rows = jnp.zeros_like(pat)
    cols = jnp.zeros_like(pat)
    used_r = used_c = position = 0
    while used_r < row_bits or used_c < col_bits:
        value = jnp.bitwise_and(jnp.right_shift(pat, position), 1)
        if used_r < row_bits and (used_c >= col_bits or position % 2 == 0):
            rows = rows + value * (1 << used_r)
            used_r += 1
        else:
            cols = cols + value * (1 << used_c)
            used_c += 1
        position += 1

    def spread(row):
        picked = jnp.where(place, row.astype(F32), 0.0).astype(BF16)
        return lax.dot_general(
            hits.astype(BF16), picked, (((1,), (1,)), ((), ())),
            preferred_element_type=F32,
        ).astype(jnp.int32)

    want_ref[...] = spread(blk_ref[...])
    slot = spread(cols * BPX + rows)
    group = spread(wgt_ref[...] + 1)
    lab_ref[...] = jnp.where(group > 0, (group - 1) * NPATCH + slot, -1)


def make_requests(src, blk, pat, wgt, devices, capacity):
    shape = jax.ShapeDtypeStruct((devices, capacity), jnp.int32)
    return pl.pallas_call(
        functools.partial(rank_kernel, capacity),
        out_shape=(shape, shape),
        in_specs=[VMEM] * 4,
        out_specs=(VMEM, VMEM),
        compiler_params=params(),
        name="requests",
    )(src, blk, pat, wgt)


def mix_kernel(blend_ref, atm_ref, press_ref, wind_ref):
    blend = blend_ref[0]
    keep = 1.0 - blend

    def mixed(k):
        first = atm_ref[k].astype(F32)
        second = atm_ref[3 + k].astype(F32)
        return (keep * first + blend * second).astype(BF16)

    press_ref[...] = mixed(2)
    for k in range(2):
        wind_ref[:, k * ABLK:(k + 1) * ABLK] = mixed(k)


def mix(blend, atm):
    blocks = atm.shape[1]
    return pl.pallas_call(
        mix_kernel,
        out_shape=(
            jax.ShapeDtypeStruct((blocks, ABLK), BF16),
            jax.ShapeDtypeStruct((blocks, 2 * ABLK), BF16),
        ),
        in_specs=[SMEM, VMEM],
        out_specs=(VMEM, VMEM),
        compiler_params=params(),
        name="mix",
    )(blend, atm)


def serve_kernel(after_ref, asked_ref, tiles_ref, out_ref, turned, pick):
    peers, _, capacity = asked_ref.shape
    width = turned.shape[0]
    turned[...] = jnp.zeros_like(turned)
    turned[0:peers, 0:capacity] = asked_ref[:, 0, :]
    columns = turned[...].T
    blocks = tiles_ref.shape[0]
    names = iota((capacity, blocks), 1)
    for d in range(peers):
        pick[d * capacity:(d + 1) * capacity, :] = (columns[0:capacity, d:d + 1] == names).astype(F32)
    out_ref[...] = jnp.dot(
        pick[...].astype(BF16), tiles_ref[...], preferred_element_type=F32
    ).astype(BF16)


def serve(after, asked, tiles):
    peers, _, capacity = asked.shape
    slots = peers * capacity
    width = -(-max(peers, capacity) // LANES) * LANES
    return pl.pallas_call(
        serve_kernel,
        out_shape=jax.ShapeDtypeStruct((slots, tiles.shape[1]), BF16),
        in_specs=[pl.BlockSpec(memory_space=pl.ANY), VMEM, VMEM],
        out_specs=VMEM,
        scratch_shapes=[
            pltpu.VMEM((width, width), jnp.int32),
            pltpu.VMEM((slots, tiles.shape[0]), F32),
        ],
        compiler_params=params(56 << 20),
        name="serve",
    )(after, asked, tiles)


def edges_kernel(
    dl, ml, xl, yl, dr, mr, xr, yr, dt, mt, xt, yt, db, mb, xb, yb,
    top_ref, bottom_ref, left_ref, right_ref,
):
    def rows(d, m, x, y, at, out):
        wet = m[...] == 1
        for f, ref in enumerate((d, x, y)):
            out[f:f + 1, :] = jnp.where(wet, ref[...], 0.0)[at:at + 1]

    rows(dt, mt, xt, yt, 0, top_ref)
    rows(db, mb, xb, yb, TILE - 1, bottom_ref)
    lane = iota((LANES, LANES), 1)

    def step(b, carry):
        at = pl.ds(pl.multiple_of(b * LANES, LANES), LANES)
        wl = ml[at, :] == 1
        wr = mr[at, :] == 1
        packed = jnp.where(wl, dl[at, :], 0.0)
        packed = jnp.where(lane == 1, pltpu.roll(jnp.where(wl, xl[at, :], 0.0), 1, 1), packed)
        packed = jnp.where(lane == 2, pltpu.roll(jnp.where(wl, yl[at, :], 0.0), 2, 1), packed)
        packed = jnp.where(lane == 8, pltpu.roll(jnp.where(wr, dr[at, :], 0.0), 9, 1), packed)
        packed = jnp.where(lane == 9, pltpu.roll(jnp.where(wr, xr[at, :], 0.0), 10, 1), packed)
        packed = jnp.where(lane == 10, pltpu.roll(jnp.where(wr, yr[at, :], 0.0), 11, 1), packed)
        turned = packed.T
        left_ref[:, at] = turned[0:TILE]
        right_ref[:, at] = turned[TILE:2 * TILE]
        return carry

    lax.fori_loop(0, dl.shape[0] // LANES, step, 0)


def edge_cells(depth, mask, momx, momy):
    rows, cols = depth.shape
    fields = (depth, mask, momx, momy)
    left = pl.BlockSpec((rows, LANES), lambda i: (0, 0))
    right = pl.BlockSpec((rows, LANES), lambda i: (0, cols // LANES - 1))
    top = pl.BlockSpec((TILE, cols), lambda i: (0, 0))
    bottom = pl.BlockSpec((TILE, cols), lambda i: (rows // TILE - 1, 0))
    line = jax.ShapeDtypeStruct((TILE, cols), F32)
    column = jax.ShapeDtypeStruct((TILE, rows), F32)
    return pl.pallas_call(
        edges_kernel,
        grid=(1,),
        out_shape=(line, line, column, column),
        in_specs=[left] * 4 + [right] * 4 + [top] * 4 + [bottom] * 4,
        out_specs=(
            pl.BlockSpec((TILE, cols), lambda i: (0, 0)),
            pl.BlockSpec((TILE, cols), lambda i: (0, 0)),
            pl.BlockSpec((TILE, rows), lambda i: (0, 0)),
            pl.BlockSpec((TILE, rows), lambda i: (0, 0)),
        ),
        compiler_params=params(),
        name="edges",
    )(*(fields * 4))


def send(value, axis, step):
    count = lax.axis_size(axis)
    if step > 0:
        pairs = [(i, i + 1) for i in range(count - 1)]
    else:
        pairs = [(i + 1, i) for i in range(count - 1)]
    return lax.ppermute(value, axis, pairs)


def derived(h, u, v):
    r = jnp.where(h > 0.0, lax.rsqrt(h), 0.0)
    s = h * r
    q = u * r
    p = v * r
    half = 0.5 * h * h
    return (h, u, v, s, q, p, q * q + half, p * p + half, q * p)


def along_x(c):
    return (c[0], c[1], c[2], c[3], c[4], c[5], c[6], c[8])


def along_y(c):
    return (c[0], c[2], c[1], c[3], c[5], c[4], c[7], c[8])


def flux(a, b):
    hl, nl, tl, sl, ql, pl_, fl, gl = a
    hr, nr, tr, sr, qr, pr, fr, gr = b
    both = jnp.minimum(hl, hr) > 0.0
    half = jnp.where(both, 0.5, 1.0)
    twice = half + half
    level = (hl + hr) * half
    rc = lax.rsqrt(level)
    c = level * rc
    total = sl + sr
    inv = pl.reciprocal(total, approx=True)
    inv = inv * (2.0 - total * inv)
    u = jnp.where(both, (ql + qr) * inv, 0.0)
    v = (pl_ + pr) * inv
    dh = jnp.where(both, hr - hl, 0.0)
    dn = (nr - nl) * twice
    dt = jnp.where(both, tr - tl, 0.0)
    mid = 0.5 * dh
    e = (0.5 * dn - u * mid) * rc
    s1 = u - c
    s3 = u + c
    b1 = jnp.abs(s1) * (mid - e)
    b3 = jnp.abs(s3) * (mid + e)
    b2 = jnp.abs(u) * (dt - v * dh)
    d = b1 + b3
    return (
        jnp.where(both, nl + nr, 0.0) - d,
        (fl + fr) * twice - (b1 * s1 + b3 * s3),
        jnp.where(both, gl + gr, 0.0) - (d * v + b2),
    )


CELL = 9


def stencil_kernel(opening, closing, *refs):
    fields = refs[:4]
    refs = refs[5:]
    above = () if opening else refs[:4]
    if not opening:
        refs = refs[8:]
    newh_ref, hu_ref, hv_ref, h_ref, token_ref = refs[:5]
    cell = refs[5:5 + CELL]
    gx = refs[5 + CELL:]
    step = pl.program_id(0)
    bands = pl.num_programs(0) - 1
    lane = iota((TILE, LANES), 1)

    def masked(d, m, x, y, at, cut):
        wet = m[at, cut] == 1
        return derived(*[jnp.where(wet, ref[at, cut], 0.0) for ref in (d, x, y)])

    def fill_band():
        def fill(t, carry):
            at = pl.ds(pl.multiple_of(t * TILE, TILE), TILE)
            to = pl.ds(pl.multiple_of(step * BAND + t * TILE + TILE, TILE), TILE)
            for g in range(GROUPS):
                cut = slice(g * LANES, (g + 1) * LANES)
                for dst, val in zip(cell, masked(*fields, at, cut)):
                    dst[g, to, :] = val
            return carry

        lax.fori_loop(0, BAND // TILE, fill, 0, unroll=8)

    if closing:
        pl.when(step < bands)(fill_band)
    else:
        fill_band()

    @pl.when(step == 0)
    def _():
        token_ref[...] = jnp.zeros_like(token_ref)
        if closing:
            for dst in cell:
                dst[:, dst.shape[1] - BAND:dst.shape[1] - BAND + TILE, :] = jnp.zeros(
                    (GROUPS, TILE, LANES), F32
                )
        if opening:
            for dst in gx:
                dst[:, 0:TILE, :] = jnp.zeros((GROUPS, TILE, LANES), F32)
        else:
            for g in range(GROUPS):
                cut = slice(g * LANES, (g + 1) * LANES)
                for dst, val in zip(cell, masked(*above, slice(None), cut)):
                    dst[g, 0:TILE, :] = val
                now = along_x([ref[g, 0:TILE, :] for ref in cell])
                nxt = along_x([ref[g, 1:TILE + 1, :] for ref in cell])
                for dst, val in zip(gx, flux(now, nxt)):
                    dst[g, 0:TILE, :] = val

    @pl.when(step > 0)
    def _():
        start = pl.multiple_of((step - 1) * BAND, BAND)

        def across(t, carry):
            base = pl.multiple_of(start + t * TILE + TILE, TILE)
            for g in range(GROUPS):
                now = along_x([ref[g, pl.ds(base, TILE), :] for ref in cell])
                nxt = along_x([ref[g, pl.ds(base + 1, TILE), :] for ref in cell])
                for dst, val in zip(gx, flux(now, nxt)):
                    dst[g, pl.ds(base, TILE), :] = val
            return carry

        lax.fori_loop(0, BAND // TILE, across, 0, unroll=16)

        if closing:
            @pl.when(step == bands)
            def _():
                for dst in gx:
                    at = dst.shape[1] - BAND - 1
                    dst[:, at:at + 1, :] = jnp.zeros((GROUPS, 1, LANES), F32)

        def body(t, carry):
            mark = pl.multiple_of(start + t * TILE, TILE)
            base = pl.multiple_of(mark + TILE, TILE)
            at = pl.ds(pl.multiple_of(t * TILE, TILE), TILE)
            before = [jnp.zeros((TILE, LANES), F32)] * 3
            for g in range(GROUPS):
                now = [ref[g, pl.ds(base, TILE), :] for ref in cell]
                if g < GROUPS - 1:
                    other = [ref[g + 1, pl.ds(base, TILE), :] for ref in cell[:3]]
                else:
                    other = now[:3]
                right = [
                    pltpu.roll(jnp.where(lane == 0, o, c), LANES - 1, 1)
                    for o, c in zip(other, now[:3])
                ]
                fy = flux(along_y(now), along_y(derived(*right)))
                if g == GROUPS - 1:
                    fy = [jnp.where(lane == LANES - 1, 0.0, val) for val in fy]
                py = [
                    pltpu.roll(jnp.where(lane == LANES - 1, o, c), 1, 1)
                    for o, c in zip(before, fy)
                ]
                before = fy
                fx = [src[g, pl.ds(base, TILE), :] for src in gx]
                px = [src[g, pl.ds(base - 1, TILE), :] for src in gx]
                h, u, v = now[:3]
                ch = (fx[0] - px[0]) + (fy[0] - py[0])
                cx = (fx[1] - px[1]) + (fy[2] - py[2])
                cy = (fx[2] - px[2]) + (fy[1] - py[1])
                newh_ref[at, g * LANES:(g + 1) * LANES] = jnp.where(
                    h > 0.0, h - (0.5 * DT_DX) * ch, 0.0
                )
                hu_ref[g, at, :] = u - (0.5 * DT_DX) * cx
                hv_ref[g, at, :] = v - (0.5 * DT_DX) * cy
                h_ref[g, at, :] = h
            return carry

        lax.fori_loop(0, BAND // TILE, body, 0, unroll=16)


def stencil(fields, after, first, count, old=()):
    rows, cols = fields[0].shape
    bands = rows // BAND
    opening = first == 0
    closing = first + count == bands
    plane = jax.ShapeDtypeStruct((GROUPS, rows, LANES), F32)
    scratch = pltpu.VMEM((GROUPS, (count + 1) * BAND + TILE, LANES), F32)
    band = pl.BlockSpec((BAND, cols), lambda i: (jnp.minimum(first + i, bands - 1), 0))
    above = pl.BlockSpec((TILE, cols), lambda i: (first * BAND // TILE - 1, 0))
    whole = pl.BlockSpec(memory_space=pl.ANY)
    part = pl.BlockSpec((GROUPS, BAND, LANES), lambda i: (0, first + jnp.maximum(i - 1, 0), 0))
    return pl.pallas_call(
        functools.partial(stencil_kernel, opening, closing),
        grid=(count + 1,),
        out_shape=(
            jax.ShapeDtypeStruct((rows, cols), F32), plane, plane, plane,
            jax.ShapeDtypeStruct((TILE, LANES), F32),
        ),
        in_specs=[band] * 4 + [whole] + ([] if opening else [above] * 4 + [whole] * 4),
        out_specs=(
            pl.BlockSpec((BAND, cols), lambda i: (first + jnp.maximum(i - 1, 0), 0)),
            part, part, part,
            pl.BlockSpec((TILE, LANES), lambda i: (0, 0)),
        ),
        scratch_shapes=[scratch] * (CELL + 3),
        input_output_aliases={} if opening else {9 + n: n for n in range(4)},
        compiler_params=params(),
        cost_estimate=pl.CostEstimate(
            flops=200 * count * BAND * cols, bytes_accessed=64 * count * BAND * cols,
            transcendentals=0,
        ),
        name="stencil",
    )(*fields, after, *(() if opening else fields), *old)


def summed_of(lab, landed):
    select = (iota((NW * NPATCH, lab.shape[1]), 0) == lab).astype(BF16)
    return jnp.dot(select, landed, preferred_element_type=F32).astype(BF16)


def stack_left(left, summed, channels):
    for k in range(channels):
        for w in range(NW):
            left[k * NPATCH:(k + 1) * NPATCH, w * ABLK:(w + 1) * ABLK] = summed[
                w * NPATCH:(w + 1) * NPATCH, k * ABLK:(k + 1) * ABLK
            ]


PART = TILE * PATCH


def weight_parts(step, w_ref, held, arrived):
    width = held.shape[2]

    def copy(n):
        at = pl.ds(pl.multiple_of(n * width, width), width)
        return pltpu.make_async_copy(w_ref.at[:, at], held.at[n], arrived.at[n])

    @pl.when(step == 0)
    def _():
        for n in range(held.shape[0]):
            copy(n).start()

    return copy(step).wait


def spread_rows(acc, field, k):
    low = iota((TILE, LANES), 1) < LANES // 2
    for t in range(TILE // 2):
        cut = slice(t * LANES, (t + 1) * LANES)
        for half in range(HALVES):
            for g in range(GROUPS):
                base = k * NPATCH + 2 * g * BPX + half * TILE
                even = acc[base:base + TILE, cut]
                odd = acc[base + BPX:base + BPX + TILE, cut]
                for i, val in (
                    (2 * t, jnp.where(low, even, pltpu.roll(odd, LANES // 2, 1))),
                    (2 * t + 1, jnp.where(low, pltpu.roll(even, LANES // 2, 1), odd)),
                ):
                    field[g, pl.ds(half * TILE * TILE + i, TILE, stride=TILE), :] = val


def press_kernel(
    lab_ref, landed_ref, w_ref, top0_ref, bottom0_ref, left0_ref, right0_ref,
    out_ref, top_ref, bottom_ref, left_ref, right_ref, row_ref,
    held, arrived, left, acc, acc2, field, field2,
):
    step = pl.program_id(0)
    take = weight_parts(step, w_ref, held, arrived)

    @pl.when(step == 0)
    def _():
        peers, capacity = lab_ref.shape
        for d in range(peers):
            row_ref[:, d * capacity:(d + 1) * capacity] = lab_ref[d:d + 1, :]
        stack_left(left, summed_of(row_ref[...], landed_ref[...]), 1)

    take()
    acc[...] = jnp.dot(left[...], held[step, :, :PART], preferred_element_type=F32)
    acc2[...] = jnp.dot(left[...], held[step, :, PART:], preferred_element_type=F32)
    for part, (src, mid) in enumerate(((acc, field), (acc2, field2))):
        spread_rows(src, mid, 0)
        for g in range(GROUPS):
            for r in range(BPX):
                to = pl.ds(pl.multiple_of(TILE + r * PATCH + (2 * step + part) * TILE, TILE), TILE)
                out_ref[g, to, :] = mid[g, r * TILE:(r + 1) * TILE, :]

    @pl.when(step == pl.num_programs(0) - 1)
    def _():
        rows = out_ref.shape[1] - 2 * TILE
        mine = iota((TILE, LANES), 0) == 3
        blank = jnp.zeros((TILE, LANES), F32)
        for g in range(GROUPS):
            cut = slice(g * LANES, (g + 1) * LANES)
            head = pltpu.roll(out_ref[g, TILE:2 * TILE, :], 3, 0)
            tail = pltpu.roll(out_ref[g, rows:rows + TILE, :], 4, 0)
            out_ref[g, 0:TILE, :] = blank
            out_ref[g, rows + TILE:, :] = blank
            top_ref[:, cut] = jnp.where(mine, head, top0_ref[:, cut])
            bottom_ref[:, cut] = jnp.where(mine, tail, bottom0_ref[:, cut])
        lane = iota((LANES, LANES), 1)
        for b in range(rows // LANES):
            at = slice(b * LANES, (b + 1) * LANES)
            inner = slice(TILE + b * LANES, TILE + (b + 1) * LANES)
            packed = jnp.where(
                lane == TILE + 3,
                pltpu.roll(out_ref[GROUPS - 1, inner, :], TILE + 4, 1),
                pltpu.roll(out_ref[0, inner, :], 3, 1),
            )
            turned = packed.T
            left_ref[:, at] = jnp.where(mine, turned[0:TILE], left0_ref[:, at])
            right_ref[:, at] = jnp.where(mine, turned[TILE:2 * TILE], right0_ref[:, at])


def pressure_field(lab, landed, weights, edges):
    steps = PATCH // (2 * TILE)
    rows = BPX * PATCH
    line = (TILE, BPY * PATCH)
    column = (TILE, rows)
    whole = (GROUPS, rows + 2 * TILE, LANES)

    def const(shape):
        return pl.BlockSpec(shape, lambda i: (0,) * len(shape))

    return pl.pallas_call(
        press_kernel,
        grid=(steps,),
        out_shape=tuple(jax.ShapeDtypeStruct(x, F32) for x in (whole, line, line, column, column))
        + (jax.ShapeDtypeStruct((1, lab.size), jnp.int32),),
        in_specs=[
            const(lab.shape),
            const(landed.shape),
            pl.BlockSpec(memory_space=pl.ANY),
        ] + [const(x) for x in (line, line, column, column)],
        out_specs=tuple(const(x) for x in (whole, line, line, column, column, (1, lab.size))),
        scratch_shapes=[
            pltpu.VMEM((steps, NW * ABLK, 2 * PART), BF16),
            pltpu.SemaphoreType.DMA((steps,)),
            pltpu.VMEM((NPATCH, NW * ABLK), BF16),
            pltpu.VMEM((NPATCH, PART), F32),
            pltpu.VMEM((NPATCH, PART), F32),
            pltpu.VMEM((GROUPS, BPX * TILE, LANES), F32),
            pltpu.VMEM((GROUPS, BPX * TILE, LANES), F32),
        ],
        compiler_params=params(),
        cost_estimate=pl.CostEstimate(
            flops=2 * NPATCH * NW * ABLK * PATCH * PATCH, bytes_accessed=12 << 20, transcendentals=0
        ),
        name="pressure",
    )(lab, landed, weights, *edges)


def border_kernel(
    up_ref, dn_ref, lh_ref, rh_ref, top_ref, bottom_ref, left_ref, right_ref, old_ref,
    new_ref, sides_ref, ends_ref, edge, first, last, head, tail, load, save,
):
    rows, cols = old_ref.shape
    middle = pl.ds(LANES, cols - 2 * LANES)
    places = (
        (slice(None), pl.ds(0, LANES)),
        (slice(None), pl.ds(cols - LANES, LANES)),
        (pl.ds(0, TILE), middle),
        (pl.ds(rows - TILE, TILE), middle),
    )
    parts = (first, last, head, tail)
    loads = [
        pltpu.make_async_copy(old_ref.at[at], part, load.at[n])
        for n, (at, part) in enumerate(zip(places, parts))
    ]
    for copy in loads:
        copy.start()

    def cells(ref):
        return derived(ref[0:1, :], ref[1:2, :], ref[2:3, :])

    pull = TIME_STEP * PRESS * 0.5
    edge[...] = jnp.zeros_like(edge)
    for at, before, after, own, far, sign in (
        (0, lh_ref, left_ref, left_ref, lh_ref, 1.0),
        (3, right_ref, rh_ref, right_ref, rh_ref, -1.0),
    ):
        gh, gn, gt = flux(along_y(cells(before)), along_y(cells(after)))
        wet = own[0:1, :] > 0.0
        press = (pull * own[0:1, :]) * far[3:4, :]
        for f, val in enumerate((gh * (0.5 * DT_DX), gt * (0.5 * DT_DX), gn * (0.5 * DT_DX) + press)):
            edge[at + f:at + f + 1, :] = jnp.where(wet, sign * val, 0.0)
    blank = jnp.zeros((LANES - TILE, LANES), F32)
    for b in range(rows // LANES):
        cut = slice(b * LANES, (b + 1) * LANES)
        sides_ref[cut, :] = jnp.concatenate([edge[:, cut], blank], axis=0).T
    ends_ref[...] = jnp.zeros_like(ends_ref)
    for at, before, after, own, far, sign in (
        (0, up_ref, top_ref, top_ref, up_ref, 1.0),
        (3, bottom_ref, dn_ref, bottom_ref, dn_ref, -1.0),
    ):
        gh, gn, gt = flux(along_x(cells(before)), along_x(cells(after)))
        wet = own[0:1, :] > 0.0
        press = (pull * own[0:1, :]) * far[3:4, :]
        for f, val in enumerate((gh * (0.5 * DT_DX), gn * (0.5 * DT_DX) + press, gt * (0.5 * DT_DX))):
            ends_ref[at + f:at + f + 1, :] = jnp.where(wet, sign * val, 0.0)

    for copy in loads:
        copy.wait()
    lane = iota((rows, LANES), 1)
    sides = sides_ref[...]
    first[...] += jnp.where(lane == 0, sides, 0.0)
    last[...] += jnp.where(lane == LANES - 1, pltpu.roll(sides, LANES - 4, 1), 0.0)
    for at, line in ((0, 0), (rows - 1, 3)):
        first[at:at + 1, :] += ends_ref[line:line + 1, 0:LANES]
        last[at:at + 1, :] += ends_ref[line:line + 1, cols - LANES:cols]
    head[0:1, :] += ends_ref[0:1, LANES:cols - LANES]
    tail[TILE - 1:TILE, :] += ends_ref[3:4, LANES:cols - LANES]
    saves = [
        pltpu.make_async_copy(part, new_ref.at[at], save.at[n])
        for n, (at, part) in enumerate(zip(places, parts))
    ]
    for copy in saves:
        copy.start()
    for copy in saves:
        copy.wait()


def border(halos, edges, newh):
    rows, cols = newh.shape
    whole = pl.BlockSpec(memory_space=pl.ANY)
    return pl.pallas_call(
        border_kernel,
        out_shape=(
            jax.ShapeDtypeStruct((rows, cols), F32),
            jax.ShapeDtypeStruct((rows, LANES), F32),
            jax.ShapeDtypeStruct((TILE, cols), F32),
        ),
        in_specs=[VMEM] * 8 + [whole],
        out_specs=(whole, VMEM, VMEM),
        input_output_aliases={8: 0},
        scratch_shapes=[
            pltpu.VMEM((TILE, rows), F32),
            pltpu.VMEM((rows, LANES), F32),
            pltpu.VMEM((rows, LANES), F32),
            pltpu.VMEM((TILE, cols - 2 * LANES), F32),
            pltpu.VMEM((TILE, cols - 2 * LANES), F32),
            pltpu.SemaphoreType.DMA((4,)),
            pltpu.SemaphoreType.DMA((4,)),
        ],
        compiler_params=params(),
        name="border",
    )(*halos, *edges, newh)


def finish_kernel(
    lab_ref, landed_ref, w_ref, p_ref, sides_ref, ends_ref,
    hu_ref, hv_ref, h_ref, ox_ref, oy_ref,
    held, arrived, left, acc, acc2, fx, fy, fx2, fy2,
):
    step = pl.program_id(0)

    take = weight_parts(step, w_ref, held, arrived)

    @pl.when(step == 0)
    def _():
        stack_left(left, summed_of(lab_ref[...], landed_ref[...]), 2)

    take()
    acc[...] = jnp.dot(left[...], held[step, :, :PART], preferred_element_type=F32)
    acc2[...] = jnp.dot(left[...], held[step, :, PART:], preferred_element_type=F32)
    lane = iota((TILE, LANES), 1)
    for part, (src, mx, my) in enumerate(((acc, fx, fy), (acc2, fx2, fy2))):
        spread_rows(src, mx, 0)
        spread_rows(src, my, 1)
        cells = slice(part * TILE, (part + 1) * TILE)
        for r in range(BPX):
            at = slice(r * TILE, (r + 1) * TILE)
            mark = pl.multiple_of(r * PATCH + (2 * step + part) * TILE, TILE)
            base = pl.multiple_of(mark + TILE, TILE)
            ends = sides_ref[pl.ds(mark, TILE), :]
            tiles = [p_ref[g, pl.ds(base, TILE), :] for g in range(GROUPS)]
            for g in range(GROUPS):
                before = tiles[g - 1] if g else 0.0
                after = tiles[g + 1] if g < GROUPS - 1 else 0.0
                prev = pltpu.roll(jnp.where(lane == LANES - 1, before, tiles[g]), 1, 1)
                nxt = pltpu.roll(jnp.where(lane == 0, after, tiles[g]), LANES - 1, 1)
                h = h_ref[g, r, cells, :]
                wet = h > 0.0
                scale = (TIME_STEP * PRESS * 0.5) * h
                gx = p_ref[g, pl.ds(base + 1, TILE), :] - p_ref[g, pl.ds(base - 1, TILE), :]
                wx = mx[g, at, :]
                wy = my[g, at, :]
                power = wx * wx + wy * wy
                speed = jnp.where(power > 0.0, power * lax.rsqrt(power), 0.0) * (TIME_STEP * STRESS)
                new = [
                    hu_ref[g, r, cells, :] - scale * gx + speed * wx,
                    hv_ref[g, r, cells, :] - scale * (nxt - prev) + speed * wy,
                ]
                for own, edge, shift in ((0, 0, 1), (GROUPS - 1, LANES - 1, 4)):
                    if g == own:
                        new = [
                            jnp.where(
                                lane == edge,
                                a + pltpu.roll(ends, (edge - shift - f) % LANES, 1),
                                a,
                            )
                            for f, a in enumerate(new)
                        ]
                cut = slice(g * LANES, (g + 1) * LANES)
                ox_ref[r, cells, cut] = jnp.where(wet, new[0], 0.0)
                oy_ref[r, cells, cut] = jnp.where(wet, new[1], 0.0)

    @pl.when(step == 0)
    def _():
        ox_ref[0, 0:1, :] += ends_ref[1:2, :]
        oy_ref[0, 0:1, :] += ends_ref[2:3, :]

    @pl.when(step == pl.num_programs(0) - 1)
    def _():
        deep = ox_ref.shape[1]
        ox_ref[BPX - 1, deep - 1:deep, :] += ends_ref[4:5, :]
        oy_ref[BPX - 1, deep - 1:deep, :] += ends_ref[5:6, :]


def finish(lab, landed, weights, p, sides, ends, hu, hv, h):
    deep = 2 * TILE
    steps = PATCH // deep
    cols = BPY * PATCH
    split = (GROUPS, BPX, PATCH, LANES)
    slab = pl.BlockSpec((GROUPS, BPX, deep, LANES), lambda i: (0, 0, i, 0))
    out = pl.BlockSpec((BPX, deep, cols), lambda i: (0, i, 0))
    shape = jax.ShapeDtypeStruct((BPX, PATCH, cols), F32)
    field = pltpu.VMEM((GROUPS, BPX * TILE, LANES), F32)

    def const(x):
        return pl.BlockSpec(x.shape, lambda i: (0,) * x.ndim)

    return pl.pallas_call(
        finish_kernel,
        grid=(steps,),
        out_shape=(shape, shape),
        in_specs=[
            const(lab), const(landed),
            pl.BlockSpec(memory_space=pl.ANY),
            const(p), const(sides), const(ends),
            slab, slab, slab,
        ],
        out_specs=(out, out),
        scratch_shapes=[
            pltpu.VMEM((steps, NW * ABLK, 2 * PART), BF16),
            pltpu.SemaphoreType.DMA((steps,)),
            pltpu.VMEM((2 * NPATCH, NW * ABLK), BF16),
            pltpu.VMEM((2 * NPATCH, PART), F32),
            pltpu.VMEM((2 * NPATCH, PART), F32),
            field, field, field, field,
        ],
        compiler_params=params(),
        cost_estimate=pl.CostEstimate(
            flops=4 * NPATCH * NW * ABLK * PATCH * PATCH, bytes_accessed=20 << 20, transcendentals=0
        ),
        name="finish",
    )(
        lab, landed, weights, p, sides, ends,
        hu.reshape(split), hv.reshape(split), h.reshape(split),
    )


def body(
    atm_blocks,
    remap_weights,
    ovl_source,
    ovl_block,
    ovl_patch,
    ovl_weight,
    depth_field,
    wet_mask,
    mom_x,
    mom_y,
    blend,
):
    count_x = lax.axis_size("gx")
    count_y = lax.axis_size("gy")
    devices = count_x * count_y
    entries = ovl_source.size
    capacity = 2 * entries // devices
    slots = devices * capacity
    atm = atm_blocks.reshape(atm_blocks.shape[2:]).transpose(1, 0, 2)
    both = ("gx", "gy")
    want, lab = make_requests(
        ovl_source.reshape(1, entries), ovl_block.reshape(1, entries),
        ovl_patch.reshape(1, entries), ovl_weight.reshape(1, entries), devices, capacity,
    )
    asked = lax.all_to_all(
        want.reshape(devices, 1, capacity), both, split_axis=0, concat_axis=0, tiled=True
    )
    press, wind = mix(blend.reshape(1), atm)
    top, bottom, left, right = edge_cells(depth_field, wet_mask, mom_x, mom_y)

    def exchange(after, tiles):
        rows = serve(after, asked, tiles)
        parts = rows.reshape(devices, capacity, rows.shape[1])
        got = lax.all_to_all(parts, both, split_axis=0, concat_axis=0, tiled=True)
        return got.reshape(rows.shape)

    press = exchange(top, press)
    fields = (depth_field, wet_mask, mom_x, mom_y)
    bands = depth_field.shape[0] // BAND
    ahead = bands * 5 // 8
    *planes, token = stencil(fields, lab, 0, ahead)
    wind = exchange(token, wind)
    weights = remap_weights.reshape(NW * ABLK, PATCH * PATCH)
    p, *edges, lab = pressure_field(lab, press, weights, (top, bottom, left, right))
    top, bottom, left, right = edges
    halos = (
        send(bottom, "gx", 1), send(top, "gx", -1), send(right, "gy", 1), send(left, "gy", -1),
    )
    newh, hu, hv, h, _ = stencil(fields, top, ahead, bands - ahead, planes)
    newh, sides, ends = border(halos, edges, newh)
    new_x, new_y = finish(lab, wind, weights, p, sides, ends, hu, hv, h)
    return (newh, new_x.reshape(newh.shape), new_y.reshape(newh.shape))


def solution(mesh):
    placed = (
        P("gx", "gy", None, None, None),
        P(),
        P("gx", "gy", None, None),
        P("gx", "gy", None),
        P("gx", "gy", None),
        P("gx", "gy", None),
        P("gx", "gy"),
        P("gx", "gy"),
        P("gx", "gy"),
        P("gx", "gy"),
        P(),
    )
    return jax.shard_map(
        body,
        mesh=mesh,
        in_specs=placed,
        out_specs=(P("gx", "gy"), P("gx", "gy"), P("gx", "gy")),
        check_vma=False,
    )
```

```python
import functools

import jax
import jax.numpy as jnp
from jax import lax
from jax.experimental import pallas as pl
from jax.experimental.pallas import tpu as pltpu
from jax.sharding import PartitionSpec as P

PATCH = 64
ABLK = 256
NW = 4
BPX = 16
BPY = 8
NPATCH = BPX * BPY

GRAV = 1.0
DT_DX = 0.2
TIME_STEP = 0.2
STRESS = 0.5
PRESS = 0.5

F32 = jnp.float32
BF16 = jnp.bfloat16
VMEM = pl.BlockSpec(memory_space=pltpu.VMEM)
SMEM = pl.BlockSpec(memory_space=pltpu.SMEM)
LANES = 128
TILE = 8
GROUPS = BPY * PATCH // LANES
HALVES = BPX // TILE
BAND = 128


def params(limit=56 << 20, **kw):
    return pltpu.CompilerParams(vmem_limit_bytes=limit, **kw)


def iota(shape, dim):
    return lax.broadcasted_iota(jnp.int32, shape, dim)


def rank_kernel(capacity, src_ref, blk_ref, pat_ref, wgt_ref, want_ref, lab_ref):
    devices = want_ref.shape[0]
    src = src_ref[...]
    ent = src.shape[1]
    hits = (iota((devices, ent), 0) == src).astype(F32)
    order = (iota((ent, ent), 0) <= iota((ent, ent), 1)).astype(BF16)
    ranks = jnp.dot(hits.astype(BF16), order, preferred_element_type=F32)
    mine = jnp.sum(hits * ranks, axis=0, keepdims=True).astype(jnp.int32) - 1
    place = iota((capacity, ent), 0) == mine
    pat = pat_ref[...]
    row_bits = BPX.bit_length() - 1
    col_bits = BPY.bit_length() - 1
    rows = jnp.zeros_like(pat)
    cols = jnp.zeros_like(pat)
    used_r = used_c = position = 0
    while used_r < row_bits or used_c < col_bits:
        value = jnp.bitwise_and(jnp.right_shift(pat, position), 1)
        if used_r < row_bits and (used_c >= col_bits or position % 2 == 0):
            rows = rows + value * (1 << used_r)
            used_r += 1
        else:
            cols = cols + value * (1 << used_c)
            used_c += 1
        position += 1

    def spread(row):
        picked = jnp.where(place, row.astype(F32), 0.0).astype(BF16)
        return lax.dot_general(
            hits.astype(BF16), picked, (((1,), (1,)), ((), ())),
            preferred_element_type=F32,
        ).astype(jnp.int32)

    want_ref[...] = spread(blk_ref[...])
    slot = spread(cols * BPX + rows)
    group = spread(wgt_ref[...] + 1)
    lab_ref[...] = jnp.where(group > 0, (group - 1) * NPATCH + slot, -1)


def make_requests(src, blk, pat, wgt, devices, capacity):
    shape = jax.ShapeDtypeStruct((devices, capacity), jnp.int32)
    return pl.pallas_call(
        functools.partial(rank_kernel, capacity),
        out_shape=(shape, shape),
        in_specs=[VMEM] * 4,
        out_specs=(VMEM, VMEM),
        compiler_params=params(),
        name="requests",
    )(src, blk, pat, wgt)


def mix_kernel(blend_ref, atm_ref, press_ref, wind_ref):
    blend = blend_ref[0]
    keep = 1.0 - blend

    def mixed(k):
        first = atm_ref[k].astype(F32)
        second = atm_ref[3 + k].astype(F32)
        return (keep * first + blend * second).astype(BF16)

    press_ref[...] = mixed(2)
    for k in range(2):
        wind_ref[:, k * ABLK:(k + 1) * ABLK] = mixed(k)


def mix(blend, atm):
    blocks = atm.shape[1]
    return pl.pallas_call(
        mix_kernel,
        out_shape=(
            jax.ShapeDtypeStruct((blocks, ABLK), BF16),
            jax.ShapeDtypeStruct((blocks, 2 * ABLK), BF16),
        ),
        in_specs=[SMEM, VMEM],
        out_specs=(VMEM, VMEM),
        compiler_params=params(),
        name="mix",
    )(blend, atm)


def serve_kernel(after_ref, asked_ref, tiles_ref, out_ref, turned, pick):
    peers, _, capacity = asked_ref.shape
    width = turned.shape[0]
    turned[...] = jnp.zeros_like(turned)
    turned[0:peers, 0:capacity] = asked_ref[:, 0, :]
    columns = turned[...].T
    blocks = tiles_ref.shape[0]
    names = iota((capacity, blocks), 1)
    for d in range(peers):
        pick[d * capacity:(d + 1) * capacity, :] = (columns[0:capacity, d:d + 1] == names).astype(F32)
    out_ref[...] = jnp.dot(
        pick[...].astype(BF16), tiles_ref[...], preferred_element_type=F32
    ).astype(BF16)


def serve(after, asked, tiles):
    peers, _, capacity = asked.shape
    slots = peers * capacity
    width = -(-max(peers, capacity) // LANES) * LANES
    return pl.pallas_call(
        serve_kernel,
        out_shape=jax.ShapeDtypeStruct((slots, tiles.shape[1]), BF16),
        in_specs=[pl.BlockSpec(memory_space=pl.ANY), VMEM, VMEM],
        out_specs=VMEM,
        scratch_shapes=[
            pltpu.VMEM((width, width), jnp.int32),
            pltpu.VMEM((slots, tiles.shape[0]), F32),
        ],
        compiler_params=params(32 << 20),
        name="serve",
    )(after, asked, tiles)


def edges_kernel(
    dl, ml, xl, yl, dr, mr, xr, yr, dt, mt, xt, yt, db, mb, xb, yb,
    top_ref, bottom_ref, left_ref, right_ref,
):
    def rows(d, m, x, y, at, out):
        wet = m[...] == 1
        for f, ref in enumerate((d, x, y)):
            out[f:f + 1, :] = jnp.where(wet, ref[...], 0.0)[at:at + 1]

    rows(dt, mt, xt, yt, 0, top_ref)
    rows(db, mb, xb, yb, TILE - 1, bottom_ref)
    lane = iota((LANES, LANES), 1)

    def step(b, carry):
        at = pl.ds(pl.multiple_of(b * LANES, LANES), LANES)
        wl = ml[at, :] == 1
        wr = mr[at, :] == 1
        packed = jnp.where(wl, dl[at, :], 0.0)
        packed = jnp.where(lane == 1, pltpu.roll(jnp.where(wl, xl[at, :], 0.0), 1, 1), packed)
        packed = jnp.where(lane == 2, pltpu.roll(jnp.where(wl, yl[at, :], 0.0), 2, 1), packed)
        packed = jnp.where(lane == 8, pltpu.roll(jnp.where(wr, dr[at, :], 0.0), 9, 1), packed)
        packed = jnp.where(lane == 9, pltpu.roll(jnp.where(wr, xr[at, :], 0.0), 10, 1), packed)
        packed = jnp.where(lane == 10, pltpu.roll(jnp.where(wr, yr[at, :], 0.0), 11, 1), packed)
        turned = packed.T
        left_ref[:, at] = turned[0:TILE]
        right_ref[:, at] = turned[TILE:2 * TILE]
        return carry

    lax.fori_loop(0, dl.shape[0] // LANES, step, 0)


def edge_cells(depth, mask, momx, momy):
    rows, cols = depth.shape
    fields = (depth, mask, momx, momy)
    left = pl.BlockSpec((rows, LANES), lambda i: (0, 0))
    right = pl.BlockSpec((rows, LANES), lambda i: (0, cols // LANES - 1))
    top = pl.BlockSpec((TILE, cols), lambda i: (0, 0))
    bottom = pl.BlockSpec((TILE, cols), lambda i: (rows // TILE - 1, 0))
    line = jax.ShapeDtypeStruct((TILE, cols), F32)
    column = jax.ShapeDtypeStruct((TILE, rows), F32)
    return pl.pallas_call(
        edges_kernel,
        grid=(1,),
        out_shape=(line, line, column, column),
        in_specs=[left] * 4 + [right] * 4 + [top] * 4 + [bottom] * 4,
        out_specs=(
            pl.BlockSpec((TILE, cols), lambda i: (0, 0)),
            pl.BlockSpec((TILE, cols), lambda i: (0, 0)),
            pl.BlockSpec((TILE, rows), lambda i: (0, 0)),
            pl.BlockSpec((TILE, rows), lambda i: (0, 0)),
        ),
        compiler_params=params(),
        name="edges",
    )(*(fields * 4))


def send(value, axis, step):
    count = lax.axis_size(axis)
    if step > 0:
        pairs = [(i, i + 1) for i in range(count - 1)]
    else:
        pairs = [(i + 1, i) for i in range(count - 1)]
    return lax.ppermute(value, axis, pairs)


def derived(h, u, v):
    r = jnp.where(h > 0.0, lax.rsqrt(h), 0.0)
    s = h * r
    q = u * r
    p = v * r
    half = 0.5 * h * h
    return (h, u, v, s, q, p, q * q + half, p * p + half, q * p)


def along_x(c):
    return (c[0], c[1], c[2], c[3], c[4], c[5], c[6], c[8])


def along_y(c):
    return (c[0], c[2], c[1], c[3], c[5], c[4], c[7], c[8])


def flux(a, b):
    hl, nl, tl, sl, ql, pl_, fl, gl = a
    hr, nr, tr, sr, qr, pr, fr, gr = b
    both = jnp.minimum(hl, hr) > 0.0
    half = jnp.where(both, 0.5, 1.0)
    twice = half + half
    level = (hl + hr) * half
    rc = lax.rsqrt(level)
    c = level * rc
    total = sl + sr
    inv = pl.reciprocal(total, approx=True)
    inv = inv * (2.0 - total * inv)
    u = jnp.where(both, (ql + qr) * inv, 0.0)
    v = (pl_ + pr) * inv
    dh = jnp.where(both, hr - hl, 0.0)
    dn = (nr - nl) * twice
    dt = jnp.where(both, tr - tl, 0.0)
    mid = 0.5 * dh
    e = (0.5 * dn - u * mid) * rc
    s1 = u - c
    s3 = u + c
    b1 = jnp.abs(s1) * (mid - e)
    b3 = jnp.abs(s3) * (mid + e)
    b2 = jnp.abs(u) * (dt - v * dh)
    d = b1 + b3
    return (
        jnp.where(both, nl + nr, 0.0) - d,
        (fl + fr) * twice - (b1 * s1 + b3 * s3),
        jnp.where(both, gl + gr, 0.0) - (d * v + b2),
    )


CELL = 9


def stencil_kernel(opening, closing, *refs):
    fields = refs[:4]
    refs = refs[5:]
    above = () if opening else refs[:4]
    if not opening:
        refs = refs[8:]
    newh_ref, hu_ref, hv_ref, h_ref, token_ref = refs[:5]
    cell = refs[5:5 + CELL]
    gx = refs[5 + CELL:]
    step = pl.program_id(0)
    bands = pl.num_programs(0) - 1
    lane = iota((TILE, LANES), 1)

    def masked(d, m, x, y, at, cut):
        wet = m[at, cut] == 1
        return derived(*[jnp.where(wet, ref[at, cut], 0.0) for ref in (d, x, y)])

    def fill_band():
        def fill(t, carry):
            at = pl.ds(pl.multiple_of(t * TILE, TILE), TILE)
            to = pl.ds(pl.multiple_of(step * BAND + t * TILE + TILE, TILE), TILE)
            for g in range(GROUPS):
                cut = slice(g * LANES, (g + 1) * LANES)
                for dst, val in zip(cell, masked(*fields, at, cut)):
                    dst[g, to, :] = val
            return carry

        lax.fori_loop(0, BAND // TILE, fill, 0, unroll=8)

    if closing:
        pl.when(step < bands)(fill_band)
    else:
        fill_band()

    @pl.when(step == 0)
    def _():
        token_ref[...] = jnp.zeros_like(token_ref)
        if closing:
            for dst in cell:
                dst[:, dst.shape[1] - BAND:dst.shape[1] - BAND + TILE, :] = jnp.zeros(
                    (GROUPS, TILE, LANES), F32
                )
        if opening:
            for dst in gx:
                dst[:, 0:TILE, :] = jnp.zeros((GROUPS, TILE, LANES), F32)
        else:
            for g in range(GROUPS):
                cut = slice(g * LANES, (g + 1) * LANES)
                for dst, val in zip(cell, masked(*above, slice(None), cut)):
                    dst[g, 0:TILE, :] = val
                now = along_x([ref[g, 0:TILE, :] for ref in cell])
                nxt = along_x([ref[g, 1:TILE + 1, :] for ref in cell])
                for dst, val in zip(gx, flux(now, nxt)):
                    dst[g, 0:TILE, :] = val

    @pl.when(step > 0)
    def _():
        start = pl.multiple_of((step - 1) * BAND, BAND)

        def across(t, carry):
            base = pl.multiple_of(start + t * TILE + TILE, TILE)
            for g in range(GROUPS):
                now = along_x([ref[g, pl.ds(base, TILE), :] for ref in cell])
                nxt = along_x([ref[g, pl.ds(base + 1, TILE), :] for ref in cell])
                for dst, val in zip(gx, flux(now, nxt)):
                    dst[g, pl.ds(base, TILE), :] = val
            return carry

        lax.fori_loop(0, BAND // TILE, across, 0, unroll=8)

        if closing:
            @pl.when(step == bands)
            def _():
                for dst in gx:
                    at = dst.shape[1] - BAND - 1
                    dst[:, at:at + 1, :] = jnp.zeros((GROUPS, 1, LANES), F32)

        def body(t, carry):
            mark = pl.multiple_of(start + t * TILE, TILE)
            base = pl.multiple_of(mark + TILE, TILE)
            at = pl.ds(pl.multiple_of(t * TILE, TILE), TILE)
            before = [jnp.zeros((TILE, LANES), F32)] * 3
            for g in range(GROUPS):
                now = [ref[g, pl.ds(base, TILE), :] for ref in cell]
                if g < GROUPS - 1:
                    other = [ref[g + 1, pl.ds(base, TILE), :] for ref in cell[:3]]
                else:
                    other = now[:3]
                right = [
                    pltpu.roll(jnp.where(lane == 0, o, c), LANES - 1, 1)
                    for o, c in zip(other, now[:3])
                ]
                fy = flux(along_y(now), along_y(derived(*right)))
                if g == GROUPS - 1:
                    fy = [jnp.where(lane == LANES - 1, 0.0, val) for val in fy]
                py = [
                    pltpu.roll(jnp.where(lane == LANES - 1, o, c), 1, 1)
                    for o, c in zip(before, fy)
                ]
                before = fy
                fx = [src[g, pl.ds(base, TILE), :] for src in gx]
                px = [src[g, pl.ds(base - 1, TILE), :] for src in gx]
                h, u, v = now[:3]
                ch = (fx[0] - px[0]) + (fy[0] - py[0])
                cx = (fx[1] - px[1]) + (fy[2] - py[2])
                cy = (fx[2] - px[2]) + (fy[1] - py[1])
                newh_ref[at, g * LANES:(g + 1) * LANES] = jnp.where(
                    h > 0.0, h - (0.5 * DT_DX) * ch, 0.0
                )
                hu_ref[g, at, :] = u - (0.5 * DT_DX) * cx
                hv_ref[g, at, :] = v - (0.5 * DT_DX) * cy
                h_ref[g, at, :] = h
            return carry

        lax.fori_loop(0, BAND // TILE, body, 0, unroll=8)


def stencil(fields, after, first, count, old=()):
    rows, cols = fields[0].shape
    bands = rows // BAND
    opening = first == 0
    closing = first + count == bands
    plane = jax.ShapeDtypeStruct((GROUPS, rows, LANES), F32)
    scratch = pltpu.VMEM((GROUPS, (count + 1) * BAND + TILE, LANES), F32)
    band = pl.BlockSpec((BAND, cols), lambda i: (jnp.minimum(first + i, bands - 1), 0))
    above = pl.BlockSpec((TILE, cols), lambda i: (first * BAND // TILE - 1, 0))
    whole = pl.BlockSpec(memory_space=pl.ANY)
    part = pl.BlockSpec((GROUPS, BAND, LANES), lambda i: (0, first + jnp.maximum(i - 1, 0), 0))
    return pl.pallas_call(
        functools.partial(stencil_kernel, opening, closing),
        grid=(count + 1,),
        out_shape=(
            jax.ShapeDtypeStruct((rows, cols), F32), plane, plane, plane,
            jax.ShapeDtypeStruct((TILE, LANES), F32),
        ),
        in_specs=[band] * 4 + [whole] + ([] if opening else [above] * 4 + [whole] * 4),
        out_specs=(
            pl.BlockSpec((BAND, cols), lambda i: (first + jnp.maximum(i - 1, 0), 0)),
            part, part, part,
            pl.BlockSpec((TILE, LANES), lambda i: (0, 0)),
        ),
        scratch_shapes=[scratch] * (CELL + 3),
        input_output_aliases={} if opening else {9 + n: n for n in range(4)},
        compiler_params=params(),
        cost_estimate=pl.CostEstimate(
            flops=200 * count * BAND * cols, bytes_accessed=64 * count * BAND * cols,
            transcendentals=0,
        ),
        name="stencil",
    )(*fields, after, *(() if opening else fields), *old)


def summed_of(lab, landed):
    select = (iota((NW * NPATCH, lab.shape[1]), 0) == lab).astype(BF16)
    return jnp.dot(select, landed, preferred_element_type=F32).astype(BF16)


def stack_left(left, summed, channels):
    for k in range(channels):
        for w in range(NW):
            left[k * NPATCH:(k + 1) * NPATCH, w * ABLK:(w + 1) * ABLK] = summed[
                w * NPATCH:(w + 1) * NPATCH, k * ABLK:(k + 1) * ABLK
            ]


PART = TILE * PATCH


def weight_parts(step, w_ref, held, arrived):
    width = held.shape[2]

    def copy(n):
        at = pl.ds(pl.multiple_of(n * width, width), width)
        return pltpu.make_async_copy(w_ref.at[:, at], held.at[n], arrived.at[n])

    @pl.when(step == 0)
    def _():
        for n in range(held.shape[0]):
            copy(n).start()

    return copy(step).wait


def spread_rows(acc, field, k):
    low = iota((TILE, LANES), 1) < LANES // 2
    for t in range(TILE // 2):
        cut = slice(t * LANES, (t + 1) * LANES)
        for half in range(HALVES):
            for g in range(GROUPS):
                base = k * NPATCH + 2 * g * BPX + half * TILE
                even = acc[base:base + TILE, cut]
                odd = acc[base + BPX:base + BPX + TILE, cut]
                for i, val in (
                    (2 * t, jnp.where(low, even, pltpu.roll(odd, LANES // 2, 1))),
                    (2 * t + 1, jnp.where(low, pltpu.roll(even, LANES // 2, 1), odd)),
                ):
                    field[g, pl.ds(half * TILE * TILE + i, TILE, stride=TILE), :] = val


def press_kernel(
    lab_ref, landed_ref, w_ref, top0_ref, bottom0_ref, left0_ref, right0_ref,
    out_ref, top_ref, bottom_ref, left_ref, right_ref, row_ref,
    held, arrived, left, acc, acc2, field, field2,
):
    step = pl.program_id(0)
    take = weight_parts(step, w_ref, held, arrived)

    @pl.when(step == 0)
    def _():
        peers, capacity = lab_ref.shape
        for d in range(peers):
            row_ref[:, d * capacity:(d + 1) * capacity] = lab_ref[d:d + 1, :]
        stack_left(left, summed_of(row_ref[...], landed_ref[...]), 1)

    take()
    acc[...] = jnp.dot(left[...], held[step, :, :PART], preferred_element_type=F32)
    acc2[...] = jnp.dot(left[...], held[step, :, PART:], preferred_element_type=F32)
    for part, (src, mid) in enumerate(((acc, field), (acc2, field2))):
        spread_rows(src, mid, 0)
        for g in range(GROUPS):
            for r in range(BPX):
                to = pl.ds(pl.multiple_of(TILE + r * PATCH + (2 * step + part) * TILE, TILE), TILE)
                out_ref[g, to, :] = mid[g, r * TILE:(r + 1) * TILE, :]

    @pl.when(step == pl.num_programs(0) - 1)
    def _():
        rows = out_ref.shape[1] - 2 * TILE
        mine = iota((TILE, LANES), 0) == 3
        blank = jnp.zeros((TILE, LANES), F32)
        for g in range(GROUPS):
            cut = slice(g * LANES, (g + 1) * LANES)
            head = pltpu.roll(out_ref[g, TILE:2 * TILE, :], 3, 0)
            tail = pltpu.roll(out_ref[g, rows:rows + TILE, :], 4, 0)
            out_ref[g, 0:TILE, :] = blank
            out_ref[g, rows + TILE:, :] = blank
            top_ref[:, cut] = jnp.where(mine, head, top0_ref[:, cut])
            bottom_ref[:, cut] = jnp.where(mine, tail, bottom0_ref[:, cut])
        lane = iota((LANES, LANES), 1)
        for b in range(rows // LANES):
            at = slice(b * LANES, (b + 1) * LANES)
            inner = slice(TILE + b * LANES, TILE + (b + 1) * LANES)
            packed = jnp.where(
                lane == TILE + 3,
                pltpu.roll(out_ref[GROUPS - 1, inner, :], TILE + 4, 1),
                pltpu.roll(out_ref[0, inner, :], 3, 1),
            )
            turned = packed.T
            left_ref[:, at] = jnp.where(mine, turned[0:TILE], left0_ref[:, at])
            right_ref[:, at] = jnp.where(mine, turned[TILE:2 * TILE], right0_ref[:, at])


def pressure_field(lab, landed, weights, edges):
    steps = PATCH // (2 * TILE)
    rows = BPX * PATCH
    line = (TILE, BPY * PATCH)
    column = (TILE, rows)
    whole = (GROUPS, rows + 2 * TILE, LANES)

    def const(shape):
        return pl.BlockSpec(shape, lambda i: (0,) * len(shape))

    return pl.pallas_call(
        press_kernel,
        grid=(steps,),
        out_shape=tuple(jax.ShapeDtypeStruct(x, F32) for x in (whole, line, line, column, column))
        + (jax.ShapeDtypeStruct((1, lab.size), jnp.int32),),
        in_specs=[
            const(lab.shape),
            const(landed.shape),
            pl.BlockSpec(memory_space=pl.ANY),
        ] + [const(x) for x in (line, line, column, column)],
        out_specs=tuple(const(x) for x in (whole, line, line, column, column, (1, lab.size))),
        scratch_shapes=[
            pltpu.VMEM((steps, NW * ABLK, 2 * PART), BF16),
            pltpu.SemaphoreType.DMA((steps,)),
            pltpu.VMEM((NPATCH, NW * ABLK), BF16),
            pltpu.VMEM((NPATCH, PART), F32),
            pltpu.VMEM((NPATCH, PART), F32),
            pltpu.VMEM((GROUPS, BPX * TILE, LANES), F32),
            pltpu.VMEM((GROUPS, BPX * TILE, LANES), F32),
        ],
        compiler_params=params(),
        cost_estimate=pl.CostEstimate(
            flops=2 * NPATCH * NW * ABLK * PATCH * PATCH, bytes_accessed=12 << 20, transcendentals=0
        ),
        name="pressure",
    )(lab, landed, weights, *edges)


def border_places(rows, cols):
    middle = pl.ds(LANES, cols - 2 * LANES)
    return (
        (slice(None), pl.ds(0, LANES)),
        (slice(None), pl.ds(cols - LANES, LANES)),
        (pl.ds(0, TILE), middle),
        (pl.ds(rows - TILE, TILE), middle),
    )


def border_additions(halos, edges, edge, sides, ends):
    up_ref, dn_ref, lh_ref, rh_ref = halos
    top_ref, bottom_ref, left_ref, right_ref = edges

    def cells(ref):
        return derived(ref[0:1, :], ref[1:2, :], ref[2:3, :])

    pull = TIME_STEP * PRESS * 0.5
    step = 0.5 * DT_DX
    for out, turned in ((edge, along_y), (ends, along_x)):
        out[...] = jnp.zeros_like(out)
        far_low, far_high, own_low, own_high = (
            (lh_ref, rh_ref, left_ref, right_ref) if out is edge
            else (up_ref, dn_ref, top_ref, bottom_ref)
        )
        for at, before, after, own, far, sign in (
            (0, far_low, own_low, own_low, far_low, 1.0),
            (3, own_high, far_high, own_high, far_high, -1.0),
        ):
            gh, gn, gt = flux(turned(cells(before)), turned(cells(after)))
            wet = own[0:1, :] > 0.0
            normal = gn * step + (pull * own[0:1, :]) * far[3:4, :]
            pair = (gt * step, normal) if out is edge else (normal, gt * step)
            for f, val in enumerate((gh * step,) + pair):
                out[at + f:at + f + 1, :] = jnp.where(wet, sign * val, 0.0)
    blank = jnp.zeros((LANES - TILE, LANES), F32)
    for b in range(sides.shape[0] // LANES):
        cut = slice(b * LANES, (b + 1) * LANES)
        sides[cut, :] = jnp.concatenate([edge[:, cut], blank], axis=0).T


def patch_border(parts, sides, ends):
    first, last, head, tail = parts
    rows = first.shape[0]
    cols = ends.shape[1]
    lane = iota((rows, LANES), 1)
    values = sides[...]
    first[...] += jnp.where(lane == 0, values, 0.0)
    last[...] += jnp.where(lane == LANES - 1, pltpu.roll(values, LANES - 4, 1), 0.0)
    for at, line in ((0, 0), (rows - 1, 3)):
        first[at:at + 1, :] += ends[line:line + 1, 0:LANES]
        last[at:at + 1, :] += ends[line:line + 1, cols - LANES:cols]
    head[0:1, :] += ends[0:1, LANES:cols - LANES]
    tail[TILE - 1:TILE, :] += ends[3:4, LANES:cols - LANES]


def finish_kernel(
    lab_ref, landed_ref, w_ref, p_ref, up_ref, dn_ref, lh_ref, rh_ref,
    top_ref, bottom_ref, left_ref, right_ref, old_ref,
    hu_ref, hv_ref, h_ref, ox_ref, oy_ref, new_ref,
    held, arrived, left, acc, acc2, fx, fy, fx2, fy2,
    edge, sides_ref, ends_ref, first, last, head, tail, loaded, saved,
):
    step = pl.program_id(0)
    take = weight_parts(step, w_ref, held, arrived)
    parts = (first, last, head, tail)
    places = border_places(*old_ref.shape)
    loads = [
        pltpu.make_async_copy(old_ref.at[at], part, loaded.at[n])
        for n, (at, part) in enumerate(zip(places, parts))
    ]
    saves = [
        pltpu.make_async_copy(part, new_ref.at[at], saved.at[n])
        for n, (at, part) in enumerate(zip(places, parts))
    ]

    @pl.when(step == 0)
    def _():
        for copy in loads:
            copy.start()
        border_additions(
            (up_ref, dn_ref, lh_ref, rh_ref), (top_ref, bottom_ref, left_ref, right_ref),
            edge, sides_ref, ends_ref,
        )
        stack_left(left, summed_of(lab_ref[...], landed_ref[...]), 2)

    take()
    acc[...] = jnp.dot(left[...], held[step, :, :PART], preferred_element_type=F32)
    acc2[...] = jnp.dot(left[...], held[step, :, PART:], preferred_element_type=F32)
    lane = iota((TILE, LANES), 1)
    for part, (src, mx, my) in enumerate(((acc, fx, fy), (acc2, fx2, fy2))):
        spread_rows(src, mx, 0)
        spread_rows(src, my, 1)
        cells = slice(part * TILE, (part + 1) * TILE)
        for r in range(BPX):
            at = slice(r * TILE, (r + 1) * TILE)
            mark = pl.multiple_of(r * PATCH + (2 * step + part) * TILE, TILE)
            base = pl.multiple_of(mark + TILE, TILE)
            ends = sides_ref[pl.ds(mark, TILE), :]
            tiles = [p_ref[g, pl.ds(base, TILE), :] for g in range(GROUPS)]
            for g in range(GROUPS):
                before = tiles[g - 1] if g else 0.0
                after = tiles[g + 1] if g < GROUPS - 1 else 0.0
                prev = pltpu.roll(jnp.where(lane == LANES - 1, before, tiles[g]), 1, 1)
                nxt = pltpu.roll(jnp.where(lane == 0, after, tiles[g]), LANES - 1, 1)
                h = h_ref[g, r, cells, :]
                wet = h > 0.0
                scale = (TIME_STEP * PRESS * 0.5) * h
                gx = p_ref[g, pl.ds(base + 1, TILE), :] - p_ref[g, pl.ds(base - 1, TILE), :]
                wx = mx[g, at, :]
                wy = my[g, at, :]
                power = wx * wx + wy * wy
                speed = jnp.where(power > 0.0, power * lax.rsqrt(power), 0.0) * (TIME_STEP * STRESS)
                new = [
                    hu_ref[g, r, cells, :] - scale * gx + speed * wx,
                    hv_ref[g, r, cells, :] - scale * (nxt - prev) + speed * wy,
                ]
                for own, edge, shift in ((0, 0, 1), (GROUPS - 1, LANES - 1, 4)):
                    if g == own:
                        new = [
                            jnp.where(
                                lane == edge,
                                a + pltpu.roll(ends, (edge - shift - f) % LANES, 1),
                                a,
                            )
                            for f, a in enumerate(new)
                        ]
                cut = slice(g * LANES, (g + 1) * LANES)
                ox_ref[r, cells, cut] = jnp.where(wet, new[0], 0.0)
                oy_ref[r, cells, cut] = jnp.where(wet, new[1], 0.0)

    @pl.when(step == 1)
    def _():
        for copy in loads:
            copy.wait()
        patch_border(parts, sides_ref, ends_ref)
        for copy in saves:
            copy.start()

    @pl.when(step == 0)
    def _():
        ox_ref[0, 0:1, :] += ends_ref[1:2, :]
        oy_ref[0, 0:1, :] += ends_ref[2:3, :]

    @pl.when(step == pl.num_programs(0) - 1)
    def _():
        deep = ox_ref.shape[1]
        ox_ref[BPX - 1, deep - 1:deep, :] += ends_ref[4:5, :]
        oy_ref[BPX - 1, deep - 1:deep, :] += ends_ref[5:6, :]
        for copy in saves:
            copy.wait()


def finish(lab, landed, weights, p, halos, edges, newh, hu, hv, h):
    deep = 2 * TILE
    steps = PATCH // deep
    cols = BPY * PATCH
    split = (GROUPS, BPX, PATCH, LANES)
    slab = pl.BlockSpec((GROUPS, BPX, deep, LANES), lambda i: (0, 0, i, 0))
    out = pl.BlockSpec((BPX, deep, cols), lambda i: (0, i, 0))
    shape = jax.ShapeDtypeStruct((BPX, PATCH, cols), F32)
    rows = newh.shape[0]
    whole = pl.BlockSpec(memory_space=pl.ANY)
    field = pltpu.VMEM((GROUPS, BPX * TILE, LANES), F32)

    def const(x):
        return pl.BlockSpec(x.shape, lambda i: (0,) * x.ndim)

    return pl.pallas_call(
        finish_kernel,
        grid=(steps,),
        out_shape=(shape, shape, jax.ShapeDtypeStruct(newh.shape, F32)),
        in_specs=[
            const(lab), const(landed),
            whole,
            const(p), *[const(x) for x in (*halos, *edges)], whole,
            slab, slab, slab,
        ],
        out_specs=(out, out, whole),
        input_output_aliases={12: 2},
        scratch_shapes=[
            pltpu.VMEM((steps, NW * ABLK, 2 * PART), BF16),
            pltpu.SemaphoreType.DMA((steps,)),
            pltpu.VMEM((2 * NPATCH, NW * ABLK), BF16),
            pltpu.VMEM((2 * NPATCH, PART), F32),
            pltpu.VMEM((2 * NPATCH, PART), F32),
            field, field, field, field,
            pltpu.VMEM((TILE, rows), F32),
            pltpu.VMEM((rows, LANES), F32),
            pltpu.VMEM((TILE, cols), F32),
            pltpu.VMEM((rows, LANES), F32),
            pltpu.VMEM((rows, LANES), F32),
            pltpu.VMEM((TILE, cols - 2 * LANES), F32),
            pltpu.VMEM((TILE, cols - 2 * LANES), F32),
            pltpu.SemaphoreType.DMA((4,)),
            pltpu.SemaphoreType.DMA((4,)),
        ],
        compiler_params=params(),
        cost_estimate=pl.CostEstimate(
            flops=4 * NPATCH * NW * ABLK * PATCH * PATCH, bytes_accessed=20 << 20, transcendentals=0
        ),
        name="finish",
    )(
        lab, landed, weights, p, *halos, *edges, newh,
        hu.reshape(split), hv.reshape(split), h.reshape(split),
    )


def body(
    atm_blocks,
    remap_weights,
    ovl_source,
    ovl_block,
    ovl_patch,
    ovl_weight,
    depth_field,
    wet_mask,
    mom_x,
    mom_y,
    blend,
):
    count_x = lax.axis_size("gx")
    count_y = lax.axis_size("gy")
    devices = count_x * count_y
    entries = ovl_source.size
    capacity = 2 * entries // devices
    slots = devices * capacity
    atm = atm_blocks.reshape(atm_blocks.shape[2:]).transpose(1, 0, 2)
    both = ("gx", "gy")
    want, lab = make_requests(
        ovl_source.reshape(1, entries), ovl_block.reshape(1, entries),
        ovl_patch.reshape(1, entries), ovl_weight.reshape(1, entries), devices, capacity,
    )
    asked = lax.all_to_all(
        want.reshape(devices, 1, capacity), both, split_axis=0, concat_axis=0, tiled=True
    )
    press, wind = mix(blend.reshape(1), atm)
    top, bottom, left, right = edge_cells(depth_field, wet_mask, mom_x, mom_y)

    def exchange(after, tiles):
        rows = serve(after, asked, tiles)
        parts = rows.reshape(devices, capacity, rows.shape[1])
        got = lax.all_to_all(parts, both, split_axis=0, concat_axis=0, tiled=True)
        return got.reshape(rows.shape)

    press = exchange(top, press)
    fields = (depth_field, wet_mask, mom_x, mom_y)
    bands = depth_field.shape[0] // BAND
    ahead = bands * 5 // 8
    *planes, token = stencil(fields, lab, 0, ahead)
    wind = exchange(token, wind)
    weights = remap_weights.reshape(NW * ABLK, PATCH * PATCH)
    p, *edges, lab = pressure_field(lab, press, weights, (top, bottom, left, right))
    top, bottom, left, right = edges
    halos = (
        send(bottom, "gx", 1), send(top, "gx", -1), send(right, "gy", 1), send(left, "gy", -1),
    )
    newh, hu, hv, h, _ = stencil(fields, top, ahead, bands - ahead, planes)
    new_x, new_y, newh = finish(lab, wind, weights, p, halos, edges, newh, hu, hv, h)
    return (newh, new_x.reshape(newh.shape), new_y.reshape(newh.shape))


def solution(mesh):
    placed = (
        P("gx", "gy", None, None, None),
        P(),
        P("gx", "gy", None, None),
        P("gx", "gy", None),
        P("gx", "gy", None),
        P("gx", "gy", None),
        P("gx", "gy"),
        P("gx", "gy"),
        P("gx", "gy"),
        P("gx", "gy"),
        P(),
    )
    return jax.shard_map(
        body,
        mesh=mesh,
        in_specs=placed,
        out_specs=(P("gx", "gy"), P("gx", "gy"), P("gx", "gy")),
        check_vma=False,
    )
```

```python
import functools

import jax
import jax.numpy as jnp
from jax import lax
from jax.experimental import pallas as pl
from jax.experimental.pallas import tpu as pltpu
from jax.sharding import PartitionSpec as P

PATCH = 64
ABLK = 256
NW = 4
BPX = 16
BPY = 8
NPATCH = BPX * BPY

GRAV = 1.0
DT_DX = 0.2
TIME_STEP = 0.2
STRESS = 0.5
PRESS = 0.5

F32 = jnp.float32
BF16 = jnp.bfloat16
VMEM = pl.BlockSpec(memory_space=pltpu.VMEM)
SMEM = pl.BlockSpec(memory_space=pltpu.SMEM)
LANES = 128
TILE = 8
GROUPS = BPY * PATCH // LANES
HALVES = BPX // TILE
BAND = 128


def params(limit=56 << 20, **kw):
    return pltpu.CompilerParams(vmem_limit_bytes=limit, **kw)


def iota(shape, dim):
    return lax.broadcasted_iota(jnp.int32, shape, dim)


def rank_kernel(capacity, src_ref, blk_ref, pat_ref, wgt_ref, want_ref, lab_ref):
    devices = want_ref.shape[0]
    src = src_ref[...]
    ent = src.shape[1]
    hits = (iota((devices, ent), 0) == src).astype(F32)
    order = (iota((ent, ent), 0) <= iota((ent, ent), 1)).astype(BF16)
    ranks = jnp.dot(hits.astype(BF16), order, preferred_element_type=F32)
    mine = jnp.sum(hits * ranks, axis=0, keepdims=True).astype(jnp.int32) - 1
    place = iota((capacity, ent), 0) == mine
    pat = pat_ref[...]
    row_bits = BPX.bit_length() - 1
    col_bits = BPY.bit_length() - 1
    rows = jnp.zeros_like(pat)
    cols = jnp.zeros_like(pat)
    used_r = used_c = position = 0
    while used_r < row_bits or used_c < col_bits:
        value = jnp.bitwise_and(jnp.right_shift(pat, position), 1)
        if used_r < row_bits and (used_c >= col_bits or position % 2 == 0):
            rows = rows + value * (1 << used_r)
            used_r += 1
        else:
            cols = cols + value * (1 << used_c)
            used_c += 1
        position += 1

    def spread(row):
        picked = jnp.where(place, row.astype(F32), 0.0).astype(BF16)
        return lax.dot_general(
            hits.astype(BF16), picked, (((1,), (1,)), ((), ())),
            preferred_element_type=F32,
        ).astype(jnp.int32)

    want_ref[...] = spread(blk_ref[...])
    slot = spread(cols * BPX + rows)
    group = spread(wgt_ref[...] + 1)
    lab_ref[...] = jnp.where(group > 0, (group - 1) * NPATCH + slot, -1)


def make_requests(src, blk, pat, wgt, devices, capacity):
    shape = jax.ShapeDtypeStruct((devices, capacity), jnp.int32)
    return pl.pallas_call(
        functools.partial(rank_kernel, capacity),
        out_shape=(shape, shape),
        in_specs=[VMEM] * 4,
        out_specs=(VMEM, VMEM),
        compiler_params=params(),
        name="requests",
    )(src, blk, pat, wgt)


def mix_kernel(after_ref, blend_ref, atm_ref, press_ref, wind_ref):
    blend = blend_ref[0]
    keep = 1.0 - blend

    def mixed(k):
        first = atm_ref[k].astype(F32)
        second = atm_ref[3 + k].astype(F32)
        return (keep * first + blend * second).astype(BF16)

    press_ref[...] = mixed(2)
    for k in range(2):
        wind_ref[:, k * ABLK:(k + 1) * ABLK] = mixed(k)


def mix(after, blend, atm):
    blocks = atm.shape[1]
    return pl.pallas_call(
        mix_kernel,
        out_shape=(
            jax.ShapeDtypeStruct((blocks, ABLK), BF16),
            jax.ShapeDtypeStruct((blocks, 2 * ABLK), BF16),
        ),
        in_specs=[pl.BlockSpec(memory_space=pl.ANY), SMEM, VMEM],
        out_specs=(VMEM, VMEM),
        compiler_params=params(),
        name="mix",
    )(after, blend, atm)


def serve_kernel(*refs):
    asked_ref, tiles_ref, out_ref, turned, pick = refs[-5:]
    peers, _, capacity = asked_ref.shape
    width = turned.shape[0]
    turned[...] = jnp.zeros_like(turned)
    turned[0:peers, 0:capacity] = asked_ref[:, 0, :]
    columns = turned[...].T
    blocks = tiles_ref.shape[0]
    names = iota((capacity, blocks), 1)
    for d in range(peers):
        pick[d * capacity:(d + 1) * capacity, :] = (columns[0:capacity, d:d + 1] == names).astype(F32)
    out_ref[...] = jnp.dot(
        pick[...].astype(BF16), tiles_ref[...], preferred_element_type=F32
    ).astype(BF16)


def serve(after, asked, tiles):
    peers, _, capacity = asked.shape
    slots = peers * capacity
    width = -(-max(peers, capacity) // LANES) * LANES
    return pl.pallas_call(
        serve_kernel,
        out_shape=jax.ShapeDtypeStruct((slots, tiles.shape[1]), BF16),
        in_specs=[pl.BlockSpec(memory_space=pl.ANY)] * len(after) + [VMEM, VMEM],
        out_specs=VMEM,
        scratch_shapes=[
            pltpu.VMEM((width, width), jnp.int32),
            pltpu.VMEM((slots, tiles.shape[0]), F32),
        ],
        compiler_params=params(32 << 20),
        name="serve",
    )(*after, asked, tiles)


def edges_kernel(
    dl, ml, xl, yl, dr, mr, xr, yr, dt, mt, xt, yt, db, mb, xb, yb,
    top_ref, bottom_ref, left_ref, right_ref,
):
    def rows(d, m, x, y, at, out):
        wet = m[...] == 1
        for f, ref in enumerate((d, x, y)):
            out[f:f + 1, :] = jnp.where(wet, ref[...], 0.0)[at:at + 1]

    rows(dt, mt, xt, yt, 0, top_ref)
    rows(db, mb, xb, yb, TILE - 1, bottom_ref)
    lane = iota((LANES, LANES), 1)

    def step(b, carry):
        at = pl.ds(pl.multiple_of(b * LANES, LANES), LANES)
        wl = ml[at, :] == 1
        wr = mr[at, :] == 1
        packed = jnp.where(wl, dl[at, :], 0.0)
        packed = jnp.where(lane == 1, pltpu.roll(jnp.where(wl, xl[at, :], 0.0), 1, 1), packed)
        packed = jnp.where(lane == 2, pltpu.roll(jnp.where(wl, yl[at, :], 0.0), 2, 1), packed)
        packed = jnp.where(lane == 8, pltpu.roll(jnp.where(wr, dr[at, :], 0.0), 9, 1), packed)
        packed = jnp.where(lane == 9, pltpu.roll(jnp.where(wr, xr[at, :], 0.0), 10, 1), packed)
        packed = jnp.where(lane == 10, pltpu.roll(jnp.where(wr, yr[at, :], 0.0), 11, 1), packed)
        turned = packed.T
        left_ref[:, at] = turned[0:TILE]
        right_ref[:, at] = turned[TILE:2 * TILE]
        return carry

    lax.fori_loop(0, dl.shape[0] // LANES, step, 0)


def edge_cells(depth, mask, momx, momy):
    rows, cols = depth.shape
    fields = (depth, mask, momx, momy)
    left = pl.BlockSpec((rows, LANES), lambda i: (0, 0))
    right = pl.BlockSpec((rows, LANES), lambda i: (0, cols // LANES - 1))
    top = pl.BlockSpec((TILE, cols), lambda i: (0, 0))
    bottom = pl.BlockSpec((TILE, cols), lambda i: (rows // TILE - 1, 0))
    line = jax.ShapeDtypeStruct((TILE, cols), F32)
    column = jax.ShapeDtypeStruct((TILE, rows), F32)
    return pl.pallas_call(
        edges_kernel,
        grid=(1,),
        out_shape=(line, line, column, column),
        in_specs=[left] * 4 + [right] * 4 + [top] * 4 + [bottom] * 4,
        out_specs=(
            pl.BlockSpec((TILE, cols), lambda i: (0, 0)),
            pl.BlockSpec((TILE, cols), lambda i: (0, 0)),
            pl.BlockSpec((TILE, rows), lambda i: (0, 0)),
            pl.BlockSpec((TILE, rows), lambda i: (0, 0)),
        ),
        compiler_params=params(),
        name="edges",
    )(*(fields * 4))


def send(value, axis, step):
    count = lax.axis_size(axis)
    if step > 0:
        pairs = [(i, i + 1) for i in range(count - 1)]
    else:
        pairs = [(i + 1, i) for i in range(count - 1)]
    return lax.ppermute(value, axis, pairs)


def derived(h, u, v):
    r = jnp.where(h > 0.0, lax.rsqrt(h), 0.0)
    s = h * r
    q = u * r
    p = v * r
    half = 0.5 * h * h
    return (h, u, v, s, q, p, q * q + half, p * p + half, q * p)


def along_x(c):
    return (c[0], c[1], c[2], c[3], c[4], c[5], c[6], c[8])


def along_y(c):
    return (c[0], c[2], c[1], c[3], c[5], c[4], c[7], c[8])


def flux(a, b):
    hl, nl, tl, sl, ql, pl_, fl, gl = a
    hr, nr, tr, sr, qr, pr, fr, gr = b
    both = jnp.minimum(hl, hr) > 0.0
    half = jnp.where(both, 0.5, 1.0)
    twice = half + half
    level = (hl + hr) * half
    rc = lax.rsqrt(level)
    c = level * rc
    total = sl + sr
    inv = pl.reciprocal(total, approx=True)
    inv = inv * (2.0 - total * inv)
    u = jnp.where(both, (ql + qr) * inv, 0.0)
    v = (pl_ + pr) * inv
    dh = jnp.where(both, hr - hl, 0.0)
    dn = (nr - nl) * twice
    dt = jnp.where(both, tr - tl, 0.0)
    mid = 0.5 * dh
    e = (0.5 * dn - u * mid) * rc
    s1 = u - c
    s3 = u + c
    b1 = jnp.abs(s1) * (mid - e)
    b3 = jnp.abs(s3) * (mid + e)
    b2 = jnp.abs(u) * (dt - v * dh)
    d = b1 + b3
    return (
        jnp.where(both, nl + nr, 0.0) - d,
        (fl + fr) * twice - (b1 * s1 + b3 * s3),
        jnp.where(both, gl + gr, 0.0) - (d * v + b2),
    )


CELL = 9


def stencil_kernel(opening, closing, *refs):
    fields = refs[:4]
    refs = refs[5:]
    above = () if opening else refs[:4]
    if not opening:
        refs = refs[8:]
    newh_ref, hu_ref, hv_ref, h_ref, token_ref = refs[:5]
    cell = refs[5:5 + CELL]
    gx = refs[5 + CELL:]
    step = pl.program_id(0)
    bands = pl.num_programs(0) - 1
    lane = iota((TILE, LANES), 1)

    def masked(d, m, x, y, at, cut):
        wet = m[at, cut] == 1
        return derived(*[jnp.where(wet, ref[at, cut], 0.0) for ref in (d, x, y)])

    def fill_band():
        def fill(t, carry):
            at = pl.ds(pl.multiple_of(t * TILE, TILE), TILE)
            to = pl.ds(pl.multiple_of(step * BAND + t * TILE + TILE, TILE), TILE)
            for g in range(GROUPS):
                cut = slice(g * LANES, (g + 1) * LANES)
                for dst, val in zip(cell, masked(*fields, at, cut)):
                    dst[g, to, :] = val
            return carry

        lax.fori_loop(0, BAND // TILE, fill, 0, unroll=8)

    if closing:
        pl.when(step < bands)(fill_band)
    else:
        fill_band()

    @pl.when(step == 0)
    def _():
        token_ref[...] = jnp.zeros_like(token_ref)
        if closing:
            for dst in cell:
                dst[:, dst.shape[1] - BAND:dst.shape[1] - BAND + TILE, :] = jnp.zeros(
                    (GROUPS, TILE, LANES), F32
                )
        if opening:
            for dst in gx:
                dst[:, 0:TILE, :] = jnp.zeros((GROUPS, TILE, LANES), F32)
        else:
            for g in range(GROUPS):
                cut = slice(g * LANES, (g + 1) * LANES)
                for dst, val in zip(cell, masked(*above, slice(None), cut)):
                    dst[g, 0:TILE, :] = val
                now = along_x([ref[g, 0:TILE, :] for ref in cell])
                nxt = along_x([ref[g, 1:TILE + 1, :] for ref in cell])
                for dst, val in zip(gx, flux(now, nxt)):
                    dst[g, 0:TILE, :] = val

    @pl.when(step > 0)
    def _():
        start = pl.multiple_of((step - 1) * BAND, BAND)

        def across(t, carry):
            base = pl.multiple_of(start + t * TILE + TILE, TILE)
            for g in range(GROUPS):
                now = along_x([ref[g, pl.ds(base, TILE), :] for ref in cell])
                nxt = along_x([ref[g, pl.ds(base + 1, TILE), :] for ref in cell])
                for dst, val in zip(gx, flux(now, nxt)):
                    dst[g, pl.ds(base, TILE), :] = val
            return carry

        lax.fori_loop(0, BAND // TILE, across, 0, unroll=8)

        if closing:
            @pl.when(step == bands)
            def _():
                for dst in gx:
                    at = dst.shape[1] - BAND - 1
                    dst[:, at:at + 1, :] = jnp.zeros((GROUPS, 1, LANES), F32)

        def body(t, carry):
            mark = pl.multiple_of(start + t * TILE, TILE)
            base = pl.multiple_of(mark + TILE, TILE)
            at = pl.ds(pl.multiple_of(t * TILE, TILE), TILE)
            before = [jnp.zeros((TILE, LANES), F32)] * 3
            for g in range(GROUPS):
                now = [ref[g, pl.ds(base, TILE), :] for ref in cell]
                if g < GROUPS - 1:
                    other = [ref[g + 1, pl.ds(base, TILE), :] for ref in cell[:3]]
                else:
                    other = now[:3]
                right = [
                    pltpu.roll(jnp.where(lane == 0, o, c), LANES - 1, 1)
                    for o, c in zip(other, now[:3])
                ]
                fy = flux(along_y(now), along_y(derived(*right)))
                if g == GROUPS - 1:
                    fy = [jnp.where(lane == LANES - 1, 0.0, val) for val in fy]
                py = [
                    pltpu.roll(jnp.where(lane == LANES - 1, o, c), 1, 1)
                    for o, c in zip(before, fy)
                ]
                before = fy
                fx = [src[g, pl.ds(base, TILE), :] for src in gx]
                px = [src[g, pl.ds(base - 1, TILE), :] for src in gx]
                h, u, v = now[:3]
                ch = (fx[0] - px[0]) + (fy[0] - py[0])
                cx = (fx[1] - px[1]) + (fy[2] - py[2])
                cy = (fx[2] - px[2]) + (fy[1] - py[1])
                newh_ref[at, g * LANES:(g + 1) * LANES] = jnp.where(
                    h > 0.0, h - (0.5 * DT_DX) * ch, 0.0
                )
                hu_ref[g, at, :] = u - (0.5 * DT_DX) * cx
                hv_ref[g, at, :] = v - (0.5 * DT_DX) * cy
                h_ref[g, at, :] = h
            return carry

        lax.fori_loop(0, BAND // TILE, body, 0, unroll=8)


def stencil(fields, after, first, count, old=()):
    rows, cols = fields[0].shape
    bands = rows // BAND
    opening = first == 0
    closing = first + count == bands
    plane = jax.ShapeDtypeStruct((GROUPS, rows, LANES), F32)
    scratch = pltpu.VMEM((GROUPS, (count + 1) * BAND + TILE, LANES), F32)
    band = pl.BlockSpec((BAND, cols), lambda i: (jnp.minimum(first + i, bands - 1), 0))
    above = pl.BlockSpec((TILE, cols), lambda i: (first * BAND // TILE - 1, 0))
    whole = pl.BlockSpec(memory_space=pl.ANY)
    part = pl.BlockSpec((GROUPS, BAND, LANES), lambda i: (0, first + jnp.maximum(i - 1, 0), 0))
    return pl.pallas_call(
        functools.partial(stencil_kernel, opening, closing),
        grid=(count + 1,),
        out_shape=(
            jax.ShapeDtypeStruct((rows, cols), F32), plane, plane, plane,
            jax.ShapeDtypeStruct((TILE, LANES), F32),
        ),
        in_specs=[band] * 4 + [whole] + ([] if opening else [above] * 4 + [whole] * 4),
        out_specs=(
            pl.BlockSpec((BAND, cols), lambda i: (first + jnp.maximum(i - 1, 0), 0)),
            part, part, part,
            pl.BlockSpec((TILE, LANES), lambda i: (0, 0)),
        ),
        scratch_shapes=[scratch] * (CELL + 3),
        input_output_aliases={} if opening else {9 + n: n for n in range(4)},
        compiler_params=params(),
        cost_estimate=pl.CostEstimate(
            flops=200 * count * BAND * cols, bytes_accessed=64 * count * BAND * cols,
            transcendentals=0,
        ),
        name="stencil",
    )(*fields, after, *(() if opening else fields), *old)


def summed_of(lab, landed):
    select = (iota((NW * NPATCH, lab.shape[1]), 0) == lab).astype(BF16)
    return jnp.dot(select, landed, preferred_element_type=F32).astype(BF16)


def stack_left(left, summed, channels):
    for k in range(channels):
        for w in range(NW):
            left[k * NPATCH:(k + 1) * NPATCH, w * ABLK:(w + 1) * ABLK] = summed[
                w * NPATCH:(w + 1) * NPATCH, k * ABLK:(k + 1) * ABLK
            ]


PART = TILE * PATCH


def weight_parts(step, w_ref, held, arrived):
    width = held.shape[2]

    def copy(n):
        at = pl.ds(pl.multiple_of(n * width, width), width)
        return pltpu.make_async_copy(w_ref.at[:, at], held.at[n], arrived.at[n])

    @pl.when(step == 0)
    def _():
        for n in range(held.shape[0]):
            copy(n).start()

    return copy(step).wait


def spread_rows(acc, field, k):
    low = iota((TILE, LANES), 1) < LANES // 2
    for t in range(TILE // 2):
        cut = slice(t * LANES, (t + 1) * LANES)
        for half in range(HALVES):
            for g in range(GROUPS):
                base = k * NPATCH + 2 * g * BPX + half * TILE
                even = acc[base:base + TILE, cut]
                odd = acc[base + BPX:base + BPX + TILE, cut]
                for i, val in (
                    (2 * t, jnp.where(low, even, pltpu.roll(odd, LANES // 2, 1))),
                    (2 * t + 1, jnp.where(low, pltpu.roll(even, LANES // 2, 1), odd)),
                ):
                    field[g, pl.ds(half * TILE * TILE + i, TILE, stride=TILE), :] = val


def press_kernel(
    lab_ref, landed_ref, w_ref, top0_ref, bottom0_ref, left0_ref, right0_ref,
    out_ref, top_ref, bottom_ref, left_ref, right_ref, row_ref,
    held, arrived, left, acc, acc2, field, field2,
):
    step = pl.program_id(0)
    take = weight_parts(step, w_ref, held, arrived)

    @pl.when(step == 0)
    def _():
        peers, capacity = lab_ref.shape
        for d in range(peers):
            row_ref[:, d * capacity:(d + 1) * capacity] = lab_ref[d:d + 1, :]
        stack_left(left, summed_of(row_ref[...], landed_ref[...]), 1)

    take()
    acc[...] = jnp.dot(left[...], held[step, :, :PART], preferred_element_type=F32)
    acc2[...] = jnp.dot(left[...], held[step, :, PART:], preferred_element_type=F32)
    for part, (src, mid) in enumerate(((acc, field), (acc2, field2))):
        spread_rows(src, mid, 0)
        for g in range(GROUPS):
            for r in range(BPX):
                to = pl.ds(pl.multiple_of(TILE + r * PATCH + (2 * step + part) * TILE, TILE), TILE)
                out_ref[g, to, :] = mid[g, r * TILE:(r + 1) * TILE, :]

    @pl.when(step == pl.num_programs(0) - 1)
    def _():
        rows = out_ref.shape[1] - 2 * TILE
        mine = iota((TILE, LANES), 0) == 3
        blank = jnp.zeros((TILE, LANES), F32)
        for g in range(GROUPS):
            cut = slice(g * LANES, (g + 1) * LANES)
            head = pltpu.roll(out_ref[g, TILE:2 * TILE, :], 3, 0)
            tail = pltpu.roll(out_ref[g, rows:rows + TILE, :], 4, 0)
            out_ref[g, 0:TILE, :] = blank
            out_ref[g, rows + TILE:, :] = blank
            top_ref[:, cut] = jnp.where(mine, head, top0_ref[:, cut])
            bottom_ref[:, cut] = jnp.where(mine, tail, bottom0_ref[:, cut])
        lane = iota((LANES, LANES), 1)
        for b in range(rows // LANES):
            at = slice(b * LANES, (b + 1) * LANES)
            inner = slice(TILE + b * LANES, TILE + (b + 1) * LANES)
            packed = jnp.where(
                lane == TILE + 3,
                pltpu.roll(out_ref[GROUPS - 1, inner, :], TILE + 4, 1),
                pltpu.roll(out_ref[0, inner, :], 3, 1),
            )
            turned = packed.T
            left_ref[:, at] = jnp.where(mine, turned[0:TILE], left0_ref[:, at])
            right_ref[:, at] = jnp.where(mine, turned[TILE:2 * TILE], right0_ref[:, at])


def pressure_field(lab, landed, weights, edges):
    steps = PATCH // (2 * TILE)
    rows = BPX * PATCH
    line = (TILE, BPY * PATCH)
    column = (TILE, rows)
    whole = (GROUPS, rows + 2 * TILE, LANES)

    def const(shape):
        return pl.BlockSpec(shape, lambda i: (0,) * len(shape))

    return pl.pallas_call(
        press_kernel,
        grid=(steps,),
        out_shape=tuple(jax.ShapeDtypeStruct(x, F32) for x in (whole, line, line, column, column))
        + (jax.ShapeDtypeStruct((1, lab.size), jnp.int32),),
        in_specs=[
            const(lab.shape),
            const(landed.shape),
            pl.BlockSpec(memory_space=pl.ANY),
        ] + [const(x) for x in (line, line, column, column)],
        out_specs=tuple(const(x) for x in (whole, line, line, column, column, (1, lab.size))),
        scratch_shapes=[
            pltpu.VMEM((steps, NW * ABLK, 2 * PART), BF16),
            pltpu.SemaphoreType.DMA((steps,)),
            pltpu.VMEM((NPATCH, NW * ABLK), BF16),
            pltpu.VMEM((NPATCH, PART), F32),
            pltpu.VMEM((NPATCH, PART), F32),
            pltpu.VMEM((GROUPS, BPX * TILE, LANES), F32),
            pltpu.VMEM((GROUPS, BPX * TILE, LANES), F32),
        ],
        compiler_params=params(),
        cost_estimate=pl.CostEstimate(
            flops=2 * NPATCH * NW * ABLK * PATCH * PATCH, bytes_accessed=12 << 20, transcendentals=0
        ),
        name="pressure",
    )(lab, landed, weights, *edges)


def border_places(rows, cols):
    middle = pl.ds(LANES, cols - 2 * LANES)
    return (
        (slice(None), pl.ds(0, LANES)),
        (slice(None), pl.ds(cols - LANES, LANES)),
        (pl.ds(0, TILE), middle),
        (pl.ds(rows - TILE, TILE), middle),
    )


def border_additions(halos, edges, edge, sides, ends):
    up_ref, dn_ref, lh_ref, rh_ref = halos
    top_ref, bottom_ref, left_ref, right_ref = edges

    def cells(ref):
        return derived(ref[0:1, :], ref[1:2, :], ref[2:3, :])

    pull = TIME_STEP * PRESS * 0.5
    step = 0.5 * DT_DX
    for out, turned in ((edge, along_y), (ends, along_x)):
        out[...] = jnp.zeros_like(out)
        far_low, far_high, own_low, own_high = (
            (lh_ref, rh_ref, left_ref, right_ref) if out is edge
            else (up_ref, dn_ref, top_ref, bottom_ref)
        )
        for at, before, after, own, far, sign in (
            (0, far_low, own_low, own_low, far_low, 1.0),
            (3, own_high, far_high, own_high, far_high, -1.0),
        ):
            gh, gn, gt = flux(turned(cells(before)), turned(cells(after)))
            wet = own[0:1, :] > 0.0
            normal = gn * step + (pull * own[0:1, :]) * far[3:4, :]
            pair = (gt * step, normal) if out is edge else (normal, gt * step)
            for f, val in enumerate((gh * step,) + pair):
                out[at + f:at + f + 1, :] = jnp.where(wet, sign * val, 0.0)
    blank = jnp.zeros((LANES - TILE, LANES), F32)
    for b in range(sides.shape[0] // LANES):
        cut = slice(b * LANES, (b + 1) * LANES)
        sides[cut, :] = jnp.concatenate([edge[:, cut], blank], axis=0).T


def patch_border(parts, sides, ends):
    first, last, head, tail = parts
    rows = first.shape[0]
    cols = ends.shape[1]
    lane = iota((rows, LANES), 1)
    values = sides[...]
    first[...] += jnp.where(lane == 0, values, 0.0)
    last[...] += jnp.where(lane == LANES - 1, pltpu.roll(values, LANES - 4, 1), 0.0)
    for at, line in ((0, 0), (rows - 1, 3)):
        first[at:at + 1, :] += ends[line:line + 1, 0:LANES]
        last[at:at + 1, :] += ends[line:line + 1, cols - LANES:cols]
    head[0:1, :] += ends[0:1, LANES:cols - LANES]
    tail[TILE - 1:TILE, :] += ends[3:4, LANES:cols - LANES]


def finish_kernel(
    lab_ref, landed_ref, w_ref, p_ref, up_ref, dn_ref, lh_ref, rh_ref,
    top_ref, bottom_ref, left_ref, right_ref, old_ref,
    hu_hbm, hv_hbm, h_hbm, ox_ref, oy_ref, new_ref,
    held, arrived, left, acc, acc2, fx, fy, fx2, fy2,
    edge, sides_ref, ends_ref, first, last, head, tail, loaded, saved,
    press, got_press, hus, hvs, hs, got,
):
    step = pl.program_id(0)
    deep = hus.shape[3]
    take_press = pltpu.make_async_copy(p_ref, press, got_press)

    def state(n):
        at = pl.ds(pl.multiple_of(n * deep, deep), deep)
        return [
            pltpu.make_async_copy(src.at[:, :, at, :], dst.at[n], got.at[f, n])
            for f, (src, dst) in enumerate(((hu_hbm, hus), (hv_hbm, hvs), (h_hbm, hs)))
        ]

    @pl.when(step == 0)
    def _():
        for copy in state(0):
            copy.start()
        take_press.start()

    take = weight_parts(step, w_ref, held, arrived)

    @pl.when(step == 0)
    def _():
        for n in range(1, hus.shape[0]):
            for copy in state(n):
                copy.start()

    parts = (first, last, head, tail)
    places = border_places(*old_ref.shape)
    loads = [
        pltpu.make_async_copy(old_ref.at[at], part, loaded.at[n])
        for n, (at, part) in enumerate(zip(places, parts))
    ]
    saves = [
        pltpu.make_async_copy(part, new_ref.at[at], saved.at[n])
        for n, (at, part) in enumerate(zip(places, parts))
    ]

    @pl.when(step == 0)
    def _():
        for copy in loads:
            copy.start()
        border_additions(
            (up_ref, dn_ref, lh_ref, rh_ref), (top_ref, bottom_ref, left_ref, right_ref),
            edge, sides_ref, ends_ref,
        )
        stack_left(left, summed_of(lab_ref[...], landed_ref[...]), 2)

    take()
    acc[...] = jnp.dot(left[...], held[step, :, :PART], preferred_element_type=F32)
    acc2[...] = jnp.dot(left[...], held[step, :, PART:], preferred_element_type=F32)
    pl.when(step == 0)(take_press.wait)
    for copy in state(step):
        copy.wait()
    lane = iota((TILE, LANES), 1)
    for part, (src, mx, my) in enumerate(((acc, fx, fy), (acc2, fx2, fy2))):
        spread_rows(src, mx, 0)
        spread_rows(src, my, 1)
        cells = slice(part * TILE, (part + 1) * TILE)
        for r in range(BPX):
            at = slice(r * TILE, (r + 1) * TILE)
            mark = pl.multiple_of(r * PATCH + (2 * step + part) * TILE, TILE)
            base = pl.multiple_of(mark + TILE, TILE)
            ends = sides_ref[pl.ds(mark, TILE), :]
            tiles = [press[g, pl.ds(base, TILE), :] for g in range(GROUPS)]
            for g in range(GROUPS):
                before = tiles[g - 1] if g else 0.0
                after = tiles[g + 1] if g < GROUPS - 1 else 0.0
                prev = pltpu.roll(jnp.where(lane == LANES - 1, before, tiles[g]), 1, 1)
                nxt = pltpu.roll(jnp.where(lane == 0, after, tiles[g]), LANES - 1, 1)
                h = hs[step, g, r, cells, :]
                wet = h > 0.0
                scale = (TIME_STEP * PRESS * 0.5) * h
                gx = press[g, pl.ds(base + 1, TILE), :] - press[g, pl.ds(base - 1, TILE), :]
                wx = mx[g, at, :]
                wy = my[g, at, :]
                power = wx * wx + wy * wy
                speed = jnp.where(power > 0.0, power * lax.rsqrt(power), 0.0) * (TIME_STEP * STRESS)
                new = [
                    hus[step, g, r, cells, :] - scale * gx + speed * wx,
                    hvs[step, g, r, cells, :] - scale * (nxt - prev) + speed * wy,
                ]
                for own, edge, shift in ((0, 0, 1), (GROUPS - 1, LANES - 1, 4)):
                    if g == own:
                        new = [
                            jnp.where(
                                lane == edge,
                                a + pltpu.roll(ends, (edge - shift - f) % LANES, 1),
                                a,
                            )
                            for f, a in enumerate(new)
                        ]
                cut = slice(g * LANES, (g + 1) * LANES)
                ox_ref[r, cells, cut] = jnp.where(wet, new[0], 0.0)
                oy_ref[r, cells, cut] = jnp.where(wet, new[1], 0.0)

    @pl.when(step == 1)
    def _():
        for copy in loads:
            copy.wait()
        patch_border(parts, sides_ref, ends_ref)
        for copy in saves:
            copy.start()

    @pl.when(step == 0)
    def _():
        ox_ref[0, 0:1, :] += ends_ref[1:2, :]
        oy_ref[0, 0:1, :] += ends_ref[2:3, :]

    @pl.when(step == pl.num_programs(0) - 1)
    def _():
        ox_ref[BPX - 1, deep - 1:deep, :] += ends_ref[4:5, :]
        oy_ref[BPX - 1, deep - 1:deep, :] += ends_ref[5:6, :]
        for copy in saves:
            copy.wait()


def finish(lab, landed, weights, p, halos, edges, newh, hu, hv, h):
    deep = 2 * TILE
    steps = PATCH // deep
    cols = BPY * PATCH
    split = (GROUPS, BPX, PATCH, LANES)
    slab = pltpu.VMEM((steps, GROUPS, BPX, deep, LANES), F32)
    out = pl.BlockSpec((BPX, deep, cols), lambda i: (0, i, 0))
    shape = jax.ShapeDtypeStruct((BPX, PATCH, cols), F32)
    rows = newh.shape[0]
    whole = pl.BlockSpec(memory_space=pl.ANY)
    field = pltpu.VMEM((GROUPS, BPX * TILE, LANES), F32)

    def const(x):
        return pl.BlockSpec(x.shape, lambda i: (0,) * x.ndim)

    return pl.pallas_call(
        finish_kernel,
        grid=(steps,),
        out_shape=(shape, shape, jax.ShapeDtypeStruct(newh.shape, F32)),
        in_specs=[
            const(lab), const(landed),
            whole,
            whole, *[const(x) for x in (*halos, *edges)], whole,
            whole, whole, whole,
        ],
        out_specs=(out, out, whole),
        input_output_aliases={12: 2},
        scratch_shapes=[
            pltpu.VMEM((steps, NW * ABLK, 2 * PART), BF16),
            pltpu.SemaphoreType.DMA((steps,)),
            pltpu.VMEM((2 * NPATCH, NW * ABLK), BF16),
            pltpu.VMEM((2 * NPATCH, PART), F32),
            pltpu.VMEM((2 * NPATCH, PART), F32),
            field, field, field, field,
            pltpu.VMEM((TILE, rows), F32),
            pltpu.VMEM((rows, LANES), F32),
            pltpu.VMEM((TILE, cols), F32),
            pltpu.VMEM((rows, LANES), F32),
            pltpu.VMEM((rows, LANES), F32),
            pltpu.VMEM((TILE, cols - 2 * LANES), F32),
            pltpu.VMEM((TILE, cols - 2 * LANES), F32),
            pltpu.SemaphoreType.DMA((4,)),
            pltpu.SemaphoreType.DMA((4,)),
            pltpu.VMEM(p.shape, F32),
            pltpu.SemaphoreType.DMA(()),
            slab, slab, slab,
            pltpu.SemaphoreType.DMA((3, steps)),
        ],
        compiler_params=params(),
        cost_estimate=pl.CostEstimate(
            flops=4 * NPATCH * NW * ABLK * PATCH * PATCH, bytes_accessed=20 << 20, transcendentals=0
        ),
        name="finish",
    )(
        lab, landed, weights, p, *halos, *edges, newh,
        hu.reshape(split), hv.reshape(split), h.reshape(split),
    )


def body(
    atm_blocks,
    remap_weights,
    ovl_source,
    ovl_block,
    ovl_patch,
    ovl_weight,
    depth_field,
    wet_mask,
    mom_x,
    mom_y,
    blend,
):
    count_x = lax.axis_size("gx")
    count_y = lax.axis_size("gy")
    devices = count_x * count_y
    entries = ovl_source.size
    capacity = 2 * entries // devices
    slots = devices * capacity
    atm = atm_blocks.reshape(atm_blocks.shape[2:]).transpose(1, 0, 2)
    both = ("gx", "gy")
    want, lab = make_requests(
        ovl_source.reshape(1, entries), ovl_block.reshape(1, entries),
        ovl_patch.reshape(1, entries), ovl_weight.reshape(1, entries), devices, capacity,
    )
    asked = lax.all_to_all(
        want.reshape(devices, 1, capacity), both, split_axis=0, concat_axis=0, tiled=True
    )
    top, bottom, left, right = edge_cells(depth_field, wet_mask, mom_x, mom_y)
    press, wind = mix(top, blend.reshape(1), atm)

    def exchange(after, tiles):
        rows = serve(after, asked, tiles)
        parts = rows.reshape(devices, capacity, rows.shape[1])
        got = lax.all_to_all(parts, both, split_axis=0, concat_axis=0, tiled=True)
        return got.reshape(rows.shape)

    press = exchange((), press)
    fields = (depth_field, wet_mask, mom_x, mom_y)
    bands = depth_field.shape[0] // BAND
    ahead = bands * 5 // 8
    *planes, token = stencil(fields, lab, 0, ahead)
    wind = exchange((token,), wind)
    weights = remap_weights.reshape(NW * ABLK, PATCH * PATCH)
    p, *edges, lab = pressure_field(lab, press, weights, (top, bottom, left, right))
    top, bottom, left, right = edges
    halos = (
        send(bottom, "gx", 1), send(top, "gx", -1), send(right, "gy", 1), send(left, "gy", -1),
    )
    newh, hu, hv, h, _ = stencil(fields, top, ahead, bands - ahead, planes)
    new_x, new_y, newh = finish(lab, wind, weights, p, halos, edges, newh, hu, hv, h)
    return (newh, new_x.reshape(newh.shape), new_y.reshape(newh.shape))


def solution(mesh):
    placed = (
        P("gx", "gy", None, None, None),
        P(),
        P("gx", "gy", None, None),
        P("gx", "gy", None),
        P("gx", "gy", None),
        P("gx", "gy", None),
        P("gx", "gy"),
        P("gx", "gy"),
        P("gx", "gy"),
        P("gx", "gy"),
        P(),
    )
    return jax.shard_map(
        body,
        mesh=mesh,
        in_specs=placed,
        out_specs=(P("gx", "gy"), P("gx", "gy"), P("gx", "gy")),
        check_vma=False,
    )
```

```python
import functools

import jax
import jax.numpy as jnp
from jax import lax
from jax.experimental import pallas as pl
from jax.experimental.pallas import tpu as pltpu
from jax.sharding import PartitionSpec as P

PATCH = 64
ABLK = 256
NW = 4
BPX = 16
BPY = 8
NPATCH = BPX * BPY

GRAV = 1.0
DT_DX = 0.2
TIME_STEP = 0.2
STRESS = 0.5
PRESS = 0.5

F32 = jnp.float32
BF16 = jnp.bfloat16
VMEM = pl.BlockSpec(memory_space=pltpu.VMEM)
SMEM = pl.BlockSpec(memory_space=pltpu.SMEM)
LANES = 128
TILE = 8
GROUPS = BPY * PATCH // LANES
HALVES = BPX // TILE
BAND = 128


def params(limit=56 << 20, **kw):
    return pltpu.CompilerParams(vmem_limit_bytes=limit, **kw)


def iota(shape, dim):
    return lax.broadcasted_iota(jnp.int32, shape, dim)


def rank_kernel(capacity, src_ref, blk_ref, pat_ref, wgt_ref, want_ref, lab_ref):
    devices = want_ref.shape[0]
    src = src_ref[...]
    ent = src.shape[1]
    hits = (iota((devices, ent), 0) == src).astype(F32)
    order = (iota((ent, ent), 0) <= iota((ent, ent), 1)).astype(BF16)
    ranks = jnp.dot(hits.astype(BF16), order, preferred_element_type=F32)
    mine = jnp.sum(hits * ranks, axis=0, keepdims=True).astype(jnp.int32) - 1
    place = iota((capacity, ent), 0) == mine
    pat = pat_ref[...]
    row_bits = BPX.bit_length() - 1
    col_bits = BPY.bit_length() - 1
    rows = jnp.zeros_like(pat)
    cols = jnp.zeros_like(pat)
    used_r = used_c = position = 0
    while used_r < row_bits or used_c < col_bits:
        value = jnp.bitwise_and(jnp.right_shift(pat, position), 1)
        if used_r < row_bits and (used_c >= col_bits or position % 2 == 0):
            rows = rows + value * (1 << used_r)
            used_r += 1
        else:
            cols = cols + value * (1 << used_c)
            used_c += 1
        position += 1

    def spread(row):
        picked = jnp.where(place, row.astype(F32), 0.0).astype(BF16)
        return lax.dot_general(
            hits.astype(BF16), picked, (((1,), (1,)), ((), ())),
            preferred_element_type=F32,
        ).astype(jnp.int32)

    want_ref[...] = spread(blk_ref[...])
    slot = spread(cols * BPX + rows)
    group = spread(wgt_ref[...] + 1)
    lab_ref[...] = jnp.where(group > 0, (group - 1) * NPATCH + slot, -1)


def make_requests(src, blk, pat, wgt, devices, capacity):
    shape = jax.ShapeDtypeStruct((devices, capacity), jnp.int32)
    return pl.pallas_call(
        functools.partial(rank_kernel, capacity),
        out_shape=(shape, shape),
        in_specs=[VMEM] * 4,
        out_specs=(VMEM, VMEM),
        compiler_params=params(),
        name="requests",
    )(src, blk, pat, wgt)


def mix_kernel(blend_ref, atm_ref, press_ref, wind_ref):
    blend = blend_ref[0]
    keep = 1.0 - blend

    def mixed(k):
        first = atm_ref[k].astype(F32)
        second = atm_ref[3 + k].astype(F32)
        return (keep * first + blend * second).astype(BF16)

    press_ref[...] = mixed(2)
    for k in range(2):
        wind_ref[:, k * ABLK:(k + 1) * ABLK] = mixed(k)


def mix(blend, atm):
    blocks = atm.shape[1]
    return pl.pallas_call(
        mix_kernel,
        out_shape=(
            jax.ShapeDtypeStruct((blocks, ABLK), BF16),
            jax.ShapeDtypeStruct((blocks, 2 * ABLK), BF16),
        ),
        in_specs=[SMEM, VMEM],
        out_specs=(VMEM, VMEM),
        compiler_params=params(),
        name="mix",
    )(blend, atm)


def serve_kernel(after_ref, asked_ref, tiles_ref, out_ref, turned, pick):
    peers, _, capacity = asked_ref.shape
    width = turned.shape[0]
    turned[...] = jnp.zeros_like(turned)
    turned[0:peers, 0:capacity] = asked_ref[:, 0, :]
    columns = turned[...].T
    blocks = tiles_ref.shape[0]
    names = iota((capacity, blocks), 1)
    for d in range(peers):
        pick[d * capacity:(d + 1) * capacity, :] = (columns[0:capacity, d:d + 1] == names).astype(F32)
    out_ref[...] = jnp.dot(
        pick[...].astype(BF16), tiles_ref[...], preferred_element_type=F32
    ).astype(BF16)


def serve(after, asked, tiles):
    peers, _, capacity = asked.shape
    slots = peers * capacity
    width = -(-max(peers, capacity) // LANES) * LANES
    return pl.pallas_call(
        serve_kernel,
        out_shape=jax.ShapeDtypeStruct((slots, tiles.shape[1]), BF16),
        in_specs=[pl.BlockSpec(memory_space=pl.ANY), VMEM, VMEM],
        out_specs=VMEM,
        scratch_shapes=[
            pltpu.VMEM((width, width), jnp.int32),
            pltpu.VMEM((slots, tiles.shape[0]), F32),
        ],
        compiler_params=params(32 << 20),
        name="serve",
    )(after, asked, tiles)


def edges_kernel(
    dl, ml, xl, yl, dr, mr, xr, yr, dt, mt, xt, yt, db, mb, xb, yb,
    top_ref, bottom_ref, left_ref, right_ref,
):
    def rows(d, m, x, y, at, out):
        wet = m[...] == 1
        for f, ref in enumerate((d, x, y)):
            out[f:f + 1, :] = jnp.where(wet, ref[...], 0.0)[at:at + 1]

    rows(dt, mt, xt, yt, 0, top_ref)
    rows(db, mb, xb, yb, TILE - 1, bottom_ref)
    lane = iota((LANES, LANES), 1)

    def step(b, carry):
        at = pl.ds(pl.multiple_of(b * LANES, LANES), LANES)
        wl = ml[at, :] == 1
        wr = mr[at, :] == 1
        packed = jnp.where(wl, dl[at, :], 0.0)
        packed = jnp.where(lane == 1, pltpu.roll(jnp.where(wl, xl[at, :], 0.0), 1, 1), packed)
        packed = jnp.where(lane == 2, pltpu.roll(jnp.where(wl, yl[at, :], 0.0), 2, 1), packed)
        packed = jnp.where(lane == 8, pltpu.roll(jnp.where(wr, dr[at, :], 0.0), 9, 1), packed)
        packed = jnp.where(lane == 9, pltpu.roll(jnp.where(wr, xr[at, :], 0.0), 10, 1), packed)
        packed = jnp.where(lane == 10, pltpu.roll(jnp.where(wr, yr[at, :], 0.0), 11, 1), packed)
        turned = packed.T
        left_ref[:, at] = turned[0:TILE]
        right_ref[:, at] = turned[TILE:2 * TILE]
        return carry

    lax.fori_loop(0, dl.shape[0] // LANES, step, 0)


def edge_cells(depth, mask, momx, momy):
    rows, cols = depth.shape
    fields = (depth, mask, momx, momy)
    left = pl.BlockSpec((rows, LANES), lambda i: (0, 0))
    right = pl.BlockSpec((rows, LANES), lambda i: (0, cols // LANES - 1))
    top = pl.BlockSpec((TILE, cols), lambda i: (0, 0))
    bottom = pl.BlockSpec((TILE, cols), lambda i: (rows // TILE - 1, 0))
    line = jax.ShapeDtypeStruct((TILE, cols), F32)
    column = jax.ShapeDtypeStruct((TILE, rows), F32)
    return pl.pallas_call(
        edges_kernel,
        grid=(1,),
        out_shape=(line, line, column, column),
        in_specs=[left] * 4 + [right] * 4 + [top] * 4 + [bottom] * 4,
        out_specs=(
            pl.BlockSpec((TILE, cols), lambda i: (0, 0)),
            pl.BlockSpec((TILE, cols), lambda i: (0, 0)),
            pl.BlockSpec((TILE, rows), lambda i: (0, 0)),
            pl.BlockSpec((TILE, rows), lambda i: (0, 0)),
        ),
        compiler_params=params(),
        name="edges",
    )(*(fields * 4))


def send(value, axis, step):
    count = lax.axis_size(axis)
    if step > 0:
        pairs = [(i, i + 1) for i in range(count - 1)]
    else:
        pairs = [(i + 1, i) for i in range(count - 1)]
    return lax.ppermute(value, axis, pairs)


def derived(h, u, v):
    r = jnp.where(h > 0.0, lax.rsqrt(h), 0.0)
    s = h * r
    q = u * r
    p = v * r
    half = 0.5 * h * h
    return (h, u, v, s, q, p, q * q + half, p * p + half, q * p)


def along_x(c):
    return (c[0], c[1], c[2], c[3], c[4], c[5], c[6], c[8])


def along_y(c):
    return (c[0], c[2], c[1], c[3], c[5], c[4], c[7], c[8])


def flux(a, b):
    hl, nl, tl, sl, ql, pl_, fl, gl = a
    hr, nr, tr, sr, qr, pr, fr, gr = b
    both = jnp.minimum(hl, hr) > 0.0
    half = jnp.where(both, 0.5, 1.0)
    twice = half + half
    level = (hl + hr) * half
    rc = lax.rsqrt(level)
    c = level * rc
    total = sl + sr
    inv = pl.reciprocal(total, approx=True)
    inv = inv * (2.0 - total * inv)
    u = jnp.where(both, (ql + qr) * inv, 0.0)
    v = (pl_ + pr) * inv
    dh = jnp.where(both, hr - hl, 0.0)
    dn = (nr - nl) * twice
    dt = jnp.where(both, tr - tl, 0.0)
    mid = 0.5 * dh
    e = (0.5 * dn - u * mid) * rc
    s1 = u - c
    s3 = u + c
    b1 = jnp.abs(s1) * (mid - e)
    b3 = jnp.abs(s3) * (mid + e)
    b2 = jnp.abs(u) * (dt - v * dh)
    d = b1 + b3
    return (
        jnp.where(both, nl + nr, 0.0) - d,
        (fl + fr) * twice - (b1 * s1 + b3 * s3),
        jnp.where(both, gl + gr, 0.0) - (d * v + b2),
    )


CELL = 9


def stencil_kernel(opening, closing, *refs):
    fields = refs[:4]
    refs = refs[5:]
    above = () if opening else refs[:4]
    if not opening:
        refs = refs[8:]
    newh_ref, hu_ref, hv_ref, h_ref, token_ref = refs[:5]
    cell = refs[5:5 + CELL]
    gx = refs[5 + CELL:]
    step = pl.program_id(0)
    bands = pl.num_programs(0) - 1
    lane = iota((TILE, LANES), 1)

    def masked(d, m, x, y, at, cut):
        wet = m[at, cut] == 1
        return derived(*[jnp.where(wet, ref[at, cut], 0.0) for ref in (d, x, y)])

    def fill_band():
        def fill(t, carry):
            at = pl.ds(pl.multiple_of(t * TILE, TILE), TILE)
            to = pl.ds(pl.multiple_of(step * BAND + t * TILE + TILE, TILE), TILE)
            for g in range(GROUPS):
                cut = slice(g * LANES, (g + 1) * LANES)
                for dst, val in zip(cell, masked(*fields, at, cut)):
                    dst[g, to, :] = val
            return carry

        lax.fori_loop(0, BAND // TILE, fill, 0, unroll=8)

    if closing:
        pl.when(step < bands)(fill_band)
    else:
        fill_band()

    @pl.when(step == 0)
    def _():
        token_ref[...] = jnp.zeros_like(token_ref)
        if closing:
            for dst in cell:
                dst[:, dst.shape[1] - BAND:dst.shape[1] - BAND + TILE, :] = jnp.zeros(
                    (GROUPS, TILE, LANES), F32
                )
        if opening:
            for dst in gx:
                dst[:, 0:TILE, :] = jnp.zeros((GROUPS, TILE, LANES), F32)
        else:
            for g in range(GROUPS):
                cut = slice(g * LANES, (g + 1) * LANES)
                for dst, val in zip(cell, masked(*above, slice(None), cut)):
                    dst[g, 0:TILE, :] = val
                now = along_x([ref[g, 0:TILE, :] for ref in cell])
                nxt = along_x([ref[g, 1:TILE + 1, :] for ref in cell])
                for dst, val in zip(gx, flux(now, nxt)):
                    dst[g, 0:TILE, :] = val

    @pl.when(step > 0)
    def _():
        start = pl.multiple_of((step - 1) * BAND, BAND)

        def across(t, carry):
            base = pl.multiple_of(start + t * TILE + TILE, TILE)
            for g in range(GROUPS):
                now = along_x([ref[g, pl.ds(base, TILE), :] for ref in cell])
                nxt = along_x([ref[g, pl.ds(base + 1, TILE), :] for ref in cell])
                for dst, val in zip(gx, flux(now, nxt)):
                    dst[g, pl.ds(base, TILE), :] = val
            return carry

        lax.fori_loop(0, BAND // TILE, across, 0, unroll=8)

        if closing:
            @pl.when(step == bands)
            def _():
                for dst in gx:
                    at = dst.shape[1] - BAND - 1
                    dst[:, at:at + 1, :] = jnp.zeros((GROUPS, 1, LANES), F32)

        def body(t, carry):
            mark = pl.multiple_of(start + t * TILE, TILE)
            base = pl.multiple_of(mark + TILE, TILE)
            at = pl.ds(pl.multiple_of(t * TILE, TILE), TILE)
            before = [jnp.zeros((TILE, LANES), F32)] * 3
            for g in range(GROUPS):
                now = [ref[g, pl.ds(base, TILE), :] for ref in cell]
                if g < GROUPS - 1:
                    other = [ref[g + 1, pl.ds(base, TILE), :] for ref in cell[:3]]
                else:
                    other = now[:3]
                right = [
                    pltpu.roll(jnp.where(lane == 0, o, c), LANES - 1, 1)
                    for o, c in zip(other, now[:3])
                ]
                fy = flux(along_y(now), along_y(derived(*right)))
                if g == GROUPS - 1:
                    fy = [jnp.where(lane == LANES - 1, 0.0, val) for val in fy]
                py = [
                    pltpu.roll(jnp.where(lane == LANES - 1, o, c), 1, 1)
                    for o, c in zip(before, fy)
                ]
                before = fy
                fx = [src[g, pl.ds(base, TILE), :] for src in gx]
                px = [src[g, pl.ds(base - 1, TILE), :] for src in gx]
                h, u, v = now[:3]
                ch = (fx[0] - px[0]) + (fy[0] - py[0])
                cx = (fx[1] - px[1]) + (fy[2] - py[2])
                cy = (fx[2] - px[2]) + (fy[1] - py[1])
                newh_ref[at, g * LANES:(g + 1) * LANES] = jnp.where(
                    h > 0.0, h - (0.5 * DT_DX) * ch, 0.0
                )
                hu_ref[g, at, :] = u - (0.5 * DT_DX) * cx
                hv_ref[g, at, :] = v - (0.5 * DT_DX) * cy
                h_ref[g, at, :] = h
            return carry

        lax.fori_loop(0, BAND // TILE, body, 0, unroll=8)


def stencil(fields, after, first, count, old=()):
    rows, cols = fields[0].shape
    bands = rows // BAND
    opening = first == 0
    closing = first + count == bands
    plane = jax.ShapeDtypeStruct((GROUPS, rows, LANES), F32)
    scratch = pltpu.VMEM((GROUPS, (count + 1) * BAND + TILE, LANES), F32)
    band = pl.BlockSpec((BAND, cols), lambda i: (jnp.minimum(first + i, bands - 1), 0))
    above = pl.BlockSpec((TILE, cols), lambda i: (first * BAND // TILE - 1, 0))
    whole = pl.BlockSpec(memory_space=pl.ANY)
    part = pl.BlockSpec((GROUPS, BAND, LANES), lambda i: (0, first + jnp.maximum(i - 1, 0), 0))
    return pl.pallas_call(
        functools.partial(stencil_kernel, opening, closing),
        grid=(count + 1,),
        out_shape=(
            jax.ShapeDtypeStruct((rows, cols), F32), plane, plane, plane,
            jax.ShapeDtypeStruct((TILE, LANES), F32),
        ),
        in_specs=[band] * 4 + [whole] + ([] if opening else [above] * 4 + [whole] * 4),
        out_specs=(
            pl.BlockSpec((BAND, cols), lambda i: (first + jnp.maximum(i - 1, 0), 0)),
            part, part, part,
            pl.BlockSpec((TILE, LANES), lambda i: (0, 0)),
        ),
        scratch_shapes=[scratch] * (CELL + 3),
        input_output_aliases={} if opening else {9 + n: n for n in range(4)},
        compiler_params=params(),
        cost_estimate=pl.CostEstimate(
            flops=200 * count * BAND * cols, bytes_accessed=64 * count * BAND * cols,
            transcendentals=0,
        ),
        name="stencil",
    )(*fields, after, *(() if opening else fields), *old)


def summed_of(lab, landed):
    select = (iota((NW * NPATCH, lab.shape[1]), 0) == lab).astype(BF16)
    return jnp.dot(select, landed, preferred_element_type=F32).astype(BF16)


def stack_left(left, summed, channels):
    for k in range(channels):
        for w in range(NW):
            left[k * NPATCH:(k + 1) * NPATCH, w * ABLK:(w + 1) * ABLK] = summed[
                w * NPATCH:(w + 1) * NPATCH, k * ABLK:(k + 1) * ABLK
            ]


PART = TILE * PATCH


def weight_parts(step, w_ref, held, arrived):
    width = held.shape[2]

    def copy(n):
        at = pl.ds(pl.multiple_of(n * width, width), width)
        return pltpu.make_async_copy(w_ref.at[:, at], held.at[n], arrived.at[n])

    @pl.when(step == 0)
    def _():
        for n in range(held.shape[0]):
            copy(n).start()

    return copy(step).wait


def spread_rows(acc, field, k):
    low = iota((TILE, LANES), 1) < LANES // 2
    for t in range(TILE // 2):
        cut = slice(t * LANES, (t + 1) * LANES)
        for half in range(HALVES):
            for g in range(GROUPS):
                base = k * NPATCH + 2 * g * BPX + half * TILE
                even = acc[base:base + TILE, cut]
                odd = acc[base + BPX:base + BPX + TILE, cut]
                for i, val in (
                    (2 * t, jnp.where(low, even, pltpu.roll(odd, LANES // 2, 1))),
                    (2 * t + 1, jnp.where(low, pltpu.roll(even, LANES // 2, 1), odd)),
                ):
                    field[g, pl.ds(half * TILE * TILE + i, TILE, stride=TILE), :] = val


def press_kernel(
    lab_ref, landed_ref, w_ref, top0_ref, bottom0_ref, left0_ref, right0_ref,
    out_ref, top_ref, bottom_ref, left_ref, right_ref, row_ref,
    held, arrived, left, acc, acc2, field, field2,
):
    step = pl.program_id(0)
    take = weight_parts(step, w_ref, held, arrived)

    @pl.when(step == 0)
    def _():
        peers, capacity = lab_ref.shape
        for d in range(peers):
            row_ref[:, d * capacity:(d + 1) * capacity] = lab_ref[d:d + 1, :]
        stack_left(left, summed_of(row_ref[...], landed_ref[...]), 1)

    take()
    acc[...] = jnp.dot(left[...], held[step, :, :PART], preferred_element_type=F32)
    acc2[...] = jnp.dot(left[...], held[step, :, PART:], preferred_element_type=F32)
    for part, (src, mid) in enumerate(((acc, field), (acc2, field2))):
        spread_rows(src, mid, 0)
        for g in range(GROUPS):
            for r in range(BPX):
                to = pl.ds(pl.multiple_of(TILE + r * PATCH + (2 * step + part) * TILE, TILE), TILE)
                out_ref[g, to, :] = mid[g, r * TILE:(r + 1) * TILE, :]

    @pl.when(step == pl.num_programs(0) - 1)
    def _():
        rows = out_ref.shape[1] - 2 * TILE
        mine = iota((TILE, LANES), 0) == 3
        blank = jnp.zeros((TILE, LANES), F32)
        for g in range(GROUPS):
            cut = slice(g * LANES, (g + 1) * LANES)
            head = pltpu.roll(out_ref[g, TILE:2 * TILE, :], 3, 0)
            tail = pltpu.roll(out_ref[g, rows:rows + TILE, :], 4, 0)
            out_ref[g, 0:TILE, :] = blank
            out_ref[g, rows + TILE:, :] = blank
            top_ref[:, cut] = jnp.where(mine, head, top0_ref[:, cut])
            bottom_ref[:, cut] = jnp.where(mine, tail, bottom0_ref[:, cut])
        lane = iota((LANES, LANES), 1)
        for b in range(rows // LANES):
            at = slice(b * LANES, (b + 1) * LANES)
            inner = slice(TILE + b * LANES, TILE + (b + 1) * LANES)
            packed = jnp.where(
                lane == TILE + 3,
                pltpu.roll(out_ref[GROUPS - 1, inner, :], TILE + 4, 1),
                pltpu.roll(out_ref[0, inner, :], 3, 1),
            )
            turned = packed.T
            left_ref[:, at] = jnp.where(mine, turned[0:TILE], left0_ref[:, at])
            right_ref[:, at] = jnp.where(mine, turned[TILE:2 * TILE], right0_ref[:, at])


def pressure_field(lab, landed, weights, edges):
    steps = PATCH // (2 * TILE)
    rows = BPX * PATCH
    line = (TILE, BPY * PATCH)
    column = (TILE, rows)
    whole = (GROUPS, rows + 2 * TILE, LANES)

    def const(shape):
        return pl.BlockSpec(shape, lambda i: (0,) * len(shape))

    return pl.pallas_call(
        press_kernel,
        grid=(steps,),
        out_shape=tuple(jax.ShapeDtypeStruct(x, F32) for x in (whole, line, line, column, column))
        + (jax.ShapeDtypeStruct((1, lab.size), jnp.int32),),
        in_specs=[
            const(lab.shape),
            const(landed.shape),
            pl.BlockSpec(memory_space=pl.ANY),
        ] + [const(x) for x in (line, line, column, column)],
        out_specs=tuple(const(x) for x in (whole, line, line, column, column, (1, lab.size))),
        scratch_shapes=[
            pltpu.VMEM((steps, NW * ABLK, 2 * PART), BF16),
            pltpu.SemaphoreType.DMA((steps,)),
            pltpu.VMEM((NPATCH, NW * ABLK), BF16),
            pltpu.VMEM((NPATCH, PART), F32),
            pltpu.VMEM((NPATCH, PART), F32),
            pltpu.VMEM((GROUPS, BPX * TILE, LANES), F32),
            pltpu.VMEM((GROUPS, BPX * TILE, LANES), F32),
        ],
        compiler_params=params(),
        cost_estimate=pl.CostEstimate(
            flops=2 * NPATCH * NW * ABLK * PATCH * PATCH, bytes_accessed=12 << 20, transcendentals=0
        ),
        name="pressure",
    )(lab, landed, weights, *edges)


def border_places(rows, cols):
    middle = pl.ds(LANES, cols - 2 * LANES)
    return (
        (slice(None), pl.ds(0, LANES)),
        (slice(None), pl.ds(cols - LANES, LANES)),
        (pl.ds(0, TILE), middle),
        (pl.ds(rows - TILE, TILE), middle),
    )


def border_additions(halos, edges, edge, sides, ends):
    up_ref, dn_ref, lh_ref, rh_ref = halos
    top_ref, bottom_ref, left_ref, right_ref = edges

    def cells(ref):
        return derived(ref[0:1, :], ref[1:2, :], ref[2:3, :])

    pull = TIME_STEP * PRESS * 0.5
    step = 0.5 * DT_DX
    for out, turned in ((edge, along_y), (ends, along_x)):
        out[...] = jnp.zeros_like(out)
        far_low, far_high, own_low, own_high = (
            (lh_ref, rh_ref, left_ref, right_ref) if out is edge
            else (up_ref, dn_ref, top_ref, bottom_ref)
        )
        for at, before, after, own, far, sign in (
            (0, far_low, own_low, own_low, far_low, 1.0),
            (3, own_high, far_high, own_high, far_high, -1.0),
        ):
            gh, gn, gt = flux(turned(cells(before)), turned(cells(after)))
            wet = own[0:1, :] > 0.0
            normal = gn * step + (pull * own[0:1, :]) * far[3:4, :]
            pair = (gt * step, normal) if out is edge else (normal, gt * step)
            for f, val in enumerate((gh * step,) + pair):
                out[at + f:at + f + 1, :] = jnp.where(wet, sign * val, 0.0)
    blank = jnp.zeros((LANES - TILE, LANES), F32)
    for b in range(sides.shape[0] // LANES):
        cut = slice(b * LANES, (b + 1) * LANES)
        sides[cut, :] = jnp.concatenate([edge[:, cut], blank], axis=0).T


def patch_border(parts, sides, ends):
    first, last, head, tail = parts
    rows = first.shape[0]
    cols = ends.shape[1]
    lane = iota((rows, LANES), 1)
    values = sides[...]
    first[...] += jnp.where(lane == 0, values, 0.0)
    last[...] += jnp.where(lane == LANES - 1, pltpu.roll(values, LANES - 4, 1), 0.0)
    for at, line in ((0, 0), (rows - 1, 3)):
        first[at:at + 1, :] += ends[line:line + 1, 0:LANES]
        last[at:at + 1, :] += ends[line:line + 1, cols - LANES:cols]
    head[0:1, :] += ends[0:1, LANES:cols - LANES]
    tail[TILE - 1:TILE, :] += ends[3:4, LANES:cols - LANES]


def finish_kernel(
    lab_ref, landed_ref, w_ref, p_ref, up_ref, dn_ref, lh_ref, rh_ref,
    top_ref, bottom_ref, left_ref, right_ref, old_ref,
    hu_ref, hv_ref, h_ref, ox_ref, oy_ref, new_ref,
    held, arrived, left, acc, mx, my,
    edge, sides_ref, ends_ref, first, last, head, tail, loaded, saved,
):
    step = pl.program_id(0)
    take = weight_parts(step, w_ref, held, arrived)
    parts = (first, last, head, tail)
    places = border_places(*old_ref.shape)
    loads = [
        pltpu.make_async_copy(old_ref.at[at], part, loaded.at[n])
        for n, (at, part) in enumerate(zip(places, parts))
    ]
    saves = [
        pltpu.make_async_copy(part, new_ref.at[at], saved.at[n])
        for n, (at, part) in enumerate(zip(places, parts))
    ]

    @pl.when(step == 0)
    def _():
        for copy in loads:
            copy.start()
        border_additions(
            (up_ref, dn_ref, lh_ref, rh_ref), (top_ref, bottom_ref, left_ref, right_ref),
            edge, sides_ref, ends_ref,
        )
        stack_left(left, summed_of(lab_ref[...], landed_ref[...]), 2)

    take()
    lane = iota((TILE, LANES), 1)

    def rows_part(part, carry):
        width = pl.ds(pl.multiple_of(part * PART, PART), PART)
        acc[...] = jnp.dot(left[...], held[step, :, width], preferred_element_type=F32)
        spread_rows(acc, mx, 0)
        spread_rows(acc, my, 1)
        cells = pl.ds(pl.multiple_of(part * TILE, TILE), TILE)

        def patch_row(r, carry):
            at = pl.ds(pl.multiple_of(r * TILE, TILE), TILE)
            mark = pl.multiple_of(r * PATCH + (2 * step + part) * TILE, TILE)
            base = pl.multiple_of(mark + TILE, TILE)
            ends = sides_ref[pl.ds(mark, TILE), :]
            tiles = [p_ref[g, pl.ds(base, TILE), :] for g in range(GROUPS)]
            for g in range(GROUPS):
                before = tiles[g - 1] if g else 0.0
                after = tiles[g + 1] if g < GROUPS - 1 else 0.0
                prev = pltpu.roll(jnp.where(lane == LANES - 1, before, tiles[g]), 1, 1)
                nxt = pltpu.roll(jnp.where(lane == 0, after, tiles[g]), LANES - 1, 1)
                h = h_ref[g, r, cells, :]
                wet = h > 0.0
                scale = (TIME_STEP * PRESS * 0.5) * h
                gx = p_ref[g, pl.ds(base + 1, TILE), :] - p_ref[g, pl.ds(base - 1, TILE), :]
                wx = mx[g, at, :]
                wy = my[g, at, :]
                power = wx * wx + wy * wy
                speed = jnp.where(power > 0.0, power * lax.rsqrt(power), 0.0) * (TIME_STEP * STRESS)
                new = [
                    hu_ref[g, r, cells, :] - scale * gx + speed * wx,
                    hv_ref[g, r, cells, :] - scale * (nxt - prev) + speed * wy,
                ]
                for own, border, shift in ((0, 0, 1), (GROUPS - 1, LANES - 1, 4)):
                    if g == own:
                        new = [
                            jnp.where(
                                lane == border,
                                a + pltpu.roll(ends, (border - shift - f) % LANES, 1),
                                a,
                            )
                            for f, a in enumerate(new)
                        ]
                cut = slice(g * LANES, (g + 1) * LANES)
                ox_ref[r, cells, cut] = jnp.where(wet, new[0], 0.0)
                oy_ref[r, cells, cut] = jnp.where(wet, new[1], 0.0)
            return carry

        lax.fori_loop(0, BPX, patch_row, 0, unroll=4)
        return carry

    lax.fori_loop(0, 2, rows_part, 0)

    @pl.when(step == 1)
    def _():
        for copy in loads:
            copy.wait()
        patch_border(parts, sides_ref, ends_ref)
        for copy in saves:
            copy.start()

    @pl.when(step == 0)
    def _():
        ox_ref[0, 0:1, :] += ends_ref[1:2, :]
        oy_ref[0, 0:1, :] += ends_ref[2:3, :]

    @pl.when(step == pl.num_programs(0) - 1)
    def _():
        deep = ox_ref.shape[1]
        ox_ref[BPX - 1, deep - 1:deep, :] += ends_ref[4:5, :]
        oy_ref[BPX - 1, deep - 1:deep, :] += ends_ref[5:6, :]
        for copy in saves:
            copy.wait()


def finish(lab, landed, weights, p, halos, edges, newh, hu, hv, h):
    deep = 2 * TILE
    steps = PATCH // deep
    cols = BPY * PATCH
    split = (GROUPS, BPX, PATCH, LANES)
    slab = pl.BlockSpec((GROUPS, BPX, deep, LANES), lambda i: (0, 0, i, 0))
    out = pl.BlockSpec((BPX, deep, cols), lambda i: (0, i, 0))
    shape = jax.ShapeDtypeStruct((BPX, PATCH, cols), F32)
    rows = newh.shape[0]
    whole = pl.BlockSpec(memory_space=pl.ANY)
    field = pltpu.VMEM((GROUPS, BPX * TILE, LANES), F32)

    def const(x):
        return pl.BlockSpec(x.shape, lambda i: (0,) * x.ndim)

    return pl.pallas_call(
        finish_kernel,
        grid=(steps,),
        out_shape=(shape, shape, jax.ShapeDtypeStruct(newh.shape, F32)),
        in_specs=[
            const(lab), const(landed),
            whole,
            const(p), *[const(x) for x in (*halos, *edges)], whole,
            slab, slab, slab,
        ],
        out_specs=(out, out, whole),
        input_output_aliases={12: 2},
        scratch_shapes=[
            pltpu.VMEM((steps, NW * ABLK, 2 * PART), BF16),
            pltpu.SemaphoreType.DMA((steps,)),
            pltpu.VMEM((2 * NPATCH, NW * ABLK), BF16),
            pltpu.VMEM((2 * NPATCH, PART), F32),
            field, field,
            pltpu.VMEM((TILE, rows), F32),
            pltpu.VMEM((rows, LANES), F32),
            pltpu.VMEM((TILE, cols), F32),
            pltpu.VMEM((rows, LANES), F32),
            pltpu.VMEM((rows, LANES), F32),
            pltpu.VMEM((TILE, cols - 2 * LANES), F32),
            pltpu.VMEM((TILE, cols - 2 * LANES), F32),
            pltpu.SemaphoreType.DMA((4,)),
            pltpu.SemaphoreType.DMA((4,)),
        ],
        compiler_params=params(),
        cost_estimate=pl.CostEstimate(
            flops=4 * NPATCH * NW * ABLK * PATCH * PATCH, bytes_accessed=20 << 20, transcendentals=0
        ),
        name="finish",
    )(
        lab, landed, weights, p, *halos, *edges, newh,
        hu.reshape(split), hv.reshape(split), h.reshape(split),
    )


def body(
    atm_blocks,
    remap_weights,
    ovl_source,
    ovl_block,
    ovl_patch,
    ovl_weight,
    depth_field,
    wet_mask,
    mom_x,
    mom_y,
    blend,
):
    count_x = lax.axis_size("gx")
    count_y = lax.axis_size("gy")
    devices = count_x * count_y
    entries = ovl_source.size
    capacity = 2 * entries // devices
    slots = devices * capacity
    atm = atm_blocks.reshape(atm_blocks.shape[2:]).transpose(1, 0, 2)
    both = ("gx", "gy")
    want, lab = make_requests(
        ovl_source.reshape(1, entries), ovl_block.reshape(1, entries),
        ovl_patch.reshape(1, entries), ovl_weight.reshape(1, entries), devices, capacity,
    )
    asked = lax.all_to_all(
        want.reshape(devices, 1, capacity), both, split_axis=0, concat_axis=0, tiled=True
    )
    press, wind = mix(blend.reshape(1), atm)
    top, bottom, left, right = edge_cells(depth_field, wet_mask, mom_x, mom_y)

    def exchange(after, tiles):
        rows = serve(after, asked, tiles)
        parts = rows.reshape(devices, capacity, rows.shape[1])
        got = lax.all_to_all(parts, both, split_axis=0, concat_axis=0, tiled=True)
        return got.reshape(rows.shape)

    press = exchange(top, press)
    fields = (depth_field, wet_mask, mom_x, mom_y)
    bands = depth_field.shape[0] // BAND
    ahead = bands * 5 // 8
    *planes, token = stencil(fields, lab, 0, ahead)
    wind = exchange(token, wind)
    weights = remap_weights.reshape(NW * ABLK, PATCH * PATCH)
    p, *edges, lab = pressure_field(lab, press, weights, (top, bottom, left, right))
    top, bottom, left, right = edges
    halos = (
        send(bottom, "gx", 1), send(top, "gx", -1), send(right, "gy", 1), send(left, "gy", -1),
    )
    newh, hu, hv, h, _ = stencil(fields, top, ahead, bands - ahead, planes)
    new_x, new_y, newh = finish(lab, wind, weights, p, halos, edges, newh, hu, hv, h)
    return (newh, new_x.reshape(newh.shape), new_y.reshape(newh.shape))


def solution(mesh):
    placed = (
        P("gx", "gy", None, None, None),
        P(),
        P("gx", "gy", None, None),
        P("gx", "gy", None),
        P("gx", "gy", None),
        P("gx", "gy", None),
        P("gx", "gy"),
        P("gx", "gy"),
        P("gx", "gy"),
        P("gx", "gy"),
        P(),
    )
    return jax.shard_map(
        body,
        mesh=mesh,
        in_specs=placed,
        out_specs=(P("gx", "gy"), P("gx", "gy"), P("gx", "gy")),
        check_vma=False,
    )
```

```python
import functools

import jax
import jax.numpy as jnp
from jax import lax
from jax.experimental import pallas as pl
from jax.experimental.pallas import tpu as pltpu
from jax.sharding import PartitionSpec as P

PATCH = 64
ABLK = 256
NW = 4
BPX = 16
BPY = 8
NPATCH = BPX * BPY

GRAV = 1.0
DT_DX = 0.2
TIME_STEP = 0.2
STRESS = 0.5
PRESS = 0.5

F32 = jnp.float32
BF16 = jnp.bfloat16
VMEM = pl.BlockSpec(memory_space=pltpu.VMEM)
SMEM = pl.BlockSpec(memory_space=pltpu.SMEM)
LANES = 128
TOKEN = jax.ShapeDtypeStruct((1, 1), jnp.int32)
TILE = 8
GROUPS = BPY * PATCH // LANES
HALVES = BPX // TILE
BAND = 128


def params(limit=56 << 20, **kw):
    return pltpu.CompilerParams(vmem_limit_bytes=limit, **kw)


def iota(shape, dim):
    return lax.broadcasted_iota(jnp.int32, shape, dim)


def rank_kernel(capacity, src_ref, blk_ref, pat_ref, wgt_ref, want_ref, lab_ref):
    devices = want_ref.shape[0]
    src = src_ref[...]
    ent = src.shape[1]
    hits = (iota((devices, ent), 0) == src).astype(F32)
    order = (iota((ent, ent), 0) <= iota((ent, ent), 1)).astype(BF16)
    ranks = jnp.dot(hits.astype(BF16), order, preferred_element_type=F32)
    mine = jnp.sum(hits * ranks, axis=0, keepdims=True).astype(jnp.int32) - 1
    place = iota((capacity, ent), 0) == mine
    pat = pat_ref[...]
    row_bits = BPX.bit_length() - 1
    col_bits = BPY.bit_length() - 1
    rows = jnp.zeros_like(pat)
    cols = jnp.zeros_like(pat)
    used_r = used_c = position = 0
    while used_r < row_bits or used_c < col_bits:
        value = jnp.bitwise_and(jnp.right_shift(pat, position), 1)
        if used_r < row_bits and (used_c >= col_bits or position % 2 == 0):
            rows = rows + value * (1 << used_r)
            used_r += 1
        else:
            cols = cols + value * (1 << used_c)
            used_c += 1
        position += 1

    def spread(row):
        picked = jnp.where(place, row.astype(F32), 0.0).astype(BF16)
        return lax.dot_general(
            hits.astype(BF16), picked, (((1,), (1,)), ((), ())),
            preferred_element_type=F32,
        ).astype(jnp.int32)

    want_ref[...] = spread(blk_ref[...])
    slot = spread(cols * BPX + rows)
    group = spread(wgt_ref[...] + 1)
    lab_ref[...] = jnp.where(group > 0, (group - 1) * NPATCH + slot, -1)


def make_requests(src, blk, pat, wgt, devices, capacity):
    shape = jax.ShapeDtypeStruct((devices, capacity), jnp.int32)
    return pl.pallas_call(
        functools.partial(rank_kernel, capacity),
        out_shape=(shape, shape),
        in_specs=[VMEM] * 4,
        out_specs=(VMEM, VMEM),
        compiler_params=params(),
        name="requests",
    )(src, blk, pat, wgt)


def mix_kernel(blend_ref, atm_ref, press_ref, wind_ref):
    blend = blend_ref[0]
    keep = 1.0 - blend

    def mixed(k):
        first = atm_ref[k].astype(F32)
        second = atm_ref[3 + k].astype(F32)
        return (keep * first + blend * second).astype(BF16)

    press_ref[...] = mixed(2)
    for k in range(2):
        wind_ref[:, k * ABLK:(k + 1) * ABLK] = mixed(k)


def mix(blend, atm):
    blocks = atm.shape[1]
    return pl.pallas_call(
        mix_kernel,
        out_shape=(
            jax.ShapeDtypeStruct((blocks, ABLK), BF16),
            jax.ShapeDtypeStruct((blocks, 2 * ABLK), BF16),
        ),
        in_specs=[SMEM, VMEM],
        out_specs=(VMEM, VMEM),
        compiler_params=params(),
        name="mix",
    )(blend, atm)


def serve_kernel(after_ref, asked_ref, tiles_ref, out_ref, turned, pick):
    peers, _, capacity = asked_ref.shape
    width = turned.shape[0]
    turned[...] = jnp.zeros_like(turned)
    turned[0:peers, 0:capacity] = asked_ref[:, 0, :]
    columns = turned[...].T
    blocks = tiles_ref.shape[0]
    names = iota((capacity, blocks), 1)
    for d in range(peers):
        pick[d * capacity:(d + 1) * capacity, :] = (columns[0:capacity, d:d + 1] == names).astype(F32)
    out_ref[...] = jnp.dot(
        pick[...].astype(BF16), tiles_ref[...], preferred_element_type=F32
    ).astype(BF16)


def serve(after, asked, tiles):
    peers, _, capacity = asked.shape
    slots = peers * capacity
    width = -(-max(peers, capacity) // LANES) * LANES
    return pl.pallas_call(
        serve_kernel,
        out_shape=jax.ShapeDtypeStruct((slots, tiles.shape[1]), BF16),
        in_specs=[SMEM, VMEM, VMEM],
        out_specs=VMEM,
        scratch_shapes=[
            pltpu.VMEM((width, width), jnp.int32),
            pltpu.VMEM((slots, tiles.shape[0]), F32),
        ],
        compiler_params=params(32 << 20),
        name="serve",
    )(after, asked, tiles)


def edges_kernel(
    dl, ml, xl, yl, dr, mr, xr, yr, dt, mt, xt, yt, db, mb, xb, yb,
    top_ref, bottom_ref, left_ref, right_ref, token_ref,
):
    token_ref[0, 0] = 0

    def rows(d, m, x, y, at, out):
        wet = m[...] == 1
        for f, ref in enumerate((d, x, y)):
            out[f:f + 1, :] = jnp.where(wet, ref[...], 0.0)[at:at + 1]

    rows(dt, mt, xt, yt, 0, top_ref)
    rows(db, mb, xb, yb, TILE - 1, bottom_ref)
    lane = iota((LANES, LANES), 1)

    def step(b, carry):
        at = pl.ds(pl.multiple_of(b * LANES, LANES), LANES)
        wl = ml[at, :] == 1
        wr = mr[at, :] == 1
        packed = jnp.where(wl, dl[at, :], 0.0)
        packed = jnp.where(lane == 1, pltpu.roll(jnp.where(wl, xl[at, :], 0.0), 1, 1), packed)
        packed = jnp.where(lane == 2, pltpu.roll(jnp.where(wl, yl[at, :], 0.0), 2, 1), packed)
        packed = jnp.where(lane == 8, pltpu.roll(jnp.where(wr, dr[at, :], 0.0), 9, 1), packed)
        packed = jnp.where(lane == 9, pltpu.roll(jnp.where(wr, xr[at, :], 0.0), 10, 1), packed)
        packed = jnp.where(lane == 10, pltpu.roll(jnp.where(wr, yr[at, :], 0.0), 11, 1), packed)
        turned = packed.T
        left_ref[:, at] = turned[0:TILE]
        right_ref[:, at] = turned[TILE:2 * TILE]
        return carry

    lax.fori_loop(0, dl.shape[0] // LANES, step, 0)


def edge_cells(depth, mask, momx, momy):
    rows, cols = depth.shape
    fields = (depth, mask, momx, momy)
    left = pl.BlockSpec((rows, LANES), lambda i: (0, 0))
    right = pl.BlockSpec((rows, LANES), lambda i: (0, cols // LANES - 1))
    top = pl.BlockSpec((TILE, cols), lambda i: (0, 0))
    bottom = pl.BlockSpec((TILE, cols), lambda i: (rows // TILE - 1, 0))
    line = jax.ShapeDtypeStruct((TILE, cols), F32)
    column = jax.ShapeDtypeStruct((TILE, rows), F32)
    return pl.pallas_call(
        edges_kernel,
        grid=(1,),
        out_shape=(line, line, column, column, TOKEN),
        in_specs=[left] * 4 + [right] * 4 + [top] * 4 + [bottom] * 4,
        out_specs=(
            pl.BlockSpec((TILE, cols), lambda i: (0, 0)),
            pl.BlockSpec((TILE, cols), lambda i: (0, 0)),
            pl.BlockSpec((TILE, rows), lambda i: (0, 0)),
            pl.BlockSpec((TILE, rows), lambda i: (0, 0)),
            SMEM,
        ),
        compiler_params=params(),
        name="edges",
    )(*(fields * 4))


def send(value, axis, step):
    count = lax.axis_size(axis)
    if step > 0:
        pairs = [(i, i + 1) for i in range(count - 1)]
    else:
        pairs = [(i + 1, i) for i in range(count - 1)]
    return lax.ppermute(value, axis, pairs)


def derived(h, u, v):
    r = jnp.where(h > 0.0, lax.rsqrt(h), 0.0)
    s = h * r
    q = u * r
    p = v * r
    half = 0.5 * h * h
    return (h, u, v, s, q, p, q * q + half, p * p + half, q * p)


def along_x(c):
    return (c[0], c[1], c[2], c[3], c[4], c[5], c[6], c[8])


def along_y(c):
    return (c[0], c[2], c[1], c[3], c[5], c[4], c[7], c[8])


def flux(a, b):
    hl, nl, tl, sl, ql, pl_, fl, gl = a
    hr, nr, tr, sr, qr, pr, fr, gr = b
    both = jnp.minimum(hl, hr) > 0.0
    half = jnp.where(both, 0.5, 1.0)
    twice = half + half
    level = (hl + hr) * half
    rc = lax.rsqrt(level)
    c = level * rc
    total = sl + sr
    inv = pl.reciprocal(total, approx=True)
    inv = inv * (2.0 - total * inv)
    u = jnp.where(both, (ql + qr) * inv, 0.0)
    v = (pl_ + pr) * inv
    dh = jnp.where(both, hr - hl, 0.0)
    dn = (nr - nl) * twice
    dt = jnp.where(both, tr - tl, 0.0)
    mid = 0.5 * dh
    e = (0.5 * dn - u * mid) * rc
    s1 = u - c
    s3 = u + c
    b1 = jnp.abs(s1) * (mid - e)
    b3 = jnp.abs(s3) * (mid + e)
    b2 = jnp.abs(u) * (dt - v * dh)
    d = b1 + b3
    return (
        jnp.where(both, nl + nr, 0.0) - d,
        (fl + fr) * twice - (b1 * s1 + b3 * s3),
        jnp.where(both, gl + gr, 0.0) - (d * v + b2),
    )


CELL = 9


def stencil_kernel(opening, closing, *refs):
    fields = refs[:4]
    refs = refs[5:]
    above = () if opening else refs[:4]
    if not opening:
        refs = refs[8:]
    newh_ref, hu_ref, hv_ref, h_ref, token_ref = refs[:5]
    cell = refs[5:5 + CELL]
    gx = refs[5 + CELL:]
    step = pl.program_id(0)
    bands = pl.num_programs(0) - 1
    lane = iota((TILE, LANES), 1)

    def masked(d, m, x, y, at, cut):
        wet = m[at, cut] == 1
        return derived(*[jnp.where(wet, ref[at, cut], 0.0) for ref in (d, x, y)])

    def fill_band():
        def fill(t, carry):
            at = pl.ds(pl.multiple_of(t * TILE, TILE), TILE)
            to = pl.ds(pl.multiple_of(step * BAND + t * TILE + TILE, TILE), TILE)
            for g in range(GROUPS):
                cut = slice(g * LANES, (g + 1) * LANES)
                for dst, val in zip(cell, masked(*fields, at, cut)):
                    dst[g, to, :] = val
            return carry

        lax.fori_loop(0, BAND // TILE, fill, 0, unroll=8)

    if closing:
        pl.when(step < bands)(fill_band)
    else:
        fill_band()

    @pl.when(step == 0)
    def _():
        token_ref[0, 0] = 0
        if closing:
            for dst in cell:
                dst[:, dst.shape[1] - BAND:dst.shape[1] - BAND + TILE, :] = jnp.zeros(
                    (GROUPS, TILE, LANES), F32
                )
        if opening:
            for dst in gx:
                dst[:, 0:TILE, :] = jnp.zeros((GROUPS, TILE, LANES), F32)
        else:
            for g in range(GROUPS):
                cut = slice(g * LANES, (g + 1) * LANES)
                for dst, val in zip(cell, masked(*above, slice(None), cut)):
                    dst[g, 0:TILE, :] = val
                now = along_x([ref[g, 0:TILE, :] for ref in cell])
                nxt = along_x([ref[g, 1:TILE + 1, :] for ref in cell])
                for dst, val in zip(gx, flux(now, nxt)):
                    dst[g, 0:TILE, :] = val

    @pl.when(step > 0)
    def _():
        start = pl.multiple_of((step - 1) * BAND, BAND)

        def across(t, carry):
            base = pl.multiple_of(start + t * TILE + TILE, TILE)
            for g in range(GROUPS):
                now = along_x([ref[g, pl.ds(base, TILE), :] for ref in cell])
                nxt = along_x([ref[g, pl.ds(base + 1, TILE), :] for ref in cell])
                for dst, val in zip(gx, flux(now, nxt)):
                    dst[g, pl.ds(base, TILE), :] = val
            return carry

        lax.fori_loop(0, BAND // TILE, across, 0, unroll=8)

        if closing:
            @pl.when(step == bands)
            def _():
                for dst in gx:
                    at = dst.shape[1] - BAND - 1
                    dst[:, at:at + 1, :] = jnp.zeros((GROUPS, 1, LANES), F32)

        def body(t, carry):
            mark = pl.multiple_of(start + t * TILE, TILE)
            base = pl.multiple_of(mark + TILE, TILE)
            at = pl.ds(pl.multiple_of(t * TILE, TILE), TILE)
            before = [jnp.zeros((TILE, LANES), F32)] * 3
            for g in range(GROUPS):
                now = [ref[g, pl.ds(base, TILE), :] for ref in cell]
                if g < GROUPS - 1:
                    other = [ref[g + 1, pl.ds(base, TILE), :] for ref in cell[:3]]
                else:
                    other = now[:3]
                right = [
                    pltpu.roll(jnp.where(lane == 0, o, c), LANES - 1, 1)
                    for o, c in zip(other, now[:3])
                ]
                fy = flux(along_y(now), along_y(derived(*right)))
                if g == GROUPS - 1:
                    fy = [jnp.where(lane == LANES - 1, 0.0, val) for val in fy]
                py = [
                    pltpu.roll(jnp.where(lane == LANES - 1, o, c), 1, 1)
                    for o, c in zip(before, fy)
                ]
                before = fy
                fx = [src[g, pl.ds(base, TILE), :] for src in gx]
                px = [src[g, pl.ds(base - 1, TILE), :] for src in gx]
                h, u, v = now[:3]
                ch = (fx[0] - px[0]) + (fy[0] - py[0])
                cx = (fx[1] - px[1]) + (fy[2] - py[2])
                cy = (fx[2] - px[2]) + (fy[1] - py[1])
                newh_ref[at, g * LANES:(g + 1) * LANES] = jnp.where(
                    h > 0.0, h - (0.5 * DT_DX) * ch, 0.0
                )
                hu_ref[g, at, :] = u - (0.5 * DT_DX) * cx
                hv_ref[g, at, :] = v - (0.5 * DT_DX) * cy
                h_ref[g, at, :] = h
            return carry

        lax.fori_loop(0, BAND // TILE, body, 0, unroll=8)


def stencil(fields, after, first, count, old=()):
    rows, cols = fields[0].shape
    bands = rows // BAND
    opening = first == 0
    closing = first + count == bands
    plane = jax.ShapeDtypeStruct((GROUPS, rows, LANES), F32)
    scratch = pltpu.VMEM((GROUPS, (count + 1) * BAND + TILE, LANES), F32)
    band = pl.BlockSpec((BAND, cols), lambda i: (jnp.minimum(first + i, bands - 1), 0))
    above = pl.BlockSpec((TILE, cols), lambda i: (first * BAND // TILE - 1, 0))
    whole = pl.BlockSpec(memory_space=pl.ANY)
    part = pl.BlockSpec((GROUPS, BAND, LANES), lambda i: (0, first + jnp.maximum(i - 1, 0), 0))
    return pl.pallas_call(
        functools.partial(stencil_kernel, opening, closing),
        grid=(count + 1,),
        out_shape=(
            jax.ShapeDtypeStruct((rows, cols), F32), plane, plane, plane, TOKEN,
        ),
        in_specs=[band] * 4 + [whole] + ([] if opening else [above] * 4 + [whole] * 4),
        out_specs=(
            pl.BlockSpec((BAND, cols), lambda i: (first + jnp.maximum(i - 1, 0), 0)),
            part, part, part, SMEM,
        ),
        scratch_shapes=[scratch] * (CELL + 3),
        input_output_aliases={} if opening else {9 + n: n for n in range(4)},
        compiler_params=params(),
        cost_estimate=pl.CostEstimate(
            flops=200 * count * BAND * cols, bytes_accessed=64 * count * BAND * cols,
            transcendentals=0,
        ),
        name="stencil",
    )(*fields, after, *(() if opening else fields), *old)


def summed_of(lab, landed):
    select = (iota((NW * NPATCH, lab.shape[1]), 0) == lab).astype(BF16)
    return jnp.dot(select, landed, preferred_element_type=F32).astype(BF16)


def stack_left(left, summed, channels):
    for k in range(channels):
        for w in range(NW):
            left[k * NPATCH:(k + 1) * NPATCH, w * ABLK:(w + 1) * ABLK] = summed[
                w * NPATCH:(w + 1) * NPATCH, k * ABLK:(k + 1) * ABLK
            ]


PART = TILE * PATCH


def weight_parts(step, w_ref, held, arrived):
    width = held.shape[2]

    def copy(n):
        at = pl.ds(pl.multiple_of(n * width, width), width)
        return pltpu.make_async_copy(w_ref.at[:, at], held.at[n], arrived.at[n])

    @pl.when(step == 0)
    def _():
        for n in range(held.shape[0]):
            copy(n).start()

    return copy(step).wait


def spread_rows(acc, field, k):
    low = iota((TILE, LANES), 1) < LANES // 2
    for t in range(TILE // 2):
        cut = slice(t * LANES, (t + 1) * LANES)
        for half in range(HALVES):
            for g in range(GROUPS):
                base = k * NPATCH + 2 * g * BPX + half * TILE
                even = acc[base:base + TILE, cut]
                odd = acc[base + BPX:base + BPX + TILE, cut]
                for i, val in (
                    (2 * t, jnp.where(low, even, pltpu.roll(odd, LANES // 2, 1))),
                    (2 * t + 1, jnp.where(low, pltpu.roll(even, LANES // 2, 1), odd)),
                ):
                    field[g, pl.ds(half * TILE * TILE + i, TILE, stride=TILE), :] = val


def press_kernel(
    lab_ref, landed_ref, w_ref, top0_ref, bottom0_ref, left0_ref, right0_ref,
    out_ref, top_ref, bottom_ref, left_ref, right_ref, row_ref,
    held, arrived, left, acc, acc2, field, field2,
):
    step = pl.program_id(0)
    take = weight_parts(step, w_ref, held, arrived)

    @pl.when(step == 0)
    def _():
        peers, capacity = lab_ref.shape
        for d in range(peers):
            row_ref[:, d * capacity:(d + 1) * capacity] = lab_ref[d:d + 1, :]
        stack_left(left, summed_of(row_ref[...], landed_ref[...]), 1)

    take()
    acc[...] = jnp.dot(left[...], held[step, :, :PART], preferred_element_type=F32)
    acc2[...] = jnp.dot(left[...], held[step, :, PART:], preferred_element_type=F32)
    for part, (src, mid) in enumerate(((acc, field), (acc2, field2))):
        spread_rows(src, mid, 0)
        for g in range(GROUPS):
            for r in range(BPX):
                to = pl.ds(pl.multiple_of(TILE + r * PATCH + (2 * step + part) * TILE, TILE), TILE)
                out_ref[g, to, :] = mid[g, r * TILE:(r + 1) * TILE, :]

    @pl.when(step == pl.num_programs(0) - 1)
    def _():
        rows = out_ref.shape[1] - 2 * TILE
        mine = iota((TILE, LANES), 0) == 3
        blank = jnp.zeros((TILE, LANES), F32)
        for g in range(GROUPS):
            cut = slice(g * LANES, (g + 1) * LANES)
            head = pltpu.roll(out_ref[g, TILE:2 * TILE, :], 3, 0)
            tail = pltpu.roll(out_ref[g, rows:rows + TILE, :], 4, 0)
            out_ref[g, 0:TILE, :] = blank
            out_ref[g, rows + TILE:, :] = blank
            top_ref[:, cut] = jnp.where(mine, head, top0_ref[:, cut])
            bottom_ref[:, cut] = jnp.where(mine, tail, bottom0_ref[:, cut])
        lane = iota((LANES, LANES), 1)
        for b in range(rows // LANES):
            at = slice(b * LANES, (b + 1) * LANES)
            inner = slice(TILE + b * LANES, TILE + (b + 1) * LANES)
            packed = jnp.where(
                lane == TILE + 3,
                pltpu.roll(out_ref[GROUPS - 1, inner, :], TILE + 4, 1),
                pltpu.roll(out_ref[0, inner, :], 3, 1),
            )
            turned = packed.T
            left_ref[:, at] = jnp.where(mine, turned[0:TILE], left0_ref[:, at])
            right_ref[:, at] = jnp.where(mine, turned[TILE:2 * TILE], right0_ref[:, at])


def pressure_field(lab, landed, weights, edges):
    steps = PATCH // (2 * TILE)
    rows = BPX * PATCH
    line = (TILE, BPY * PATCH)
    column = (TILE, rows)
    whole = (GROUPS, rows + 2 * TILE, LANES)

    def const(shape):
        return pl.BlockSpec(shape, lambda i: (0,) * len(shape))

    return pl.pallas_call(
        press_kernel,
        grid=(steps,),
        out_shape=tuple(jax.ShapeDtypeStruct(x, F32) for x in (whole, line, line, column, column))
        + (jax.ShapeDtypeStruct((1, lab.size), jnp.int32),),
        in_specs=[
            const(lab.shape),
            const(landed.shape),
            pl.BlockSpec(memory_space=pl.ANY),
        ] + [const(x) for x in (line, line, column, column)],
        out_specs=tuple(const(x) for x in (whole, line, line, column, column, (1, lab.size))),
        scratch_shapes=[
            pltpu.VMEM((steps, NW * ABLK, 2 * PART), BF16),
            pltpu.SemaphoreType.DMA((steps,)),
            pltpu.VMEM((NPATCH, NW * ABLK), BF16),
            pltpu.VMEM((NPATCH, PART), F32),
            pltpu.VMEM((NPATCH, PART), F32),
            pltpu.VMEM((GROUPS, BPX * TILE, LANES), F32),
            pltpu.VMEM((GROUPS, BPX * TILE, LANES), F32),
        ],
        compiler_params=params(),
        cost_estimate=pl.CostEstimate(
            flops=2 * NPATCH * NW * ABLK * PATCH * PATCH, bytes_accessed=12 << 20, transcendentals=0
        ),
        name="pressure",
    )(lab, landed, weights, *edges)


def border_places(rows, cols):
    middle = pl.ds(LANES, cols - 2 * LANES)
    return (
        (slice(None), pl.ds(0, LANES)),
        (slice(None), pl.ds(cols - LANES, LANES)),
        (pl.ds(0, TILE), middle),
        (pl.ds(rows - TILE, TILE), middle),
    )


def border_additions(halos, edges, edge, sides, ends):
    up_ref, dn_ref, lh_ref, rh_ref = halos
    top_ref, bottom_ref, left_ref, right_ref = edges

    def cells(ref):
        return derived(ref[0:1, :], ref[1:2, :], ref[2:3, :])

    pull = TIME_STEP * PRESS * 0.5
    step = 0.5 * DT_DX
    for out, turned in ((edge, along_y), (ends, along_x)):
        out[...] = jnp.zeros_like(out)
        far_low, far_high, own_low, own_high = (
            (lh_ref, rh_ref, left_ref, right_ref) if out is edge
            else (up_ref, dn_ref, top_ref, bottom_ref)
        )
        for at, before, after, own, far, sign in (
            (0, far_low, own_low, own_low, far_low, 1.0),
            (3, own_high, far_high, own_high, far_high, -1.0),
        ):
            gh, gn, gt = flux(turned(cells(before)), turned(cells(after)))
            wet = own[0:1, :] > 0.0
            normal = gn * step + (pull * own[0:1, :]) * far[3:4, :]
            pair = (gt * step, normal) if out is edge else (normal, gt * step)
            for f, val in enumerate((gh * step,) + pair):
                out[at + f:at + f + 1, :] = jnp.where(wet, sign * val, 0.0)
    blank = jnp.zeros((LANES - TILE, LANES), F32)
    for b in range(sides.shape[0] // LANES):
        cut = slice(b * LANES, (b + 1) * LANES)
        sides[cut, :] = jnp.concatenate([edge[:, cut], blank], axis=0).T


def patch_border(parts, sides, ends):
    first, last, head, tail = parts
    rows = first.shape[0]
    cols = ends.shape[1]
    lane = iota((rows, LANES), 1)
    values = sides[...]
    first[...] += jnp.where(lane == 0, values, 0.0)
    last[...] += jnp.where(lane == LANES - 1, pltpu.roll(values, LANES - 4, 1), 0.0)
    for at, line in ((0, 0), (rows - 1, 3)):
        first[at:at + 1, :] += ends[line:line + 1, 0:LANES]
        last[at:at + 1, :] += ends[line:line + 1, cols - LANES:cols]
    head[0:1, :] += ends[0:1, LANES:cols - LANES]
    tail[TILE - 1:TILE, :] += ends[3:4, LANES:cols - LANES]


def finish_kernel(
    lab_ref, landed_ref, w_ref, p_ref, up_ref, dn_ref, lh_ref, rh_ref,
    top_ref, bottom_ref, left_ref, right_ref, old_ref,
    hu_ref, hv_ref, h_ref, ox_ref, oy_ref, new_ref,
    held, arrived, left, acc, acc2, fx, fy, fx2, fy2,
    edge, sides_ref, ends_ref, first, last, head, tail, loaded, saved,
):
    step = pl.program_id(0)
    take = weight_parts(step, w_ref, held, arrived)
    parts = (first, last, head, tail)
    places = border_places(*old_ref.shape)
    loads = [
        pltpu.make_async_copy(old_ref.at[at], part, loaded.at[n])
        for n, (at, part) in enumerate(zip(places, parts))
    ]
    saves = [
        pltpu.make_async_copy(part, new_ref.at[at], saved.at[n])
        for n, (at, part) in enumerate(zip(places, parts))
    ]

    @pl.when(step == 0)
    def _():
        for copy in loads:
            copy.start()
        border_additions(
            (up_ref, dn_ref, lh_ref, rh_ref), (top_ref, bottom_ref, left_ref, right_ref),
            edge, sides_ref, ends_ref,
        )
        stack_left(left, summed_of(lab_ref[...], landed_ref[...]), 2)

    take()
    acc[...] = jnp.dot(left[...], held[step, :, :PART], preferred_element_type=F32)
    acc2[...] = jnp.dot(left[...], held[step, :, PART:], preferred_element_type=F32)
    lane = iota((TILE, LANES), 1)
    for part, (src, mx, my) in enumerate(((acc, fx, fy), (acc2, fx2, fy2))):
        spread_rows(src, mx, 0)
        spread_rows(src, my, 1)
        cells = slice(part * TILE, (part + 1) * TILE)
        for r in range(BPX):
            at = slice(r * TILE, (r + 1) * TILE)
            mark = pl.multiple_of(r * PATCH + (2 * step + part) * TILE, TILE)
            base = pl.multiple_of(mark + TILE, TILE)
            ends = sides_ref[pl.ds(mark, TILE), :]
            tiles = [p_ref[g, pl.ds(base, TILE), :] for g in range(GROUPS)]
            for g in range(GROUPS):
                before = tiles[g - 1] if g else 0.0
                after = tiles[g + 1] if g < GROUPS - 1 else 0.0
                prev = pltpu.roll(jnp.where(lane == LANES - 1, before, tiles[g]), 1, 1)
                nxt = pltpu.roll(jnp.where(lane == 0, after, tiles[g]), LANES - 1, 1)
                h = h_ref[g, r, cells, :]
                wet = h > 0.0
                scale = (TIME_STEP * PRESS * 0.5) * h
                gx = p_ref[g, pl.ds(base + 1, TILE), :] - p_ref[g, pl.ds(base - 1, TILE), :]
                wx = mx[g, at, :]
                wy = my[g, at, :]
                power = wx * wx + wy * wy
                speed = jnp.where(power > 0.0, power * lax.rsqrt(power), 0.0) * (TIME_STEP * STRESS)
                new = [
                    hu_ref[g, r, cells, :] - scale * gx + speed * wx,
                    hv_ref[g, r, cells, :] - scale * (nxt - prev) + speed * wy,
                ]
                for own, edge, shift in ((0, 0, 1), (GROUPS - 1, LANES - 1, 4)):
                    if g == own:
                        new = [
                            jnp.where(
                                lane == edge,
                                a + pltpu.roll(ends, (edge - shift - f) % LANES, 1),
                                a,
                            )
                            for f, a in enumerate(new)
                        ]
                cut = slice(g * LANES, (g + 1) * LANES)
                ox_ref[r, cells, cut] = jnp.where(wet, new[0], 0.0)
                oy_ref[r, cells, cut] = jnp.where(wet, new[1], 0.0)

    @pl.when(step == 1)
    def _():
        for copy in loads:
            copy.wait()
        patch_border(parts, sides_ref, ends_ref)
        for copy in saves:
            copy.start()

    @pl.when(step == 0)
    def _():
        ox_ref[0, 0:1, :] += ends_ref[1:2, :]
        oy_ref[0, 0:1, :] += ends_ref[2:3, :]

    @pl.when(step == pl.num_programs(0) - 1)
    def _():
        deep = ox_ref.shape[1]
        ox_ref[BPX - 1, deep - 1:deep, :] += ends_ref[4:5, :]
        oy_ref[BPX - 1, deep - 1:deep, :] += ends_ref[5:6, :]
        for copy in saves:
            copy.wait()


def finish(lab, landed, weights, p, halos, edges, newh, hu, hv, h):
    deep = 2 * TILE
    steps = PATCH // deep
    cols = BPY * PATCH
    split = (GROUPS, BPX, PATCH, LANES)
    slab = pl.BlockSpec((GROUPS, BPX, deep, LANES), lambda i: (0, 0, i, 0))
    out = pl.BlockSpec((BPX, deep, cols), lambda i: (0, i, 0))
    shape = jax.ShapeDtypeStruct((BPX, PATCH, cols), F32)
    rows = newh.shape[0]
    whole = pl.BlockSpec(memory_space=pl.ANY)
    field = pltpu.VMEM((GROUPS, BPX * TILE, LANES), F32)

    def const(x):
        return pl.BlockSpec(x.shape, lambda i: (0,) * x.ndim)

    return pl.pallas_call(
        finish_kernel,
        grid=(steps,),
        out_shape=(shape, shape, jax.ShapeDtypeStruct(newh.shape, F32)),
        in_specs=[
            const(lab), const(landed),
            whole,
            const(p), *[const(x) for x in (*halos, *edges)], whole,
            slab, slab, slab,
        ],
        out_specs=(out, out, whole),
        input_output_aliases={12: 2},
        scratch_shapes=[
            pltpu.VMEM((steps, NW * ABLK, 2 * PART), BF16),
            pltpu.SemaphoreType.DMA((steps,)),
            pltpu.VMEM((2 * NPATCH, NW * ABLK), BF16),
            pltpu.VMEM((2 * NPATCH, PART), F32),
            pltpu.VMEM((2 * NPATCH, PART), F32),
            field, field, field, field,
            pltpu.VMEM((TILE, rows), F32),
            pltpu.VMEM((rows, LANES), F32),
            pltpu.VMEM((TILE, cols), F32),
            pltpu.VMEM((rows, LANES), F32),
            pltpu.VMEM((rows, LANES), F32),
            pltpu.VMEM((TILE, cols - 2 * LANES), F32),
            pltpu.VMEM((TILE, cols - 2 * LANES), F32),
            pltpu.SemaphoreType.DMA((4,)),
            pltpu.SemaphoreType.DMA((4,)),
        ],
        compiler_params=params(),
        cost_estimate=pl.CostEstimate(
            flops=4 * NPATCH * NW * ABLK * PATCH * PATCH, bytes_accessed=20 << 20, transcendentals=0
        ),
        name="finish",
    )(
        lab, landed, weights, p, *halos, *edges, newh,
        hu.reshape(split), hv.reshape(split), h.reshape(split),
    )


def body(
    atm_blocks,
    remap_weights,
    ovl_source,
    ovl_block,
    ovl_patch,
    ovl_weight,
    depth_field,
    wet_mask,
    mom_x,
    mom_y,
    blend,
):
    count_x = lax.axis_size("gx")
    count_y = lax.axis_size("gy")
    devices = count_x * count_y
    entries = ovl_source.size
    capacity = 2 * entries // devices
    slots = devices * capacity
    atm = atm_blocks.reshape(atm_blocks.shape[2:]).transpose(1, 0, 2)
    both = ("gx", "gy")
    want, lab = make_requests(
        ovl_source.reshape(1, entries), ovl_block.reshape(1, entries),
        ovl_patch.reshape(1, entries), ovl_weight.reshape(1, entries), devices, capacity,
    )
    asked = lax.all_to_all(
        want.reshape(devices, 1, capacity), both, split_axis=0, concat_axis=0, tiled=True
    )
    press, wind = mix(blend.reshape(1), atm)
    top, bottom, left, right, placed = edge_cells(depth_field, wet_mask, mom_x, mom_y)

    def exchange(after, tiles):
        rows = serve(after, asked, tiles)
        parts = rows.reshape(devices, capacity, rows.shape[1])
        got = lax.all_to_all(parts, both, split_axis=0, concat_axis=0, tiled=True)
        return got.reshape(rows.shape)

    press = exchange(placed, press)
    fields = (depth_field, wet_mask, mom_x, mom_y)
    bands = depth_field.shape[0] // BAND
    ahead = bands * 5 // 8
    *planes, token = stencil(fields, lab, 0, ahead)
    wind = exchange(token, wind)
    weights = remap_weights.reshape(NW * ABLK, PATCH * PATCH)
    p, *edges, lab = pressure_field(lab, press, weights, (top, bottom, left, right))
    top, bottom, left, right = edges
    halos = (
        send(bottom, "gx", 1), send(top, "gx", -1), send(right, "gy", 1), send(left, "gy", -1),
    )
    newh, hu, hv, h, _ = stencil(fields, top, ahead, bands - ahead, planes)
    new_x, new_y, newh = finish(lab, wind, weights, p, halos, edges, newh, hu, hv, h)
    return (newh, new_x.reshape(newh.shape), new_y.reshape(newh.shape))


def solution(mesh):
    placed = (
        P("gx", "gy", None, None, None),
        P(),
        P("gx", "gy", None, None),
        P("gx", "gy", None),
        P("gx", "gy", None),
        P("gx", "gy", None),
        P("gx", "gy"),
        P("gx", "gy"),
        P("gx", "gy"),
        P("gx", "gy"),
        P(),
    )
    return jax.shard_map(
        body,
        mesh=mesh,
        in_specs=placed,
        out_specs=(P("gx", "gy"), P("gx", "gy"), P("gx", "gy")),
        check_vma=False,
    )
```

```python
import functools

import jax
import jax.numpy as jnp
from jax import lax
from jax.experimental import pallas as pl
from jax.experimental.pallas import tpu as pltpu
from jax.sharding import PartitionSpec as P

PATCH = 64
ABLK = 256
NW = 4
BPX = 16
BPY = 8
NPATCH = BPX * BPY

GRAV = 1.0
DT_DX = 0.2
TIME_STEP = 0.2
STRESS = 0.5
PRESS = 0.5

F32 = jnp.float32
BF16 = jnp.bfloat16
VMEM = pl.BlockSpec(memory_space=pltpu.VMEM)
SMEM = pl.BlockSpec(memory_space=pltpu.SMEM)
LANES = 128
TOKEN = jax.ShapeDtypeStruct((1, 1), jnp.int32)
TILE = 8
GROUPS = BPY * PATCH // LANES
HALVES = BPX // TILE
BAND = 128


def params(limit=56 << 20, **kw):
    return pltpu.CompilerParams(vmem_limit_bytes=limit, **kw)


def iota(shape, dim):
    return lax.broadcasted_iota(jnp.int32, shape, dim)


def rank_kernel(capacity, src_ref, blk_ref, pat_ref, wgt_ref, want_ref, lab_ref):
    devices = want_ref.shape[0]
    src = src_ref[...]
    ent = src.shape[1]
    hits = (iota((devices, ent), 0) == src).astype(F32)
    order = (iota((ent, ent), 0) <= iota((ent, ent), 1)).astype(BF16)
    ranks = jnp.dot(hits.astype(BF16), order, preferred_element_type=F32)
    mine = jnp.sum(hits * ranks, axis=0, keepdims=True).astype(jnp.int32) - 1
    place = iota((capacity, ent), 0) == mine
    pat = pat_ref[...]
    row_bits = BPX.bit_length() - 1
    col_bits = BPY.bit_length() - 1
    rows = jnp.zeros_like(pat)
    cols = jnp.zeros_like(pat)
    used_r = used_c = position = 0
    while used_r < row_bits or used_c < col_bits:
        value = jnp.bitwise_and(jnp.right_shift(pat, position), 1)
        if used_r < row_bits and (used_c >= col_bits or position % 2 == 0):
            rows = rows + value * (1 << used_r)
            used_r += 1
        else:
            cols = cols + value * (1 << used_c)
            used_c += 1
        position += 1

    def spread(row):
        picked = jnp.where(place, row.astype(F32), 0.0).astype(BF16)
        return lax.dot_general(
            hits.astype(BF16), picked, (((1,), (1,)), ((), ())),
            preferred_element_type=F32,
        ).astype(jnp.int32)

    want_ref[...] = spread(blk_ref[...])
    slot = spread(cols * BPX + rows)
    group = spread(wgt_ref[...] + 1)
    lab_ref[...] = jnp.where(group > 0, (group - 1) * NPATCH + slot, -1)


def make_requests(src, blk, pat, wgt, devices, capacity):
    shape = jax.ShapeDtypeStruct((devices, capacity), jnp.int32)
    return pl.pallas_call(
        functools.partial(rank_kernel, capacity),
        out_shape=(shape, shape),
        in_specs=[VMEM] * 4,
        out_specs=(VMEM, VMEM),
        compiler_params=params(),
        name="requests",
    )(src, blk, pat, wgt)


def mix_kernel(blend_ref, atm_ref, press_ref, wind_ref):
    blend = blend_ref[0]
    keep = 1.0 - blend

    def mixed(k):
        first = atm_ref[k].astype(F32)
        second = atm_ref[3 + k].astype(F32)
        return (keep * first + blend * second).astype(BF16)

    press_ref[...] = mixed(2)
    for k in range(2):
        wind_ref[:, k * ABLK:(k + 1) * ABLK] = mixed(k)


def mix(blend, atm):
    blocks = atm.shape[1]
    return pl.pallas_call(
        mix_kernel,
        out_shape=(
            jax.ShapeDtypeStruct((blocks, ABLK), BF16),
            jax.ShapeDtypeStruct((blocks, 2 * ABLK), BF16),
        ),
        in_specs=[SMEM, VMEM],
        out_specs=(VMEM, VMEM),
        compiler_params=params(),
        name="mix",
    )(blend, atm)


def serve_kernel(after_ref, asked_ref, tiles_ref, out_ref, turned, pick):
    peers, _, capacity = asked_ref.shape
    width = turned.shape[0]
    turned[...] = jnp.zeros_like(turned)
    turned[0:peers, 0:capacity] = asked_ref[:, 0, :]
    columns = turned[...].T
    blocks = tiles_ref.shape[0]
    names = iota((capacity, blocks), 1)
    for d in range(peers):
        pick[d * capacity:(d + 1) * capacity, :] = (columns[0:capacity, d:d + 1] == names).astype(F32)
    out_ref[...] = jnp.dot(
        pick[...].astype(BF16), tiles_ref[...], preferred_element_type=F32
    ).astype(BF16)


def serve(after, asked, tiles):
    peers, _, capacity = asked.shape
    slots = peers * capacity
    width = -(-max(peers, capacity) // LANES) * LANES
    return pl.pallas_call(
        serve_kernel,
        out_shape=jax.ShapeDtypeStruct((slots, tiles.shape[1]), BF16),
        in_specs=[SMEM, VMEM, VMEM],
        out_specs=VMEM,
        scratch_shapes=[
            pltpu.VMEM((width, width), jnp.int32),
            pltpu.VMEM((slots, tiles.shape[0]), F32),
        ],
        compiler_params=params(32 << 20),
        name="serve",
    )(after, asked, tiles)


def edges_kernel(
    dl, ml, xl, yl, dr, mr, xr, yr, dt, mt, xt, yt, db, mb, xb, yb,
    top_ref, bottom_ref, left_ref, right_ref, token_ref,
):
    token_ref[0, 0] = 0

    def rows(d, m, x, y, at, out):
        wet = m[...] == 1
        for f, ref in enumerate((d, x, y)):
            out[f:f + 1, :] = jnp.where(wet, ref[...], 0.0)[at:at + 1]

    rows(dt, mt, xt, yt, 0, top_ref)
    rows(db, mb, xb, yb, TILE - 1, bottom_ref)
    lane = iota((LANES, LANES), 1)

    def step(b, carry):
        at = pl.ds(pl.multiple_of(b * LANES, LANES), LANES)
        wl = ml[at, :] == 1
        wr = mr[at, :] == 1
        packed = jnp.where(wl, dl[at, :], 0.0)
        packed = jnp.where(lane == 1, pltpu.roll(jnp.where(wl, xl[at, :], 0.0), 1, 1), packed)
        packed = jnp.where(lane == 2, pltpu.roll(jnp.where(wl, yl[at, :], 0.0), 2, 1), packed)
        packed = jnp.where(lane == 8, pltpu.roll(jnp.where(wr, dr[at, :], 0.0), 9, 1), packed)
        packed = jnp.where(lane == 9, pltpu.roll(jnp.where(wr, xr[at, :], 0.0), 10, 1), packed)
        packed = jnp.where(lane == 10, pltpu.roll(jnp.where(wr, yr[at, :], 0.0), 11, 1), packed)
        turned = packed.T
        left_ref[:, at] = turned[0:TILE]
        right_ref[:, at] = turned[TILE:2 * TILE]
        return carry

    lax.fori_loop(0, dl.shape[0] // LANES, step, 0)


def edge_cells(depth, mask, momx, momy):
    rows, cols = depth.shape
    fields = (depth, mask, momx, momy)
    left = pl.BlockSpec((rows, LANES), lambda i: (0, 0))
    right = pl.BlockSpec((rows, LANES), lambda i: (0, cols // LANES - 1))
    top = pl.BlockSpec((TILE, cols), lambda i: (0, 0))
    bottom = pl.BlockSpec((TILE, cols), lambda i: (rows // TILE - 1, 0))
    line = jax.ShapeDtypeStruct((TILE, cols), F32)
    column = jax.ShapeDtypeStruct((TILE, rows), F32)
    return pl.pallas_call(
        edges_kernel,
        grid=(1,),
        out_shape=(line, line, column, column, TOKEN),
        in_specs=[left] * 4 + [right] * 4 + [top] * 4 + [bottom] * 4,
        out_specs=(
            pl.BlockSpec((TILE, cols), lambda i: (0, 0)),
            pl.BlockSpec((TILE, cols), lambda i: (0, 0)),
            pl.BlockSpec((TILE, rows), lambda i: (0, 0)),
            pl.BlockSpec((TILE, rows), lambda i: (0, 0)),
            SMEM,
        ),
        compiler_params=params(),
        name="edges",
    )(*(fields * 4))


def send(value, axis, step):
    count = lax.axis_size(axis)
    if step > 0:
        pairs = [(i, i + 1) for i in range(count - 1)]
    else:
        pairs = [(i + 1, i) for i in range(count - 1)]
    return lax.ppermute(value, axis, pairs)


def derived(h, u, v):
    r = jnp.where(h > 0.0, lax.rsqrt(h), 0.0)
    s = h * r
    q = u * r
    p = v * r
    half = 0.5 * h * h
    return (h, u, v, s, q, p, q * q + half, p * p + half, q * p)


def along_x(c):
    return (c[0], c[1], c[2], c[3], c[4], c[5], c[6], c[8])


def along_y(c):
    return (c[0], c[2], c[1], c[3], c[5], c[4], c[7], c[8])


def flux(a, b):
    hl, nl, tl, sl, ql, pl_, fl, gl = a
    hr, nr, tr, sr, qr, pr, fr, gr = b
    both = jnp.minimum(hl, hr) > 0.0
    half = jnp.where(both, 0.5, 1.0)
    twice = half + half
    level = (hl + hr) * half
    rc = lax.rsqrt(level)
    c = level * rc
    total = sl + sr
    inv = pl.reciprocal(total, approx=True)
    inv = inv * (2.0 - total * inv)
    u = jnp.where(both, (ql + qr) * inv, 0.0)
    v = (pl_ + pr) * inv
    dh = jnp.where(both, hr - hl, 0.0)
    dn = (nr - nl) * twice
    dt = jnp.where(both, tr - tl, 0.0)
    mid = 0.5 * dh
    e = (0.5 * dn - u * mid) * rc
    s1 = u - c
    s3 = u + c
    b1 = jnp.abs(s1) * (mid - e)
    b3 = jnp.abs(s3) * (mid + e)
    b2 = jnp.abs(u) * (dt - v * dh)
    d = b1 + b3
    return (
        jnp.where(both, nl + nr, 0.0) - d,
        (fl + fr) * twice - (b1 * s1 + b3 * s3),
        jnp.where(both, gl + gr, 0.0) - (d * v + b2),
    )


CELL = 9


def stencil_kernel(opening, closing, *refs):
    fields = refs[:4]
    refs = refs[5:]
    above = () if opening else refs[:4]
    if not opening:
        refs = refs[8:]
    newh_ref, hu_ref, hv_ref, h_ref, token_ref = refs[:5]
    cell = refs[5:5 + CELL]
    gx = refs[5 + CELL:]
    step = pl.program_id(0)
    bands = pl.num_programs(0) - 1
    lane = iota((TILE, LANES), 1)

    def masked(d, m, x, y, at, cut):
        wet = m[at, cut] == 1
        return derived(*[jnp.where(wet, ref[at, cut], 0.0) for ref in (d, x, y)])

    def fill_band():
        def fill(t, carry):
            at = pl.ds(pl.multiple_of(t * TILE, TILE), TILE)
            to = pl.ds(pl.multiple_of(step * BAND + t * TILE + TILE, TILE), TILE)
            for g in range(GROUPS):
                cut = slice(g * LANES, (g + 1) * LANES)
                for dst, val in zip(cell, masked(*fields, at, cut)):
                    dst[g, to, :] = val
            return carry

        lax.fori_loop(0, BAND // TILE, fill, 0, unroll=8)

    if closing:
        pl.when(step < bands)(fill_band)
    else:
        fill_band()

    @pl.when(step == 0)
    def _():
        token_ref[0, 0] = 0
        if closing:
            for dst in cell:
                dst[:, dst.shape[1] - BAND:dst.shape[1] - BAND + TILE, :] = jnp.zeros(
                    (GROUPS, TILE, LANES), F32
                )
        if opening:
            for dst in gx:
                dst[:, 0:TILE, :] = jnp.zeros((GROUPS, TILE, LANES), F32)
        else:
            for g in range(GROUPS):
                cut = slice(g * LANES, (g + 1) * LANES)
                for dst, val in zip(cell, masked(*above, slice(None), cut)):
                    dst[g, 0:TILE, :] = val
                now = along_x([ref[g, 0:TILE, :] for ref in cell])
                nxt = along_x([ref[g, 1:TILE + 1, :] for ref in cell])
                for dst, val in zip(gx, flux(now, nxt)):
                    dst[g, 0:TILE, :] = val

    @pl.when(step > 0)
    def _():
        start = pl.multiple_of((step - 1) * BAND, BAND)

        def across(t, carry):
            base = pl.multiple_of(start + t * TILE + TILE, TILE)
            for g in range(GROUPS):
                now = along_x([ref[g, pl.ds(base, TILE), :] for ref in cell])
                nxt = along_x([ref[g, pl.ds(base + 1, TILE), :] for ref in cell])
                for dst, val in zip(gx, flux(now, nxt)):
                    dst[g, pl.ds(base, TILE), :] = val
            return carry

        lax.fori_loop(0, BAND // TILE, across, 0, unroll=8)

        if closing:
            @pl.when(step == bands)
            def _():
                for dst in gx:
                    at = dst.shape[1] - BAND - 1
                    dst[:, at:at + 1, :] = jnp.zeros((GROUPS, 1, LANES), F32)

        def body(t, carry):
            mark = pl.multiple_of(start + t * TILE, TILE)
            base = pl.multiple_of(mark + TILE, TILE)
            at = pl.ds(pl.multiple_of(t * TILE, TILE), TILE)
            before = [jnp.zeros((TILE, LANES), F32)] * 3
            for g in range(GROUPS):
                now = [ref[g, pl.ds(base, TILE), :] for ref in cell]
                if g < GROUPS - 1:
                    other = [ref[g + 1, pl.ds(base, TILE), :] for ref in cell[:3]]
                else:
                    other = now[:3]
                right = [
                    pltpu.roll(jnp.where(lane == 0, o, c), LANES - 1, 1)
                    for o, c in zip(other, now[:3])
                ]
                fy = flux(along_y(now), along_y(derived(*right)))
                if g == GROUPS - 1:
                    fy = [jnp.where(lane == LANES - 1, 0.0, val) for val in fy]
                py = [
                    pltpu.roll(jnp.where(lane == LANES - 1, o, c), 1, 1)
                    for o, c in zip(before, fy)
                ]
                before = fy
                fx = [src[g, pl.ds(base, TILE), :] for src in gx]
                px = [src[g, pl.ds(base - 1, TILE), :] for src in gx]
                h, u, v = now[:3]
                ch = (fx[0] - px[0]) + (fy[0] - py[0])
                cx = (fx[1] - px[1]) + (fy[2] - py[2])
                cy = (fx[2] - px[2]) + (fy[1] - py[1])
                newh_ref[at, g * LANES:(g + 1) * LANES] = jnp.where(
                    h > 0.0, h - (0.5 * DT_DX) * ch, 0.0
                )
                hu_ref[g, at, :] = u - (0.5 * DT_DX) * cx
                hv_ref[g, at, :] = v - (0.5 * DT_DX) * cy
                h_ref[g, at, :] = h
            return carry

        lax.fori_loop(0, BAND // TILE, body, 0, unroll=8)


def stencil(fields, after, first, count, old=()):
    rows, cols = fields[0].shape
    bands = rows // BAND
    opening = first == 0
    closing = first + count == bands
    plane = jax.ShapeDtypeStruct((GROUPS, rows, LANES), F32)
    scratch = pltpu.VMEM((GROUPS, (count + 1) * BAND + TILE, LANES), F32)
    band = pl.BlockSpec((BAND, cols), lambda i: (jnp.minimum(first + i, bands - 1), 0))
    above = pl.BlockSpec((TILE, cols), lambda i: (first * BAND // TILE - 1, 0))
    whole = pl.BlockSpec(memory_space=pl.ANY)
    part = pl.BlockSpec((GROUPS, BAND, LANES), lambda i: (0, first + jnp.maximum(i - 1, 0), 0))
    return pl.pallas_call(
        functools.partial(stencil_kernel, opening, closing),
        grid=(count + 1,),
        out_shape=(
            jax.ShapeDtypeStruct((rows, cols), F32), plane, plane, plane, TOKEN,
        ),
        in_specs=[band] * 4 + [whole] + ([] if opening else [above] * 4 + [whole] * 4),
        out_specs=(
            pl.BlockSpec((BAND, cols), lambda i: (first + jnp.maximum(i - 1, 0), 0)),
            part, part, part, SMEM,
        ),
        scratch_shapes=[scratch] * (CELL + 3),
        input_output_aliases={} if opening else {9 + n: n for n in range(4)},
        compiler_params=params(),
        cost_estimate=pl.CostEstimate(
            flops=200 * count * BAND * cols, bytes_accessed=64 * count * BAND * cols,
            transcendentals=0,
        ),
        name="stencil",
    )(*fields, after, *(() if opening else fields), *old)


def summed_of(lab, landed):
    select = (iota((NW * NPATCH, lab.shape[1]), 0) == lab).astype(BF16)
    return jnp.dot(select, landed, preferred_element_type=F32).astype(BF16)


def stack_left(left, summed, channels):
    for k in range(channels):
        for w in range(NW):
            left[k * NPATCH:(k + 1) * NPATCH, w * ABLK:(w + 1) * ABLK] = summed[
                w * NPATCH:(w + 1) * NPATCH, k * ABLK:(k + 1) * ABLK
            ]


PART = TILE * PATCH


def weight_parts(step, w_ref, held, arrived):
    width = held.shape[2]

    def copy(n):
        at = pl.ds(pl.multiple_of(n * width, width), width)
        return pltpu.make_async_copy(w_ref.at[:, at], held.at[n], arrived.at[n])

    @pl.when(step == 0)
    def _():
        for n in range(held.shape[0]):
            copy(n).start()

    return copy(step).wait


def spread_rows(acc, field, k):
    low = iota((TILE, LANES), 1) < LANES // 2
    for t in range(TILE // 2):
        cut = slice(t * LANES, (t + 1) * LANES)
        for half in range(HALVES):
            for g in range(GROUPS):
                base = k * NPATCH + 2 * g * BPX + half * TILE
                even = acc[base:base + TILE, cut]
                odd = acc[base + BPX:base + BPX + TILE, cut]
                for i, val in (
                    (2 * t, jnp.where(low, even, pltpu.roll(odd, LANES // 2, 1))),
                    (2 * t + 1, jnp.where(low, pltpu.roll(even, LANES // 2, 1), odd)),
                ):
                    field[g, pl.ds(half * TILE * TILE + i, TILE, stride=TILE), :] = val


def press_kernel(
    lab_ref, landed_ref, w_ref, top0_ref, bottom0_ref, left0_ref, right0_ref,
    out_ref, top_ref, bottom_ref, left_ref, right_ref, row_ref,
    held, arrived, left, acc, acc2, field, field2,
):
    step = pl.program_id(0)
    take = weight_parts(step, w_ref, held, arrived)

    @pl.when(step == 0)
    def _():
        peers, capacity = lab_ref.shape
        for d in range(peers):
            row_ref[:, d * capacity:(d + 1) * capacity] = lab_ref[d:d + 1, :]
        stack_left(left, summed_of(row_ref[...], landed_ref[...]), 1)

    take()
    acc[...] = jnp.dot(left[...], held[step, :, :PART], preferred_element_type=F32)
    acc2[...] = jnp.dot(left[...], held[step, :, PART:], preferred_element_type=F32)
    for part, (src, mid) in enumerate(((acc, field), (acc2, field2))):
        spread_rows(src, mid, 0)
        for g in range(GROUPS):
            for r in range(BPX):
                to = pl.ds(pl.multiple_of(TILE + r * PATCH + (2 * step + part) * TILE, TILE), TILE)
                out_ref[g, to, :] = mid[g, r * TILE:(r + 1) * TILE, :]

    @pl.when(step == pl.num_programs(0) - 1)
    def _():
        rows = out_ref.shape[1] - 2 * TILE
        mine = iota((TILE, LANES), 0) == 3
        blank = jnp.zeros((TILE, LANES), F32)
        for g in range(GROUPS):
            cut = slice(g * LANES, (g + 1) * LANES)
            head = pltpu.roll(out_ref[g, TILE:2 * TILE, :], 3, 0)
            tail = pltpu.roll(out_ref[g, rows:rows + TILE, :], 4, 0)
            out_ref[g, 0:TILE, :] = blank
            out_ref[g, rows + TILE:, :] = blank
            top_ref[:, cut] = jnp.where(mine, head, top0_ref[:, cut])
            bottom_ref[:, cut] = jnp.where(mine, tail, bottom0_ref[:, cut])
        lane = iota((LANES, LANES), 1)
        for b in range(rows // LANES):
            at = slice(b * LANES, (b + 1) * LANES)
            inner = slice(TILE + b * LANES, TILE + (b + 1) * LANES)
            packed = jnp.where(
                lane == TILE + 3,
                pltpu.roll(out_ref[GROUPS - 1, inner, :], TILE + 4, 1),
                pltpu.roll(out_ref[0, inner, :], 3, 1),
            )
            turned = packed.T
            left_ref[:, at] = jnp.where(mine, turned[0:TILE], left0_ref[:, at])
            right_ref[:, at] = jnp.where(mine, turned[TILE:2 * TILE], right0_ref[:, at])


def pressure_field(lab, landed, weights, edges):
    steps = PATCH // (2 * TILE)
    rows = BPX * PATCH
    line = (TILE, BPY * PATCH)
    column = (TILE, rows)
    whole = (GROUPS, rows + 2 * TILE, LANES)

    def const(shape):
        return pl.BlockSpec(shape, lambda i: (0,) * len(shape))

    return pl.pallas_call(
        press_kernel,
        grid=(steps,),
        out_shape=tuple(jax.ShapeDtypeStruct(x, F32) for x in (whole, line, line, column, column))
        + (jax.ShapeDtypeStruct((1, lab.size), jnp.int32),),
        in_specs=[
            const(lab.shape),
            const(landed.shape),
            pl.BlockSpec(memory_space=pl.ANY),
        ] + [const(x) for x in (line, line, column, column)],
        out_specs=tuple(const(x) for x in (whole, line, line, column, column, (1, lab.size))),
        scratch_shapes=[
            pltpu.VMEM((steps, NW * ABLK, 2 * PART), BF16),
            pltpu.SemaphoreType.DMA((steps,)),
            pltpu.VMEM((NPATCH, NW * ABLK), BF16),
            pltpu.VMEM((NPATCH, PART), F32),
            pltpu.VMEM((NPATCH, PART), F32),
            pltpu.VMEM((GROUPS, BPX * TILE, LANES), F32),
            pltpu.VMEM((GROUPS, BPX * TILE, LANES), F32),
        ],
        compiler_params=params(),
        cost_estimate=pl.CostEstimate(
            flops=2 * NPATCH * NW * ABLK * PATCH * PATCH, bytes_accessed=12 << 20, transcendentals=0
        ),
        name="pressure",
    )(lab, landed, weights, *edges)


def border_places(rows, cols):
    middle = pl.ds(LANES, cols - 2 * LANES)
    return (
        (slice(None), pl.ds(0, LANES)),
        (slice(None), pl.ds(cols - LANES, LANES)),
        (pl.ds(0, TILE), middle),
        (pl.ds(rows - TILE, TILE), middle),
    )


def border_additions(halos, edges, edge, sides, ends):
    up_ref, dn_ref, lh_ref, rh_ref = halos
    top_ref, bottom_ref, left_ref, right_ref = edges

    def cells(ref):
        return derived(ref[0:1, :], ref[1:2, :], ref[2:3, :])

    pull = TIME_STEP * PRESS * 0.5
    step = 0.5 * DT_DX
    for out, turned in ((edge, along_y), (ends, along_x)):
        out[...] = jnp.zeros_like(out)
        far_low, far_high, own_low, own_high = (
            (lh_ref, rh_ref, left_ref, right_ref) if out is edge
            else (up_ref, dn_ref, top_ref, bottom_ref)
        )
        for at, before, after, own, far, sign in (
            (0, far_low, own_low, own_low, far_low, 1.0),
            (3, own_high, far_high, own_high, far_high, -1.0),
        ):
            gh, gn, gt = flux(turned(cells(before)), turned(cells(after)))
            wet = own[0:1, :] > 0.0
            normal = gn * step + (pull * own[0:1, :]) * far[3:4, :]
            pair = (gt * step, normal) if out is edge else (normal, gt * step)
            for f, val in enumerate((gh * step,) + pair):
                out[at + f:at + f + 1, :] = jnp.where(wet, sign * val, 0.0)
    blank = jnp.zeros((LANES - TILE, LANES), F32)
    for b in range(sides.shape[0] // LANES):
        cut = slice(b * LANES, (b + 1) * LANES)
        sides[cut, :] = jnp.concatenate([edge[:, cut], blank], axis=0).T


def patch_border(parts, sides, ends):
    first, last, head, tail = parts
    rows = first.shape[0]
    cols = ends.shape[1]
    lane = iota((rows, LANES), 1)
    values = sides[...]
    first[...] += jnp.where(lane == 0, values, 0.0)
    last[...] += jnp.where(lane == LANES - 1, pltpu.roll(values, LANES - 4, 1), 0.0)
    for at, line in ((0, 0), (rows - 1, 3)):
        first[at:at + 1, :] += ends[line:line + 1, 0:LANES]
        last[at:at + 1, :] += ends[line:line + 1, cols - LANES:cols]
    head[0:1, :] += ends[0:1, LANES:cols - LANES]
    tail[TILE - 1:TILE, :] += ends[3:4, LANES:cols - LANES]


def finish_kernel(
    lab_ref, landed_ref, w_ref, p_ref, up_ref, dn_ref, lh_ref, rh_ref,
    top_ref, bottom_ref, left_ref, right_ref, old_ref,
    hu_ref, hv_ref, h_ref, ox_ref, oy_ref, new_ref,
    held, arrived, left, acc, acc2, fx, fy, fx2, fy2,
    edge, sides_ref, ends_ref, first, last, head, tail, loaded, saved,
):
    step = pl.program_id(0)
    take = weight_parts(step, w_ref, held, arrived)
    parts = (first, last, head, tail)
    places = border_places(*old_ref.shape)
    loads = [
        pltpu.make_async_copy(old_ref.at[at], part, loaded.at[n])
        for n, (at, part) in enumerate(zip(places, parts))
    ]
    saves = [
        pltpu.make_async_copy(part, new_ref.at[at], saved.at[n])
        for n, (at, part) in enumerate(zip(places, parts))
    ]

    @pl.when(step == 0)
    def _():
        for copy in loads:
            copy.start()
        border_additions(
            (up_ref, dn_ref, lh_ref, rh_ref), (top_ref, bottom_ref, left_ref, right_ref),
            edge, sides_ref, ends_ref,
        )
        stack_left(left, summed_of(lab_ref[...], landed_ref[...]), 2)

    take()
    acc[...] = jnp.dot(left[...], held[step, :, :PART], preferred_element_type=F32)
    acc2[...] = jnp.dot(left[...], held[step, :, PART:], preferred_element_type=F32)
    lane = iota((TILE, LANES), 1)
    for part, (src, mx, my) in enumerate(((acc, fx, fy), (acc2, fx2, fy2))):
        spread_rows(src, mx, 0)
        spread_rows(src, my, 1)
        cells = slice(part * TILE, (part + 1) * TILE)
        for r in range(BPX):
            at = slice(r * TILE, (r + 1) * TILE)
            mark = pl.multiple_of(r * PATCH + (2 * step + part) * TILE, TILE)
            base = pl.multiple_of(mark + TILE, TILE)
            ends = sides_ref[pl.ds(mark, TILE), :]
            tiles = [p_ref[g, pl.ds(base, TILE), :] for g in range(GROUPS)]
            for g in range(GROUPS):
                before = tiles[g - 1] if g else 0.0
                after = tiles[g + 1] if g < GROUPS - 1 else 0.0
                prev = pltpu.roll(jnp.where(lane == LANES - 1, before, tiles[g]), 1, 1)
                nxt = pltpu.roll(jnp.where(lane == 0, after, tiles[g]), LANES - 1, 1)
                h = h_ref[g, r, cells, :]
                wet = h > 0.0
                scale = (TIME_STEP * PRESS * 0.5) * h
                gx = p_ref[g, pl.ds(base + 1, TILE), :] - p_ref[g, pl.ds(base - 1, TILE), :]
                wx = mx[g, at, :]
                wy = my[g, at, :]
                power = wx * wx + wy * wy
                speed = jnp.where(power > 0.0, power * lax.rsqrt(power), 0.0) * (TIME_STEP * STRESS)
                new = [
                    hu_ref[g, r, cells, :] - scale * gx + speed * wx,
                    hv_ref[g, r, cells, :] - scale * (nxt - prev) + speed * wy,
                ]
                for own, edge, shift in ((0, 0, 1), (GROUPS - 1, LANES - 1, 4)):
                    if g == own:
                        new = [
                            jnp.where(
                                lane == edge,
                                a + pltpu.roll(ends, (edge - shift - f) % LANES, 1),
                                a,
                            )
                            for f, a in enumerate(new)
                        ]
                cut = slice(g * LANES, (g + 1) * LANES)
                ox_ref[r, cells, cut] = jnp.where(wet, new[0], 0.0)
                oy_ref[r, cells, cut] = jnp.where(wet, new[1], 0.0)

    @pl.when(step == 1)
    def _():
        for copy in loads:
            copy.wait()
        patch_border(parts, sides_ref, ends_ref)
        for copy in saves:
            copy.start()

    @pl.when(step == 0)
    def _():
        ox_ref[0, 0:1, :] += ends_ref[1:2, :]
        oy_ref[0, 0:1, :] += ends_ref[2:3, :]

    @pl.when(step == pl.num_programs(0) - 1)
    def _():
        deep = ox_ref.shape[1]
        ox_ref[BPX - 1, deep - 1:deep, :] += ends_ref[4:5, :]
        oy_ref[BPX - 1, deep - 1:deep, :] += ends_ref[5:6, :]
        for copy in saves:
            copy.wait()


def finish(lab, landed, weights, p, halos, edges, newh, hu, hv, h):
    deep = 2 * TILE
    steps = PATCH // deep
    cols = BPY * PATCH
    split = (GROUPS, BPX, PATCH, LANES)
    slab = pl.BlockSpec((GROUPS, BPX, deep, LANES), lambda i: (0, 0, i, 0))
    out = pl.BlockSpec((BPX, deep, cols), lambda i: (0, i, 0))
    shape = jax.ShapeDtypeStruct((BPX, PATCH, cols), F32)
    rows = newh.shape[0]
    whole = pl.BlockSpec(memory_space=pl.ANY)
    field = pltpu.VMEM((GROUPS, BPX * TILE, LANES), F32)

    def const(x):
        return pl.BlockSpec(x.shape, lambda i: (0,) * x.ndim)

    return pl.pallas_call(
        finish_kernel,
        grid=(steps,),
        out_shape=(shape, shape, jax.ShapeDtypeStruct(newh.shape, F32)),
        in_specs=[
            const(lab), const(landed),
            whole,
            const(p), *[const(x) for x in (*halos, *edges)], whole,
            slab, slab, slab,
        ],
        out_specs=(out, out, whole),
        input_output_aliases={12: 2},
        scratch_shapes=[
            pltpu.VMEM((steps, NW * ABLK, 2 * PART), BF16),
            pltpu.SemaphoreType.DMA((steps,)),
            pltpu.VMEM((2 * NPATCH, NW * ABLK), BF16),
            pltpu.VMEM((2 * NPATCH, PART), F32),
            pltpu.VMEM((2 * NPATCH, PART), F32),
            field, field, field, field,
            pltpu.VMEM((TILE, rows), F32),
            pltpu.VMEM((rows, LANES), F32),
            pltpu.VMEM((TILE, cols), F32),
            pltpu.VMEM((rows, LANES), F32),
            pltpu.VMEM((rows, LANES), F32),
            pltpu.VMEM((TILE, cols - 2 * LANES), F32),
            pltpu.VMEM((TILE, cols - 2 * LANES), F32),
            pltpu.SemaphoreType.DMA((4,)),
            pltpu.SemaphoreType.DMA((4,)),
        ],
        compiler_params=params(48 << 20),
        cost_estimate=pl.CostEstimate(
            flops=4 * NPATCH * NW * ABLK * PATCH * PATCH, bytes_accessed=20 << 20, transcendentals=0
        ),
        name="finish",
    )(
        lab, landed, weights, p, *halos, *edges, newh,
        hu.reshape(split), hv.reshape(split), h.reshape(split),
    )


def body(
    atm_blocks,
    remap_weights,
    ovl_source,
    ovl_block,
    ovl_patch,
    ovl_weight,
    depth_field,
    wet_mask,
    mom_x,
    mom_y,
    blend,
):
    count_x = lax.axis_size("gx")
    count_y = lax.axis_size("gy")
    devices = count_x * count_y
    entries = ovl_source.size
    capacity = 2 * entries // devices
    slots = devices * capacity
    atm = atm_blocks.reshape(atm_blocks.shape[2:]).transpose(1, 0, 2)
    both = ("gx", "gy")
    want, lab = make_requests(
        ovl_source.reshape(1, entries), ovl_block.reshape(1, entries),
        ovl_patch.reshape(1, entries), ovl_weight.reshape(1, entries), devices, capacity,
    )
    asked = lax.all_to_all(
        want.reshape(devices, 1, capacity), both, split_axis=0, concat_axis=0, tiled=True
    )
    press, wind = mix(blend.reshape(1), atm)
    top, bottom, left, right, placed = edge_cells(depth_field, wet_mask, mom_x, mom_y)

    def exchange(after, tiles):
        rows = serve(after, asked, tiles)
        parts = rows.reshape(devices, capacity, rows.shape[1])
        got = lax.all_to_all(parts, both, split_axis=0, concat_axis=0, tiled=True)
        return got.reshape(rows.shape)

    press = exchange(placed, press)
    fields = (depth_field, wet_mask, mom_x, mom_y)
    bands = depth_field.shape[0] // BAND
    ahead = bands * 5 // 8
    *planes, token = stencil(fields, lab, 0, ahead)
    wind = exchange(token, wind)
    weights = remap_weights.reshape(NW * ABLK, PATCH * PATCH)
    p, *edges, lab = pressure_field(lab, press, weights, (top, bottom, left, right))
    top, bottom, left, right = edges
    halos = (
        send(bottom, "gx", 1), send(top, "gx", -1), send(right, "gy", 1), send(left, "gy", -1),
    )
    newh, hu, hv, h, _ = stencil(fields, top, ahead, bands - ahead, planes)
    new_x, new_y, newh = finish(lab, wind, weights, p, halos, edges, newh, hu, hv, h)
    return (newh, new_x.reshape(newh.shape), new_y.reshape(newh.shape))


def solution(mesh):
    placed = (
        P("gx", "gy", None, None, None),
        P(),
        P("gx", "gy", None, None),
        P("gx", "gy", None),
        P("gx", "gy", None),
        P("gx", "gy", None),
        P("gx", "gy"),
        P("gx", "gy"),
        P("gx", "gy"),
        P("gx", "gy"),
        P(),
    )
    return jax.shard_map(
        body,
        mesh=mesh,
        in_specs=placed,
        out_specs=(P("gx", "gy"), P("gx", "gy"), P("gx", "gy")),
        check_vma=False,
    )
```
